32 devices in a mesh: wide: 4 (over x, core), narrow: 8 (over z, y).
Axes of the slice: x: 2, y: 2, z: 4, core: 2. Of those that a mesh axis runs over, the one named last changes fastest.
Arguments:
- block_input: bfloat16 [8, 1024, 1024], P('wide'), may hold values from -6 to 6
- output_cotangent: bfloat16 [8, 1024, 1024], P('wide'), may hold values from -8 to 8
- loss_weight: float32 [8, 1024], P('wide'), may hold values from 0.25 to 5.25, as said below
- segments: int32 [8, 1024], P('wide'), may hold values from 0 to 5, never falling along the last dimension, each value on 1 to 512 neighbouring positions
- nbr_keys: bfloat16 [8, 1024, 1024, 128], P('wide', None, 'narrow'), may hold values from -0.375 to 0.375
- nbr_count: int32 [8, 1024], P('wide'), may hold values from 1 to 128, as said below
- nbr_ids: int32 [8, 1024, 128], P('wide'), may hold values from 0 to 249999
- targets: int32 [8, 1024], P('wide'), may hold values from 0 to 249999
- base_prob: float32 [8, 1024], P('wide'), may hold values from 0.001 to 0.05
- w_query: bfloat16 [1024, 1024], P('narrow'), may hold values from -0.1875 to 0.1875
- w_key: bfloat16 [1024, 1024], P('narrow'), may hold values from -0.1875 to 0.1875
- w_value: bfloat16 [1024, 1024], P('narrow'), may hold values from -0.1875 to 0.1875
- w_proj: bfloat16 [1024, 1024], P('narrow'), may hold values from -0.75 to 0.75
- w_in: bfloat16 [1024, 4096], P(None, 'narrow'), may hold values from -0.1875 to 0.1875
- w_out: bfloat16 [4096, 1024], P('narrow'), may hold values from -0.125 to 0.125
- gain_attn: float32 [1024], replicated, may hold values from 0.5 to 1.5
- gain_ffn: float32 [1024], replicated, may hold values from 0.5 to 1.5
- gain_key: float32 [1024], replicated, may hold values from 0.5 to 1.5
- temper: float32 [1], replicated, may hold values from 1 to 4
- mix_weight: float32 [1], replicated, may hold values from 0.2 to 0.8
Outputs:
- block_output: bfloat16 [8, 1024, 1024], P('wide')
- token_loss: float32 [8, 1024], P('wide')
- grad_input: float32 [8, 1024, 1024], P('wide')
- grad_w_query: float32 [1024, 1024], P('narrow', 'wide')
- grad_w_key: float32 [1024, 1024], P('narrow', 'wide')
- grad_w_value: float32 [1024, 1024], P('narrow', 'wide')
- grad_w_proj: float32 [1024, 1024], P('narrow', 'wide')
- grad_w_in: float32 [1024, 4096], P('wide', 'narrow')
- grad_w_out: float32 [4096, 1024], P('narrow', 'wide')
- grad_gain_attn: float32 [1024], P('wide')
- grad_gain_ffn: float32 [1024], P('wide')
- grad_gain_key: float32 [1024], P('wide')
- grad_temper: float32 [1], replicated
- grad_mix_weight: float32 [1], replicated
The draws below stay inside these ranges and needn't reach their ends.
Inputs may be any that keep to these rules, and one draw needn't show every extreme that they name: `nbr_count`: every token has 1 to 128 valid neighbours; some token has 128, some 1. `loss_weight`: Positive.
All inputs are finite; a program needn't handle non-finite values.
Results may differ from the reference program's by a relative error of at most 0.013.
Values may be sent and summed in bfloat16 or wider, within the bound.
A program may use at most 256 MiB of HBM per device.

```python
import math
import jax
import jax.numpy as jnp
import numpy as np
from jax import lax

D = 1024
HEADS = 16
HD = 64
FF = 4096
VOCAB = 267744
NBR = 128
LEN = 1024
SEQS = 8


def id_tables(key):
    base_key = jax.random.fold_in(key, 17)
    key_first, key_second, key_third = jax.random.split(base_key, 3)
    id_limit = min(VOCAB, 250000)
    target_ids = jax.random.randint(key_first, (SEQS, LEN), 0, id_limit, dtype=jnp.int32)
    target_ids = target_ids.at[0, 0].set(id_limit - 1)
    others = jax.random.randint(key_second, (SEQS, LEN, NBR), 0, id_limit, dtype=jnp.int32)
    others = others.at[0, 0, 1].set(id_limit - 1).at[0, 0, 2].set(0)
    chosen = jax.random.randint(key_third, (SEQS, LEN, NBR), 0, 3, dtype=jnp.int32) == 0
    return (target_ids.at[0, 1].set(0), jnp.where(chosen, target_ids[:, :, None], others))


def draw_targets(key, part):
    return id_tables(key)[0]


def draw_nbr_ids(key, part):
    return id_tables(key)[1]


def draw_nbr_count(key, part):
    counts = jax.random.randint(jax.random.fold_in(key, 29), (SEQS, LEN), 1, NBR + 1, dtype=jnp.int32)
    return counts.at[:, 0].set(NBR).at[:, 1].set(1)


def draw_loss_weight(key, part):
    values = jax.random.uniform(jax.random.fold_in(key, 31), (SEQS, LEN), jnp.float32, 0.5, 1.5)
    growth = 1.0 + 2.0 * jnp.arange(SEQS, dtype=jnp.float32)[:, None] / max(SEQS - 1, 1)
    return values * growth


def spiked(values, stream_key, source, target, parts, factor):
    owner, partner = [(jnp.arange(values.shape[position]) // (values.shape[position] // parts)).reshape([-1 if axis == position else 1 for axis in range(values.ndim)]) for position in (source, target)]
    chosen = jax.random.permutation(stream_key, parts)[partner]
    strong = (owner == chosen) | (owner == (partner + parts // 2) % parts)
    return jnp.where(strong, factor * values, values)


def levels(rng, shape, cuts, least, top_value):
    def one(dim, blocks):
        draws = jax.random.uniform(jax.random.fold_in(jax.random.fold_in(rng, 6), dim), (blocks,), jnp.float32, least / len(cuts), top_value / len(cuts))
        return jnp.repeat(jnp.exp(draws), shape[dim] // blocks).reshape((-1,) + (1,) * (len(shape) - dim - 1))

    level = one(*cuts[0])
    for cut in cuts[1:]:
        level = level * one(*cut)
    return level


def length_profile(number_of, total, limit, slope):
    loads = [(1 << 20) // math.isqrt(rank ** slope) + 1 for rank in range(2, number_of + 1)]
    spare, given = total - limit - (number_of - 1), [1] * (number_of - 1)
    while spare > 0:
        movable = [i for i in range(number_of - 1) if given[i] < limit]
        mass, budget = sum([loads[i] for i in movable]), spare
        for i in movable:
            extra = min(limit - given[i], max(1, budget * loads[i] // mass), spare)
            given[i] = given[i] + extra
            spare = spare - extra
    return np.array([limit] + given)


def uneven_parts(stream_key, amount, total, reach, slope):
    if amount == 2:
        one = jax.random.randint(stream_key, (), max(1, total - reach), min(reach, total - 1) + 1)
        return jnp.stack([one, total - one])
    sizes = jnp.asarray(length_profile(amount, total, reach, slope), jnp.int32)
    twos = (amount - 1) // 2
    donor, taker = sizes[1:1 + 2 * twos:2], sizes[2:2 + 2 * twos:2]
    slack = jnp.minimum(donor - 1, reach - taker)
    moved = jax.random.randint(jax.random.fold_in(stream_key, 1), (twos,), 0, 1 << 20) % (slack + 1)
    sizes = sizes.at[1:1 + 2 * twos:2].set(donor - moved).at[2:2 + 2 * twos:2].set(taker + moved)
    return sizes[jax.random.permutation(jax.random.fold_in(stream_key, 2), amount)]


def normal_values(stream_key, dims, deviation, most, cuts=(), held_as=jnp.bfloat16):
    entries = deviation * jax.random.normal(stream_key, dims, jnp.float32)
    if cuts:
        entries = entries * levels(stream_key, dims, cuts, -0.22, 0.18)
    return jnp.clip(entries, -most, most).astype(held_as)


def heavy_noise(key, extent, scale, limit, pieces, heavy, kind=jnp.bfloat16):
    array = scale * jax.random.normal(key, extent, jnp.float32)
    if pieces:
        array = array * levels(key, extent, pieces, -0.22, 0.18)
    return jnp.clip(spiked(array, jax.random.fold_in(key, 3), *heavy), -limit, limit).astype(kind)


def setup_inputs(seed: int = 0) -> dict:
    arg_keys = jax.random.split(jax.random.key(seed), 21)
    block_input = normal_values(arg_keys[0], (SEQS, LEN, D), 1.0, 6.0, ((0, 4),))
    output_cotangent = heavy_noise(arg_keys[1], (SEQS, LEN, D), 1.0, 8.0, ((0, 4),), (0, 2, 4, 2.0))
    loss_weight = draw_loss_weight(jax.random.fold_in(arg_keys[20], 71), 0)
    segments = jax.vmap(lambda own: jnp.searchsorted(jnp.cumsum(uneven_parts(own, 6, LEN, LEN // 2, 2)), jnp.arange(LEN), side="right"))(jax.random.split(arg_keys[3], SEQS)).reshape((SEQS, LEN)).astype(jnp.int32)
    nbr_keys = normal_values(arg_keys[4], (SEQS, LEN, D, NBR), 0.0625, 0.375, ((0, 4), (2, 8)))
    nbr_count = draw_nbr_count(jax.random.fold_in(arg_keys[20], 71), 0)
    nbr_ids = draw_nbr_ids(jax.random.fold_in(arg_keys[20], 71), 0)
    targets = draw_targets(jax.random.fold_in(arg_keys[20], 71), 0)
    base_prob = jnp.clip(jnp.exp(math.log(0.05) - 3.912023 * jax.random.uniform(arg_keys[8], (SEQS, LEN), jnp.float32) ** levels(arg_keys[8], (SEQS, LEN), ((0, 4),), -0.2, 0.2)), 0.001, 0.05)
    w_query = normal_values(arg_keys[9], (D, D), D ** -0.5, 0.1875, ((0, 8),))
    w_key = normal_values(arg_keys[10], (D, D), D ** -0.5, 0.1875, ((0, 8),))
    w_value = normal_values(arg_keys[11], (D, D), D ** -0.5, 0.1875, ((0, 8),))
    w_proj = normal_values(arg_keys[12], (D, D), (D // 16) ** -0.5, 0.75, ((0, 8),))
    w_in = normal_values(arg_keys[13], (D, FF), D ** -0.5, 0.1875, ((1, 8),))
    w_out = normal_values(arg_keys[14], (FF, D), (FF // 2) ** -0.5, 0.125, ((0, 8),))
    gain_attn = jnp.clip(1.0 + 0.1 * jax.random.normal(arg_keys[15], (D,), jnp.float32), 0.5, 1.5)
    gain_ffn = jnp.clip(1.0 + 0.1 * jax.random.normal(arg_keys[16], (D,), jnp.float32), 0.5, 1.5)
    gain_key = jnp.clip(1.0 + 0.1 * jax.random.normal(arg_keys[17], (D,), jnp.float32), 0.5, 1.5)
    temper = jnp.clip(jnp.exp(jax.random.uniform(arg_keys[18], (1,), jnp.float32, math.log(1.0), math.log(4.0))), 1.0, 4.0)
    mix_weight = jnp.clip(jax.random.uniform(arg_keys[19], (1,), jnp.float32, 0.2, 0.8), 0.2, 0.8)
    return {"block_input": block_input, "output_cotangent": output_cotangent, "loss_weight": loss_weight, "segments": segments, "nbr_keys": nbr_keys, "nbr_count": nbr_count, "nbr_ids": nbr_ids, "targets": targets, "base_prob": base_prob, "w_query": w_query, "w_key": w_key, "w_value": w_value, "w_proj": w_proj, "w_in": w_in, "w_out": w_out, "gain_attn": gain_attn, "gain_ffn": gain_ffn, "gain_key": gain_key, "temper": temper, "mix_weight": mix_weight}


@jax.custom_vjp
def low(v):
    return lax.optimization_barrier(v.astype(jnp.bfloat16)).astype(jnp.float32)

@jax.custom_vjp
def low_back(v):
    return v

def low_keep(v):
    return (low(v), None)

def low_pass(kept, grad):
    return (grad,)

def back_keep(v):
    return (v, None)

def back_low(kept, grad):
    return (low(grad),)
low.defvjp(low_keep, low_pass)
low_back.defvjp(back_keep, back_low)
EPSILON = 1e-05

def matmul_high(left, right):
    return jnp.dot(left, right, precision=lax.Precision.HIGHEST)

def layer_norm(values, gain):
    centred = values - lax.optimization_barrier(jnp.mean(values, axis=-1, keepdims=True))
    variance = lax.optimization_barrier(jnp.mean(centred * centred, axis=-1, keepdims=True))
    return centred * lax.rsqrt(variance + EPSILON) * gain

def attention_seq(normed, w_query, w_key, w_value, segment_ids):
    scale = HD ** (-0.5)
    queries = low(low_back(matmul_high(normed, w_query.T) * scale))
    keys_attn = low(low_back(matmul_high(normed, w_key.T)))
    values_attn = low(low_back(matmul_high(normed, w_value.T)))
    query_heads = queries.reshape(LEN, HEADS, HD).transpose(1, 0, 2)
    key_heads = keys_attn.reshape(LEN, HEADS, HD).transpose(1, 0, 2)
    value_heads = values_attn.reshape(LEN, HEADS, HD).transpose(1, 0, 2)
    q_rows = min(512, LEN)
    n_blocks = LEN // q_rows
    query_blocks = query_heads.reshape(HEADS, n_blocks, q_rows, HD).transpose(1, 0, 2, 3)
    row_starts = jnp.arange(n_blocks, dtype=jnp.int32) * q_rows
    key_pos = jnp.arange(LEN, dtype=jnp.int32)

    def attend(block_item):
        query_block, row_start = block_item
        query_pos = row_start + jnp.arange(q_rows, dtype=jnp.int32)
        query_segs = lax.dynamic_slice_in_dim(segment_ids, row_start, q_rows)
        scores = jnp.einsum('hqd,hkd->hqk', query_block, key_heads, precision=lax.Precision.HIGHEST)
        scores = low_back(scores)
        allowed = (key_pos[None, :] <= query_pos[:, None]) & (segment_ids[None, :] == query_segs[:, None])
        scores = jnp.where(allowed[None], scores, -1e+30)
        peak = lax.optimization_barrier(jnp.max(scores, axis=-1, keepdims=True))
        expo = jnp.exp(scores - peak)
        probs = low(expo / lax.optimization_barrier(jnp.sum(expo, axis=-1, keepdims=True)))
        return jnp.einsum('hqk,hkd->hqd', probs, value_heads, precision=lax.Precision.HIGHEST)
    mixed = lax.map(jax.checkpoint(attend), (query_blocks, row_starts))
    mixed = mixed.transpose(1, 0, 2, 3).reshape(HEADS, LEN, HD).transpose(1, 0, 2)
    return mixed.reshape(LEN, HEADS * HD)

def sequence_forward(params, inputs, segment_ids, neighbour_keys, key_norms, valid_count, neighbour_ids, target_ids, base_values):
    w_query, w_key, w_value, w_proj, w_in, w_out, gain_attn, gain_ffn, gain_key, temper, mix_weight = params
    normed_one = low(layer_norm(inputs, gain_attn))
    attended = low(low_back(attention_seq(normed_one, w_query, w_key, w_value, segment_ids)))
    branch = low_back(matmul_high(attended, w_proj))
    hidden_one = inputs + branch
    normed_two = low(layer_norm(hidden_one, gain_ffn))
    pre_act = low_back(matmul_high(normed_two, w_in))
    activated = low(jax.nn.gelu(pre_act, approximate=True))
    ffn_branch = low_back(matmul_high(activated, w_out))
    hidden_two = hidden_one + ffn_branch
    query_key = low(layer_norm(hidden_two, gain_key))
    k_rows = min(256, LEN)
    k_blocks = LEN // k_rows

    def inner(block_item):
        query_rows, key_rows = block_item
        return jnp.einsum('td,tdj->tj', query_rows, key_rows.astype(jnp.float32), precision=lax.Precision.HIGHEST)
    products = lax.map(jax.checkpoint(inner), (query_key.reshape(k_blocks, k_rows, D), neighbour_keys.reshape(k_blocks, k_rows, D, NBR)))
    products = low_back(products.reshape(LEN, NBR))
    logits = (2.0 * products - key_norms) / temper[0]
    live = jnp.arange(NBR, dtype=jnp.int32)[None, :] < valid_count[:, None]
    logits = jnp.where(live, logits, -1e+30)
    peak = lax.optimization_barrier(jnp.max(logits, axis=-1, keepdims=True))
    expo = jnp.exp(logits - peak)
    weights = expo / lax.optimization_barrier(jnp.sum(expo, axis=-1, keepdims=True))
    matches = (neighbour_ids == target_ids[:, None]).astype(jnp.float32)
    knn_prob = lax.optimization_barrier(jnp.sum(weights * matches, axis=-1))
    mixture = mix_weight[0] * knn_prob + (1.0 - mix_weight[0]) * base_values
    return (hidden_two, -jnp.log(mixture))

def reference(block_input, output_cotangent, loss_weight, segments, nbr_keys, nbr_count, nbr_ids, targets, base_prob, w_query, w_key, w_value, w_proj, w_in, w_out, gain_attn, gain_ffn, gain_key, temper, mix_weight):
    params = tuple((param.astype(jnp.float32) for param in (w_query, w_key, w_value, w_proj, w_in, w_out, gain_attn, gain_ffn, gain_key, temper, mix_weight)))

    def one_sequence(grad_sums, seq_item):
        seq_input, seq_cot, seq_weight, seq_segs, seq_keys, seq_count, seq_ids, seq_targets, seq_base = seq_item
        key_norms = lax.optimization_barrier(jnp.sum(jnp.square(seq_keys.astype(jnp.float32)), axis=-2))

        def forward(param_set, inputs):
            return sequence_forward(param_set, inputs, seq_segs, seq_keys, key_norms, seq_count, seq_ids, seq_targets, seq_base)
        (hidden_two, loss_seq), pull = jax.vjp(forward, params, seq_input.astype(jnp.float32))
        grad_params, grad_seq_input = pull((seq_cot.astype(jnp.float32), seq_weight))
        grad_sums = tuple((accum + fresh for accum, fresh in zip(grad_sums, grad_params)))
        return (grad_sums, (hidden_two.astype(jnp.bfloat16), loss_seq, grad_seq_input))
    zero_sums = tuple((jnp.zeros_like(param) for param in params))
    grad_sums, (outputs, loss_all, grad_inputs) = lax.scan(one_sequence, zero_sums, (block_input, output_cotangent, loss_weight, segments, nbr_keys, nbr_count, nbr_ids, targets, base_prob))
    return (outputs, loss_all, grad_inputs, grad_sums[0], grad_sums[1], grad_sums[2], grad_sums[3], grad_sums[4], grad_sums[5], grad_sums[6], grad_sums[7], grad_sums[8], grad_sums[9], grad_sums[10])
```

```python
import functools

import jax
import jax.numpy as jnp
from jax import lax
from jax.experimental import pallas as pl
from jax.experimental.pallas import tpu as pltpu
from jax.sharding import PartitionSpec as P

HD = 64
EPSILON = 1e-05
F32 = jnp.float32
BF16 = jnp.bfloat16
MESH = pl.DeviceIdType.MESH
J = 128
KEPT_BYTES = 44 * 2**20


def product(left, right):
    return jnp.dot(left, right, preferred_element_type=F32)


def through_t(grads, weight):
    return lax.dot_general(grads, weight, (((1,), (1,)), ((), ())), preferred_element_type=F32)


def outer_sum(left, right):
    return jnp.einsum("ta,tb->ab", left, right, preferred_element_type=F32)


def norm_parts(values):
    centred = values - jnp.mean(values, axis=-1, keepdims=True)
    inverse = lax.rsqrt(jnp.mean(centred * centred, axis=-1, keepdims=True) + EPSILON)
    return (centred * inverse, inverse)


def norm_back(grad_out, normed, inverse, gain):
    scaled = grad_out * gain
    grad_in = inverse * (
        scaled
        - jnp.mean(scaled, axis=-1, keepdims=True)
        - normed * jnp.mean(scaled * normed, axis=-1, keepdims=True)
    )
    return (grad_in, jnp.sum(grad_out * normed, axis=0))


def gelu_tanh(values):
    return jax.nn.gelu(values, approximate=True)


def gather_weight(shard):
    wide, nar = lax.axis_size("wide"), lax.axis_size("narrow")
    rows = shard.shape[0] // wide
    own = lax.dynamic_slice_in_dim(shard, lax.axis_index("wide") * rows, rows, 0)
    full = lax.all_gather(own, ("narrow", "wide"), axis=0, tiled=True)
    return full.reshape(nar, shard.shape[0], shard.shape[1])


def normalise(values):
    centred = values - jnp.mean(values, axis=-1, keepdims=True)
    inverse = lax.rsqrt(jnp.mean(centred * centred, axis=-1, keepdims=True) + EPSILON)
    return centred * inverse, inverse


def normalise_back(grad_out, normed, inverse, gain):
    scaled = grad_out * gain
    return inverse * (
        scaled
        - jnp.mean(scaled, axis=-1, keepdims=True)
        - normed * jnp.mean(scaled * normed, axis=-1, keepdims=True)
    )


def head_lanes(values, head):
    lanes = lax.broadcasted_iota(jnp.int32, values.shape, 1)
    return jnp.where(lanes // HD == head, values, jnp.zeros_like(values))


def allowed_keys(col_ref, row_ref, start, count, keys):
    query_segment = col_ref[pl.ds(start, count), 0:1]
    key_segment = row_ref[0, 0:1, 0:keys]
    spot = lax.broadcasted_iota(jnp.int32, (count, keys), 1)
    own = lax.broadcasted_iota(jnp.int32, (count, keys), 0) + start
    return (spot <= own) & (query_segment == key_segment)


def attend_kernel(heads, block, qkv_ref, col_ref, row_ref, out_ref, lse_ref):
    length = qkv_ref.shape[0]
    width = heads * HD
    for start in range(0, length, block):
        keys = start + block
        allowed = allowed_keys(col_ref, row_ref, start, block, keys)
        query = qkv_ref[start : start + block, 0:width]
        key = qkv_ref[0:keys, width : 2 * width]
        value = qkv_ref[0:keys, 2 * width : 3 * width]
        total = jnp.zeros((block, width), F32)
        for head in range(heads):
            scores = lax.dot_general(
                head_lanes(query, head), key, (((1,), (1,)), ((), ())), preferred_element_type=F32
            )
            scores = jnp.where(allowed, scores, -1e30)
            peak = jnp.max(scores, axis=-1, keepdims=True)
            expo = jnp.exp(scores - peak)
            sums = jnp.sum(expo, axis=-1, keepdims=True)
            out = jnp.dot(expo.astype(BF16), value, preferred_element_type=F32) / sums
            total = total + head_lanes(out, head)
            lse_ref[start : start + block, head : head + 1] = peak + jnp.log(sums)
        out_ref[start : start + block, :] = total.astype(BF16)


def attend(qkv, columns, row_form, seqs, heads):
    rows, wide = qkv.shape
    length = rows // seqs
    width = wide // 3
    return pl.pallas_call(
        functools.partial(attend_kernel, heads, min(256, length)),
        grid=(seqs,),
        out_shape=(
            jax.ShapeDtypeStruct((rows, width), BF16),
            jax.ShapeDtypeStruct((rows, heads), F32),
        ),
        in_specs=[
            pl.BlockSpec((length, wide), lambda s: (s, 0)),
            pl.BlockSpec((length, 1), lambda s: (s, 0)),
            pl.BlockSpec((1, 1, length), lambda s: (s, 0, 0)),
        ],
        out_specs=(
            pl.BlockSpec((length, width), lambda s: (s, 0)),
            pl.BlockSpec((length, heads), lambda s: (s, 0)),
        ),
        compiler_params=pltpu.CompilerParams(vmem_limit_bytes=40 * 2**20),
    )(qkv, columns, row_form)


def attend_back_kernel(
    heads, block, qkv_ref, grad_ref, lse_ref, col_ref, row_ref, out_ref, grad_key, grad_value
):
    length = qkv_ref.shape[0]
    width = heads * HD
    grad_key[...] = jnp.zeros_like(grad_key)
    grad_value[...] = jnp.zeros_like(grad_value)
    across = (((0,), (0,)), ((), ()))
    last = (((1,), (1,)), ((), ()))
    for start in range(0, length, block):
        keys = start + block
        allowed = allowed_keys(col_ref, row_ref, start, block, keys)
        query = qkv_ref[start : start + block, 0:width]
        key = qkv_ref[0:keys, width : 2 * width]
        value = qkv_ref[0:keys, 2 * width : 3 * width]
        grad = grad_ref[start : start + block, :]
        total = jnp.zeros((block, width), F32)
        for head in range(heads):
            own_query = head_lanes(query, head)
            own_grad = head_lanes(grad, head)
            scores = lax.dot_general(own_query, key, last, preferred_element_type=F32)
            probs = jnp.where(
                allowed, jnp.exp(scores - lse_ref[start : start + block, head : head + 1]), 0.0
            )
            grad_probs = lax.dot_general(own_grad, value, last, preferred_element_type=F32)
            delta = jnp.sum(probs * grad_probs, axis=-1, keepdims=True)
            grad_scores = (probs * (grad_probs - delta)).astype(BF16)
            total = total + head_lanes(
                jnp.dot(grad_scores, key, preferred_element_type=F32), head
            )
            grad_key[0:keys, :] += lax.dot_general(
                grad_scores, own_query, across, preferred_element_type=F32
            )
            grad_value[0:keys, :] += lax.dot_general(
                probs.astype(BF16), own_grad, across, preferred_element_type=F32
            )
        out_ref[start : start + block, 0:width] = (total * HD ** (-0.5)).astype(BF16)
    out_ref[:, width : 2 * width] = grad_key[...].astype(BF16)
    out_ref[:, 2 * width : 3 * width] = grad_value[...].astype(BF16)


def attend_back(qkv, grad, lse, columns, row_form, seqs, heads):
    rows, wide = qkv.shape
    length = rows // seqs
    width = wide // 3
    return pl.pallas_call(
        functools.partial(attend_back_kernel, heads, min(256, length)),
        grid=(seqs,),
        out_shape=jax.ShapeDtypeStruct((rows, wide), BF16),
        in_specs=[
            pl.BlockSpec((length, wide), lambda s: (s, 0)),
            pl.BlockSpec((length, width), lambda s: (s, 0)),
            pl.BlockSpec((length, heads), lambda s: (s, 0)),
            pl.BlockSpec((length, 1), lambda s: (s, 0)),
            pl.BlockSpec((1, 1, length), lambda s: (s, 0, 0)),
        ],
        out_specs=pl.BlockSpec((length, wide), lambda s: (s, 0)),
        scratch_shapes=[pltpu.VMEM((length, width), F32)] * 2,
        compiler_params=pltpu.CompilerParams(vmem_limit_bytes=48 * 2**20),
    )(qkv, grad, lse, columns, row_form)


INNER = 0.7978845608028654
CUBIC = 0.044715


def gelu_parts(values):
    tanh = jnp.tanh(INNER * (values + CUBIC * values * values * values))
    return 0.5 * values * (1.0 + tanh), tanh


def ffn_kernel(
    parts,
    att_ref,
    input_ref,
    gains_ref,
    proj_ref,
    bundle_ref,
    one_ref,
    two_ref,
    normed_ref,
    output_ref,
    key_ref,
    pre_ref,
    total,
):
    step = pl.program_id(0)
    nar, tok, local = att_ref.shape
    width = input_ref.shape[1]
    hidden = pre_ref.shape[2]
    piece = width // parts

    @pl.when(step == 0)
    def _():
        branch = input_ref[...].astype(F32)
        for n in range(nar):
            branch = branch + jnp.dot(att_ref[n], proj_ref[n], preferred_element_type=F32)
        one_ref[...] = branch
        total[...] = branch
        normed, _ = normalise(branch)
        normed_ref[...] = (normed * gains_ref[1:2, :]).astype(BF16)

    pre = jnp.zeros((tok, hidden), F32)
    for i in range(parts):
        pre = pre + jnp.dot(
            normed_ref[:, i * piece : (i + 1) * piece],
            bundle_ref[0, 0:piece, i * hidden : (i + 1) * hidden],
            preferred_element_type=F32,
        )
    pre_ref[0] = pre
    activated = gelu_parts(pre)[0].astype(BF16)
    total[...] += jnp.dot(activated, bundle_ref[0, piece:, :], preferred_element_type=F32)

    @pl.when(step == nar - 1)
    def _():
        hidden_two = total[...]
        two_ref[...] = hidden_two
        output_ref[...] = hidden_two.astype(BF16)
        normed, _ = normalise(hidden_two)
        query_key = (normed * gains_ref[2:3, :]).astype(BF16)
        for n in range(nar):
            key_ref[n] = query_key[:, n * (width // nar) : (n + 1) * (width // nar)]


def ffn(att, inputs, gains, bundle, hidden):
    nar, tok, local = att.shape
    width = inputs.shape[1]
    rows = 2 * hidden
    whole = pl.BlockSpec((tok, width), lambda s: (0, 0))
    return pl.pallas_call(
        functools.partial(ffn_kernel, width // hidden),
        grid=(nar,),
        out_shape=(
            jax.ShapeDtypeStruct((tok, width), F32),
            jax.ShapeDtypeStruct((tok, width), F32),
            jax.ShapeDtypeStruct((tok, width), BF16),
            jax.ShapeDtypeStruct((tok, width), BF16),
            jax.ShapeDtypeStruct((nar, tok, width // nar), BF16),
            jax.ShapeDtypeStruct((nar, tok, hidden), F32),
        ),
        in_specs=[
            pl.BlockSpec((nar, tok, local), lambda s: (0, 0, 0)),
            whole,
            pl.BlockSpec((3, width), lambda s: (0, 0)),
            pl.BlockSpec((nar, local, width), lambda s: (0, rows // local, 0)),
            pl.BlockSpec((1, rows, width), lambda s: (s, 0, 0)),
        ],
        out_specs=(
            whole,
            whole,
            whole,
            whole,
            pl.BlockSpec((nar, tok, width // nar), lambda s: (0, 0, 0)),
            pl.BlockSpec((1, tok, hidden), lambda s: (s, 0, 0)),
        ),
        scratch_shapes=[pltpu.VMEM((tok, width), F32)],
        compiler_params=pltpu.CompilerParams(vmem_limit_bytes=48 * 2**20),
    )(att, inputs, gains, bundle, bundle)


def ffn_back_kernel(
    parts,
    slices_ref,
    att_ref,
    cot_ref,
    one_ref,
    two_ref,
    gains_ref,
    pre_ref,
    proj_ref,
    bundle_ref,
    ffn_ref,
    grad_one_ref,
    grad_att_ref,
    proj_part_ref,
    gain_ref,
    grad_two,
    total,
):
    step = pl.program_id(0)
    nar, tok, local = att_ref.shape
    width = cot_ref.shape[1]
    hidden = pre_ref.shape[2]
    piece = width // parts
    last = (((1,), (1,)), ((), ()))

    @pl.when(step == 0)
    def _():
        grad_key = jnp.concatenate([slices_ref[n] for n in range(nar)], axis=1).astype(F32)
        normed, inverse = normalise(two_ref[...])
        gain_ref[1:2, :] = jnp.sum(grad_key * normed, axis=0, keepdims=True)
        grad = cot_ref[...].astype(F32) + normalise_back(
            grad_key, normed, inverse, gains_ref[2:3, :]
        )
        grad_two[...] = grad
        ffn_ref[...] = grad.astype(BF16)
        total[...] = jnp.zeros_like(total)

    pre = pre_ref[0]
    tanh = gelu_parts(pre)[1]
    slope = 0.5 * (1.0 + tanh) + 0.5 * pre * (1.0 - tanh * tanh) * INNER * (
        1.0 + 3.0 * CUBIC * pre * pre
    )
    grad_act = lax.dot_general(
        ffn_ref[...], bundle_ref[0, piece:, :], last, preferred_element_type=F32
    )
    grad_pre = (slope * grad_act).astype(BF16)
    for i in range(parts):
        total[:, i * piece : (i + 1) * piece] += lax.dot_general(
            grad_pre,
            bundle_ref[0, 0:piece, i * hidden : (i + 1) * hidden],
            last,
            preferred_element_type=F32,
        )

    @pl.when(step == nar - 1)
    def _():
        normed, inverse = normalise(one_ref[...])
        gain_ref[0:1, :] = jnp.sum(total[...] * normed, axis=0, keepdims=True)
        grad = grad_two[...] + normalise_back(total[...], normed, inverse, gains_ref[1:2, :])
        grad_one_ref[...] = grad
        branch = grad.astype(BF16)
        for n in range(nar):
            grad_att_ref[n] = lax.dot_general(
                branch, proj_ref[n], last, preferred_element_type=F32
            ).astype(BF16)
            proj_part_ref[n] = lax.dot_general(
                att_ref[n], branch, (((0,), (0,)), ((), ())), preferred_element_type=F32
            ).astype(BF16)


def ffn_back(slices, att, cot, one, two, gains, pre, bundle):
    nar, tok, local = att.shape
    width = cot.shape[1]
    hidden = pre.shape[2]
    rows = 2 * hidden
    whole = pl.BlockSpec((tok, width), lambda s: (0, 0))
    stack = pl.BlockSpec((nar, tok, local), lambda s: (0, 0, 0))
    return pl.pallas_call(
        functools.partial(ffn_back_kernel, width // hidden),
        grid=(nar,),
        out_shape=(
            jax.ShapeDtypeStruct((tok, width), BF16),
            jax.ShapeDtypeStruct((tok, width), F32),
            jax.ShapeDtypeStruct((nar, tok, local), BF16),
            jax.ShapeDtypeStruct((nar, local, width), BF16),
            jax.ShapeDtypeStruct((2, width), F32),
        ),
        in_specs=[
            pl.BlockSpec(slices.shape, lambda s: (0, 0, 0)),
            stack,
            whole,
            whole,
            whole,
            pl.BlockSpec((3, width), lambda s: (0, 0)),
            pl.BlockSpec((1, tok, hidden), lambda s: (s, 0, 0)),
            pl.BlockSpec((nar, local, width), lambda s: (0, rows // local, 0)),
            pl.BlockSpec((1, rows, width), lambda s: (s, 0, 0)),
        ],
        out_specs=(
            whole,
            whole,
            stack,
            pl.BlockSpec((nar, local, width), lambda s: (0, 0, 0)),
            pl.BlockSpec((2, width), lambda s: (0, 0)),
        ),
        scratch_shapes=[pltpu.VMEM((tok, width), F32)] * 2,
        compiler_params=pltpu.CompilerParams(vmem_limit_bytes=48 * 2**20),
    )(slices, att, cot, one, two, gains, pre, bundle, bundle)


def exchange_kernel(nar, in_ref, out_ref, send, recv):
    me = lax.axis_index("narrow")
    greet([{"narrow": lax.rem(me + k, nar)} for k in range(1, nar)])

    def copy(k):
        target = lax.rem(me + k, nar)
        return pltpu.make_async_remote_copy(
            src_ref=in_ref.at[target],
            dst_ref=out_ref.at[me],
            send_sem=send.at[k],
            recv_sem=recv.at[k],
            device_id={"narrow": target},
            device_id_type=MESH,
        )

    for k in range(1, nar):
        copy(k).start()
    out_ref[me] = in_ref[me]
    for k in range(1, nar):
        copy(k).wait()


def exchange(values, name):
    nar = values.shape[0]
    vmem = pl.BlockSpec(memory_space=pltpu.VMEM)
    return pl.pallas_call(
        functools.partial(exchange_kernel, nar),
        out_shape=jax.ShapeDtypeStruct(values.shape, values.dtype),
        in_specs=[vmem],
        out_specs=vmem,
        scratch_shapes=[pltpu.SemaphoreType.DMA((nar,))] * 2,
        compiler_params=pltpu.CompilerParams(collective_id=name, has_side_effects=True),
    )(values)


def greet(peers):
    barrier = pltpu.get_barrier_semaphore()
    for peer in peers:
        pl.semaphore_signal(barrier, inc=1, device_id=peer, device_id_type=MESH)
    pl.semaphore_wait(barrier, len(peers))


def tail_kernel(
    nar,
    wid,
    first,
    chunks,
    grad_ref,
    weight_ref,
    input_ref,
    above_ref,
    gain_ref,
    sums_ref,
    out_ref,
    total_ref,
    got,
    own_sums,
    all_sums,
    pieces_out,
    pieces_in,
    a_send,
    a_recv,
    z_send,
    z_recv,
    y_send,
    y_recv,
    s_send,
    s_recv,
    p_send,
    p_recv,
):
    me = lax.axis_index("narrow")
    mine = lax.axis_index("wide")
    second = nar // first
    za, yb = me // second, lax.rem(me, second)
    tok = input_ref.shape[0]
    piece = total_ref.shape[1]
    part = tok // chunks

    def peer(k):
        return lax.rem(me + k, nar)

    greet(
        [{"narrow": peer(k)} for k in range(1, nar)]
        + [{"wide": lax.rem(mine + w, wid)} for w in range(1, wid)]
    )

    def remote(src, dst, send, recv, target):
        return pltpu.make_async_remote_copy(
            src_ref=src,
            dst_ref=dst,
            send_sem=send,
            recv_sem=recv,
            device_id=target,
            device_id_type=MESH,
        )

    def a_copy(k):
        return remote(
            grad_ref.at[peer(k)], got.at[k], a_send.at[k], a_recv.at[k], {"narrow": peer(k)}
        )

    def z_copy(i, c):
        rows = out_ref.at[me, pl.ds(c * part, part)]
        target = lax.rem(za + i, first) * second + yb
        return remote(rows, rows, z_send.at[i, c], z_recv.at[i, c], {"narrow": target})

    def y_copy(i, j, c):
        source = lax.rem(za + first - i, first) * second + yb
        rows = out_ref.at[source, pl.ds(c * part, part)]
        target = za * second + lax.rem(yb + j, second)
        return remote(rows, rows, y_send.at[i, j, c], y_recv.at[i, j, c], {"narrow": target})

    def s_copy(k):
        return remote(own_sums, all_sums.at[k], s_send.at[k], s_recv.at[k], {"narrow": peer(k)})

    def p_copy(w):
        target = lax.rem(mine + w, wid)
        return remote(
            pieces_out.at[target], pieces_in.at[w], p_send.at[w], p_recv.at[w], {"wide": target}
        )

    for k in range(1, nar):
        a_copy(k).start()
    normed, inverse = normalise(input_ref[...].astype(F32))
    total = jnp.dot(grad_ref[me], weight_ref[me], preferred_element_type=F32)
    for k in range(1, nar):
        a_copy(k).wait_recv()
        total = total + jnp.dot(
            got[k], weight_ref[lax.rem(me + nar - k, nar)], preferred_element_type=F32
        )
    grad = above_ref[...] + normalise_back(total, normed, inverse, gain_ref[0:1, :])
    out_ref[me] = grad.astype(BF16)
    own_sums[...] = sums_ref[...]
    own_sums[0:1, :] = jnp.sum(total * normed, axis=0, keepdims=True)
    for k in range(1, nar):
        s_copy(k).start()
    for c in range(chunks):
        for i in range(1, first):
            z_copy(i, c).start()
        for j in range(1, second):
            y_copy(0, j, c).start()
    sums = own_sums[...]
    for k in range(1, nar):
        s_copy(k).wait_recv()
        sums = sums + all_sums[k]
    for w in range(wid):
        pieces_out[w] = sums[:, w * piece : (w + 1) * piece]
    for w in range(1, wid):
        p_copy(w).start()
    for c in range(chunks):
        for i in range(1, first):
            z_copy(i, c).wait_recv()
            for j in range(1, second):
                y_copy(i, j, c).start()
    answer = pieces_out[mine]
    for w in range(1, wid):
        p_copy(w).wait()
        answer = answer + pieces_in[w]
    total_ref[...] = answer
    for k in range(1, nar):
        a_copy(k).wait_send()
        s_copy(k).wait_send()
    for c in range(chunks):
        for i in range(1, first):
            z_copy(i, c).wait_send()
        for i in range(first):
            for j in range(1, second):
                y_copy(i, j, c).wait()


def tail(grads, weights, inputs, above, gain, sums, wid, name):
    nar, tok, columns = grads.shape
    width = inputs.shape[1]
    first = 4 if nar % 4 == 0 else nar
    second = nar // first
    chunks = 4
    vmem = pl.BlockSpec(memory_space=pltpu.VMEM)
    dma = pltpu.SemaphoreType.DMA
    return pl.pallas_call(
        functools.partial(tail_kernel, nar, wid, first, chunks),
        out_shape=(
            jax.ShapeDtypeStruct((nar, tok, width), BF16),
            jax.ShapeDtypeStruct((8, width // wid), F32),
        ),
        in_specs=[vmem] * 6,
        out_specs=(vmem, vmem),
        scratch_shapes=[
            pltpu.VMEM((nar, tok, columns), BF16),
            pltpu.VMEM((8, width), F32),
            pltpu.VMEM((nar, 8, width), F32),
            pltpu.VMEM((wid, 8, width // wid), F32),
            pltpu.VMEM((wid, 8, width // wid), F32),
            dma((nar,)),
            dma((nar,)),
            dma((first, chunks)),
            dma((first, chunks)),
            dma((first, second, chunks)),
            dma((first, second, chunks)),
            dma((nar,)),
            dma((nar,)),
            dma((wid,)),
            dma((wid,)),
        ],
        compiler_params=pltpu.CompilerParams(
            collective_id=name, has_side_effects=True, vmem_limit_bytes=48 * 2**20
        ),
    )(grads, weights, inputs, above, gain, sums)


def neighbour_kernel(
    nar,
    tiles,
    tile,
    kept,
    ring,
    query_ref,
    keys_ref,
    norms_ref,
    ids_ref,
    cols_ref,
    scal_ref,
    grad_ref,
    loss_ref,
    stat_ref,
    queries,
    partial,
    dist,
    grads,
    sends,
    slots,
    loss_own,
    slot_sem,
    q_send,
    q_recv,
    d_send,
    d_recv,
    g_send,
    g_recv,
    l_send,
    l_recv,
    o_send,
    o_recv,
):
    me = lax.axis_index("narrow")
    tok = query_ref.shape[1]
    depth = query_ref.shape[2]
    group = 16
    per_block = tok // tile
    late = tiles - kept

    def peer(k):
        return lax.rem(me + k, nar)

    def origin(k):
        return lax.rem(me + nar - k, nar)

    def remote(src, dst, send, recv, target):
        return pltpu.make_async_remote_copy(
            src_ref=src,
            dst_ref=dst,
            send_sem=send,
            recv_sem=recv,
            device_id={"narrow": target},
            device_id_type=MESH,
        )

    def load(index, slot):
        block, sub = index // per_block, lax.rem(index, per_block)
        row = origin(block) * tok + sub * tile
        return pltpu.make_async_copy(
            keys_ref.at[pl.ds(row, tile)], slots.at[slot], slot_sem.at[slot]
        )

    for i in range(kept + ring):
        load(i, i).start()

    barrier = pltpu.get_barrier_semaphore()
    for k in range(1, nar):
        pl.semaphore_signal(
            barrier, inc=1, device_id={"narrow": peer(k)}, device_id_type=MESH
        )
    pl.semaphore_wait(barrier, nar - 1)

    def q_copy(k):
        return remote(
            query_ref.at[peer(k)], queries.at[k], q_send.at[k], q_recv.at[k], peer(k)
        )

    def d_copy(k):
        return remote(partial.at[k], dist.at[k], d_send.at[k], d_recv.at[k], origin(k))

    def g_copy(k):
        return remote(grads.at[0], grads.at[k], g_send.at[k], g_recv.at[k], peer(k))

    def l_copy(k):
        return remote(loss_own, loss_ref.at[me], l_send.at[k], l_recv.at[k], peer(k))

    def o_copy(k):
        return remote(sends.at[k], grad_ref.at[me], o_send.at[k], o_recv.at[k], origin(k))

    for k in range(1, nar):
        q_copy(k).start()
    queries[0] = query_ref[me]

    row_of = lax.broadcasted_iota(jnp.int32, (group, J), 0)

    def slot_of(index):
        return jnp.where(index < kept, index, kept + lax.rem(index - kept, ring))

    def slot_late(n):
        return kept + lax.rem(n, ring)

    def forward_tile(k, sub, slot):
        def one(g, carry):
            at = pl.multiple_of(sub * tile + g * group, group)
            own = queries[k, pl.ds(at, group), :].astype(F32)
            keys = slots[slot, pl.ds(g * group, group), :, :].reshape(group * depth, J)
            wide = jnp.concatenate(
                [jnp.where(row_of[:, :depth] == t, own, 0.0) for t in range(group)], axis=1
            ).astype(BF16)
            out = jnp.dot(wide, keys, preferred_element_type=F32)
            row = pl.multiple_of(origin(k) * tok + at, group)
            partial[k, pl.ds(at, group), :] = 2.0 * out - norms_ref[pl.ds(row, group), :]
            return carry

        lax.fori_loop(0, tile // group, one, 0, unroll=True)

    def forward_block(k):
        def body(sub, carry):
            index = k * per_block + sub
            slot = slot_of(index)
            load(index, slot).wait()
            forward_tile(k, sub, slot)

            @pl.when(index >= kept)
            def _():
                nxt = index - kept + ring

                @pl.when(nxt < 2 * late)
                def _():
                    load(kept + lax.rem(nxt, late), slot).start()

            return carry

        lax.fori_loop(0, per_block, body, 0)

    forward_block(0)

    def forward_rest(k, carry):
        q_copy(k).wait_recv()
        forward_block(k)
        d_copy(k).start()
        return carry

    lax.fori_loop(1, nar, forward_rest, 0)

    def collect(k, total):
        d_copy(k).wait_recv()
        return total + dist[k]

    distance = lax.fori_loop(1, nar, collect, partial[0])
    temper_value = scal_ref[0]
    mix_value = scal_ref[1]
    count = cols_ref[:, 0:1]
    target = cols_ref[:, 1:2]
    base = cols_ref[:, 2:3]
    loss_weight = cols_ref[:, 3:4]
    logits = distance / temper_value
    spot = lax.broadcasted_iota(jnp.int32, (tok, J), 1).astype(F32)
    masked = jnp.where(spot < count, logits, -1e30)
    peak = jnp.max(masked, axis=-1, keepdims=True)
    expo = jnp.exp(masked - peak)
    weights = expo / jnp.sum(expo, axis=-1, keepdims=True)
    matches = jnp.where(ids_ref[...].astype(F32) == target, 1.0, 0.0)
    knn_prob = jnp.sum(weights * matches, axis=-1, keepdims=True)
    mixture = mix_value * knn_prob + (1.0 - mix_value) * base
    grad_mixture = -loss_weight / mixture
    grad_logits = weights * (mix_value * grad_mixture) * (matches - knn_prob)
    grads[0] = (2.0 * grad_logits / temper_value).astype(BF16)
    for k in range(1, nar):
        g_copy(k).start()
    loss = jnp.transpose(jnp.broadcast_to(-jnp.log(mixture), (tok, J)))[0:8, :]
    loss_own[...] = loss
    for k in range(1, nar):
        l_copy(k).start()
    loss_ref[me] = loss
    term_temper = -jnp.sum(grad_logits * logits, axis=0, keepdims=True) / temper_value
    term_mix = jnp.sum((knn_prob - base) * grad_mixture, axis=0, keepdims=True)
    stat_ref[0:1, :] = term_temper
    stat_ref[1:2, :] = jnp.broadcast_to(term_mix, (1, J))

    def backward_tile(k, sub, slot):
        def one(g, carry):
            at = pl.multiple_of(sub * tile + g * group, group)
            own = grads[k, pl.ds(at, group), :]
            keys = slots[slot, pl.ds(g * group, group), :, :].reshape(group * depth, J)
            out = lax.dot_general(
                own, keys, (((1,), (1,)), ((), ())), preferred_element_type=F32
            )
            total = jnp.zeros((group, depth), F32)
            for t in range(group):
                total = jnp.where(
                    row_of[:, :depth] == t, out[:, t * depth : (t + 1) * depth], total
                )
            sends[k, pl.ds(at, group), :] = total.astype(BF16)
            return carry

        lax.fori_loop(0, tile // group, one, 0, unroll=True)

    def backward_block(k):
        def body(sub, carry):
            index = k * per_block + sub

            @pl.when(index < kept)
            def _():
                backward_tile(k, sub, index)

            @pl.when(index >= kept)
            def _():
                n = index - kept + late
                slot = slot_late(n)
                load(index, slot).wait()
                backward_tile(k, sub, slot)

                @pl.when(n + ring < 2 * late)
                def _():
                    load(kept + lax.rem(n + ring, late), slot).start()

            return carry

        lax.fori_loop(0, per_block, body, 0)

    backward_block(0)
    grad_ref[me] = sends[0]

    def backward_rest(k, carry):
        g_copy(k).wait_recv()
        backward_block(k)
        o_copy(k).start()
        return carry

    lax.fori_loop(1, nar, backward_rest, 0)

    for k in range(1, nar):
        q_copy(k).wait_send()
        d_copy(k).wait_send()
        g_copy(k).wait_send()
        l_copy(k).wait()
        o_copy(k).wait()


def neighbours(nar, query, keys, norms, ids, cols, scal):
    tok, depth = query.shape[1:]
    rows = keys.shape[0]
    tile = 32
    tiles = rows // tile
    bytes_tile = tile * depth * J * 2
    ring = 4
    kept = min(tiles - 2 * ring, (KEPT_BYTES // bytes_tile))
    late = tiles - kept
    vmem = pl.BlockSpec(memory_space=pltpu.VMEM)
    dma = pltpu.SemaphoreType.DMA((nar,))
    return pl.pallas_call(
        functools.partial(neighbour_kernel, nar, tiles, tile, kept, ring),
        out_shape=(
            jax.ShapeDtypeStruct((nar, tok, depth), BF16),
            jax.ShapeDtypeStruct((nar, 8, tok), F32),
            jax.ShapeDtypeStruct((2, J), F32),
        ),
        in_specs=[
            vmem,
            pl.BlockSpec(memory_space=pl.ANY),
            vmem,
            vmem,
            vmem,
            pl.BlockSpec(memory_space=pltpu.SMEM),
        ],
        out_specs=(vmem, vmem, vmem),
        scratch_shapes=[
            pltpu.VMEM((nar, tok, depth), BF16),
            pltpu.VMEM((nar, tok, J), F32),
            pltpu.VMEM((nar, tok, J), F32),
            pltpu.VMEM((nar, tok, J), BF16),
            pltpu.VMEM((nar, tok, depth), BF16),
            pltpu.VMEM((kept + ring, tile, depth, J), BF16),
            pltpu.VMEM((8, tok), F32),
            pltpu.SemaphoreType.DMA((kept + ring,)),
        ]
        + [dma] * 10,
        compiler_params=pltpu.CompilerParams(
            collective_id=1, has_side_effects=True, vmem_limit_bytes=60 * 2**20
        ),
    )(query, keys, norms, ids, cols, scal)


def on_device(
    block_input,
    output_cotangent,
    loss_weight,
    segments,
    nbr_keys,
    nbr_count,
    nbr_ids,
    targets,
    base_prob,
    w_query,
    w_key,
    w_value,
    w_proj,
    w_in,
    w_out,
    gain_attn,
    gain_ffn,
    gain_key,
    temper,
    mix_weight,
):
    seqs_here, length, width = block_input.shape
    rows = seqs_here * length
    nar = lax.axis_size("narrow")
    own = lax.axis_index("narrow")
    tok = rows // nar
    local_width = w_query.shape[0]
    heads_here = local_width // HD
    scale = HD ** (-0.5)

    def mine(values):
        flat = values.reshape((rows,) + values.shape[2:])
        return lax.dynamic_slice_in_dim(flat, own * tok, tok, 0)

    wid = lax.axis_size("wide")
    hidden = w_in.shape[1]
    parts = width // hidden
    packed = w_in.reshape(parts, width // parts, hidden).transpose(1, 0, 2)
    bundle = gather_weight(
        jnp.concatenate([packed.reshape(width // parts, width), w_out, w_proj], axis=0)
    )

    inputs = block_input.reshape(rows, width).astype(F32)
    normed_in, _ = norm_parts(inputs)
    normed_one = (normed_in * gain_attn).astype(BF16)
    w_qkv = jnp.concatenate([w_query, w_key, w_value], axis=0)
    column_scale = jnp.where(jnp.arange(3 * local_width) < local_width, scale, 1.0)
    qkv = (through_t(normed_one, w_qkv) * column_scale[None, :]).astype(BF16)
    seg_column = segments.reshape(rows, 1)
    seg_row = segments.reshape(seqs_here, 1, length)
    attended, lse = attend(qkv, seg_column, seg_row, seqs_here, heads_here)

    key_slices = nbr_keys.reshape(rows, nbr_keys.shape[2], nbr_keys.shape[3])
    part_norms = jnp.einsum("tdj,tdj->tj", key_slices, key_slices, preferred_element_type=F32)

    attended_own = exchange(attended.reshape(nar, tok, local_width), 2)
    inputs_own = mine(block_input)
    gains = jnp.stack([gain_attn, gain_ffn, gain_key])
    hidden_one, hidden_two, normed_two, output_own, query_key, pre_act = ffn(
        attended_own, inputs_own, gains, bundle, hidden
    )
    normed_two_all = lax.all_gather(normed_two, "narrow", axis=0, tiled=True)
    block_output = lax.all_gather(output_own, "narrow", axis=0, tiled=True)
    cols = jnp.stack(
        [
            mine(nbr_count).astype(F32),
            mine(targets).astype(F32),
            mine(base_prob),
            mine(loss_weight),
        ],
        axis=1,
    )
    grad_slices, losses, stats = neighbours(
        nar,
        query_key,
        key_slices,
        part_norms,
        mine(nbr_ids),
        cols,
        jnp.concatenate([temper, mix_weight]),
    )
    token_loss = losses[:, 0, :]
    grad_ffn, grad_hidden_one, grad_attended, proj_part, gain_sums = ffn_back(
        grad_slices,
        attended_own,
        mine(output_cotangent),
        hidden_one,
        hidden_two,
        gains,
        pre_act,
        bundle,
    )
    grad_ffn_all = lax.all_gather(grad_ffn, "narrow", axis=0, tiled=True)
    grad_w_proj = lax.psum_scatter(proj_part, "narrow", scatter_dimension=0, tiled=True)[0]
    qkv_all = gather_weight(w_qkv)

    grad_attended = exchange(grad_attended, 3).reshape(rows, local_width)
    grad_qkv = attend_back(qkv, grad_attended, lse, seg_column, seg_row, seqs_here, heads_here)
    sums = jnp.concatenate(
        [
            jnp.zeros((1, width), F32),
            gain_sums,
            jnp.broadcast_to(jnp.sum(stats[0]), (1, width)),
            jnp.broadcast_to(stats[1, 0], (1, width)),
            jnp.zeros((3, width), F32),
        ],
        axis=0,
    )
    grad_input, totals = tail(
        grad_qkv.reshape(nar, tok, 3 * local_width),
        qkv_all,
        inputs_own,
        grad_hidden_one,
        gains,
        sums,
        wid,
        4,
    )

    pre_loc = product(normed_two_all, w_in)
    act_loc = gelu_tanh(pre_loc).astype(BF16)
    grad_pre_loc = jax.vjp(gelu_tanh, pre_loc)[1](through_t(grad_ffn_all, w_out))[0].astype(BF16)
    grad_w_in = outer_sum(normed_two_all, grad_pre_loc)
    grad_w_out = outer_sum(act_loc, grad_ffn_all)
    grad_w_qkv = outer_sum(grad_qkv, normed_one)

    by_column = jnp.concatenate(
        [grad_w_qkv.astype(BF16), grad_w_proj, grad_w_out.astype(BF16)], axis=0
    )
    by_column = lax.psum_scatter(by_column, "wide", scatter_dimension=1, tiled=True).astype(F32)
    by_row = lax.psum_scatter(
        grad_w_in.astype(BF16), "wide", scatter_dimension=0, tiled=True
    ).astype(F32)

    return (
        block_output.reshape(seqs_here, length, width),
        token_loss.reshape(seqs_here, length),
        grad_input.astype(F32).reshape(seqs_here, length, width),
        by_column[:local_width],
        by_column[local_width : 2 * local_width],
        by_column[2 * local_width : 3 * local_width],
        by_column[3 * local_width : 4 * local_width],
        by_row,
        by_column[4 * local_width :],
        totals[0],
        totals[1],
        totals[2],
        totals[3, 0:1],
        totals[4, 0:1],
    )


def solution(mesh):
    return jax.shard_map(
        on_device,
        mesh=mesh,
        in_specs=(
            P("wide", None, None),
            P("wide", None, None),
            P("wide", None),
            P("wide", None),
            P("wide", None, "narrow", None),
            P("wide", None),
            P("wide", None, None),
            P("wide", None),
            P("wide", None),
            P("narrow", None),
            P("narrow", None),
            P("narrow", None),
            P("narrow", None),
            P(None, "narrow"),
            P("narrow", None),
            P(),
            P(),
            P(),
            P(),
            P(),
        ),
        out_specs=(
            P("wide", None, None),
            P("wide", None),
            P("wide", None, None),
            P("narrow", "wide"),
            P("narrow", "wide"),
            P("narrow", "wide"),
            P("narrow", "wide"),
            P("wide", "narrow"),
            P("narrow", "wide"),
            P("wide"),
            P("wide"),
            P("wide"),
            P(),
            P(),
        ),
        check_vma=False,
    )
```

```python
import functools

import jax
import jax.numpy as jnp
from jax import lax
from jax.experimental import pallas as pl
from jax.experimental.pallas import tpu as pltpu
from jax.sharding import PartitionSpec as P

HD = 64
EPSILON = 1e-05
F32 = jnp.float32
BF16 = jnp.bfloat16
MESH = pl.DeviceIdType.MESH
J = 128
KEPT_BYTES = 44 * 2**20


def outer_sum(left, right):
    return jnp.einsum("ta,tb->ab", left, right, preferred_element_type=F32)


def place(index, second):
    return {"z": index // second, "y": lax.rem(index, second)}


def push(src, dst, send, recv, target):
    return pltpu.make_async_remote_copy(
        src_ref=src,
        dst_ref=dst,
        send_sem=send,
        recv_sem=recv,
        device_id=target,
        device_id_type=MESH,
    )


def greet(peers):
    barrier = pltpu.get_barrier_semaphore()
    for peer in peers:
        pl.semaphore_signal(barrier, inc=1, device_id=peer, device_id_type=MESH)
    pl.semaphore_wait(barrier, len(peers))


def normalise(values):
    centred = values - jnp.mean(values, axis=-1, keepdims=True)
    inverse = lax.rsqrt(jnp.mean(centred * centred, axis=-1, keepdims=True) + EPSILON)
    return centred * inverse, inverse


def normalise_back(grad_out, normed, inverse, gain):
    scaled = grad_out * gain
    return inverse * (
        scaled
        - jnp.mean(scaled, axis=-1, keepdims=True)
        - normed * jnp.mean(scaled * normed, axis=-1, keepdims=True)
    )


def head_lanes(values, head):
    lanes = lax.broadcasted_iota(jnp.int32, values.shape, 1)
    return jnp.where(lanes // HD == head, values, jnp.zeros_like(values))


def head_kernel(
    nar,
    first,
    wid,
    seqs,
    heads,
    block,
    tile,
    ring,
    input_ref,
    gain_ref,
    qkv_weight_ref,
    col_ref,
    row_ref,
    keys_ref,
    in_ref,
    out_ref,
    pq_ref,
    normed_ref,
    qkv_ref,
    lse_ref,
    norms_ref,
    att_ref,
    in_all,
    out_all,
    pq_all,
    attended,
    slots,
    slot_sem,
    own_sem,
    a_send,
    a_recv,
    z_send,
    z_recv,
    y_send,
    y_recv,
    x_send,
    x_recv,
    c_send,
    c_recv,
):
    second = nar // first
    outer = wid // 2
    za, yb = lax.axis_index("z"), lax.axis_index("y")
    me = za * second + yb
    wide = lax.axis_index("wide")
    chip, core = wide // 2, lax.rem(wide, 2)
    rows, width = input_ref.shape
    tok = rows // nar
    length = rows // seqs
    local = heads * HD
    tiles = rows // tile
    last = (((1,), (1,)), ((), ()))

    def fetch(index, slot):
        return pltpu.make_async_copy(
            keys_ref.at[pl.ds(index * tile, tile)], slots.at[slot], slot_sem.at[slot]
        )

    for i in range(ring):
        fetch(i, i).start()

    greet(
        [place(lax.rem(me + k, nar), second) for k in range(1, nar)]
        + [{"wide": chip * 2 + (1 - core)}]
        + [{"wide": lax.rem(chip + o, outer) * 2 + core} for o in range(1, outer)]
    )

    stacks = ((pq_ref, pq_all), (in_ref, in_all), (out_ref, out_all))

    def shard_of(t, source):
        return source if t == 0 else source // second

    def quarter(t, source, owner):
        own, stack = stacks[t]
        count = own.shape[0] // wid
        at = pl.ds(pl.multiple_of(owner * count, count), count)
        return stack.at[shard_of(t, source), at]

    def own_quarter(t):
        own, _ = stacks[t]
        count = own.shape[0] // wid
        return own.at[pl.ds(pl.multiple_of(wide * count, count), count)]

    reach = ((1, 2), (0, 2), (1, 3), (2, 1))
    relay = {1: (0, (2, 3)), 2: (3, (0, 1))}
    if first != 4:
        reach = tuple(tuple(b for b in range(first) if b != a) for a in range(first))
        relay = {}

    def line_copy(t, source, z, slot, own):
        return push(
            own_quarter(t) if own else quarter(t, source, wide),
            quarter(t, source, wide),
            z_send.at[t, source // second, slot],
            z_recv.at[t, source // second],
            {"z": z, "y": yb},
        )

    def owner_of(o):
        return lax.rem(chip + outer - o, outer) * 2 + core

    def row_copy(source, j, o, own):
        owner = owner_of(o)
        count = pq_ref.shape[0] // wid
        at = pl.ds(pl.multiple_of(owner * count, count), count)
        return push(
            pq_ref.at[at] if own else quarter(0, source, owner),
            quarter(0, source, owner),
            y_send.at[source, j, o],
            y_recv.at[source, j, o],
            {"z": za, "y": lax.rem(yb + j, second)},
        )

    def chip_copy(t, source, o):
        return push(
            quarter(t, source, wide),
            quarter(t, source, wide),
            x_send.at[t, source, o],
            x_recv.at[t, source, o],
            {"wide": lax.rem(chip + o, outer) * 2 + core},
        )

    def chip_arrival(t, source, o):
        owner = owner_of(o)
        return push(
            quarter(t, source, owner),
            quarter(t, source, owner),
            x_send.at[t, source, o],
            x_recv.at[t, source, o],
            {"wide": owner},
        )

    def core_copy(t, source, o, away):
        owner = lax.rem(chip + outer - o, outer) * 2 + jnp.where(away, 1 - core, core)
        return push(
            quarter(t, source, owner),
            quarter(t, source, owner),
            c_send.at[t, source, o],
            c_recv.at[t, source, o],
            {"wide": chip * 2 + (1 - core)},
        )

    def att_copy(target, source):
        return push(
            attended.at[target],
            att_ref.at[source],
            a_send.at[target],
            a_recv.at[source],
            place(target, second),
        )

    own_copies = [
        pltpu.make_async_copy(own, stack.at[shard_of(t, me)], own_sem.at[t])
        for t, (own, stack) in enumerate(stacks)
    ]

    def send_own(t):
        for z in range(first):

            @pl.when(za == z)
            def _(z=z):
                for slot, target in enumerate(reach[z]):
                    line_copy(t, me, target, slot, True).start()

        if t == 0:
            for j in range(1, second):
                for o in range(outer):
                    row_copy(me, j, o, True).start()
        own_copies[t].start()

    def line_arrivals(t, begin, end):
        for d in range(begin, end):
            for way in (-1, 1):
                z = za + way * d

                @pl.when((z >= 0) & (z < first))
                def _(z=z):
                    source = z * second + yb
                    line_copy(t, source, za, 0, False).wait_recv()
                    for middle, (target, sources) in relay.items():

                        @pl.when((za == middle) & ((z == sources[0]) | (z == sources[1])))
                        def _(target=target):
                            line_copy(t, source, target, 0, False).start()

                    for o in range(1, outer):
                        chip_copy(t, source, o).start()
                    core_copy(t, source, 0, False).start()

    def chip_arrivals(t):
        for n in range(first):
            source = n * second + yb

            @pl.when(source != me)
            def _(source=source):
                for o in range(1, outer):
                    chip_arrival(t, source, o).wait_recv()
                    core_copy(t, source, o, False).start()
                if t == 0:
                    for j in range(1, second):
                        for o in range(outer):
                            row_copy(source, j, o, False).start()

    def row_arrivals():
        for j in range(1, second):
            for z in range(first):
                source = z * second + lax.rem(yb + second - j, second)
                for o in range(outer):
                    row_copy(source, j, o, False).wait_recv()
                    core_copy(0, source, o, False).start()

    def each_source(t, do):
        for n in range(nar if t == 0 else first):
            source = n if t == 0 else n * second + yb

            @pl.when(source != me)
            def _(source=source):
                do(source)

    def core_arrivals(t):
        def do(source):
            for o in range(outer):
                core_copy(t, source, o, True).wait_recv()

        each_source(t, do)

    for t in range(3):
        send_own(t)

    def project(r, carry):
        at = pl.ds(pl.multiple_of(r * block, block), block)
        normed, _ = normalise(input_ref[at, :].astype(F32))
        low = (normed * gain_ref[0:1, :]).astype(BF16)
        normed_ref[at, :] = low
        out = lax.dot_general(low, qkv_weight_ref[...], last, preferred_element_type=F32)
        lanes = lax.broadcasted_iota(jnp.int32, out.shape, 1)
        qkv_ref[at, :] = jnp.where(lanes < local, out * HD ** (-0.5), out).astype(BF16)
        return carry

    lax.fori_loop(0, rows // block, project, 0)
    line_arrivals(0, 1, 2)

    def sequence(seq, carry):
        base = seq * length
        for start in range(0, length, block):
            keys = start + block
            at = pl.ds(pl.multiple_of(base + start, block), block)
            whole = pl.ds(pl.multiple_of(base, length), keys)
            query_segment = col_ref[at, 0:1]
            key_segment = row_ref[seq, 0:1, 0:keys]
            spot = lax.broadcasted_iota(jnp.int32, (block, keys), 1)
            own = lax.broadcasted_iota(jnp.int32, (block, keys), 0) + start
            allowed = (spot <= own) & (query_segment == key_segment)
            query = qkv_ref[at, 0:local]
            key = qkv_ref[whole, local : 2 * local]
            value = qkv_ref[whole, 2 * local : 3 * local]
            total = jnp.zeros((block, local), F32)
            for head in range(heads):
                scores = lax.dot_general(
                    head_lanes(query, head), key, last, preferred_element_type=F32
                )
                scores = jnp.where(allowed, scores, -1e30)
                peak = jnp.max(scores, axis=-1, keepdims=True)
                expo = jnp.exp(scores - peak)
                sums = jnp.sum(expo, axis=-1, keepdims=True)
                out = jnp.dot(expo.astype(BF16), value, preferred_element_type=F32) / sums
                total = total + head_lanes(out, head)
                lse_ref[at, head : head + 1] = peak + jnp.log(sums)
            each = min(tok, block)
            for r in range(0, block, each):
                target = seq * (nar // seqs) + (start + r) // tok
                spot_row = (start + r) % tok
                attended[target, spot_row : spot_row + each, :] = total[r : r + each, :].astype(
                    BF16
                )

        def leave(b, c):
            target = seq * (nar // seqs) + b

            @pl.when(target != me)
            def _():
                att_copy(target, me).start()

            return c

        lax.fori_loop(0, nar // seqs, leave, 0)
        return carry

    lax.fori_loop(0, seqs, sequence, 0)
    att_ref[me] = attended[me]

    def norms(begin, end):
        def body(index, carry):
            slot = lax.rem(index, ring)
            fetch(index, slot).wait()
            keys = slots[slot].astype(F32)
            at = pl.ds(pl.multiple_of(index * tile, tile), tile)
            norms_ref[at, :] = jnp.sum(keys * keys, axis=1)

            @pl.when(index + ring < tiles)
            def _():
                fetch(index + ring, slot).start()

            return carry

        lax.fori_loop(begin, end, body, 0)

    def some(*calls):
        def run():
            for call in calls:
                call()

        return run

    steps = [
        some(lambda: line_arrivals(1, 1, 2), lambda: line_arrivals(0, 2, first)),
        some(lambda: chip_arrivals(0), lambda: line_arrivals(2, 1, 2)),
        lambda: line_arrivals(1, 2, first),
        lambda: line_arrivals(2, 2, first),
    ]
    share_of = tiles // len(steps)
    for n, step in enumerate(steps):
        step()
        norms(n * share_of, tiles if n == len(steps) - 1 else (n + 1) * share_of)
    row_arrivals()
    chip_arrivals(1)
    chip_arrivals(2)
    for t in range(3):
        core_arrivals(t)
    for k in range(1, nar):
        source = lax.rem(me + k, nar)
        att_copy(source, source).wait_recv()
        att_copy(source, me).wait_send()
    for t in range(3):
        own_copies[t].wait()

        def sent(source, t=t):
            for o in range(outer):
                core_copy(t, source, o, False).wait_send()

        each_source(t, sent)
        for n in range(first):
            source = n * second + yb

            @pl.when(source != me)
            def _(source=source, t=t):
                for o in range(1, outer):
                    chip_copy(t, source, o).wait_send()

        for z in range(first):

            @pl.when(za == z)
            def _(z=z, t=t):
                for slot, target in enumerate(reach[z]):
                    line_copy(t, me, target, slot, True).wait_send()
                if z in relay:
                    target, sources = relay[z]
                    for n in sources:
                        line_copy(t, n * second + yb, target, 0, False).wait_send()

    for z in range(first):
        for j in range(1, second):
            for o in range(outer):
                row_copy(z * second + yb, j, o, False).wait_send()


def head(block_input, gain, w_qkv, columns, row_form, keys, w_in, w_out, pq, first, nar, wid, name):
    rows, width = block_input.shape
    seqs, _, length = row_form.shape
    second = nar // first
    outer = wid // 2
    local = w_qkv.shape[0] // 3
    heads = local // HD
    hidden = w_in.shape[1]
    tok = rows // nar
    depth = keys.shape[1]
    tile, ring = 32, 4
    block = min(256, length)
    vmem = pl.BlockSpec(memory_space=pltpu.VMEM)
    dma = pltpu.SemaphoreType.DMA
    return pl.pallas_call(
        functools.partial(head_kernel, nar, first, wid, seqs, heads, block, tile, ring),
        out_shape=(
            jax.ShapeDtypeStruct((rows, width), BF16),
            jax.ShapeDtypeStruct((rows, 3 * local), BF16),
            jax.ShapeDtypeStruct((rows, heads), F32),
            jax.ShapeDtypeStruct((rows, J), F32),
            jax.ShapeDtypeStruct((nar, tok, local), BF16),
            jax.ShapeDtypeStruct((first, width, hidden), BF16),
            jax.ShapeDtypeStruct((first, hidden, width), BF16),
            jax.ShapeDtypeStruct((nar,) + pq.shape, BF16),
        ),
        in_specs=[vmem] * 5 + [pl.BlockSpec(memory_space=pl.ANY)] + [vmem] * 3,
        out_specs=(vmem,) * 8,
        scratch_shapes=[
            pltpu.VMEM((nar, tok, local), BF16),
            pltpu.VMEM((ring, tile, depth, J), BF16),
            dma((ring,)),
            dma((3,)),
            dma((nar,)),
            dma((nar,)),
            dma((3, first, 2)),
            dma((3, first)),
            dma((nar, second, outer)),
            dma((nar, second, outer)),
            dma((3, nar, outer)),
            dma((3, nar, outer)),
            dma((3, nar, outer)),
            dma((3, nar, outer)),
        ],
        compiler_params=pltpu.CompilerParams(
            collective_id=name, has_side_effects=True, vmem_limit_bytes=58 * 2**20
        ),
    )(block_input, gain, w_qkv, columns, row_form, keys, w_in, w_out, pq)


INNER = 0.7978845608028654
CUBIC = 0.044715


def gelu_parts(values):
    tanh = jnp.tanh(INNER * (values + CUBIC * values * values * values))
    return 0.5 * values * (1.0 + tanh), tanh


def ffn_kernel(
    chunks,
    att_ref,
    input_ref,
    gains_ref,
    proj_ref,
    in_ref,
    mid_ref,
    one_ref,
    two_ref,
    output_ref,
    key_ref,
    normed_ref,
    pre_ref,
    back_out,
    back_in,
    n_send,
    n_recv,
    b_send,
    b_recv,
):
    nar, tok, local = att_ref.shape
    first, width, hidden = in_ref.shape
    second = nar // first
    part = tok // chunks
    za, yb = lax.axis_index("z"), lax.axis_index("y")

    greet([{"z": za, "y": lax.rem(yb + j, second)} for j in range(1, second)])

    def n_copy(j, c):
        at = pl.ds(c * part, part)
        target = {"z": za, "y": lax.rem(yb + j, second)}
        return push(
            normed_ref.at[0, at], normed_ref.at[j, at], n_send.at[j, c], n_recv.at[j, c], target
        )

    def b_copy(j, c):
        at = pl.ds(c * part, part)
        target = {"z": za, "y": lax.rem(yb + second - j, second)}
        return push(
            back_out.at[j, at], back_in.at[j, at], b_send.at[j, c], b_recv.at[j, c], target
        )

    def through(j, start, count):
        total = jnp.zeros((count, width), F32)
        for z in range(first):
            pre = jnp.dot(
                normed_ref[j, start : start + count, :], in_ref[z], preferred_element_type=F32
            )
            pre_ref[j, start : start + count, z * hidden : (z + 1) * hidden] = pre
            activated = gelu_parts(pre)[0].astype(BF16)
            total = total + jnp.dot(activated, mid_ref[z], preferred_element_type=F32)
        return total

    att = jnp.concatenate([att_ref[n] for n in range(nar)], axis=1)
    one = input_ref[...].astype(F32) + jnp.dot(
        att, proj_ref[...].reshape(nar * local, width), preferred_element_type=F32
    )
    one_ref[...] = one
    normed, _ = normalise(one)
    normed_ref[0] = (normed * gains_ref[1:2, :]).astype(BF16)
    for c in range(chunks):
        for j in range(1, second):
            n_copy(j, c).start()
    two_ref[...] = one_ref[...] + through(0, 0, tok)
    for c in range(chunks):
        for j in range(1, second):
            n_copy(j, c).wait_recv()
            back_out[j, c * part : (c + 1) * part, :] = through(j, c * part, part).astype(BF16)
            b_copy(j, c).start()
    for c in range(chunks):
        at = slice(c * part, (c + 1) * part)
        for j in range(1, second):
            b_copy(j, c).wait_recv()
            two_ref[at, :] += back_in[j, at, :].astype(F32)
    hidden_two = two_ref[...]
    output_ref[...] = hidden_two.astype(BF16)
    normed, _ = normalise(hidden_two)
    query_key = (normed * gains_ref[2:3, :]).astype(BF16)
    for n in range(nar):
        key_ref[n] = query_key[:, n * (width // nar) : (n + 1) * (width // nar)]
    for c in range(chunks):
        for j in range(1, second):
            n_copy(j, c).wait_send()
            b_copy(j, c).wait_send()


def ffn(att, inputs, gains, proj, in_all, out_all, name):
    nar, tok, local = att.shape
    first, width, hidden = in_all.shape
    second = nar // first
    chunks = 2
    vmem = pl.BlockSpec(memory_space=pltpu.VMEM)
    dma = pltpu.SemaphoreType.DMA((second, chunks))
    return pl.pallas_call(
        functools.partial(ffn_kernel, chunks),
        out_shape=(
            jax.ShapeDtypeStruct((tok, width), F32),
            jax.ShapeDtypeStruct((tok, width), F32),
            jax.ShapeDtypeStruct((tok, width), BF16),
            jax.ShapeDtypeStruct((nar, tok, width // nar), BF16),
            jax.ShapeDtypeStruct((second, tok, width), BF16),
            jax.ShapeDtypeStruct((second, tok, first * hidden), F32),
        ),
        in_specs=[vmem] * 6,
        out_specs=(vmem,) * 6,
        scratch_shapes=[pltpu.VMEM((second, tok, width), BF16)] * 2 + [dma] * 4,
        compiler_params=pltpu.CompilerParams(
            collective_id=name, has_side_effects=True, vmem_limit_bytes=48 * 2**20
        ),
    )(att, inputs, gains, proj, in_all, out_all)


def ffn_back_kernel(
    chunks,
    slices_ref,
    att_ref,
    cot_ref,
    one_ref,
    two_ref,
    gains_ref,
    pre_ref,
    normed_ref,
    proj_ref,
    in_ref,
    mid_ref,
    grad_one_ref,
    grad_att_ref,
    gain_ref,
    pre_turned_ref,
    act_turned_ref,
    att_turned_ref,
    normed_cols_ref,
    ffn_cols_ref,
    branch_cols_ref,
    grads,
    grad_two,
    total,
    back_out,
    back_in,
    n_send,
    n_recv,
    b_send,
    b_recv,
):
    nar, tok, local = att_ref.shape
    first, width, hidden = in_ref.shape
    second = nar // first
    wid = branch_cols_ref.shape[0]
    columns = width // wid
    part = tok // chunks
    last = (((1,), (1,)), ((), ()))
    za, yb = lax.axis_index("z"), lax.axis_index("y")

    greet([{"z": za, "y": lax.rem(yb + j, second)} for j in range(1, second)])

    def n_copy(j, c):
        at = pl.ds(c * part, part)
        target = {"z": za, "y": lax.rem(yb + j, second)}
        return push(grads.at[0, at], grads.at[j, at], n_send.at[j, c], n_recv.at[j, c], target)

    def b_copy(j, c):
        at = pl.ds(c * part, part)
        target = {"z": za, "y": lax.rem(yb + second - j, second)}
        return push(
            back_out.at[j, at], back_in.at[j, at], b_send.at[j, c], b_recv.at[j, c], target
        )

    def through(j, start, count):
        at = slice(start, start + count)
        sums = jnp.zeros((count, width), F32)
        for z in range(first):
            own = slice(z * hidden, (z + 1) * hidden)
            pre = pre_ref[j, at, own]
            activated, tanh = gelu_parts(pre)
            slope = 0.5 * (1.0 + tanh) + 0.5 * pre * (1.0 - tanh * tanh) * INNER * (
                1.0 + 3.0 * CUBIC * pre * pre
            )
            grad_act = lax.dot_general(
                grads[j, at, :], mid_ref[z], last, preferred_element_type=F32
            )
            grad_pre = slope * grad_act
            to = slice(j * tok + start, j * tok + start + count)
            act_turned_ref[own, to] = jnp.transpose(activated).astype(BF16)
            pre_turned_ref[own, to] = jnp.transpose(grad_pre).astype(BF16)
            sums = sums + lax.dot_general(
                grad_pre.astype(BF16), in_ref[z], last, preferred_element_type=F32
            )
        return sums

    grad_key = jnp.concatenate([slices_ref[n] for n in range(nar)], axis=1).astype(F32)
    normed, inverse = normalise(two_ref[...])
    gain_ref[1:2, :] = jnp.sum(grad_key * normed, axis=0, keepdims=True)
    grad = cot_ref[...].astype(F32) + normalise_back(
        grad_key, normed, inverse, gains_ref[2:3, :]
    )
    grad_two[...] = grad
    grads[0] = grad.astype(BF16)
    for c in range(chunks):
        for j in range(1, second):
            n_copy(j, c).start()
    total[...] = through(0, 0, tok)
    for c in range(chunks):
        for j in range(1, second):
            n_copy(j, c).wait_recv()
            back_out[j, c * part : (c + 1) * part, :] = through(j, c * part, part).astype(BF16)
            b_copy(j, c).start()
    att_turned_ref[...] = jnp.concatenate(
        [jnp.transpose(att_ref[n].astype(F32)).astype(BF16) for n in range(nar)], axis=0
    )
    for j in range(second):
        for w in range(wid):
            own = slice(w * columns, (w + 1) * columns)
            normed_cols_ref[w, j * tok : (j + 1) * tok, :] = normed_ref[j, :, own]
            ffn_cols_ref[w, j * tok : (j + 1) * tok, :] = grads[j, :, own]
    for c in range(chunks):
        at = slice(c * part, (c + 1) * part)
        for j in range(1, second):
            b_copy(j, c).wait_recv()
            total[at, :] += back_in[j, at, :].astype(F32)
    normed, inverse = normalise(one_ref[...])
    gain_ref[0:1, :] = jnp.sum(total[...] * normed, axis=0, keepdims=True)
    grad = grad_two[...] + normalise_back(total[...], normed, inverse, gains_ref[1:2, :])
    grad_one_ref[...] = grad
    branch = grad.astype(BF16)
    grad_att = lax.dot_general(
        branch, proj_ref[...].reshape(nar * local, width), last, preferred_element_type=F32
    ).astype(BF16)
    for n in range(nar):
        grad_att_ref[n] = grad_att[:, n * local : (n + 1) * local]
    for w in range(wid):
        branch_cols_ref[w] = branch[:, w * columns : (w + 1) * columns]
    for c in range(chunks):
        for j in range(1, second):
            n_copy(j, c).wait_send()
            b_copy(j, c).wait_send()


def ffn_back(slices, att, cot, one, two, gains, pre, normed, proj, in_all, out_all, wid, name):
    nar, tok, local = att.shape
    first, width, hidden = in_all.shape
    second = nar // first
    chunks = 2
    columns = width // wid
    vmem = pl.BlockSpec(memory_space=pltpu.VMEM)
    dma = pltpu.SemaphoreType.DMA((second, chunks))
    return pl.pallas_call(
        functools.partial(ffn_back_kernel, chunks),
        out_shape=(
            jax.ShapeDtypeStruct((tok, width), F32),
            jax.ShapeDtypeStruct((nar, tok, local), BF16),
            jax.ShapeDtypeStruct((2, width), F32),
            jax.ShapeDtypeStruct((first * hidden, second * tok), BF16),
            jax.ShapeDtypeStruct((first * hidden, second * tok), BF16),
            jax.ShapeDtypeStruct((nar * local, tok), BF16),
            jax.ShapeDtypeStruct((wid, second * tok, columns), BF16),
            jax.ShapeDtypeStruct((wid, second * tok, columns), BF16),
            jax.ShapeDtypeStruct((wid, tok, columns), BF16),
        ),
        in_specs=[vmem] * 11,
        out_specs=(vmem,) * 9,
        scratch_shapes=[
            pltpu.VMEM((second, tok, width), BF16),
            pltpu.VMEM((tok, width), F32),
            pltpu.VMEM((tok, width), F32),
            pltpu.VMEM((second, tok, width), BF16),
            pltpu.VMEM((second, tok, width), BF16),
        ]
        + [dma] * 4,
        compiler_params=pltpu.CompilerParams(
            collective_id=name, has_side_effects=True, vmem_limit_bytes=52 * 2**20
        ),
    )(slices, att, cot, one, two, gains, pre, normed, proj, in_all, out_all)


def grad_kernel(
    nar,
    first,
    wid,
    seqs,
    heads,
    block,
    grad_ref,
    qkv_ref,
    lse_ref,
    col_ref,
    row_ref,
    weight_ref,
    input_ref,
    above_ref,
    gain_ref,
    pre_ref,
    act_ref,
    att_ref,
    normed_ref,
    ffn_ref,
    branch_ref,
    out_ref,
    own_ref,
    sum_ref,
    ffn_grad_ref,
    proj_grad_ref,
    grads,
    got,
    grad_key,
    grad_value,
    core_out,
    core_in,
    chip_out,
    chip_in,
    held,
    turn_out,
    turn_in,
    line_out,
    line_in,
    a_send,
    a_recv,
    b_send,
    b_recv,
    c_send,
    c_recv,
    x_send,
    x_recv,
    y_send,
    y_recv,
    z_send,
    z_recv,
):
    second = nar // first
    outer = wid // 2
    za, yb = lax.axis_index("z"), lax.axis_index("y")
    me = za * second + yb
    wide = lax.axis_index("wide")
    chip, core = wide // 2, lax.rem(wide, 2)
    tok, local = grad_ref.shape[1:]
    hidden = pre_ref.shape[0] // first
    columns = normed_ref.shape[2]
    rows = 2 * hidden
    body = first * rows
    length = nar * tok // seqs
    per_seq = nar // seqs
    width = heads * HD
    across = (((0,), (0,)), ((), ()))
    last = (((1,), (1,)), ((), ()))

    greet(
        [place(lax.rem(me + k, nar), second) for k in range(1, nar)]
        + [{"wide": chip * 2 + (1 - core)}]
        + [{"wide": lax.rem(chip + i, outer) * 2 + core} for i in range(1, outer)]
    )

    def a_copy(target, source):
        return push(
            grad_ref.at[target],
            grads.at[source],
            a_send.at[target],
            a_recv.at[source],
            place(target, second),
        )

    def b_copy(target, source):
        return push(
            out_ref.at[pl.ds(pl.multiple_of(target * tok, tok), tok)],
            got.at[source],
            b_send.at[target],
            b_recv.at[source],
            place(target, second),
        )

    def c_copy(o):
        return push(
            core_out.at[o],
            core_in.at[o],
            c_send.at[o],
            c_recv.at[o],
            {"wide": chip * 2 + (1 - core)},
        )

    def span(z):
        return pl.ds(pl.multiple_of(z * rows, rows), rows)

    tail_rows = pl.ds(body, nar * local)

    def x_copy(i, q, at):
        return push(
            chip_out.at[i, at],
            chip_in.at[i, at],
            x_send.at[i, q],
            x_recv.at[i, q],
            {"wide": lax.rem(chip + i, outer) * 2 + core},
        )

    def y_copy(j):
        target = {"z": za, "y": lax.rem(yb + j, second)}
        return push(turn_out.at[j], turn_in.at[j], y_send.at[j], y_recv.at[j], target)

    def z_copy(i):
        target = {"z": lax.rem(za + i, first), "y": yb}
        return push(line_out.at[i], line_in.at[i], z_send.at[i], z_recv.at[i], target)

    def product_rows(w, z):
        own = pl.ds(pl.multiple_of(z * hidden, hidden), hidden)
        return (
            jnp.dot(pre_ref[own, :], normed_ref[w], preferred_element_type=F32),
            jnp.dot(act_ref[own, :], ffn_ref[w], preferred_element_type=F32),
        )

    def product_tail(w):
        return jnp.dot(att_ref[...], branch_ref[w], preferred_element_type=F32)

    for k in range(1, nar):
        a_copy(lax.rem(me + k, nar), me).start()
    grads[me] = grad_ref[me]

    def for_core(o, carry):
        w = o * 2 + (1 - core)

        def line(z, c):
            upper, lower = product_rows(w, z)
            at = pl.multiple_of(z * rows, rows)
            core_out[o, pl.ds(at, hidden), :] = upper.astype(BF16)
            core_out[o, pl.ds(at + hidden, hidden), :] = lower.astype(BF16)
            return c

        lax.fori_loop(0, first, line, 0)
        core_out[o, tail_rows, :] = product_tail(w).astype(BF16)
        c_copy(o).start()
        return carry

    for i in range(1, outer + 1):
        for_core(lax.rem(chip + i, outer), 0)

    for i in range(1, outer):
        o = lax.rem(chip + i, outer)
        w = o * 2 + core
        c_copy(o).wait_recv()
        total = product_tail(w) + core_in[o, tail_rows, :].astype(F32)
        chip_out[i, tail_rows, :] = total.astype(BF16)
        x_copy(i, 0, tail_rows).start()

        def line(n, c, o=o, w=w, i=i):
            z = lax.rem(za + n, first)
            upper, lower = product_rows(w, z)
            at = pl.multiple_of(z * rows, rows)
            high, low = pl.ds(at, hidden), pl.ds(at + hidden, hidden)
            chip_out[i, high, :] = (upper + core_in[o, high, :].astype(F32)).astype(BF16)
            chip_out[i, low, :] = (lower + core_in[o, low, :].astype(F32)).astype(BF16)
            x_copy(i, n, span(z)).start()
            return c

        lax.fori_loop(1, first + 1, line, 0)

    def sequence(seq, carry):
        base = seq * length

        def arrive(b, c):
            source = seq * per_seq + b

            @pl.when(source != me)
            def _():
                a_copy(source, source).wait_recv()

            return c

        lax.fori_loop(0, per_seq, arrive, 0)
        grad_key[...] = jnp.zeros_like(grad_key)
        grad_value[...] = jnp.zeros_like(grad_value)
        for start in range(0, length, block):
            keys = start + block
            at = pl.multiple_of(base + start, block)
            query_segment = col_ref[pl.ds(at, block), 0:1]
            key_segment = row_ref[seq, 0:1, 0:keys]
            spot = lax.broadcasted_iota(jnp.int32, (block, keys), 1)
            own = lax.broadcasted_iota(jnp.int32, (block, keys), 0) + start
            allowed = (spot <= own) & (query_segment == key_segment)
            whole = pl.ds(pl.multiple_of(base, length), keys)
            query = qkv_ref[pl.ds(at, block), 0:width]
            key = qkv_ref[whole, width : 2 * width]
            value = qkv_ref[whole, 2 * width : 3 * width]
            each = min(tok, block)
            grad = jnp.concatenate(
                [
                    grads[
                        seq * per_seq + (start + r) // tok,
                        (start + r) % tok : (start + r) % tok + each,
                        :,
                    ]
                    for r in range(0, block, each)
                ],
                axis=0,
            )
            total = jnp.zeros((block, width), F32)
            for head in range(heads):
                own_query = head_lanes(query, head)
                own_grad = head_lanes(grad, head)
                scores = lax.dot_general(own_query, key, last, preferred_element_type=F32)
                probs = jnp.where(
                    allowed, jnp.exp(scores - lse_ref[pl.ds(at, block), head : head + 1]), 0.0
                )
                grad_probs = lax.dot_general(own_grad, value, last, preferred_element_type=F32)
                delta = jnp.sum(probs * grad_probs, axis=-1, keepdims=True)
                grad_scores = (probs * (grad_probs - delta)).astype(BF16)
                total = total + head_lanes(
                    jnp.dot(grad_scores, key, preferred_element_type=F32), head
                )
                grad_key[0:keys, :] += lax.dot_general(
                    grad_scores, own_query, across, preferred_element_type=F32
                )
                grad_value[0:keys, :] += lax.dot_general(
                    probs.astype(BF16), own_grad, across, preferred_element_type=F32
                )
            out_ref[pl.ds(at, block), 0:width] = (total * HD ** (-0.5)).astype(BF16)
        every = pl.ds(pl.multiple_of(base, length), length)
        out_ref[every, width : 2 * width] = grad_key[...].astype(BF16)
        out_ref[every, 2 * width : 3 * width] = grad_value[...].astype(BF16)

        def leave(b, c):
            target = seq * per_seq + b

            @pl.when(target != me)
            def _():
                b_copy(target, me).start()

            return c

        lax.fori_loop(0, per_seq, leave, 0)
        return carry

    lax.fori_loop(0, seqs, sequence, 0)

    w = chip * 2 + core
    c_copy(chip).wait_recv()
    held[tail_rows, :] = product_tail(w) + core_in[chip, tail_rows, :].astype(F32)

    def line_own(z, c):
        upper, lower = product_rows(w, z)
        at = pl.multiple_of(z * rows, rows)
        high, low = pl.ds(at, hidden), pl.ds(at + hidden, hidden)
        held[high, :] = upper + core_in[chip, high, :].astype(F32)
        held[low, :] = lower + core_in[chip, low, :].astype(F32)
        return c

    lax.fori_loop(0, first, line_own, 0)

    for i in range(1, outer):
        x_copy(i, 0, tail_rows).wait_recv()
        held[tail_rows, :] += chip_in[i, tail_rows, :].astype(F32)
    for j in range(1, second):
        column = lax.rem(yb + j, second)
        for z in range(first):
            at = pl.ds(pl.multiple_of(body + (z * second + column) * local, local), local)
            turn_out[j, z] = held[at, :].astype(BF16)
        y_copy(j).start()

    normed, inverse = normalise(input_ref[...].astype(F32))
    mine = out_ref[pl.ds(pl.multiple_of(me * tok, tok), tok), :]
    total = jnp.dot(mine, weight_ref[me], preferred_element_type=F32)
    for k in range(1, nar):
        source = lax.rem(me + k, nar)
        b_copy(source, source).wait_recv()
        total = total + jnp.dot(got[source], weight_ref[source], preferred_element_type=F32)
    grad = above_ref[...] + normalise_back(total, normed, inverse, gain_ref[0:1, :])
    own_ref[...] = grad.astype(BF16)
    sum_ref[...] = jnp.sum(total * normed, axis=0, keepdims=True)

    for j in range(1, second):
        y_copy(j).wait_recv()
    for n in range(1, first + 1):
        z = lax.rem(za + n, first)
        at = pl.ds(pl.multiple_of(body + (z * second + yb) * local, local), local)
        part = held[at, :]
        for j in range(1, second):
            part = part + turn_in[j, z].astype(F32)
        whole = held[span(z), :]
        for i in range(1, outer):
            x_copy(i, n, span(z)).wait_recv()
            whole = whole + chip_in[i, span(z), :].astype(F32)
        if n < first:
            line_out[n, 0:rows, :] = whole.astype(BF16)
            line_out[n, rows:, :] = part.astype(BF16)
            z_copy(n).start()
        else:
            ffn_grad_ref[...] = whole
            proj_grad_ref[...] = part
    for n in range(1, first):
        z_copy(n).wait_recv()
        ffn_grad_ref[...] += line_in[n, 0:rows, :].astype(F32)
        proj_grad_ref[...] += line_in[n, rows:, :].astype(F32)

    for k in range(1, nar):
        a_copy(lax.rem(me + k, nar), me).wait_send()
        b_copy(lax.rem(me + k, nar), me).wait_send()
    for o in range(outer):
        c_copy(o).wait_send()
    for i in range(1, outer):
        x_copy(i, 0, tail_rows).wait_send()
        for n in range(1, first + 1):
            x_copy(i, n, span(lax.rem(za + n, first))).wait_send()
    for j in range(1, second):
        y_copy(j).wait_send()
    for n in range(1, first):
        z_copy(n).wait_send()


def attention_grads(
    grads, qkv, lse, columns, row_form, weights, inputs, above, gain, first, wid, sides, name
):
    nar, tok, local = grads.shape
    rows, wide = qkv.shape
    width = inputs.shape[1]
    seqs, _, length = row_form.shape
    second = nar // first
    outer = wid // 2
    hidden = sides[0].shape[0] // first
    piece = width // wid
    body = first * 2 * hidden + nar * local
    line = 2 * hidden + local
    vmem = pl.BlockSpec(memory_space=pltpu.VMEM)
    dma = pltpu.SemaphoreType.DMA
    return pl.pallas_call(
        functools.partial(grad_kernel, nar, first, wid, seqs, local // HD, min(256, length)),
        out_shape=(
            jax.ShapeDtypeStruct((rows, wide), BF16),
            jax.ShapeDtypeStruct((tok, width), BF16),
            jax.ShapeDtypeStruct((1, width), F32),
            jax.ShapeDtypeStruct((2 * hidden, piece), F32),
            jax.ShapeDtypeStruct((local, piece), F32),
        ),
        in_specs=[vmem] * 15,
        out_specs=(vmem,) * 5,
        scratch_shapes=[
            pltpu.VMEM((nar, tok, local), BF16),
            pltpu.VMEM((nar, tok, wide), BF16),
            pltpu.VMEM((length, local), F32),
            pltpu.VMEM((length, local), F32),
            pltpu.VMEM((outer, body, piece), BF16),
            pltpu.VMEM((outer, body, piece), BF16),
            pltpu.VMEM((outer, body, piece), BF16),
            pltpu.VMEM((outer, body, piece), BF16),
            pltpu.VMEM((body, piece), F32),
            pltpu.VMEM((second, first, local, piece), BF16),
            pltpu.VMEM((second, first, local, piece), BF16),
            pltpu.VMEM((first, line, piece), BF16),
            pltpu.VMEM((first, line, piece), BF16),
            dma((nar,)),
            dma((nar,)),
            dma((nar,)),
            dma((nar,)),
            dma((outer,)),
            dma((outer,)),
            dma((outer, first + 1)),
            dma((outer, first + 1)),
            dma((second,)),
            dma((second,)),
            dma((first,)),
            dma((first,)),
        ],
        compiler_params=pltpu.CompilerParams(
            collective_id=name, has_side_effects=True, vmem_limit_bytes=60 * 2**20
        ),
    )(grads, qkv, lse, columns, row_form, weights, inputs, above, gain, *sides)


def tail_kernel(
    nar,
    wid,
    first,
    chunks,
    own_ref,
    sums_ref,
    out_ref,
    total_ref,
    all_sums,
    pieces_out,
    pieces_in,
    z_send,
    z_recv,
    y_send,
    y_recv,
    s_send,
    s_recv,
    p_send,
    p_recv,
):
    second = nar // first
    za, yb = lax.axis_index("z"), lax.axis_index("y")
    me = za * second + yb
    mine = lax.axis_index("wide")
    tok = own_ref.shape[0]
    piece = total_ref.shape[1]
    part = tok // chunks

    greet(
        [place(lax.rem(me + k, nar), second) for k in range(1, nar)]
        + [{"wide": lax.rem(mine + w, wid)} for w in range(1, wid)]
    )

    def z_copy(i, c):
        rows = pl.ds(c * part, part)
        target = lax.rem(za + i, first) * second + yb
        return push(
            own_ref.at[rows],
            out_ref.at[me, rows],
            z_send.at[i, c],
            z_recv.at[i, c],
            place(target, second),
        )

    def y_copy(i, j, c):
        source = lax.rem(za + first - i, first) * second + yb
        rows = pl.ds(c * part, part)
        target = za * second + lax.rem(yb + j, second)
        return push(
            own_ref.at[rows] if i == 0 else out_ref.at[source, rows],
            out_ref.at[source, rows],
            y_send.at[i, j, c],
            y_recv.at[i, j, c],
            place(target, second),
        )

    def s_copy(k):
        return push(
            sums_ref,
            all_sums.at[k],
            s_send.at[k],
            s_recv.at[k],
            place(lax.rem(me + k, nar), second),
        )

    def p_copy(w):
        target = lax.rem(mine + w, wid)
        return push(
            pieces_out.at[target], pieces_in.at[w], p_send.at[w], p_recv.at[w], {"wide": target}
        )

    for k in range(1, nar):
        s_copy(k).start()
    for c in range(chunks):
        for i in range(1, first):
            z_copy(i, c).start()
        for j in range(1, second):
            y_copy(0, j, c).start()
    out_ref[me] = own_ref[...]
    sums = sums_ref[...]
    for k in range(1, nar):
        s_copy(k).wait_recv()
        sums = sums + all_sums[k]
    for w in range(wid):
        pieces_out[w] = sums[:, w * piece : (w + 1) * piece]
    for w in range(1, wid):
        p_copy(w).start()
    for c in range(chunks):
        for i in range(1, first):
            z_copy(i, c).wait_recv()
            for j in range(1, second):
                y_copy(i, j, c).start()
    answer = pieces_out[mine]
    for w in range(1, wid):
        p_copy(w).wait()
        answer = answer + pieces_in[w]
    total_ref[...] = answer
    for k in range(1, nar):
        s_copy(k).wait_send()
    for c in range(chunks):
        for i in range(1, first):
            z_copy(i, c).wait_send()
        for i in range(first):
            for j in range(1, second):
                y_copy(i, j, c).wait()


def tail(own, sums, nar, first, wid, name):
    tok, width = own.shape
    second = nar // first
    chunks = 4
    vmem = pl.BlockSpec(memory_space=pltpu.VMEM)
    dma = pltpu.SemaphoreType.DMA
    return pl.pallas_call(
        functools.partial(tail_kernel, nar, wid, first, chunks),
        out_shape=(
            jax.ShapeDtypeStruct((nar, tok, width), BF16),
            jax.ShapeDtypeStruct((8, width // wid), F32),
        ),
        in_specs=[vmem] * 2,
        out_specs=(vmem, vmem),
        scratch_shapes=[
            pltpu.VMEM((nar, 8, width), F32),
            pltpu.VMEM((wid, 8, width // wid), F32),
            pltpu.VMEM((wid, 8, width // wid), F32),
            dma((first, chunks)),
            dma((first, chunks)),
            dma((first, second, chunks)),
            dma((first, second, chunks)),
            dma((nar,)),
            dma((nar,)),
            dma((wid,)),
            dma((wid,)),
        ],
        compiler_params=pltpu.CompilerParams(
            collective_id=name, has_side_effects=True, vmem_limit_bytes=48 * 2**20
        ),
    )(own, sums)


def neighbour_kernel(
    nar,
    first,
    tiles,
    tile,
    kept,
    ring,
    query_ref,
    keys_ref,
    norms_ref,
    ids_ref,
    cols_ref,
    scal_ref,
    grad_ref,
    loss_ref,
    stat_ref,
    queries,
    partial,
    dist,
    grads,
    sends,
    slots,
    loss_own,
    slot_sem,
    q_send,
    q_recv,
    d_send,
    d_recv,
    g_send,
    g_recv,
    l_send,
    l_recv,
    o_send,
    o_recv,
):
    second = nar // first
    me = lax.axis_index("z") * second + lax.axis_index("y")
    tok = query_ref.shape[1]
    depth = query_ref.shape[2]
    group = 16
    per_block = tok // tile
    late = tiles - kept

    def peer(k):
        return lax.rem(me + k, nar)

    def origin(k):
        return lax.rem(me + nar - k, nar)

    def load(index, slot):
        block, sub = index // per_block, lax.rem(index, per_block)
        row = origin(block) * tok + sub * tile
        return pltpu.make_async_copy(
            keys_ref.at[pl.ds(row, tile)], slots.at[slot], slot_sem.at[slot]
        )

    for i in range(kept + ring):
        load(i, i).start()

    greet([place(peer(k), second) for k in range(1, nar)])

    def q_copy(k):
        return push(
            query_ref.at[peer(k)],
            queries.at[k],
            q_send.at[k],
            q_recv.at[k],
            place(peer(k), second),
        )

    def d_copy(k):
        return push(
            partial.at[k], dist.at[k], d_send.at[k], d_recv.at[k], place(origin(k), second)
        )

    def g_copy(k):
        return push(
            grads.at[0], grads.at[k], g_send.at[k], g_recv.at[k], place(peer(k), second)
        )

    def l_copy(k):
        return push(
            loss_own, loss_ref.at[me], l_send.at[k], l_recv.at[k], place(peer(k), second)
        )

    def o_copy(k):
        return push(
            sends.at[k], grad_ref.at[me], o_send.at[k], o_recv.at[k], place(origin(k), second)
        )

    for k in range(1, nar):
        q_copy(k).start()
    queries[0] = query_ref[me]

    row_of = lax.broadcasted_iota(jnp.int32, (group, J), 0)

    def slot_of(index):
        return jnp.where(index < kept, index, kept + lax.rem(index - kept, ring))

    def slot_late(n):
        return kept + lax.rem(n, ring)

    def forward_tile(k, sub, slot):
        def one(g, carry):
            at = pl.multiple_of(sub * tile + g * group, group)
            own = queries[k, pl.ds(at, group), :].astype(F32)
            keys = slots[slot, pl.ds(g * group, group), :, :].reshape(group * depth, J)
            wide = jnp.concatenate(
                [jnp.where(row_of[:, :depth] == t, own, 0.0) for t in range(group)], axis=1
            ).astype(BF16)
            out = jnp.dot(wide, keys, preferred_element_type=F32)
            row = pl.multiple_of(origin(k) * tok + at, group)
            partial[k, pl.ds(at, group), :] = 2.0 * out - norms_ref[pl.ds(row, group), :]
            return carry

        lax.fori_loop(0, tile // group, one, 0, unroll=True)

    def forward_block(k):
        def body(sub, carry):
            index = k * per_block + sub
            slot = slot_of(index)
            load(index, slot).wait()
            forward_tile(k, sub, slot)

            @pl.when(index >= kept)
            def _():
                nxt = index - kept + ring

                @pl.when(nxt < 2 * late)
                def _():
                    load(kept + lax.rem(nxt, late), slot).start()

            return carry

        lax.fori_loop(0, per_block, body, 0)

    forward_block(0)

    def forward_rest(k, carry):
        q_copy(k).wait_recv()
        forward_block(k)
        d_copy(k).start()
        return carry

    lax.fori_loop(1, nar, forward_rest, 0)

    def collect(k, total):
        d_copy(k).wait_recv()
        return total + dist[k]

    distance = lax.fori_loop(1, nar, collect, partial[0])
    temper_value = scal_ref[0]
    mix_value = scal_ref[1]
    count = cols_ref[:, 0:1]
    target = cols_ref[:, 1:2]
    base = cols_ref[:, 2:3]
    loss_weight = cols_ref[:, 3:4]
    logits = distance / temper_value
    spot = lax.broadcasted_iota(jnp.int32, (tok, J), 1).astype(F32)
    masked = jnp.where(spot < count, logits, -1e30)
    peak = jnp.max(masked, axis=-1, keepdims=True)
    expo = jnp.exp(masked - peak)
    weights = expo / jnp.sum(expo, axis=-1, keepdims=True)
    matches = jnp.where(ids_ref[...].astype(F32) == target, 1.0, 0.0)
    knn_prob = jnp.sum(weights * matches, axis=-1, keepdims=True)
    mixture = mix_value * knn_prob + (1.0 - mix_value) * base
    grad_mixture = -loss_weight / mixture
    grad_logits = weights * (mix_value * grad_mixture) * (matches - knn_prob)
    grads[0] = (2.0 * grad_logits / temper_value).astype(BF16)
    for k in range(1, nar):
        g_copy(k).start()
    loss = jnp.transpose(jnp.broadcast_to(-jnp.log(mixture), (tok, J)))[0:8, :]
    loss_own[...] = loss
    for k in range(1, nar):
        l_copy(k).start()
    loss_ref[me] = loss
    term_temper = -jnp.sum(grad_logits * logits, axis=0, keepdims=True) / temper_value
    term_mix = jnp.sum((knn_prob - base) * grad_mixture, axis=0, keepdims=True)
    stat_ref[0:1, :] = term_temper
    stat_ref[1:2, :] = jnp.broadcast_to(term_mix, (1, J))

    def backward_tile(k, sub, slot):
        def one(g, carry):
            at = pl.multiple_of(sub * tile + g * group, group)
            own = grads[k, pl.ds(at, group), :]
            keys = slots[slot, pl.ds(g * group, group), :, :].reshape(group * depth, J)
            out = lax.dot_general(
                own, keys, (((1,), (1,)), ((), ())), preferred_element_type=F32
            )
            total = jnp.zeros((group, depth), F32)
            for t in range(group):
                total = jnp.where(
                    row_of[:, :depth] == t, out[:, t * depth : (t + 1) * depth], total
                )
            sends[k, pl.ds(at, group), :] = total.astype(BF16)
            return carry

        lax.fori_loop(0, tile // group, one, 0, unroll=True)

    def backward_block(k):
        def body(sub, carry):
            index = k * per_block + sub

            @pl.when(index < kept)
            def _():
                backward_tile(k, sub, index)

            @pl.when(index >= kept)
            def _():
                n = index - kept + late
                slot = slot_late(n)
                load(index, slot).wait()
                backward_tile(k, sub, slot)

                @pl.when(n + ring < 2 * late)
                def _():
                    load(kept + lax.rem(n + ring, late), slot).start()

            return carry

        lax.fori_loop(0, per_block, body, 0)

    backward_block(0)
    grad_ref[me] = sends[0]

    def backward_rest(k, carry):
        g_copy(k).wait_recv()
        backward_block(k)
        o_copy(k).start()
        return carry

    lax.fori_loop(1, nar, backward_rest, 0)

    for k in range(1, nar):
        q_copy(k).wait_send()
        d_copy(k).wait_send()
        g_copy(k).wait_send()
        l_copy(k).wait()
        o_copy(k).wait()


def neighbours(nar, first, query, keys, norms, ids, cols, scal):
    tok, depth = query.shape[1:]
    rows = keys.shape[0]
    tile = 32
    tiles = rows // tile
    bytes_tile = tile * depth * J * 2
    ring = 4
    kept = min(tiles - 2 * ring, (KEPT_BYTES // bytes_tile))
    vmem = pl.BlockSpec(memory_space=pltpu.VMEM)
    dma = pltpu.SemaphoreType.DMA((nar,))
    return pl.pallas_call(
        functools.partial(neighbour_kernel, nar, first, tiles, tile, kept, ring),
        out_shape=(
            jax.ShapeDtypeStruct((nar, tok, depth), BF16),
            jax.ShapeDtypeStruct((nar, 8, tok), F32),
            jax.ShapeDtypeStruct((2, J), F32),
        ),
        in_specs=[
            vmem,
            pl.BlockSpec(memory_space=pl.ANY),
            vmem,
            vmem,
            vmem,
            pl.BlockSpec(memory_space=pltpu.SMEM),
        ],
        out_specs=(vmem, vmem, vmem),
        scratch_shapes=[
            pltpu.VMEM((nar, tok, depth), BF16),
            pltpu.VMEM((nar, tok, J), F32),
            pltpu.VMEM((nar, tok, J), F32),
            pltpu.VMEM((nar, tok, J), BF16),
            pltpu.VMEM((nar, tok, depth), BF16),
            pltpu.VMEM((kept + ring, tile, depth, J), BF16),
            pltpu.VMEM((8, tok), F32),
            pltpu.SemaphoreType.DMA((kept + ring,)),
        ]
        + [dma] * 10,
        compiler_params=pltpu.CompilerParams(
            collective_id=1, has_side_effects=True, vmem_limit_bytes=60 * 2**20
        ),
    )(query, keys, norms, ids, cols, scal)


def on_device(
    block_input,
    output_cotangent,
    loss_weight,
    segments,
    nbr_keys,
    nbr_count,
    nbr_ids,
    targets,
    base_prob,
    w_query,
    w_key,
    w_value,
    w_proj,
    w_in,
    w_out,
    gain_attn,
    gain_ffn,
    gain_key,
    temper,
    mix_weight,
):
    seqs_here, length, width = block_input.shape
    rows = seqs_here * length
    wid = lax.axis_size("wide")
    first = lax.axis_size("z")
    nar = first * lax.axis_size("y")
    own = lax.axis_index("z") * lax.axis_size("y") + lax.axis_index("y")
    tok = rows // nar
    local_width = w_query.shape[0]

    def mine(values):
        flat = values.reshape((rows,) + values.shape[2:])
        return lax.dynamic_slice_in_dim(flat, own * tok, tok, 0)

    hidden = w_in.shape[1]
    seg_column = segments.reshape(rows, 1)
    seg_row = segments.reshape(seqs_here, 1, length)
    key_slices = nbr_keys.reshape(rows, nbr_keys.shape[2], nbr_keys.shape[3])
    gains = jnp.stack([gain_attn, gain_ffn, gain_key])
    w_qkv = jnp.concatenate([w_query, w_key, w_value], axis=0)
    normed_one, qkv, lse, part_norms, attended_own, in_all, out_all, pq_all = head(
        block_input.reshape(rows, width),
        gains,
        w_qkv,
        seg_column,
        seg_row,
        key_slices,
        w_in,
        w_out,
        jnp.concatenate([w_proj, w_qkv], axis=0),
        first,
        nar,
        wid,
        2,
    )
    proj_all = pq_all[:, :local_width]
    qkv_all = pq_all[:, local_width:]
    inputs_own = mine(block_input)
    hidden_one, hidden_two, output_own, query_key, normed_two, pre_act = ffn(
        attended_own, inputs_own, gains, proj_all, in_all, out_all, 3
    )
    block_output = lax.all_gather(output_own, ("z", "y"), axis=0, tiled=True)
    cols = jnp.stack(
        [
            mine(nbr_count).astype(F32),
            mine(targets).astype(F32),
            mine(base_prob),
            mine(loss_weight),
        ],
        axis=1,
    )
    grad_slices, losses, stats = neighbours(
        nar,
        first,
        query_key,
        key_slices,
        part_norms,
        mine(nbr_ids),
        cols,
        jnp.concatenate([temper, mix_weight]),
    )
    token_loss = losses[:, 0, :]
    grad_hidden_one, grad_attended, gain_sums, *sides = ffn_back(
        grad_slices,
        attended_own,
        mine(output_cotangent),
        hidden_one,
        hidden_two,
        gains,
        pre_act,
        normed_two,
        proj_all,
        in_all,
        out_all,
        wid,
        5,
    )
    grad_attended, block_output = lax.optimization_barrier((grad_attended, block_output))
    grad_qkv, grad_own, attn_sums, grad_ffn_pair, grad_w_proj = attention_grads(
        grad_attended,
        qkv,
        lse,
        seg_column,
        seg_row,
        qkv_all,
        inputs_own,
        grad_hidden_one,
        gains,
        first,
        wid,
        sides,
        6,
    )
    grad_w_qkv = outer_sum(grad_qkv, normed_one).astype(BF16)
    grad_w_qkv, grad_own = lax.optimization_barrier((grad_w_qkv, grad_own))
    grad_w_qkv = lax.psum_scatter(grad_w_qkv, "wide", scatter_dimension=1, tiled=True).astype(F32)
    sums = jnp.concatenate(
        [
            attn_sums,
            gain_sums,
            jnp.broadcast_to(jnp.sum(stats[0]), (1, width)),
            jnp.broadcast_to(stats[1, 0], (1, width)),
            jnp.zeros((3, width), F32),
        ],
        axis=0,
    )
    grad_input, totals = tail(grad_own, sums, nar, first, wid, 4)

    return (
        block_output.reshape(seqs_here, length, width),
        token_loss.reshape(seqs_here, length),
        grad_input.astype(F32).reshape(seqs_here, length, width),
        grad_w_qkv[:local_width],
        grad_w_qkv[local_width : 2 * local_width],
        grad_w_qkv[2 * local_width :],
        grad_w_proj,
        grad_ffn_pair[:hidden].T,
        grad_ffn_pair[hidden:],
        totals[0],
        totals[1],
        totals[2],
        totals[3, 0:1],
        totals[4, 0:1],
    )


def solution(mesh):
    wide, narrow = mesh.devices.shape
    first = 4 if narrow % 4 == 0 else narrow
    split = jax.sharding.Mesh(
        mesh.devices.reshape(wide, first, narrow // first), ("wide", "z", "y")
    )
    narrow = ("z", "y")
    return jax.shard_map(
        on_device,
        mesh=split,
        in_specs=(
            P("wide", None, None),
            P("wide", None, None),
            P("wide", None),
            P("wide", None),
            P("wide", None, narrow, None),
            P("wide", None),
            P("wide", None, None),
            P("wide", None),
            P("wide", None),
            P(narrow, None),
            P(narrow, None),
            P(narrow, None),
            P(narrow, None),
            P(None, narrow),
            P(narrow, None),
            P(),
            P(),
            P(),
            P(),
            P(),
        ),
        out_specs=(
            P("wide", None, None),
            P("wide", None),
            P("wide", None, None),
            P(narrow, "wide"),
            P(narrow, "wide"),
            P(narrow, "wide"),
            P(narrow, "wide"),
            P("wide", narrow),
            P(narrow, "wide"),
            P("wide"),
            P("wide"),
            P("wide"),
            P(),
            P(),
        ),
        check_vma=False,
    )
```

```python
import functools

import jax
import jax.numpy as jnp
from jax import lax
from jax.experimental import pallas as pl
from jax.experimental.pallas import tpu as pltpu
from jax.sharding import PartitionSpec as P

HD = 64
EPSILON = 1e-05
F32 = jnp.float32
BF16 = jnp.bfloat16
MESH = pl.DeviceIdType.MESH
J = 128
KEPT_BYTES = 44 * 2**20


def place(index, second):
    return {"z": index // second, "y": lax.rem(index, second)}


def push(src, dst, send, recv, target):
    return pltpu.make_async_remote_copy(
        src_ref=src,
        dst_ref=dst,
        send_sem=send,
        recv_sem=recv,
        device_id=target,
        device_id_type=MESH,
    )


def greet(peers):
    barrier = pltpu.get_barrier_semaphore()
    for peer in peers:
        pl.semaphore_signal(barrier, inc=1, device_id=peer, device_id_type=MESH)
    pl.semaphore_wait(barrier, len(peers))


def normalise(values):
    centred = values - jnp.mean(values, axis=-1, keepdims=True)
    inverse = lax.rsqrt(jnp.mean(centred * centred, axis=-1, keepdims=True) + EPSILON)
    return centred * inverse, inverse


def normalise_back(grad_out, normed, inverse, gain):
    scaled = grad_out * gain
    return inverse * (
        scaled
        - jnp.mean(scaled, axis=-1, keepdims=True)
        - normed * jnp.mean(scaled * normed, axis=-1, keepdims=True)
    )


def head_lanes(values, head):
    lanes = lax.broadcasted_iota(jnp.int32, values.shape, 1)
    return jnp.where(lanes // HD == head, values, jnp.zeros_like(values))


def head_kernel(
    nar,
    first,
    wid,
    seqs,
    heads,
    block,
    tile,
    ring,
    input_ref,
    gain_ref,
    qkv_weight_ref,
    col_ref,
    row_ref,
    keys_ref,
    in_ref,
    out_ref,
    pq_ref,
    normed_ref,
    qkv_ref,
    lse_ref,
    norms_ref,
    att_ref,
    in_all,
    out_all,
    pq_all,
    attended,
    slots,
    slot_sem,
    own_sem,
    a_send,
    a_recv,
    z_send,
    z_recv,
    y_send,
    y_recv,
    x_send,
    x_recv,
    c_send,
    c_recv,
):
    second = nar // first
    outer = wid // 2
    za, yb = lax.axis_index("z"), lax.axis_index("y")
    me = za * second + yb
    wide = lax.axis_index("wide")
    chip, core = wide // 2, lax.rem(wide, 2)
    rows, width = input_ref.shape
    tok = rows // nar
    length = rows // seqs
    local = heads * HD
    tiles = rows // tile
    last = (((1,), (1,)), ((), ()))

    def fetch(index, slot):
        return pltpu.make_async_copy(
            keys_ref.at[pl.ds(index * tile, tile)], slots.at[slot], slot_sem.at[slot]
        )

    for i in range(ring):
        fetch(i, i).start()

    greet(
        [place(lax.rem(me + k, nar), second) for k in range(1, nar)]
        + [{"wide": chip * 2 + (1 - core)}]
        + [{"wide": lax.rem(chip + o, outer) * 2 + core} for o in range(1, outer)]
    )

    stacks = ((pq_ref, pq_all), (in_ref, in_all), (out_ref, out_all))

    def shard_of(t, source):
        return source if t == 0 else source // second

    def quarter(t, source, owner):
        own, stack = stacks[t]
        count = own.shape[0] // wid
        at = pl.ds(pl.multiple_of(owner * count, count), count)
        return stack.at[shard_of(t, source), at]

    def own_quarter(t):
        own, _ = stacks[t]
        count = own.shape[0] // wid
        return own.at[pl.ds(pl.multiple_of(wide * count, count), count)]

    reach = ((1, 2), (0, 2), (1, 3), (2, 1))
    relay = {1: (0, (2, 3)), 2: (3, (0, 1))}
    if first != 4:
        reach = tuple(tuple(b for b in range(first) if b != a) for a in range(first))
        relay = {}

    def line_copy(t, source, z, slot, own):
        return push(
            own_quarter(t) if own else quarter(t, source, wide),
            quarter(t, source, wide),
            z_send.at[t, source // second, slot],
            z_recv.at[t, source // second],
            {"z": z, "y": yb},
        )

    def owner_of(o):
        return lax.rem(chip + outer - o, outer) * 2 + core

    def row_copy(source, j, o, own):
        owner = owner_of(o)
        count = pq_ref.shape[0] // wid
        at = pl.ds(pl.multiple_of(owner * count, count), count)
        return push(
            pq_ref.at[at] if own else quarter(0, source, owner),
            quarter(0, source, owner),
            y_send.at[source, j, o],
            y_recv.at[source, j, o],
            {"z": za, "y": lax.rem(yb + j, second)},
        )

    def chip_copy(t, source, o):
        return push(
            quarter(t, source, wide),
            quarter(t, source, wide),
            x_send.at[t, source, o],
            x_recv.at[t, source, o],
            {"wide": lax.rem(chip + o, outer) * 2 + core},
        )

    def chip_arrival(t, source, o):
        owner = owner_of(o)
        return push(
            quarter(t, source, owner),
            quarter(t, source, owner),
            x_send.at[t, source, o],
            x_recv.at[t, source, o],
            {"wide": owner},
        )

    def core_copy(t, source, o, away):
        owner = lax.rem(chip + outer - o, outer) * 2 + jnp.where(away, 1 - core, core)
        return push(
            quarter(t, source, owner),
            quarter(t, source, owner),
            c_send.at[t, source, o],
            c_recv.at[t, source, o],
            {"wide": chip * 2 + (1 - core)},
        )

    def att_copy(target, source):
        return push(
            attended.at[target],
            att_ref.at[source],
            a_send.at[target],
            a_recv.at[source],
            place(target, second),
        )

    own_copies = [
        pltpu.make_async_copy(own, stack.at[shard_of(t, me)], own_sem.at[t])
        for t, (own, stack) in enumerate(stacks)
    ]

    def send_own(t):
        for z in range(first):

            @pl.when(za == z)
            def _(z=z):
                for slot, target in enumerate(reach[z]):
                    line_copy(t, me, target, slot, True).start()

        if t == 0:
            for j in range(1, second):
                for o in range(outer):
                    row_copy(me, j, o, True).start()
        own_copies[t].start()

    def line_arrivals(t, begin, end):
        for d in range(begin, end):
            for way in (-1, 1):
                z = za + way * d

                @pl.when((z >= 0) & (z < first))
                def _(z=z):
                    source = z * second + yb
                    line_copy(t, source, za, 0, False).wait_recv()
                    for middle, (target, sources) in relay.items():

                        @pl.when((za == middle) & ((z == sources[0]) | (z == sources[1])))
                        def _(target=target):
                            line_copy(t, source, target, 0, False).start()

                    for o in range(1, outer):
                        chip_copy(t, source, o).start()
                    core_copy(t, source, 0, False).start()

    def chip_arrivals(t):
        for n in range(first):
            source = n * second + yb

            @pl.when(source != me)
            def _(source=source):
                for o in range(1, outer):
                    chip_arrival(t, source, o).wait_recv()
                    core_copy(t, source, o, False).start()
                if t == 0:
                    for j in range(1, second):
                        for o in range(outer):
                            row_copy(source, j, o, False).start()

    def row_arrivals():
        for j in range(1, second):
            for z in range(first):
                source = z * second + lax.rem(yb + second - j, second)
                for o in range(outer):
                    row_copy(source, j, o, False).wait_recv()
                    core_copy(0, source, o, False).start()

    def each_source(t, do):
        for n in range(nar if t == 0 else first):
            source = n if t == 0 else n * second + yb

            @pl.when(source != me)
            def _(source=source):
                do(source)

    def core_arrivals(t):
        def do(source):
            for o in range(outer):
                core_copy(t, source, o, True).wait_recv()

        each_source(t, do)

    for t in range(3):
        send_own(t)

    def project(r, carry):
        at = pl.ds(pl.multiple_of(r * block, block), block)
        normed, _ = normalise(input_ref[at, :].astype(F32))
        low = (normed * gain_ref[0:1, :]).astype(BF16)
        normed_ref[at, :] = low
        out = lax.dot_general(low, qkv_weight_ref[...], last, preferred_element_type=F32)
        lanes = lax.broadcasted_iota(jnp.int32, out.shape, 1)
        qkv_ref[at, :] = jnp.where(lanes < local, out * HD ** (-0.5), out).astype(BF16)
        return carry

    lax.fori_loop(0, rows // block, project, 0)
    line_arrivals(0, 1, 2)

    def sequence(seq, carry):
        base = seq * length
        for start in range(0, length, block):
            keys = start + block
            at = pl.ds(pl.multiple_of(base + start, block), block)
            whole = pl.ds(pl.multiple_of(base, length), keys)
            query_segment = col_ref[at, 0:1]
            key_segment = row_ref[seq, 0:1, 0:keys]
            spot = lax.broadcasted_iota(jnp.int32, (block, keys), 1)
            own = lax.broadcasted_iota(jnp.int32, (block, keys), 0) + start
            allowed = (spot <= own) & (query_segment == key_segment)
            query = qkv_ref[at, 0:local]
            key = qkv_ref[whole, local : 2 * local]
            value = qkv_ref[whole, 2 * local : 3 * local]
            total = jnp.zeros((block, local), F32)
            for head in range(heads):
                scores = lax.dot_general(
                    head_lanes(query, head), key, last, preferred_element_type=F32
                )
                scores = jnp.where(allowed, scores, -1e30)
                peak = jnp.max(scores, axis=-1, keepdims=True)
                expo = jnp.exp(scores - peak)
                sums = jnp.sum(expo, axis=-1, keepdims=True)
                out = jnp.dot(expo.astype(BF16), value, preferred_element_type=F32) / sums
                total = total + head_lanes(out, head)
                lse_ref[at, head : head + 1] = peak + jnp.log(sums)
            each = min(tok, block)
            for r in range(0, block, each):
                target = seq * (nar // seqs) + (start + r) // tok
                spot_row = (start + r) % tok
                attended[target, spot_row : spot_row + each, :] = total[r : r + each, :].astype(
                    BF16
                )

        def leave(b, c):
            target = seq * (nar // seqs) + b

            @pl.when(target != me)
            def _():
                att_copy(target, me).start()

            return c

        lax.fori_loop(0, nar // seqs, leave, 0)
        return carry

    lax.fori_loop(0, seqs, sequence, 0)
    att_ref[me] = attended[me]

    def norms(begin, end):
        def body(index, carry):
            slot = lax.rem(index, ring)
            fetch(index, slot).wait()
            keys = slots[slot].astype(F32)
            at = pl.ds(pl.multiple_of(index * tile, tile), tile)
            norms_ref[at, :] = jnp.sum(keys * keys, axis=1)

            @pl.when(index + ring < tiles)
            def _():
                fetch(index + ring, slot).start()

            return carry

        lax.fori_loop(begin, end, body, 0)

    def some(*calls):
        def run():
            for call in calls:
                call()

        return run

    steps = [
        some(lambda: line_arrivals(1, 1, 2), lambda: line_arrivals(0, 2, first)),
        some(lambda: chip_arrivals(0), lambda: line_arrivals(2, 1, 2)),
        lambda: line_arrivals(1, 2, first),
        lambda: line_arrivals(2, 2, first),
    ]
    share_of = tiles // len(steps)
    for n, step in enumerate(steps):
        step()
        norms(n * share_of, tiles if n == len(steps) - 1 else (n + 1) * share_of)
    row_arrivals()
    chip_arrivals(1)
    chip_arrivals(2)
    for t in range(3):
        core_arrivals(t)
    for k in range(1, nar):
        source = lax.rem(me + k, nar)
        att_copy(source, source).wait_recv()
        att_copy(source, me).wait_send()
    for t in range(3):
        own_copies[t].wait()

        def sent(source, t=t):
            for o in range(outer):
                core_copy(t, source, o, False).wait_send()

        each_source(t, sent)
        for n in range(first):
            source = n * second + yb

            @pl.when(source != me)
            def _(source=source, t=t):
                for o in range(1, outer):
                    chip_copy(t, source, o).wait_send()

        for z in range(first):

            @pl.when(za == z)
            def _(z=z, t=t):
                for slot, target in enumerate(reach[z]):
                    line_copy(t, me, target, slot, True).wait_send()
                if z in relay:
                    target, sources = relay[z]
                    for n in sources:
                        line_copy(t, n * second + yb, target, 0, False).wait_send()

    for z in range(first):
        for j in range(1, second):
            for o in range(outer):
                row_copy(z * second + yb, j, o, False).wait_send()


def head(block_input, gain, w_qkv, columns, row_form, keys, w_in, w_out, pq, first, nar, wid, name):
    rows, width = block_input.shape
    seqs, _, length = row_form.shape
    second = nar // first
    outer = wid // 2
    local = w_qkv.shape[0] // 3
    heads = local // HD
    hidden = w_in.shape[1]
    tok = rows // nar
    depth = keys.shape[1]
    tile, ring = 32, 4
    block = min(256, length)
    vmem = pl.BlockSpec(memory_space=pltpu.VMEM)
    dma = pltpu.SemaphoreType.DMA
    return pl.pallas_call(
        functools.partial(head_kernel, nar, first, wid, seqs, heads, block, tile, ring),
        out_shape=(
            jax.ShapeDtypeStruct((rows, width), BF16),
            jax.ShapeDtypeStruct((rows, 3 * local), BF16),
            jax.ShapeDtypeStruct((rows, heads), F32),
            jax.ShapeDtypeStruct((rows, J), F32),
            jax.ShapeDtypeStruct((nar, tok, local), BF16),
            jax.ShapeDtypeStruct((first, width, hidden), BF16),
            jax.ShapeDtypeStruct((first, hidden, width), BF16),
            jax.ShapeDtypeStruct((nar,) + pq.shape, BF16),
        ),
        in_specs=[vmem] * 5 + [pl.BlockSpec(memory_space=pl.ANY)] + [vmem] * 3,
        out_specs=(vmem,) * 8,
        scratch_shapes=[
            pltpu.VMEM((nar, tok, local), BF16),
            pltpu.VMEM((ring, tile, depth, J), BF16),
            dma((ring,)),
            dma((3,)),
            dma((nar,)),
            dma((nar,)),
            dma((3, first, 2)),
            dma((3, first)),
            dma((nar, second, outer)),
            dma((nar, second, outer)),
            dma((3, nar, outer)),
            dma((3, nar, outer)),
            dma((3, nar, outer)),
            dma((3, nar, outer)),
        ],
        compiler_params=pltpu.CompilerParams(
            collective_id=name, has_side_effects=True, vmem_limit_bytes=58 * 2**20
        ),
    )(block_input, gain, w_qkv, columns, row_form, keys, w_in, w_out, pq)


INNER = 0.7978845608028654
CUBIC = 0.044715


def gelu_parts(values):
    tanh = jnp.tanh(INNER * (values + CUBIC * values * values * values))
    return 0.5 * values * (1.0 + tanh), tanh


def ffn_kernel(
    chunks,
    att_ref,
    input_ref,
    gains_ref,
    proj_ref,
    in_ref,
    mid_ref,
    one_ref,
    two_ref,
    output_ref,
    key_ref,
    normed_ref,
    pre_ref,
    back_out,
    back_in,
    n_send,
    n_recv,
    b_send,
    b_recv,
):
    nar, tok, local = att_ref.shape
    first, width, hidden = in_ref.shape
    second = nar // first
    part = tok // chunks
    za, yb = lax.axis_index("z"), lax.axis_index("y")

    greet([{"z": za, "y": lax.rem(yb + j, second)} for j in range(1, second)])

    def n_copy(j, c):
        at = pl.ds(c * part, part)
        target = {"z": za, "y": lax.rem(yb + j, second)}
        return push(
            normed_ref.at[0, at], normed_ref.at[j, at], n_send.at[j, c], n_recv.at[j, c], target
        )

    def b_copy(j, c):
        at = pl.ds(c * part, part)
        target = {"z": za, "y": lax.rem(yb + second - j, second)}
        return push(
            back_out.at[j, at], back_in.at[j, at], b_send.at[j, c], b_recv.at[j, c], target
        )

    def through(j, start, count):
        total = jnp.zeros((count, width), F32)
        for z in range(first):
            pre = jnp.dot(
                normed_ref[j, start : start + count, :], in_ref[z], preferred_element_type=F32
            )
            pre_ref[j, start : start + count, z * hidden : (z + 1) * hidden] = pre
            activated = gelu_parts(pre)[0].astype(BF16)
            total = total + jnp.dot(activated, mid_ref[z], preferred_element_type=F32)
        return total

    att = jnp.concatenate([att_ref[n] for n in range(nar)], axis=1)
    one = input_ref[...].astype(F32) + jnp.dot(
        att, proj_ref[...].reshape(nar * local, width), preferred_element_type=F32
    )
    one_ref[...] = one
    normed, _ = normalise(one)
    normed_ref[0] = (normed * gains_ref[1:2, :]).astype(BF16)
    for c in range(chunks):
        for j in range(1, second):
            n_copy(j, c).start()
    two_ref[...] = one_ref[...] + through(0, 0, tok)
    for c in range(chunks):
        for j in range(1, second):
            n_copy(j, c).wait_recv()
            back_out[j, c * part : (c + 1) * part, :] = through(j, c * part, part).astype(BF16)
            b_copy(j, c).start()
    for c in range(chunks):
        at = slice(c * part, (c + 1) * part)
        for j in range(1, second):
            b_copy(j, c).wait_recv()
            two_ref[at, :] += back_in[j, at, :].astype(F32)
    hidden_two = two_ref[...]
    output_ref[...] = hidden_two.astype(BF16)
    normed, _ = normalise(hidden_two)
    query_key = (normed * gains_ref[2:3, :]).astype(BF16)
    for n in range(nar):
        key_ref[n] = query_key[:, n * (width // nar) : (n + 1) * (width // nar)]
    for c in range(chunks):
        for j in range(1, second):
            n_copy(j, c).wait_send()
            b_copy(j, c).wait_send()


def ffn(att, inputs, gains, proj, in_all, out_all, name):
    nar, tok, local = att.shape
    first, width, hidden = in_all.shape
    second = nar // first
    chunks = 2
    vmem = pl.BlockSpec(memory_space=pltpu.VMEM)
    dma = pltpu.SemaphoreType.DMA((second, chunks))
    return pl.pallas_call(
        functools.partial(ffn_kernel, chunks),
        out_shape=(
            jax.ShapeDtypeStruct((tok, width), F32),
            jax.ShapeDtypeStruct((tok, width), F32),
            jax.ShapeDtypeStruct((tok, width), BF16),
            jax.ShapeDtypeStruct((nar, tok, width // nar), BF16),
            jax.ShapeDtypeStruct((second, tok, width), BF16),
            jax.ShapeDtypeStruct((second, tok, first * hidden), F32),
        ),
        in_specs=[vmem] * 6,
        out_specs=(vmem,) * 6,
        scratch_shapes=[pltpu.VMEM((second, tok, width), BF16)] * 2 + [dma] * 4,
        compiler_params=pltpu.CompilerParams(
            collective_id=name, has_side_effects=True, vmem_limit_bytes=48 * 2**20
        ),
    )(att, inputs, gains, proj, in_all, out_all)


def ffn_back_kernel(
    chunks,
    slices_ref,
    att_ref,
    cot_ref,
    one_ref,
    two_ref,
    gains_ref,
    pre_ref,
    normed_ref,
    proj_ref,
    in_ref,
    mid_ref,
    stat_ref,
    grad_one_ref,
    grad_att_ref,
    gain_ref,
    pre_turned_ref,
    act_turned_ref,
    att_turned_ref,
    normed_cols_ref,
    ffn_cols_ref,
    branch_cols_ref,
    grads,
    grad_two,
    total,
    back_out,
    back_in,
    n_send,
    n_recv,
    b_send,
    b_recv,
):
    nar, tok, local = att_ref.shape
    first, width, hidden = in_ref.shape
    second = nar // first
    wid = branch_cols_ref.shape[0]
    columns = width // wid
    part = tok // chunks
    last = (((1,), (1,)), ((), ()))
    za, yb = lax.axis_index("z"), lax.axis_index("y")

    greet([{"z": za, "y": lax.rem(yb + j, second)} for j in range(1, second)])

    def n_copy(j, c):
        at = pl.ds(c * part, part)
        target = {"z": za, "y": lax.rem(yb + j, second)}
        return push(grads.at[0, at], grads.at[j, at], n_send.at[j, c], n_recv.at[j, c], target)

    def b_copy(j, c):
        at = pl.ds(c * part, part)
        target = {"z": za, "y": lax.rem(yb + second - j, second)}
        return push(
            back_out.at[j, at], back_in.at[j, at], b_send.at[j, c], b_recv.at[j, c], target
        )

    def through(j, start, count):
        at = slice(start, start + count)
        sums = jnp.zeros((count, width), F32)
        for z in range(first):
            own = slice(z * hidden, (z + 1) * hidden)
            pre = pre_ref[j, at, own]
            activated, tanh = gelu_parts(pre)
            slope = 0.5 * (1.0 + tanh) + 0.5 * pre * (1.0 - tanh * tanh) * INNER * (
                1.0 + 3.0 * CUBIC * pre * pre
            )
            grad_act = lax.dot_general(
                grads[j, at, :], mid_ref[z], last, preferred_element_type=F32
            )
            grad_pre = slope * grad_act
            to = slice(j * tok + start, j * tok + start + count)
            act_turned_ref[own, to] = jnp.transpose(activated).astype(BF16)
            pre_turned_ref[own, to] = jnp.transpose(grad_pre).astype(BF16)
            sums = sums + lax.dot_general(
                grad_pre.astype(BF16), in_ref[z], last, preferred_element_type=F32
            )
        return sums

    grad_key = jnp.concatenate([slices_ref[n] for n in range(nar)], axis=1).astype(F32)
    normed, inverse = normalise(two_ref[...])
    gain_ref[...] = jnp.zeros_like(gain_ref)
    gain_ref[2:3, :] = jnp.sum(grad_key * normed, axis=0, keepdims=True)
    temper_sum = jnp.sum(stat_ref[0:1, :], axis=1, keepdims=True)
    gain_ref[3:4, :] = jnp.broadcast_to(temper_sum, (1, width))
    gain_ref[4:5, :] = jnp.broadcast_to(stat_ref[1:2, 0:1], (1, width))
    grad = cot_ref[...].astype(F32) + normalise_back(
        grad_key, normed, inverse, gains_ref[2:3, :]
    )
    grad_two[...] = grad
    grads[0] = grad.astype(BF16)
    for c in range(chunks):
        for j in range(1, second):
            n_copy(j, c).start()
    total[...] = through(0, 0, tok)
    for c in range(chunks):
        for j in range(1, second):
            n_copy(j, c).wait_recv()
            back_out[j, c * part : (c + 1) * part, :] = through(j, c * part, part).astype(BF16)
            b_copy(j, c).start()
    att_turned_ref[...] = jnp.concatenate(
        [jnp.transpose(att_ref[n].astype(F32)).astype(BF16) for n in range(nar)], axis=0
    )
    for j in range(second):
        for w in range(wid):
            own = slice(w * columns, (w + 1) * columns)
            normed_cols_ref[w, j * tok : (j + 1) * tok, :] = normed_ref[j, :, own]
            ffn_cols_ref[w, j * tok : (j + 1) * tok, :] = grads[j, :, own]
    for c in range(chunks):
        at = slice(c * part, (c + 1) * part)
        for j in range(1, second):
            b_copy(j, c).wait_recv()
            total[at, :] += back_in[j, at, :].astype(F32)
    normed, inverse = normalise(one_ref[...])
    gain_ref[1:2, :] = jnp.sum(total[...] * normed, axis=0, keepdims=True)
    grad = grad_two[...] + normalise_back(total[...], normed, inverse, gains_ref[1:2, :])
    grad_one_ref[...] = grad
    branch = grad.astype(BF16)
    grad_att = lax.dot_general(
        branch, proj_ref[...].reshape(nar * local, width), last, preferred_element_type=F32
    ).astype(BF16)
    for n in range(nar):
        grad_att_ref[n] = grad_att[:, n * local : (n + 1) * local]
    for w in range(wid):
        branch_cols_ref[w] = branch[:, w * columns : (w + 1) * columns]
    for c in range(chunks):
        for j in range(1, second):
            n_copy(j, c).wait_send()
            b_copy(j, c).wait_send()


def ffn_back(
    slices, att, cot, one, two, gains, pre, normed, proj, in_all, out_all, stats, wid, name
):
    nar, tok, local = att.shape
    first, width, hidden = in_all.shape
    second = nar // first
    chunks = 2
    columns = width // wid
    vmem = pl.BlockSpec(memory_space=pltpu.VMEM)
    dma = pltpu.SemaphoreType.DMA((second, chunks))
    return pl.pallas_call(
        functools.partial(ffn_back_kernel, chunks),
        out_shape=(
            jax.ShapeDtypeStruct((tok, width), F32),
            jax.ShapeDtypeStruct((nar, tok, local), BF16),
            jax.ShapeDtypeStruct((8, width), F32),
            jax.ShapeDtypeStruct((first * hidden, second * tok), BF16),
            jax.ShapeDtypeStruct((first * hidden, second * tok), BF16),
            jax.ShapeDtypeStruct((nar * local, tok), BF16),
            jax.ShapeDtypeStruct((wid, second * tok, columns), BF16),
            jax.ShapeDtypeStruct((wid, second * tok, columns), BF16),
            jax.ShapeDtypeStruct((wid, tok, columns), BF16),
        ),
        in_specs=[vmem] * 12,
        out_specs=(vmem,) * 9,
        scratch_shapes=[
            pltpu.VMEM((second, tok, width), BF16),
            pltpu.VMEM((tok, width), F32),
            pltpu.VMEM((tok, width), F32),
            pltpu.VMEM((second, tok, width), BF16),
            pltpu.VMEM((second, tok, width), BF16),
        ]
        + [dma] * 4,
        compiler_params=pltpu.CompilerParams(
            collective_id=name, has_side_effects=True, vmem_limit_bytes=52 * 2**20
        ),
    )(slices, att, cot, one, two, gains, pre, normed, proj, in_all, out_all, stats)


REACH = ((1, 2), (0, 2), (1, 3), (2, 1))
RELAY = {1: (0, (2, 3)), 2: (3, (0, 1))}


def line_plan(first):
    if first == 4:
        return REACH, RELAY
    return tuple(tuple(b for b in range(first) if b != a) for a in range(first)), {}


def segment_column(seg_ref, seq, start, block):
    row = seg_ref[pl.ds(seq, 1), start : start + block].astype(F32)
    return jnp.transpose(jnp.broadcast_to(row, (8, block)))[:, 0:1]


def grad_kernel(
    nar,
    first,
    wid,
    seqs,
    heads,
    block,
    chunks,
    grad_ref,
    seg_ref,
    gain_ref,
    sums_ref,
    pre_any,
    act_any,
    att_any,
    normed_any,
    ffn_any,
    branch_any,
    qkv_any,
    lse_any,
    one_any,
    input_any,
    above_any,
    pq_any,
    all_ref,
    total_ref,
    in_grad_ref,
    out_grad_ref,
    proj_grad_ref,
    qkv_grad_ref,
    pre_ref,
    act_ref,
    att_ref,
    normed_ref,
    ffn_ref,
    branch_ref,
    qkv_ref,
    lse_ref,
    one_ref,
    input_ref,
    above_ref,
    pq_ref,
    load_sem,
    out_ref,
    grads,
    got,
    grad_key,
    grad_value,
    core_out,
    core_in,
    chip_out,
    chip_in,
    tail_sum,
    turn_out,
    turn_in,
    line_in,
    qkv_out,
    qkv_in,
    own_ref,
    own_sums,
    all_sums,
    pieces_out,
    pieces_in,
    own_sem,
    a_send,
    a_recv,
    b_send,
    b_recv,
    c_send,
    c_recv,
    x_send,
    x_recv,
    y_send,
    y_recv,
    z_send,
    z_recv,
    w_send,
    w_recv,
    g_send,
    g_recv,
    h_send,
    h_recv,
    s_send,
    s_recv,
    p_send,
    p_recv,
):
    second = nar // first
    outer = wid // 2
    za, yb = lax.axis_index("z"), lax.axis_index("y")
    me = za * second + yb
    wide = lax.axis_index("wide")
    chip, core = wide // 2, lax.rem(wide, 2)
    tok, local = grad_ref.shape[1:]
    hidden = pre_ref.shape[0] // first
    columns = normed_ref.shape[2]
    rows = 2 * hidden
    body = first * rows
    line = rows + local
    length = nar * tok // seqs
    per_seq = nar // seqs
    width = heads * HD
    part = tok // chunks
    across = (((0,), (0,)), ((), ()))
    last = (((1,), (1,)), ((), ()))
    reach, relay = line_plan(first)

    pairs = (
        (pre_any, pre_ref),
        (act_any, act_ref),
        (att_any, att_ref),
        (normed_any, normed_ref),
        (ffn_any, ffn_ref),
        (branch_any, branch_ref),
        (qkv_any, qkv_ref),
        (lse_any, lse_ref),
        (one_any, one_ref),
        (input_any, input_ref),
        (above_any, above_ref),
        (pq_any, pq_ref),
    )
    loads = [
        pltpu.make_async_copy(src, dst, load_sem.at[n]) for n, (src, dst) in enumerate(pairs)
    ]
    for load in loads:
        load.start()

    greet(
        [place(lax.rem(me + k, nar), second) for k in range(1, nar)]
        + [{"wide": lax.rem(wide + w, wid)} for w in range(1, wid)]
    )

    def a_copy(target, source):
        return push(
            grad_ref.at[target],
            grads.at[source],
            a_send.at[target],
            a_recv.at[source],
            place(target, second),
        )

    def b_copy(target, source):
        return push(
            out_ref.at[pl.ds(pl.multiple_of(target * tok, tok), tok)],
            got.at[source],
            b_send.at[target],
            b_recv.at[source],
            place(target, second),
        )

    def c_copy(o):
        return push(
            core_out.at[o],
            core_in.at[o],
            c_send.at[o],
            c_recv.at[o],
            {"wide": chip * 2 + (1 - core)},
        )

    def span(z):
        return pl.ds(pl.multiple_of(z * rows, rows), rows)

    tail_rows = pl.ds(body, nar * local)

    def x_copy(i, q, at):
        return push(
            chip_out.at[i - 1, at],
            chip_in.at[i - 1, at],
            x_send.at[i, q],
            x_recv.at[i, q],
            {"wide": lax.rem(chip + i, outer) * 2 + core},
        )

    def y_copy(j):
        target = {"z": za, "y": lax.rem(yb + j, second)}
        return push(turn_out.at[j], turn_in.at[j], y_send.at[j], y_recv.at[j], target)

    def z_copy(i):
        target = {"z": lax.rem(za + i, first), "y": yb}
        return push(
            core_out.at[0, pl.ds((i - 1) * line, line)],
            line_in.at[i - 1],
            z_send.at[i],
            z_recv.at[i],
            target,
        )

    def w_copy(i):
        target = lax.rem(wide + i, wid)
        return push(
            qkv_out.at[target], qkv_in.at[i], w_send.at[i], w_recv.at[i], {"wide": target}
        )

    def g_copy(source_z, target_z, slot, c, own):
        at = pl.ds(c * part, part)
        source = source_z * second + yb
        return push(
            own_ref.at[at] if own else all_ref.at[source, at],
            all_ref.at[source, at],
            g_send.at[source_z, slot, c],
            g_recv.at[source_z, c],
            {"z": target_z, "y": yb},
        )

    def h_copy(source_z, j, c, own):
        at = pl.ds(c * part, part)
        source = source_z * second + yb
        return push(
            own_ref.at[at] if own else all_ref.at[source, at],
            all_ref.at[source, at],
            h_send.at[source_z, j, c],
            h_recv.at[source_z, j, c],
            {"z": za, "y": lax.rem(yb + j, second)},
        )

    def h_arrival(source_z, j, c):
        at = pl.ds(c * part, part)
        source = source_z * second + lax.rem(yb + second - j, second)
        return push(
            all_ref.at[source, at],
            all_ref.at[source, at],
            h_send.at[source_z, j, c],
            h_recv.at[source_z, j, c],
            {"z": za, "y": lax.rem(yb + j, second)},
        )

    def s_copy(k):
        target = place(lax.rem(me + k, nar), second)
        return push(own_sums, all_sums.at[k], s_send.at[k], s_recv.at[k], target)

    def p_copy(w):
        target = lax.rem(wide + w, wid)
        return push(
            pieces_out.at[target], pieces_in.at[w], p_send.at[w], p_recv.at[w], {"wide": target}
        )

    def product_rows(w, z):
        own = pl.ds(pl.multiple_of(z * hidden, hidden), hidden)
        return (
            jnp.dot(pre_ref[own, :], normed_ref[w], preferred_element_type=F32),
            jnp.dot(act_ref[own, :], ffn_ref[w], preferred_element_type=F32),
        )

    def product_tail(w):
        return jnp.dot(att_ref[...], branch_ref[w], preferred_element_type=F32)

    for k in range(1, nar):
        a_copy(lax.rem(me + k, nar), me).start()
    grads[me] = grad_ref[me]
    for n in range(6):
        loads[n].wait()

    for i in range(1, outer + 1):
        o = lax.rem(chip + i, outer)
        w = o * 2 + (1 - core)

        def for_core(z, carry, o=o, w=w):
            upper, lower = product_rows(w, z)
            at = pl.multiple_of(z * rows, rows)
            core_out[o, pl.ds(at, hidden), :] = upper.astype(BF16)
            core_out[o, pl.ds(at + hidden, hidden), :] = lower.astype(BF16)
            return carry

        lax.fori_loop(0, first, for_core, 0)
        core_out[o, tail_rows, :] = product_tail(w).astype(BF16)
        c_copy(o).start()

    for i in range(1, outer):
        o = lax.rem(chip + i, outer)
        w = o * 2 + core
        c_copy(o).wait_recv()
        total = product_tail(w) + core_in[o, tail_rows, :].astype(F32)
        chip_out[i - 1, tail_rows, :] = total.astype(BF16)
        x_copy(i, 0, tail_rows).start()

        def for_chip(n, carry, o=o, w=w, i=i):
            z = lax.rem(za + n, first)
            upper, lower = product_rows(w, z)
            at = pl.multiple_of(z * rows, rows)
            high, low = pl.ds(at, hidden), pl.ds(at + hidden, hidden)
            chip_out[i - 1, high, :] = (upper + core_in[o, high, :].astype(F32)).astype(BF16)
            chip_out[i - 1, low, :] = (lower + core_in[o, low, :].astype(F32)).astype(BF16)
            x_copy(i, n, span(z)).start()
            return carry

        lax.fori_loop(1, first + 1, for_chip, 0)

    loads[6].wait()
    loads[7].wait()

    def sequence(seq, carry):
        base = seq * length

        def arrive(b, c):
            source = seq * per_seq + b

            @pl.when(source != me)
            def _():
                a_copy(source, source).wait_recv()

            return c

        lax.fori_loop(0, per_seq, arrive, 0)
        grad_key[...] = jnp.zeros_like(grad_key)
        grad_value[...] = jnp.zeros_like(grad_value)
        for start in range(0, length, block):
            keys = start + block
            at = pl.multiple_of(base + start, block)
            query_segment = segment_column(seg_ref, seq, start, block)
            key_segment = seg_ref[pl.ds(seq, 1), 0:keys].astype(F32)
            spot = lax.broadcasted_iota(jnp.int32, (block, keys), 1)
            own = lax.broadcasted_iota(jnp.int32, (block, keys), 0) + start
            allowed = (spot <= own) & (query_segment == key_segment)
            whole = pl.ds(pl.multiple_of(base, length), keys)
            query = qkv_ref[pl.ds(at, block), 0:width]
            key = qkv_ref[whole, width : 2 * width]
            value = qkv_ref[whole, 2 * width : 3 * width]
            each = min(tok, block)
            grad = jnp.concatenate(
                [
                    grads[
                        seq * per_seq + (start + r) // tok,
                        (start + r) % tok : (start + r) % tok + each,
                        :,
                    ]
                    for r in range(0, block, each)
                ],
                axis=0,
            )
            total = jnp.zeros((block, width), F32)
            for head in range(heads):
                own_query = head_lanes(query, head)
                own_grad = head_lanes(grad, head)
                scores = lax.dot_general(own_query, key, last, preferred_element_type=F32)
                probs = jnp.where(
                    allowed, jnp.exp(scores - lse_ref[pl.ds(at, block), head : head + 1]), 0.0
                )
                grad_probs = lax.dot_general(own_grad, value, last, preferred_element_type=F32)
                delta = jnp.sum(probs * grad_probs, axis=-1, keepdims=True)
                grad_scores = (probs * (grad_probs - delta)).astype(BF16)
                total = total + head_lanes(
                    jnp.dot(grad_scores, key, preferred_element_type=F32), head
                )
                grad_key[0:keys, :] += lax.dot_general(
                    grad_scores, own_query, across, preferred_element_type=F32
                )
                grad_value[0:keys, :] += lax.dot_general(
                    probs.astype(BF16), own_grad, across, preferred_element_type=F32
                )
            out_ref[pl.ds(at, block), 0:width] = (total * HD ** (-0.5)).astype(BF16)
        every = pl.ds(pl.multiple_of(base, length), length)
        out_ref[every, width : 2 * width] = grad_key[...].astype(BF16)
        out_ref[every, 2 * width : 3 * width] = grad_value[...].astype(BF16)

        def leave(b, c):
            target = seq * per_seq + b

            @pl.when(target != me)
            def _():
                b_copy(target, me).start()

            return c

        lax.fori_loop(0, per_seq, leave, 0)
        return carry

    lax.fori_loop(0, seqs, sequence, 0)

    loads[8].wait()
    qkv_part = lax.dot_general(
        out_ref[...], one_ref[...], across, preferred_element_type=F32
    ).astype(BF16)
    for w in range(wid):
        qkv_out[w] = qkv_part[:, w * columns : (w + 1) * columns]
    for i in range(1, wid):
        w_copy(i).start()

    w_own = chip * 2 + core
    c_copy(chip).wait_recv()
    tail_sum[...] = product_tail(w_own) + core_in[chip, tail_rows, :].astype(F32)
    for i in range(1, outer):
        x_copy(i, 0, tail_rows).wait_recv()
        tail_sum[...] += chip_in[i - 1, tail_rows, :].astype(F32)
    for j in range(1, second):
        column = lax.rem(yb + j, second)
        for z in range(first):
            at = pl.ds(pl.multiple_of((z * second + column) * local, local), local)
            turn_out[j, z] = tail_sum[at, :].astype(BF16)
        y_copy(j).start()

    for n in range(9, 12):
        loads[n].wait()
    normed, inverse = normalise(input_ref[...].astype(F32))
    mine = out_ref[pl.ds(pl.multiple_of(me * tok, tok), tok), :]
    total = jnp.dot(mine, pq_ref[me, local:, :], preferred_element_type=F32)
    for k in range(1, nar):
        source = lax.rem(me + k, nar)
        b_copy(source, source).wait_recv()
        total = total + jnp.dot(
            got[source], pq_ref[source, local:, :], preferred_element_type=F32
        )
    grad = above_ref[...] + normalise_back(total, normed, inverse, gain_ref[0:1, :])
    own_ref[...] = grad.astype(BF16)

    for c in range(chunks):
        for z in range(first):

            @pl.when(za == z)
            def _(z=z, c=c):
                for slot, target in enumerate(reach[z]):
                    g_copy(za, target, slot, c, True).start()

        for j in range(1, second):
            h_copy(za, j, c, True).start()
    own_copy = pltpu.make_async_copy(own_ref, all_ref.at[me], own_sem)
    own_copy.start()
    own_sums[...] = sums_ref[...]
    own_sums[0:1, :] = jnp.sum(total * normed, axis=0, keepdims=True)
    for k in range(1, nar):
        s_copy(k).start()

    def gathered(begin, end):
        for c in range(chunks):
            for d in range(begin, end):
                for way in (-1, 1):
                    z = za + way * d

                    @pl.when((z >= 0) & (z < first))
                    def _(z=z, c=c):
                        g_copy(z, za, 0, c, False).wait_recv()
                        for middle, (target, sources) in relay.items():

                            @pl.when((za == middle) & ((z == sources[0]) | (z == sources[1])))
                            def _(target=target):
                                g_copy(z, target, 0, c, False).start()

                        for j in range(1, second):
                            h_copy(z, j, c, False).start()

    for o in range(outer):
        c_copy(o).wait_send()
    for j in range(1, second):
        y_copy(j).wait_recv()

    def line_parts(n):
        z = lax.rem(za + n, first)
        at = pl.ds(pl.multiple_of((z * second + yb) * local, local), local)
        low_part = tail_sum[at, :]
        for j in range(1, second):
            low_part = low_part + turn_in[j, z].astype(F32)
        upper, lower = product_rows(w_own, z)
        start = pl.multiple_of(z * rows, rows)
        high, low = pl.ds(start, hidden), pl.ds(start + hidden, hidden)
        upper = upper + core_in[chip, high, :].astype(F32)
        lower = lower + core_in[chip, low, :].astype(F32)
        for i in range(1, outer):
            x_copy(i, n, span(z)).wait_recv()
            upper = upper + chip_in[i - 1, high, :].astype(F32)
            lower = lower + chip_in[i - 1, low, :].astype(F32)
        return upper, lower, low_part

    def send_line(n):
        upper, lower, low_part = line_parts(n)
        core_out[0, (n - 1) * line : (n - 1) * line + hidden, :] = upper.astype(BF16)
        core_out[0, (n - 1) * line + hidden : (n - 1) * line + rows, :] = lower.astype(BF16)
        core_out[0, (n - 1) * line + rows : n * line, :] = low_part.astype(BF16)
        z_copy(n).start()

    send_line(1)
    gathered(1, 2)
    for n in range(2, first):
        send_line(n)
    gathered(2, first)
    upper, lower, low_part = line_parts(first)
    sums = own_sums[...]
    for k in range(1, nar):
        s_copy(k).wait_recv()
        sums = sums + all_sums[k]
    piece = total_ref.shape[1]
    for w in range(wid):
        pieces_out[w] = sums[:, w * piece : (w + 1) * piece]
    for w in range(1, wid):
        p_copy(w).start()
    qkv_sum = qkv_out[wide].astype(F32)
    for i in range(1, wid):
        w_copy(i).wait_recv()
        qkv_sum = qkv_sum + qkv_in[i].astype(F32)
    qkv_grad_ref[...] = qkv_sum
    for n in range(1, first):
        z_copy(n).wait_recv()
        upper = upper + line_in[n - 1, 0:hidden, :].astype(F32)
        lower = lower + line_in[n - 1, hidden:rows, :].astype(F32)
        low_part = low_part + line_in[n - 1, rows:, :].astype(F32)
    in_grad_ref[...] = jnp.transpose(upper)
    out_grad_ref[...] = lower
    proj_grad_ref[...] = low_part
    answer = pieces_out[wide]
    for w in range(1, wid):
        p_copy(w).wait_recv()
        answer = answer + pieces_in[w]
    total_ref[...] = answer

    for z in range(first):
        for j in range(1, second):
            for c in range(chunks):
                h_arrival(z, j, c).wait_recv()
    own_copy.wait()
    for k in range(1, nar):
        a_copy(lax.rem(me + k, nar), me).wait_send()
        b_copy(lax.rem(me + k, nar), me).wait_send()
        s_copy(k).wait_send()
    for w in range(1, wid):
        p_copy(w).wait_send()
        w_copy(w).wait_send()
    for i in range(1, outer):
        x_copy(i, 0, tail_rows).wait_send()
        for n in range(1, first + 1):
            x_copy(i, n, span(lax.rem(za + n, first))).wait_send()
    for j in range(1, second):
        y_copy(j).wait_send()
    for n in range(1, first):
        z_copy(n).wait_send()
    for c in range(chunks):
        for z in range(first):

            @pl.when(za == z)
            def _(z=z, c=c):
                for slot, target in enumerate(reach[z]):
                    g_copy(za, target, slot, c, True).wait_send()
                if z in relay:
                    target, sources = relay[z]
                    for n in sources:
                        g_copy(n, target, 0, c, False).wait_send()

            for j in range(1, second):
                h_copy(z, j, c, False).wait_send()


def attention_grads(grads, seg, gain, sums, sides, qkv, lse, one, inputs, above, pq, first, wid, name):
    nar, tok, local = grads.shape
    rows, wide = qkv.shape
    width = inputs.shape[1]
    seqs, length = seg.shape
    second = nar // first
    outer = wid // 2
    hidden = sides[0].shape[0] // first
    piece = width // wid
    body = first * 2 * hidden + nar * local
    line = 2 * hidden + local
    chunks = 2
    vmem = pl.BlockSpec(memory_space=pltpu.VMEM)
    hbm = pl.BlockSpec(memory_space=pl.ANY)
    dma = pltpu.SemaphoreType.DMA
    late = (*sides, qkv, lse, one, inputs, above, pq)
    return pl.pallas_call(
        functools.partial(
            grad_kernel, nar, first, wid, seqs, local // HD, min(256, length), chunks
        ),
        out_shape=(
            jax.ShapeDtypeStruct((nar, tok, width), BF16),
            jax.ShapeDtypeStruct((8, piece), F32),
            jax.ShapeDtypeStruct((piece, hidden), F32),
            jax.ShapeDtypeStruct((hidden, piece), F32),
            jax.ShapeDtypeStruct((local, piece), F32),
            jax.ShapeDtypeStruct((3 * local, piece), F32),
        ),
        in_specs=[vmem] * 4 + [hbm] * 12,
        out_specs=(hbm,) + (vmem,) * 5,
        scratch_shapes=[pltpu.VMEM(x.shape, x.dtype) for x in late]
        + [
            dma((12,)),
            pltpu.VMEM((rows, wide), BF16),
            pltpu.VMEM((nar, tok, local), BF16),
            pltpu.VMEM((nar, tok, wide), BF16),
            pltpu.VMEM((length, local), F32),
            pltpu.VMEM((length, local), F32),
            pltpu.VMEM((outer, body, piece), BF16),
            pltpu.VMEM((outer, body, piece), BF16),
            pltpu.VMEM((outer - 1, body, piece), BF16),
            pltpu.VMEM((outer - 1, body, piece), BF16),
            pltpu.VMEM((nar * local, piece), F32),
            pltpu.VMEM((second, first, local, piece), BF16),
            pltpu.VMEM((second, first, local, piece), BF16),
            pltpu.VMEM((first - 1, line, piece), BF16),
            pltpu.VMEM((wid, 3 * local, piece), BF16),
            pltpu.VMEM((wid, 3 * local, piece), BF16),
            pltpu.VMEM((tok, width), BF16),
            pltpu.VMEM((8, width), F32),
            pltpu.VMEM((nar, 8, width), F32),
            pltpu.VMEM((wid, 8, piece), F32),
            pltpu.VMEM((wid, 8, piece), F32),
            dma,
            dma((nar,)),
            dma((nar,)),
            dma((nar,)),
            dma((nar,)),
            dma((outer,)),
            dma((outer,)),
            dma((outer, first + 1)),
            dma((outer, first + 1)),
            dma((second,)),
            dma((second,)),
            dma((first,)),
            dma((first,)),
            dma((wid,)),
            dma((wid,)),
            dma((first, 3, chunks)),
            dma((first, chunks)),
            dma((first, second, chunks)),
            dma((first, second, chunks)),
            dma((nar,)),
            dma((nar,)),
            dma((wid,)),
            dma((wid,)),
        ],
        compiler_params=pltpu.CompilerParams(
            collective_id=name, has_side_effects=True, vmem_limit_bytes=63 * 2**20
        ),
    )(grads, seg, gain, sums, *late)


def neighbour_kernel(
    nar,
    first,
    tiles,
    tile,
    kept,
    ring,
    query_ref,
    keys_ref,
    norms_ref,
    ids_ref,
    cols_ref,
    scal_ref,
    grad_ref,
    loss_ref,
    stat_ref,
    queries,
    partial,
    dist,
    grads,
    sends,
    slots,
    loss_own,
    slot_sem,
    q_send,
    q_recv,
    d_send,
    d_recv,
    g_send,
    g_recv,
    l_send,
    l_recv,
    o_send,
    o_recv,
):
    second = nar // first
    me = lax.axis_index("z") * second + lax.axis_index("y")
    tok = query_ref.shape[1]
    depth = query_ref.shape[2]
    group = 16
    per_block = tok // tile
    late = tiles - kept

    def peer(k):
        return lax.rem(me + k, nar)

    def origin(k):
        return lax.rem(me + nar - k, nar)

    def load(index, slot):
        block, sub = index // per_block, lax.rem(index, per_block)
        row = origin(block) * tok + sub * tile
        return pltpu.make_async_copy(
            keys_ref.at[pl.ds(row, tile)], slots.at[slot], slot_sem.at[slot]
        )

    for i in range(kept + ring):
        load(i, i).start()

    greet([place(peer(k), second) for k in range(1, nar)])

    def q_copy(k):
        return push(
            query_ref.at[peer(k)],
            queries.at[k],
            q_send.at[k],
            q_recv.at[k],
            place(peer(k), second),
        )

    def d_copy(k):
        return push(
            partial.at[k], dist.at[k], d_send.at[k], d_recv.at[k], place(origin(k), second)
        )

    def g_copy(k):
        return push(
            grads.at[0], grads.at[k], g_send.at[k], g_recv.at[k], place(peer(k), second)
        )

    def l_copy(k):
        return push(
            loss_own, loss_ref.at[me], l_send.at[k], l_recv.at[k], place(peer(k), second)
        )

    def o_copy(k):
        return push(
            sends.at[k], grad_ref.at[me], o_send.at[k], o_recv.at[k], place(origin(k), second)
        )

    for k in range(1, nar):
        q_copy(k).start()
    queries[0] = query_ref[me]

    row_of = lax.broadcasted_iota(jnp.int32, (group, J), 0)

    def slot_of(index):
        return jnp.where(index < kept, index, kept + lax.rem(index - kept, ring))

    def slot_late(n):
        return kept + lax.rem(n, ring)

    def forward_tile(k, sub, slot):
        def one(g, carry):
            at = pl.multiple_of(sub * tile + g * group, group)
            own = queries[k, pl.ds(at, group), :].astype(F32)
            keys = slots[slot, pl.ds(g * group, group), :, :].reshape(group * depth, J)
            wide = jnp.concatenate(
                [jnp.where(row_of[:, :depth] == t, own, 0.0) for t in range(group)], axis=1
            ).astype(BF16)
            out = jnp.dot(wide, keys, preferred_element_type=F32)
            row = pl.multiple_of(origin(k) * tok + at, group)
            partial[k, pl.ds(at, group), :] = 2.0 * out - norms_ref[pl.ds(row, group), :]
            return carry

        lax.fori_loop(0, tile // group, one, 0, unroll=True)

    def forward_block(k):
        def body(sub, carry):
            index = k * per_block + sub
            slot = slot_of(index)
            load(index, slot).wait()
            forward_tile(k, sub, slot)

            @pl.when(index >= kept)
            def _():
                nxt = index - kept + ring

                @pl.when(nxt < 2 * late)
                def _():
                    load(kept + lax.rem(nxt, late), slot).start()

            return carry

        lax.fori_loop(0, per_block, body, 0)

    forward_block(0)

    def forward_rest(k, carry):
        q_copy(k).wait_recv()
        forward_block(k)
        d_copy(k).start()
        return carry

    lax.fori_loop(1, nar, forward_rest, 0)

    def collect(k, total):
        d_copy(k).wait_recv()
        return total + dist[k]

    distance = lax.fori_loop(1, nar, collect, partial[0])
    temper_value = scal_ref[0]
    mix_value = scal_ref[1]
    count = cols_ref[:, 0:1]
    target = cols_ref[:, 1:2]
    base = cols_ref[:, 2:3]
    loss_weight = cols_ref[:, 3:4]
    logits = distance / temper_value
    spot = lax.broadcasted_iota(jnp.int32, (tok, J), 1).astype(F32)
    masked = jnp.where(spot < count, logits, -1e30)
    peak = jnp.max(masked, axis=-1, keepdims=True)
    expo = jnp.exp(masked - peak)
    weights = expo / jnp.sum(expo, axis=-1, keepdims=True)
    matches = jnp.where(ids_ref[...].astype(F32) == target, 1.0, 0.0)
    knn_prob = jnp.sum(weights * matches, axis=-1, keepdims=True)
    mixture = mix_value * knn_prob + (1.0 - mix_value) * base
    grad_mixture = -loss_weight / mixture
    grad_logits = weights * (mix_value * grad_mixture) * (matches - knn_prob)
    grads[0] = (2.0 * grad_logits / temper_value).astype(BF16)
    for k in range(1, nar):
        g_copy(k).start()
    loss = jnp.transpose(jnp.broadcast_to(-jnp.log(mixture), (tok, J)))[0:8, :]
    loss_own[...] = loss
    for k in range(1, nar):
        l_copy(k).start()
    loss_ref[me] = loss
    term_temper = -jnp.sum(grad_logits * logits, axis=0, keepdims=True) / temper_value
    term_mix = jnp.sum((knn_prob - base) * grad_mixture, axis=0, keepdims=True)
    stat_ref[0:1, :] = term_temper
    stat_ref[1:2, :] = jnp.broadcast_to(term_mix, (1, J))

    def backward_tile(k, sub, slot):
        def one(g, carry):
            at = pl.multiple_of(sub * tile + g * group, group)
            own = grads[k, pl.ds(at, group), :]
            keys = slots[slot, pl.ds(g * group, group), :, :].reshape(group * depth, J)
            out = lax.dot_general(
                own, keys, (((1,), (1,)), ((), ())), preferred_element_type=F32
            )
            total = jnp.zeros((group, depth), F32)
            for t in range(group):
                total = jnp.where(
                    row_of[:, :depth] == t, out[:, t * depth : (t + 1) * depth], total
                )
            sends[k, pl.ds(at, group), :] = total.astype(BF16)
            return carry

        lax.fori_loop(0, tile // group, one, 0, unroll=True)

    def backward_block(k):
        def body(sub, carry):
            index = k * per_block + sub

            @pl.when(index < kept)
            def _():
                backward_tile(k, sub, index)

            @pl.when(index >= kept)
            def _():
                n = index - kept + late
                slot = slot_late(n)
                load(index, slot).wait()
                backward_tile(k, sub, slot)

                @pl.when(n + ring < 2 * late)
                def _():
                    load(kept + lax.rem(n + ring, late), slot).start()

            return carry

        lax.fori_loop(0, per_block, body, 0)

    backward_block(0)
    grad_ref[me] = sends[0]

    def backward_rest(k, carry):
        g_copy(k).wait_recv()
        backward_block(k)
        o_copy(k).start()
        return carry

    lax.fori_loop(1, nar, backward_rest, 0)

    for k in range(1, nar):
        q_copy(k).wait_send()
        d_copy(k).wait_send()
        g_copy(k).wait_send()
        l_copy(k).wait()
        o_copy(k).wait()


def neighbours(nar, first, query, keys, norms, ids, cols, scal):
    tok, depth = query.shape[1:]
    rows = keys.shape[0]
    tile = 32
    tiles = rows // tile
    bytes_tile = tile * depth * J * 2
    ring = 4
    kept = min(tiles - 2 * ring, (KEPT_BYTES // bytes_tile))
    vmem = pl.BlockSpec(memory_space=pltpu.VMEM)
    dma = pltpu.SemaphoreType.DMA((nar,))
    return pl.pallas_call(
        functools.partial(neighbour_kernel, nar, first, tiles, tile, kept, ring),
        out_shape=(
            jax.ShapeDtypeStruct((nar, tok, depth), BF16),
            jax.ShapeDtypeStruct((nar, 8, tok), F32),
            jax.ShapeDtypeStruct((2, J), F32),
        ),
        in_specs=[
            vmem,
            pl.BlockSpec(memory_space=pl.ANY),
            vmem,
            vmem,
            vmem,
            pl.BlockSpec(memory_space=pltpu.SMEM),
        ],
        out_specs=(vmem, vmem, vmem),
        scratch_shapes=[
            pltpu.VMEM((nar, tok, depth), BF16),
            pltpu.VMEM((nar, tok, J), F32),
            pltpu.VMEM((nar, tok, J), F32),
            pltpu.VMEM((nar, tok, J), BF16),
            pltpu.VMEM((nar, tok, depth), BF16),
            pltpu.VMEM((kept + ring, tile, depth, J), BF16),
            pltpu.VMEM((8, tok), F32),
            pltpu.SemaphoreType.DMA((kept + ring,)),
        ]
        + [dma] * 10,
        compiler_params=pltpu.CompilerParams(
            collective_id=1, has_side_effects=True, vmem_limit_bytes=60 * 2**20
        ),
    )(query, keys, norms, ids, cols, scal)


def on_device(
    block_input,
    output_cotangent,
    loss_weight,
    segments,
    nbr_keys,
    nbr_count,
    nbr_ids,
    targets,
    base_prob,
    w_query,
    w_key,
    w_value,
    w_proj,
    w_in,
    w_out,
    gain_attn,
    gain_ffn,
    gain_key,
    temper,
    mix_weight,
):
    seqs_here, length, width = block_input.shape
    rows = seqs_here * length
    wid = lax.axis_size("wide")
    first = lax.axis_size("z")
    nar = first * lax.axis_size("y")
    own = lax.axis_index("z") * lax.axis_size("y") + lax.axis_index("y")
    tok = rows // nar
    local_width = w_query.shape[0]

    def mine(values):
        flat = values.reshape((rows,) + values.shape[2:])
        return lax.dynamic_slice_in_dim(flat, own * tok, tok, 0)

    seg_column = segments.reshape(rows, 1)
    seg_row = segments.reshape(seqs_here, 1, length)
    key_slices = nbr_keys.reshape(rows, nbr_keys.shape[2], nbr_keys.shape[3])
    gains = jnp.stack([gain_attn, gain_ffn, gain_key])
    w_qkv = jnp.concatenate([w_query, w_key, w_value], axis=0)
    normed_one, qkv, lse, part_norms, attended_own, in_all, out_all, pq_all = head(
        block_input.reshape(rows, width),
        gains,
        w_qkv,
        seg_column,
        seg_row,
        key_slices,
        w_in,
        w_out,
        jnp.concatenate([w_proj, w_qkv], axis=0),
        first,
        nar,
        wid,
        2,
    )
    proj_all = pq_all[:, :local_width]
    inputs_own = mine(block_input)
    hidden_one, hidden_two, output_own, query_key, normed_two, pre_act = ffn(
        attended_own, inputs_own, gains, proj_all, in_all, out_all, 3
    )
    block_output = lax.all_gather(output_own, ("z", "y"), axis=0, tiled=True)
    cols = jnp.stack(
        [
            mine(nbr_count).astype(F32),
            mine(targets).astype(F32),
            mine(base_prob),
            mine(loss_weight),
        ],
        axis=1,
    )
    grad_slices, losses, stats = neighbours(
        nar,
        first,
        query_key,
        key_slices,
        part_norms,
        mine(nbr_ids),
        cols,
        jnp.concatenate([temper, mix_weight]),
    )
    token_loss = losses[:, 0, :]
    grad_hidden_one, grad_attended, gain_sums, *sides = ffn_back(
        grad_slices,
        attended_own,
        mine(output_cotangent),
        hidden_one,
        hidden_two,
        gains,
        pre_act,
        normed_two,
        proj_all,
        in_all,
        out_all,
        stats,
        wid,
        5,
    )
    grad_attended, block_output = lax.optimization_barrier((grad_attended, block_output))
    grad_input, totals, grad_w_in, grad_w_out, grad_w_proj, grad_w_qkv = attention_grads(
        grad_attended,
        segments,
        gains,
        gain_sums,
        sides,
        qkv,
        lse,
        normed_one,
        inputs_own,
        grad_hidden_one,
        pq_all,
        first,
        wid,
        6,
    )

    return (
        block_output.reshape(seqs_here, length, width),
        token_loss.reshape(seqs_here, length),
        grad_input.astype(F32).reshape(seqs_here, length, width),
        grad_w_qkv[:local_width],
        grad_w_qkv[local_width : 2 * local_width],
        grad_w_qkv[2 * local_width :],
        grad_w_proj,
        grad_w_in,
        grad_w_out,
        totals[0],
        totals[1],
        totals[2],
        totals[3, 0:1],
        totals[4, 0:1],
    )


def solution(mesh):
    wide, narrow = mesh.devices.shape
    first = 4 if narrow % 4 == 0 else narrow
    split = jax.sharding.Mesh(
        mesh.devices.reshape(wide, first, narrow // first), ("wide", "z", "y")
    )
    narrow = ("z", "y")
    return jax.shard_map(
        on_device,
        mesh=split,
        in_specs=(
            P("wide", None, None),
            P("wide", None, None),
            P("wide", None),
            P("wide", None),
            P("wide", None, narrow, None),
            P("wide", None),
            P("wide", None, None),
            P("wide", None),
            P("wide", None),
            P(narrow, None),
            P(narrow, None),
            P(narrow, None),
            P(narrow, None),
            P(None, narrow),
            P(narrow, None),
            P(),
            P(),
            P(),
            P(),
            P(),
        ),
        out_specs=(
            P("wide", None, None),
            P("wide", None),
            P("wide", None, None),
            P(narrow, "wide"),
            P(narrow, "wide"),
            P(narrow, "wide"),
            P(narrow, "wide"),
            P("wide", narrow),
            P(narrow, "wide"),
            P("wide"),
            P("wide"),
            P("wide"),
            P(),
            P(),
        ),
        check_vma=False,
    )
```

```python
import functools

import jax
import jax.numpy as jnp
from jax import lax
from jax.experimental import pallas as pl
from jax.experimental.pallas import tpu as pltpu
from jax.sharding import PartitionSpec as P

HD = 64
EPSILON = 1e-05
F32 = jnp.float32
BF16 = jnp.bfloat16
MESH = pl.DeviceIdType.MESH
J = 128
KEPT_BYTES = 44 * 2**20


def place(index, second):
    return {"z": index // second, "y": lax.rem(index, second)}


def push(src, dst, send, recv, target):
    return pltpu.make_async_remote_copy(
        src_ref=src,
        dst_ref=dst,
        send_sem=send,
        recv_sem=recv,
        device_id=target,
        device_id_type=MESH,
    )


def greet(peers):
    barrier = pltpu.get_barrier_semaphore()
    for peer in peers:
        pl.semaphore_signal(barrier, inc=1, device_id=peer, device_id_type=MESH)
    pl.semaphore_wait(barrier, len(peers))


def normalise(values):
    centred = values - jnp.mean(values, axis=-1, keepdims=True)
    inverse = lax.rsqrt(jnp.mean(centred * centred, axis=-1, keepdims=True) + EPSILON)
    return centred * inverse, inverse


def normalise_back(grad_out, normed, inverse, gain):
    scaled = grad_out * gain
    return inverse * (
        scaled
        - jnp.mean(scaled, axis=-1, keepdims=True)
        - normed * jnp.mean(scaled * normed, axis=-1, keepdims=True)
    )


def head_lanes(values, head):
    lanes = lax.broadcasted_iota(jnp.int32, values.shape, 1)
    return jnp.where(lanes // HD == head, values, jnp.zeros_like(values))


def head_kernel(
    nar,
    first,
    wid,
    seqs,
    heads,
    block,
    tile,
    ring,
    gain_ref,
    seg_ref,
    proj_any,
    query_any,
    key_any,
    value_any,
    input_any,
    keys_ref,
    in_any,
    out_any,
    normed_out,
    qkv_out,
    lse_out,
    norms_out,
    att_ref,
    in_all,
    out_all,
    pq_all,
    pq_ref,
    in_ref,
    out_ref,
    input_ref,
    normed_ref,
    qkv_ref,
    lse_ref,
    norms_ref,
    attended,
    slots,
    load_sem,
    store_sem,
    slot_sem,
    own_sem,
    a_send,
    a_recv,
    z_send,
    z_recv,
    y_send,
    y_recv,
    x_send,
    x_recv,
    c_send,
    c_recv,
):
    second = nar // first
    outer = wid // 2
    za, yb = lax.axis_index("z"), lax.axis_index("y")
    me = za * second + yb
    wide = lax.axis_index("wide")
    chip, core = wide // 2, lax.rem(wide, 2)
    rows, width = input_ref.shape
    tok = rows // nar
    length = rows // seqs
    local = heads * HD
    tiles = rows // tile
    last = (((1,), (1,)), ((), ()))

    def fetch(index, slot):
        return pltpu.make_async_copy(
            keys_ref.at[pl.ds(index * tile, tile)], slots.at[slot], slot_sem.at[slot]
        )

    loads = [
        pltpu.make_async_copy(src, pq_ref.at[pl.ds(n * local, local)], load_sem.at[n])
        for n, src in enumerate((proj_any, query_any, key_any, value_any))
    ] + [
        pltpu.make_async_copy(src, dst, load_sem.at[4 + n])
        for n, (src, dst) in enumerate(
            ((in_any, in_ref), (out_any, out_ref), (input_any, input_ref))
        )
    ]
    for load in loads:
        load.start()
    stores = [
        pltpu.make_async_copy(src, dst, store_sem.at[n])
        for n, (src, dst) in enumerate(
            (
                (normed_ref, normed_out),
                (qkv_ref, qkv_out),
                (lse_ref, lse_out),
                (norms_ref, norms_out),
            )
        )
    ]

    greet(
        [place(lax.rem(me + k, nar), second) for k in range(1, nar)]
        + [{"wide": chip * 2 + (1 - core)}]
        + [{"wide": lax.rem(chip + o, outer) * 2 + core} for o in range(1, outer)]
    )

    stacks = ((pq_ref, pq_all), (in_ref, in_all), (out_ref, out_all))

    def shard_of(t, source):
        return source if t == 0 else source // second

    def quarter(t, source, owner):
        own, stack = stacks[t]
        count = own.shape[0] // wid
        at = pl.ds(pl.multiple_of(owner * count, count), count)
        return stack.at[shard_of(t, source), at]

    def own_quarter(t):
        own, _ = stacks[t]
        count = own.shape[0] // wid
        return own.at[pl.ds(pl.multiple_of(wide * count, count), count)]

    reach, relay = REACH, RELAY

    def line_copy(t, source, z, slot, own):
        return push(
            own_quarter(t) if own else quarter(t, source, wide),
            quarter(t, source, wide),
            z_send.at[t, source // second, slot],
            z_recv.at[t, source // second],
            {"z": z, "y": yb},
        )

    def owner_of(o):
        return lax.rem(chip + outer - o, outer) * 2 + core

    def row_copy(source, j, o, own):
        owner = owner_of(o)
        count = pq_ref.shape[0] // wid
        at = pl.ds(pl.multiple_of(owner * count, count), count)
        return push(
            pq_ref.at[at] if own else quarter(0, source, owner),
            quarter(0, source, owner),
            y_send.at[source, j, o],
            y_recv.at[source, j, o],
            {"z": za, "y": lax.rem(yb + j, second)},
        )

    def chip_copy(t, source, o):
        return push(
            quarter(t, source, wide),
            quarter(t, source, wide),
            x_send.at[t, source, o],
            x_recv.at[t, source, o],
            {"wide": lax.rem(chip + o, outer) * 2 + core},
        )

    def chip_arrival(t, source, o):
        owner = owner_of(o)
        return push(
            quarter(t, source, owner),
            quarter(t, source, owner),
            x_send.at[t, source, o],
            x_recv.at[t, source, o],
            {"wide": owner},
        )

    def core_copy(t, source, o, away):
        owner = lax.rem(chip + outer - o, outer) * 2 + jnp.where(away, 1 - core, core)
        return push(
            quarter(t, source, owner),
            quarter(t, source, owner),
            c_send.at[t, source, o],
            c_recv.at[t, source, o],
            {"wide": chip * 2 + (1 - core)},
        )

    def att_copy(target, source):
        return push(
            attended.at[target],
            att_ref.at[source],
            a_send.at[target],
            a_recv.at[source],
            place(target, second),
        )

    own_copies = [
        pltpu.make_async_copy(own, stack.at[shard_of(t, me)], own_sem.at[t])
        for t, (own, stack) in enumerate(stacks)
    ]

    def send_own(t):
        for z in range(first):

            @pl.when(za == z)
            def _(z=z):
                for slot, target in enumerate(reach[z]):
                    line_copy(t, me, target, slot, True).start()

        if t == 0:
            for j in range(1, second):
                for o in range(outer):
                    row_copy(me, j, o, True).start()
        own_copies[t].start()

    def line_arrivals(t, begin, end):
        for d in range(begin, end):
            for way in (-1, 1):
                z = za + way * d

                @pl.when((z >= 0) & (z < first))
                def _(z=z):
                    source = z * second + yb
                    line_copy(t, source, za, 0, False).wait_recv()
                    for middle, (target, sources) in relay.items():

                        @pl.when((za == middle) & ((z == sources[0]) | (z == sources[1])))
                        def _(target=target):
                            line_copy(t, source, target, 0, False).start()

                    for o in range(1, outer):
                        chip_copy(t, source, o).start()
                    core_copy(t, source, 0, False).start()

    def chip_arrivals(t):
        for n in range(first):
            source = n * second + yb

            @pl.when(source != me)
            def _(source=source):
                for o in range(1, outer):
                    chip_arrival(t, source, o).wait_recv()
                    core_copy(t, source, o, False).start()
                if t == 0:
                    for j in range(1, second):
                        for o in range(outer):
                            row_copy(source, j, o, False).start()

    def row_arrivals():
        for j in range(1, second):
            for z in range(first):
                source = z * second + lax.rem(yb + second - j, second)
                for o in range(outer):
                    row_copy(source, j, o, False).wait_recv()
                    core_copy(0, source, o, False).start()

    def each_source(t, do):
        for n in range(nar if t == 0 else first):
            source = n if t == 0 else n * second + yb

            @pl.when(source != me)
            def _(source=source):
                do(source)

    def core_arrivals(t):
        def do(source):
            for o in range(outer):
                core_copy(t, source, o, True).wait_recv()

        each_source(t, do)

    for n in range(6):
        loads[n].wait()
    for t in range(3):
        send_own(t)
    for i in range(ring):
        fetch(i, i).start()
    loads[6].wait()

    def project(r, carry):
        at = pl.ds(pl.multiple_of(r * block, block), block)
        normed, _ = normalise(input_ref[at, :].astype(F32))
        low = (normed * gain_ref[0:1, :]).astype(BF16)
        normed_ref[at, :] = low
        out = lax.dot_general(low, pq_ref[local:, :], last, preferred_element_type=F32)
        lanes = lax.broadcasted_iota(jnp.int32, out.shape, 1)
        qkv_ref[at, :] = jnp.where(lanes < local, out * HD ** (-0.5), out).astype(BF16)
        return carry

    lax.fori_loop(0, rows // block, project, 0)
    stores[0].start()
    stores[1].start()
    line_arrivals(0, 1, 2)

    def sequence(seq, carry):
        base = seq * length
        for start in range(0, length, block):
            keys = start + block
            at = pl.ds(pl.multiple_of(base + start, block), block)
            whole = pl.ds(pl.multiple_of(base, length), keys)
            query_segment = segment_column(seg_ref, seq, start, block)
            key_segment = seg_ref[pl.ds(seq, 1), 0:keys].astype(F32)
            spot = lax.broadcasted_iota(jnp.int32, (block, keys), 1)
            own = lax.broadcasted_iota(jnp.int32, (block, keys), 0) + start
            allowed = (spot <= own) & (query_segment == key_segment)
            query = qkv_ref[at, 0:local]
            key = qkv_ref[whole, local : 2 * local]
            value = qkv_ref[whole, 2 * local : 3 * local]
            total = jnp.zeros((block, local), F32)
            for head in range(heads):
                scores = lax.dot_general(
                    head_lanes(query, head), key, last, preferred_element_type=F32
                )
                scores = jnp.where(allowed, scores, -1e30)
                peak = jnp.max(scores, axis=-1, keepdims=True)
                expo = jnp.exp(scores - peak)
                sums = jnp.sum(expo, axis=-1, keepdims=True)
                out = jnp.dot(expo.astype(BF16), value, preferred_element_type=F32) / sums
                total = total + head_lanes(out, head)
                lse_ref[at, head : head + 1] = peak + jnp.log(sums)
            each = min(tok, block)
            for r in range(0, block, each):
                target = seq * (nar // seqs) + (start + r) // tok
                spot_row = (start + r) % tok
                attended[target, spot_row : spot_row + each, :] = total[r : r + each, :].astype(
                    BF16
                )

        def leave(b, c):
            target = seq * (nar // seqs) + b

            @pl.when(target != me)
            def _():
                att_copy(target, me).start()

            return c

        lax.fori_loop(0, nar // seqs, leave, 0)
        return carry

    lax.fori_loop(0, seqs, sequence, 0)
    stores[2].start()
    own_att = pltpu.make_async_copy(attended.at[me], att_ref.at[me], own_sem.at[3])
    own_att.start()

    def norms(begin, end):
        def body(index, carry):
            slot = lax.rem(index, ring)
            fetch(index, slot).wait()
            keys = slots[slot].astype(F32)
            at = pl.ds(pl.multiple_of(index * tile, tile), tile)
            norms_ref[at, :] = jnp.sum(keys * keys, axis=1)

            @pl.when(index + ring < tiles)
            def _():
                fetch(index + ring, slot).start()

            return carry

        lax.fori_loop(begin, end, body, 0)

    def some(*calls):
        def run():
            for call in calls:
                call()

        return run

    steps = [
        some(lambda: line_arrivals(1, 1, 2), lambda: line_arrivals(0, 2, first)),
        some(lambda: chip_arrivals(0), lambda: line_arrivals(2, 1, 2)),
        lambda: line_arrivals(1, 2, first),
        lambda: line_arrivals(2, 2, first),
    ]
    share_of = tiles // len(steps)
    for n, step in enumerate(steps):
        step()
        norms(n * share_of, tiles if n == len(steps) - 1 else (n + 1) * share_of)
    stores[3].start()
    row_arrivals()
    chip_arrivals(1)
    chip_arrivals(2)
    for t in range(3):
        core_arrivals(t)
    for k in range(1, nar):
        source = lax.rem(me + k, nar)
        att_copy(source, source).wait_recv()
        att_copy(source, me).wait_send()
    for t in range(3):
        own_copies[t].wait()

        def sent(source, t=t):
            for o in range(outer):
                core_copy(t, source, o, False).wait_send()

        each_source(t, sent)
        for n in range(first):
            source = n * second + yb

            @pl.when(source != me)
            def _(source=source, t=t):
                for o in range(1, outer):
                    chip_copy(t, source, o).wait_send()

        for z in range(first):

            @pl.when(za == z)
            def _(z=z, t=t):
                for slot, target in enumerate(reach[z]):
                    line_copy(t, me, target, slot, True).wait_send()
                if z in relay:
                    target, sources = relay[z]
                    for n in sources:
                        line_copy(t, n * second + yb, target, 0, False).wait_send()

    for z in range(first):
        for j in range(1, second):
            for o in range(outer):
                row_copy(z * second + yb, j, o, False).wait_send()
    own_att.wait()
    for store in stores:
        store.wait()


def head(gain, seg, weights, block_input, keys, w_in, w_out, first, nar, wid, name):
    rows, width = block_input.shape
    seqs, length = seg.shape
    second = nar // first
    outer = wid // 2
    local = weights[0].shape[0]
    heads = local // HD
    hidden = w_in.shape[1]
    tok = rows // nar
    depth = keys.shape[1]
    tile, ring = 32, 4
    block = min(256, length)
    vmem = pl.BlockSpec(memory_space=pltpu.VMEM)
    hbm = pl.BlockSpec(memory_space=pl.ANY)
    dma = pltpu.SemaphoreType.DMA
    kept = (
        ((rows, width), BF16),
        ((rows, 3 * local), BF16),
        ((rows, heads), F32),
        ((rows, J), F32),
    )
    return pl.pallas_call(
        functools.partial(head_kernel, nar, first, wid, seqs, heads, block, tile, ring),
        out_shape=tuple(jax.ShapeDtypeStruct(*x) for x in kept)
        + (
            jax.ShapeDtypeStruct((nar, tok, local), BF16),
            jax.ShapeDtypeStruct((first, width, hidden), BF16),
            jax.ShapeDtypeStruct((first, hidden, width), BF16),
            jax.ShapeDtypeStruct((nar, 4 * local, width), BF16),
        ),
        in_specs=[vmem] * 2 + [hbm] * 8,
        out_specs=(hbm,) * 8,
        scratch_shapes=[
            pltpu.VMEM((4 * local, width), BF16),
            pltpu.VMEM((width, hidden), BF16),
            pltpu.VMEM((hidden, width), BF16),
            pltpu.VMEM((rows, width), BF16),
        ]
        + [pltpu.VMEM(*x) for x in kept]
        + [
            pltpu.VMEM((nar, tok, local), BF16),
            pltpu.VMEM((ring, tile, depth, J), BF16),
            dma((7,)),
            dma((4,)),
            dma((ring,)),
            dma((4,)),
            dma((nar,)),
            dma((nar,)),
            dma((3, first, 3)),
            dma((3, first)),
            dma((nar, second, outer)),
            dma((nar, second, outer)),
            dma((3, nar, outer)),
            dma((3, nar, outer)),
            dma((3, nar, outer)),
            dma((3, nar, outer)),
        ],
        compiler_params=pltpu.CompilerParams(
            collective_id=name, has_side_effects=True, vmem_limit_bytes=62 * 2**20
        ),
    )(gain, seg, *weights, block_input, keys, w_in, w_out)


INNER = 0.7978845608028654
CUBIC = 0.044715


def gelu_parts(values):
    tanh = jnp.tanh(INNER * (values + CUBIC * values * values * values))
    return 0.5 * values * (1.0 + tanh), tanh


def own_rows(tok, second):
    me = lax.axis_index("z") * second + lax.axis_index("y")
    return pl.ds(pl.multiple_of(me * tok, tok), tok)


def ffn_kernel(
    chunks,
    gain_two_ref,
    gain_key_ref,
    att_any,
    input_any,
    pq_any,
    in_any,
    mid_any,
    one_out,
    two_out,
    output_out,
    key_out,
    normed_out,
    pre_out,
    att_ref,
    input_ref,
    proj_ref,
    in_ref,
    mid_ref,
    one_ref,
    two_ref,
    output_ref,
    key_ref,
    normed_ref,
    pre_ref,
    back_out,
    back_in,
    load_sem,
    store_sem,
    n_send,
    n_recv,
    b_send,
    b_recv,
):
    nar, tok, local = att_ref.shape
    first, width, hidden = in_ref.shape
    second = nar // first
    part = tok // chunks
    za, yb = lax.axis_index("z"), lax.axis_index("y")

    pairs = (
        (att_any, att_ref),
        (pq_any.at[:, pl.ds(0, local)], proj_ref),
        (input_any.at[own_rows(tok, second)], input_ref),
        (in_any, in_ref),
        (mid_any, mid_ref),
    )
    loads = [
        pltpu.make_async_copy(src, dst, load_sem.at[n]) for n, (src, dst) in enumerate(pairs)
    ]
    for load in loads:
        load.start()
    kept = (
        (one_ref, one_out),
        (normed_ref, normed_out),
        (pre_ref, pre_out),
        (key_ref, key_out),
        (two_ref, two_out),
        (output_ref, output_out),
    )
    stores = [
        pltpu.make_async_copy(src, dst, store_sem.at[n]) for n, (src, dst) in enumerate(kept)
    ]

    greet([{"z": za, "y": lax.rem(yb + j, second)} for j in range(1, second)])

    def n_copy(j, c):
        at = pl.ds(c * part, part)
        target = {"z": za, "y": lax.rem(yb + j, second)}
        return push(
            normed_ref.at[0, at], normed_ref.at[j, at], n_send.at[j, c], n_recv.at[j, c], target
        )

    def b_copy(j, c):
        at = pl.ds(c * part, part)
        target = {"z": za, "y": lax.rem(yb + second - j, second)}
        return push(
            back_out.at[j, at], back_in.at[j, at], b_send.at[j, c], b_recv.at[j, c], target
        )

    def through(j, start, count):
        total = jnp.zeros((count, width), F32)
        for z in range(first):
            pre = jnp.dot(
                normed_ref[j, start : start + count, :], in_ref[z], preferred_element_type=F32
            )
            pre_ref[j, start : start + count, z * hidden : (z + 1) * hidden] = pre
            activated = gelu_parts(pre)[0].astype(BF16)
            total = total + jnp.dot(activated, mid_ref[z], preferred_element_type=F32)
        return total

    for n in range(3):
        loads[n].wait()
    att = jnp.concatenate([att_ref[n] for n in range(nar)], axis=1)
    one = input_ref[...].astype(F32) + jnp.dot(
        att, proj_ref[...].reshape(nar * local, width), preferred_element_type=F32
    )
    one_ref[...] = one
    normed, _ = normalise(one)
    normed_ref[0] = (normed * gain_two_ref[...]).astype(BF16)
    for c in range(chunks):
        for j in range(1, second):
            n_copy(j, c).start()
    stores[0].start()
    for n in range(3, 5):
        loads[n].wait()
    two_ref[...] = one_ref[...] + through(0, 0, tok)
    for c in range(chunks):
        for j in range(1, second):
            n_copy(j, c).wait_recv()
            back_out[j, c * part : (c + 1) * part, :] = through(j, c * part, part).astype(BF16)
            b_copy(j, c).start()
    stores[1].start()
    stores[2].start()
    for c in range(chunks):
        at = slice(c * part, (c + 1) * part)
        for j in range(1, second):
            b_copy(j, c).wait_recv()
            two_ref[at, :] += back_in[j, at, :].astype(F32)
    hidden_two = two_ref[...]
    normed, _ = normalise(hidden_two)
    query_key = (normed * gain_key_ref[...]).astype(BF16)
    for n in range(nar):
        key_ref[n] = query_key[:, n * (width // nar) : (n + 1) * (width // nar)]
    stores[3].start()
    stores[4].start()
    output_ref[...] = hidden_two.astype(BF16)
    stores[5].start()
    for c in range(chunks):
        for j in range(1, second):
            n_copy(j, c).wait_send()
            b_copy(j, c).wait_send()
    for store in stores:
        store.wait()


def ffn(gain_two, gain_key, att, inputs, pq, in_all, out_all, name):
    nar, tok, local = att.shape
    first, width, hidden = in_all.shape
    second = nar // first
    chunks = 2
    vmem = pl.BlockSpec(memory_space=pltpu.VMEM)
    hbm = pl.BlockSpec(memory_space=pl.ANY)
    dma = pltpu.SemaphoreType.DMA
    outs = (
        ((tok, width), F32),
        ((tok, width), F32),
        ((tok, width), BF16),
        ((nar, tok, width // nar), BF16),
        ((second, tok, width), BF16),
        ((second, tok, first * hidden), F32),
    )
    return pl.pallas_call(
        functools.partial(ffn_kernel, chunks),
        out_shape=tuple(jax.ShapeDtypeStruct(*x) for x in outs),
        in_specs=[vmem] * 2 + [hbm] * 5,
        out_specs=(hbm,) * 6,
        scratch_shapes=[
            pltpu.VMEM(att.shape, BF16),
            pltpu.VMEM((tok, width), BF16),
            pltpu.VMEM((nar, local, width), BF16),
            pltpu.VMEM(in_all.shape, BF16),
            pltpu.VMEM(out_all.shape, BF16),
        ]
        + [pltpu.VMEM(*x) for x in outs]
        + [pltpu.VMEM((second, tok, width), BF16)] * 2
        + [dma((5,)), dma((6,))]
        + [dma((second, chunks))] * 4,
        compiler_params=pltpu.CompilerParams(
            collective_id=name, has_side_effects=True, vmem_limit_bytes=62 * 2**20
        ),
    )(gain_two, gain_key, att, inputs, pq, in_all, out_all)


def ffn_back_kernel(
    chunks,
    gain_two_ref,
    gain_key_ref,
    slices_ref,
    stat_ref,
    two_any,
    cot_any,
    mid_any,
    pre_any,
    in_any,
    att_any,
    normed_any,
    one_any,
    pq_any,
    share_any,
    sums_ref,
    grad_one_out,
    grad_att_out,
    pre_turned_out,
    act_turned_out,
    att_turned_out,
    normed_cols_out,
    ffn_cols_out,
    branch_cols_out,
    line_ref,
    two_ref,
    cot_ref,
    mid_ref,
    pre_ref,
    in_ref,
    att_ref,
    normed_ref,
    one_ref,
    proj_ref,
    share_ref,
    grad_one_ref,
    grad_att_ref,
    pre_turned_ref,
    act_turned_ref,
    att_turned_ref,
    normed_cols_ref,
    ffn_cols_ref,
    branch_cols_ref,
    grads,
    grad_two,
    total,
    back_out,
    back_in,
    load_sem,
    store_sem,
    own_sem,
    n_send,
    n_recv,
    b_send,
    b_recv,
    g_send,
    g_recv,
):
    nar, tok, local = att_ref.shape
    first, width, hidden = in_ref.shape
    second = nar // first
    wid = branch_cols_ref.shape[0]
    columns = width // wid
    part = tok // chunks
    last = (((1,), (1,)), ((), ()))
    za, yb = lax.axis_index("z"), lax.axis_index("y")
    reach, relay = REACH, RELAY

    pairs = (
        (share_any, share_ref),
        (two_any, two_ref),
        (cot_any.at[own_rows(tok, second)], cot_ref),
        (mid_any, mid_ref),
        (pre_any, pre_ref),
        (in_any, in_ref),
        (att_any, att_ref),
        (normed_any, normed_ref),
        (one_any, one_ref),
        (pq_any.at[:, pl.ds(0, local)], proj_ref),
    )
    loads = [
        pltpu.make_async_copy(src, dst, load_sem.at[n]) for n, (src, dst) in enumerate(pairs)
    ]
    for load in loads:
        load.start()
    kept = (
        (ffn_cols_ref, ffn_cols_out),
        (pre_turned_ref, pre_turned_out),
        (act_turned_ref, act_turned_out),
        (att_turned_ref, att_turned_out),
        (normed_cols_ref, normed_cols_out),
        (grad_att_ref, grad_att_out),
        (branch_cols_ref, branch_cols_out),
        (grad_one_ref, grad_one_out),
    )
    stores = [
        pltpu.make_async_copy(src, dst, store_sem.at[n]) for n, (src, dst) in enumerate(kept)
    ]

    greet(
        [{"z": za, "y": lax.rem(yb + j, second)} for j in range(1, second)]
        + [{"z": lax.rem(za + i, first), "y": yb} for i in range(1, first)]
    )

    def n_copy(j, c):
        at = pl.ds(c * part, part)
        target = {"z": za, "y": lax.rem(yb + j, second)}
        return push(grads.at[0, at], grads.at[j, at], n_send.at[j, c], n_recv.at[j, c], target)

    def b_copy(j, c):
        at = pl.ds(c * part, part)
        target = {"z": za, "y": lax.rem(yb + second - j, second)}
        return push(
            back_out.at[j, at], back_in.at[j, at], b_send.at[j, c], b_recv.at[j, c], target
        )

    def g_copy(source, target, slot, c, own):
        at = pl.ds(c * part, part)
        return push(
            share_ref.at[at] if own else line_ref.at[source, at],
            line_ref.at[source, at],
            g_send.at[source, slot, c],
            g_recv.at[source, c],
            {"z": target, "y": yb},
        )

    def gathered(c, begin, end):
        for d in range(begin, end):
            for way in (-1, 1):
                z = za + way * d

                @pl.when((z >= 0) & (z < first))
                def _(z=z):
                    g_copy(z, za, 0, c, False).wait_recv()
                    for middle, (target, sources) in relay.items():

                        @pl.when((za == middle) & ((z == sources[0]) | (z == sources[1])))
                        def _(target=target):
                            g_copy(z, target, 0, c, False).start()

    loads[0].wait()
    for c in range(chunks):
        for z in range(first):

            @pl.when(za == z)
            def _(z=z, c=c):
                for slot, target in enumerate(reach[z]):
                    g_copy(za, target, slot, c, True).start()

    own_copy = pltpu.make_async_copy(share_ref, line_ref.at[za], own_sem)
    own_copy.start()

    def through(j, start, count):
        at = slice(start, start + count)
        sums = jnp.zeros((count, width), F32)
        for z in range(first):
            own = slice(z * hidden, (z + 1) * hidden)
            pre = pre_ref[j, at, own]
            activated, tanh = gelu_parts(pre)
            slope = 0.5 * (1.0 + tanh) + 0.5 * pre * (1.0 - tanh * tanh) * INNER * (
                1.0 + 3.0 * CUBIC * pre * pre
            )
            grad_act = lax.dot_general(
                grads[j, at, :], mid_ref[z], last, preferred_element_type=F32
            )
            grad_pre = slope * grad_act
            to = slice(j * tok + start, j * tok + start + count)
            act_turned_ref[own, to] = jnp.transpose(activated).astype(BF16)
            pre_turned_ref[own, to] = jnp.transpose(grad_pre).astype(BF16)
            sums = sums + lax.dot_general(
                grad_pre.astype(BF16), in_ref[z], last, preferred_element_type=F32
            )
        return sums

    for n in range(1, 3):
        loads[n].wait()
    grad_key = jnp.concatenate([slices_ref[n] for n in range(nar)], axis=1).astype(F32)
    normed, inverse = normalise(two_ref[...])
    sums_ref[...] = jnp.zeros_like(sums_ref)
    sums_ref[2:3, :] = jnp.sum(grad_key * normed, axis=0, keepdims=True)
    temper_sum = jnp.sum(stat_ref[0:1, :], axis=1, keepdims=True)
    sums_ref[3:4, :] = jnp.broadcast_to(temper_sum, (1, width))
    sums_ref[4:5, :] = jnp.broadcast_to(stat_ref[1:2, 0:1], (1, width))
    grad = cot_ref[...].astype(F32) + normalise_back(
        grad_key, normed, inverse, gain_key_ref[...]
    )
    grad_two[...] = grad
    grads[0] = grad.astype(BF16)
    for c in range(chunks):
        for j in range(1, second):
            n_copy(j, c).start()
    for n in range(3, 6):
        loads[n].wait()
    total[...] = through(0, 0, tok)
    gathered(0, 1, 2)
    for c in range(chunks):
        for j in range(1, second):
            n_copy(j, c).wait_recv()
            back_out[j, c * part : (c + 1) * part, :] = through(j, c * part, part).astype(BF16)
            b_copy(j, c).start()
    gathered(0, 2, first)
    gathered(1, 1, first)
    for n in range(6, 10):
        loads[n].wait()
    for j in range(second):
        for w in range(wid):
            own = slice(w * columns, (w + 1) * columns)
            normed_cols_ref[w, j * tok : (j + 1) * tok, :] = normed_ref[j, :, own]
            ffn_cols_ref[w, j * tok : (j + 1) * tok, :] = grads[j, :, own]
    att_turned_ref[...] = jnp.concatenate(
        [jnp.transpose(att_ref[n].astype(F32)).astype(BF16) for n in range(nar)], axis=0
    )
    for n in range(5):
        stores[n].start()
    for c in range(chunks):
        at = slice(c * part, (c + 1) * part)
        for j in range(1, second):
            b_copy(j, c).wait_recv()
            total[at, :] += back_in[j, at, :].astype(F32)
    normed, inverse = normalise(one_ref[...])
    sums_ref[1:2, :] = jnp.sum(total[...] * normed, axis=0, keepdims=True)
    grad = grad_two[...] + normalise_back(total[...], normed, inverse, gain_two_ref[...])
    branch = grad.astype(BF16)
    grad_att = lax.dot_general(
        branch, proj_ref[...].reshape(nar * local, width), last, preferred_element_type=F32
    ).astype(BF16)
    for n in range(nar):
        grad_att_ref[n] = grad_att[:, n * local : (n + 1) * local]
    stores[5].start()
    for w in range(wid):
        branch_cols_ref[w] = branch[:, w * columns : (w + 1) * columns]
    stores[6].start()
    grad_one_ref[...] = grad
    stores[7].start()
    own_copy.wait()
    for c in range(chunks):
        for j in range(1, second):
            n_copy(j, c).wait_send()
            b_copy(j, c).wait_send()
        for z in range(first):

            @pl.when(za == z)
            def _(z=z, c=c):
                for slot, target in enumerate(reach[z]):
                    g_copy(za, target, slot, c, True).wait_send()
                if z in relay:
                    target, sources = relay[z]
                    for n in sources:
                        g_copy(n, target, 0, c, False).wait_send()

    for store in stores:
        store.wait()


def ffn_back(
    gain_two,
    gain_key,
    slices,
    stats,
    two,
    cot,
    out_all,
    pre,
    in_all,
    att,
    normed,
    one,
    pq,
    share,
    wid,
    name,
):
    nar, tok, local = att.shape
    first, width, hidden = in_all.shape
    second = nar // first
    chunks = 2
    columns = width // wid
    vmem = pl.BlockSpec(memory_space=pltpu.VMEM)
    hbm = pl.BlockSpec(memory_space=pl.ANY)
    dma = pltpu.SemaphoreType.DMA
    outs = (
        ((tok, width), F32),
        ((nar, tok, local), BF16),
        ((first * hidden, second * tok), BF16),
        ((first * hidden, second * tok), BF16),
        ((nar * local, tok), BF16),
        ((wid, second * tok, columns), BF16),
        ((wid, second * tok, columns), BF16),
        ((wid, tok, columns), BF16),
    )
    return pl.pallas_call(
        functools.partial(ffn_back_kernel, chunks),
        out_shape=(jax.ShapeDtypeStruct((8, width), F32),)
        + tuple(jax.ShapeDtypeStruct(*x) for x in outs)
        + (jax.ShapeDtypeStruct((first, tok, width), BF16),),
        in_specs=[vmem] * 4 + [hbm] * 10,
        out_specs=(vmem,) + (hbm,) * 9,
        scratch_shapes=[
            pltpu.VMEM((tok, width), F32),
            pltpu.VMEM((tok, width), BF16),
            pltpu.VMEM(out_all.shape, BF16),
            pltpu.VMEM(pre.shape, F32),
            pltpu.VMEM(in_all.shape, BF16),
            pltpu.VMEM(att.shape, BF16),
            pltpu.VMEM(normed.shape, BF16),
            pltpu.VMEM((tok, width), F32),
            pltpu.VMEM((nar, local, width), BF16),
            pltpu.VMEM((tok, width), BF16),
        ]
        + [pltpu.VMEM(*x) for x in outs]
        + [
            pltpu.VMEM((second, tok, width), BF16),
            pltpu.VMEM((tok, width), F32),
            pltpu.VMEM((tok, width), F32),
            pltpu.VMEM((second, tok, width), BF16),
            pltpu.VMEM((second, tok, width), BF16),
            dma((10,)),
            dma((8,)),
            dma,
        ]
        + [dma((second, chunks))] * 4
        + [dma((first, 3, chunks)), dma((first, chunks))],
        compiler_params=pltpu.CompilerParams(
            collective_id=name, has_side_effects=True, vmem_limit_bytes=62 * 2**20
        ),
    )(
        gain_two,
        gain_key,
        slices,
        stats,
        two,
        cot,
        out_all,
        pre,
        in_all,
        att,
        normed,
        one,
        pq,
        share,
    )


def finish_kernel(
    second, grad_ref, block_ref, line_ref, total_ref, loss_ref, qkv_ref, proj_ref, in_ref, mid_ref, *outs
):
    (
        block_out,
        loss_out,
        grad_out,
        query_out,
        key_out,
        value_out,
        proj_out,
        in_out,
        mid_out,
        attn_out,
        ffn_out,
        last_out,
        temper_out,
        mix_out,
    ) = outs
    grad_out[...] = grad_ref[...].astype(F32)
    near = lax.rem(pl.program_id(0), second) == lax.axis_index("y")

    @pl.when(near)
    def _():
        block_out[...] = line_ref[...]

    @pl.when(jnp.logical_not(near))
    def _():
        block_out[...] = block_ref[...]

    @pl.when(pl.program_id(0) == 0)
    def _():
        local = proj_ref.shape[0]
        query_out[...] = qkv_ref[0:local, :]
        key_out[...] = qkv_ref[local : 2 * local, :]
        value_out[...] = qkv_ref[2 * local : 3 * local, :]
        proj_out[...] = proj_ref[...]
        in_out[...] = in_ref[...]
        mid_out[...] = mid_ref[...]
        attn_out[...] = total_ref[0:1, :]
        ffn_out[...] = total_ref[1:2, :]
        last_out[...] = total_ref[2:3, :]
        temper_out[...] = total_ref[3:4, 0:1]
        mix_out[...] = total_ref[4:5, 0:1]
        nar, _, tok = loss_ref.shape
        seqs = loss_out.shape[0]
        per_seq = nar // seqs
        for n in range(nar):
            at = (n % per_seq) * tok
            loss_out[n // per_seq : n // per_seq + 1, at : at + tok] = loss_ref[n, 0:1, :]


def finish(grad, block, lines, totals, losses, qkv, proj, w_in, w_out, seqs):
    nar, tok, width = grad.shape
    second = nar // lines.shape[0]
    local, piece = proj.shape

    def whole(shape):
        return pl.BlockSpec(shape, lambda i: (0,) * len(shape))

    def each():
        return pl.BlockSpec((1, tok, width), lambda i: (i, 0, 0))

    small = [
        ((local, piece), F32),
        ((local, piece), F32),
        ((local, piece), F32),
        (proj.shape, F32),
        (w_in.shape, F32),
        (w_out.shape, F32),
        ((1, piece), F32),
        ((1, piece), F32),
        ((1, piece), F32),
        ((1, 1), F32),
        ((1, 1), F32),
    ]
    loss_shape = (seqs, nar * tok // seqs)
    return pl.pallas_call(
        functools.partial(finish_kernel, second),
        grid=(nar,),
        out_shape=(
            jax.ShapeDtypeStruct((nar, tok, width), BF16),
            jax.ShapeDtypeStruct(loss_shape, F32),
            jax.ShapeDtypeStruct((nar, tok, width), F32),
        )
        + tuple(jax.ShapeDtypeStruct(*x) for x in small),
        in_specs=[each(), each(), pl.BlockSpec((1, tok, width), lambda i: (i // second, 0, 0))]
        + [whole(x.shape) for x in (totals, losses, qkv, proj, w_in, w_out)],
        out_specs=(each(), whole(loss_shape), each()) + tuple(whole(x[0]) for x in small),
        compiler_params=pltpu.CompilerParams(vmem_limit_bytes=62 * 2**20),
    )(grad, block, lines, totals, losses, qkv, proj, w_in, w_out)


REACH = ((1, 2), (0, 2), (1, 3), (2, 1))
RELAY = {1: (0, (2, 3)), 2: (3, (0, 1))}


def segment_column(seg_ref, seq, start, block):
    row = seg_ref[pl.ds(seq, 1), start : start + block].astype(F32)
    return jnp.transpose(jnp.broadcast_to(row, (8, block)))[:, 0:1]


def grad_kernel(
    nar,
    first,
    wid,
    seqs,
    heads,
    block,
    chunks,
    seg_ref,
    gain_ref,
    sums_ref,
    grad_ref,
    line_any,
    pre_any,
    act_any,
    att_any,
    normed_any,
    ffn_any,
    branch_any,
    qkv_any,
    lse_any,
    one_any,
    input_any,
    above_any,
    pq_any,
    all_ref,
    block_ref,
    total_ref,
    in_grad_ref,
    out_grad_ref,
    proj_grad_ref,
    qkv_grad_ref,
    pre_ref,
    act_ref,
    att_ref,
    normed_ref,
    ffn_ref,
    branch_ref,
    qkv_ref,
    lse_ref,
    one_ref,
    input_ref,
    above_ref,
    pq_ref,
    load_sem,
    out_ref,
    grads,
    got,
    grad_key,
    grad_value,
    core_out,
    core_in,
    chip_out,
    chip_in,
    tail_sum,
    turn_out,
    turn_in,
    line_in,
    work,
    qkv_out,
    qkv_in,
    own_ref,
    own_sums,
    all_sums,
    pieces_out,
    pieces_in,
    own_sem,
    k_send,
    k_recv,
    a_send,
    a_recv,
    b_send,
    b_recv,
    c_send,
    c_recv,
    x_send,
    x_recv,
    y_send,
    y_recv,
    z_send,
    z_recv,
    w_send,
    w_recv,
    g_send,
    g_recv,
    h_send,
    h_recv,
    s_send,
    s_recv,
    p_send,
    p_recv,
):
    second = nar // first
    outer = wid // 2
    za, yb = lax.axis_index("z"), lax.axis_index("y")
    me = za * second + yb
    wide = lax.axis_index("wide")
    chip, core = wide // 2, lax.rem(wide, 2)
    tok, local = grads.shape[1:]
    hidden = pre_ref.shape[0] // first
    columns = normed_ref.shape[2]
    rows = 2 * hidden
    body = first * rows
    line = rows + local
    length = nar * tok // seqs
    per_seq = nar // seqs
    width = heads * HD
    part = tok // chunks
    across = (((0,), (0,)), ((), ()))
    last = (((1,), (1,)), ((), ()))
    reach, relay = REACH, RELAY

    pairs = (
        (pre_any, pre_ref),
        (act_any, act_ref),
        (att_any, att_ref),
        (normed_any, normed_ref),
        (ffn_any, ffn_ref),
        (branch_any, branch_ref),
        (qkv_any, qkv_ref),
        (lse_any, lse_ref),
        (one_any, one_ref),
        (input_any.at[own_rows(tok, second)], input_ref),
        (above_any, above_ref),
        (pq_any, pq_ref),
    )
    loads = [
        pltpu.make_async_copy(src, dst, load_sem.at[n]) for n, (src, dst) in enumerate(pairs)
    ]
    for load in loads:
        load.start()

    greet(
        [place(lax.rem(me + k, nar), second) for k in range(1, nar)]
        + [{"wide": lax.rem(wide + w, wid)} for w in range(1, wid)]
    )

    def a_copy(target, source):
        return push(
            grad_ref.at[target],
            grads.at[source],
            a_send.at[target],
            a_recv.at[source],
            place(target, second),
        )

    def b_copy(target, source):
        return push(
            out_ref.at[pl.ds(pl.multiple_of(target * tok, tok), tok)],
            got.at[source],
            b_send.at[target],
            b_recv.at[source],
            place(target, second),
        )

    def k_copy(z, j):
        return push(
            line_any.at[z],
            block_ref.at[z * second + yb],
            k_send.at[z, j],
            k_recv.at[z, j],
            {"z": za, "y": lax.rem(yb + j, second)},
        )

    def c_copy(o):
        return push(
            core_out.at[o],
            core_in.at[o],
            c_send.at[o],
            c_recv.at[o],
            {"wide": chip * 2 + (1 - core)},
        )

    def span(z):
        return pl.ds(pl.multiple_of(z * rows, rows), rows)

    tail_rows = pl.ds(body, nar * local)

    def x_copy(i, q, at):
        return push(
            chip_out.at[i - 1, at],
            chip_in.at[i - 1, at],
            x_send.at[i, q],
            x_recv.at[i, q],
            {"wide": lax.rem(chip + i, outer) * 2 + core},
        )

    def y_copy(j):
        target = {"z": za, "y": lax.rem(yb + j, second)}
        return push(turn_out.at[j], turn_in.at[j], y_send.at[j], y_recv.at[j], target)

    inner = jnp.where((za == 1) | (za == 2), 1, 0)

    def mirror(z):
        return jnp.where(za < 2, z, 3 - z)

    def dest(n):
        return mirror(jnp.where(n == 1, 3, jnp.where(n == 2, 2, jnp.where(n == 3, 1 - inner, inner))))

    def z_copy(n):
        slot = jnp.where(inner == 1, (3, 4, 0)[n - 1], n - 1)
        target = mirror(jnp.where(inner == 1, (2, 2, 0)[n - 1], 1))
        return push(
            core_out.at[0, pl.ds((n - 1) * line, line)],
            line_in.at[slot],
            z_send.at[n],
            z_recv.at[slot],
            {"z": target, "y": yb},
        )

    def z_arrival(slot):
        return push(
            core_out.at[0, pl.ds(0, line)],
            line_in.at[slot],
            z_send.at[0],
            z_recv.at[slot],
            {"z": mirror(jnp.where(inner == 1, 0, 1)), "y": yb},
        )

    def w_copy(i):
        target = lax.rem(wide + i, wid)
        return push(
            qkv_out.at[target], qkv_in.at[i], w_send.at[i], w_recv.at[i], {"wide": target}
        )

    def g_copy(source_z, target_z, slot, c, own):
        at = pl.ds(c * part, part)
        source = source_z * second + yb
        return push(
            own_ref.at[at] if own else all_ref.at[source, at],
            all_ref.at[source, at],
            g_send.at[source_z, slot, c],
            g_recv.at[source_z, c],
            {"z": target_z, "y": yb},
        )

    def h_copy(source_z, j, c, own):
        at = pl.ds(c * part, part)
        source = source_z * second + yb
        return push(
            own_ref.at[at] if own else all_ref.at[source, at],
            all_ref.at[source, at],
            h_send.at[source_z, j, c],
            h_recv.at[source_z, j, c],
            {"z": za, "y": lax.rem(yb + j, second)},
        )

    def h_arrival(source_z, j, c):
        at = pl.ds(c * part, part)
        source = source_z * second + lax.rem(yb + second - j, second)
        return push(
            all_ref.at[source, at],
            all_ref.at[source, at],
            h_send.at[source_z, j, c],
            h_recv.at[source_z, j, c],
            {"z": za, "y": lax.rem(yb + j, second)},
        )

    def s_copy(k):
        target = place(lax.rem(me + k, nar), second)
        return push(own_sums, all_sums.at[k], s_send.at[k], s_recv.at[k], target)

    def p_copy(w):
        target = lax.rem(wide + w, wid)
        return push(
            pieces_out.at[target], pieces_in.at[w], p_send.at[w], p_recv.at[w], {"wide": target}
        )

    def product_rows(w, z):
        own = pl.ds(pl.multiple_of(z * hidden, hidden), hidden)
        return (
            jnp.dot(pre_ref[own, :], normed_ref[w], preferred_element_type=F32),
            jnp.dot(act_ref[own, :], ffn_ref[w], preferred_element_type=F32),
        )

    def product_tail(w):
        return jnp.dot(att_ref[...], branch_ref[w], preferred_element_type=F32)

    for k in range(1, nar):
        a_copy(lax.rem(me + k, nar), me).start()
    own_grad = pltpu.make_async_copy(grad_ref.at[me], grads.at[me], own_sem.at[1])
    own_grad.start()
    for j in range(1, second):
        k_copy(0, j).start()
    for n in range(6):
        loads[n].wait()

    for i in range(1, outer + 1):
        o = lax.rem(chip + i, outer)
        w = o * 2 + (1 - core)

        def for_core(z, carry, o=o, w=w):
            upper, lower = product_rows(w, z)
            at = pl.multiple_of(z * rows, rows)
            core_out[o, pl.ds(at, hidden), :] = upper.astype(BF16)
            core_out[o, pl.ds(at + hidden, hidden), :] = lower.astype(BF16)
            return carry

        lax.fori_loop(0, first, for_core, 0)
        core_out[o, tail_rows, :] = product_tail(w).astype(BF16)
        c_copy(o).start()

    for i in range(1, outer):
        o = lax.rem(chip + i, outer)
        w = o * 2 + core
        c_copy(o).wait_recv()
        total = product_tail(w) + core_in[o, tail_rows, :].astype(F32)
        chip_out[i - 1, tail_rows, :] = total.astype(BF16)
        x_copy(i, 0, tail_rows).start()

        def for_chip(n, carry, o=o, w=w, i=i):
            z = dest(n)
            upper, lower = product_rows(w, z)
            at = pl.multiple_of(z * rows, rows)
            high, low = pl.ds(at, hidden), pl.ds(at + hidden, hidden)
            chip_out[i - 1, high, :] = (upper + core_in[o, high, :].astype(F32)).astype(BF16)
            chip_out[i - 1, low, :] = (lower + core_in[o, low, :].astype(F32)).astype(BF16)
            x_copy(i, n, span(z)).start()
            return carry

        lax.fori_loop(1, first + 1, for_chip, 0)

    loads[6].wait()
    loads[7].wait()
    own_grad.wait()

    def sequence(seq, carry):
        base = seq * length

        def arrive(b, c):
            source = seq * per_seq + b

            @pl.when(source != me)
            def _():
                a_copy(source, source).wait_recv()

            return c

        lax.fori_loop(0, per_seq, arrive, 0)
        grad_key[...] = jnp.zeros_like(grad_key)
        grad_value[...] = jnp.zeros_like(grad_value)
        for start in range(0, length, block):
            keys = start + block
            at = pl.multiple_of(base + start, block)
            query_segment = segment_column(seg_ref, seq, start, block)
            key_segment = seg_ref[pl.ds(seq, 1), 0:keys].astype(F32)
            spot = lax.broadcasted_iota(jnp.int32, (block, keys), 1)
            own = lax.broadcasted_iota(jnp.int32, (block, keys), 0) + start
            allowed = (spot <= own) & (query_segment == key_segment)
            whole = pl.ds(pl.multiple_of(base, length), keys)
            query = qkv_ref[pl.ds(at, block), 0:width]
            key = qkv_ref[whole, width : 2 * width]
            value = qkv_ref[whole, 2 * width : 3 * width]
            each = min(tok, block)
            grad = jnp.concatenate(
                [
                    grads[
                        seq * per_seq + (start + r) // tok,
                        (start + r) % tok : (start + r) % tok + each,
                        :,
                    ]
                    for r in range(0, block, each)
                ],
                axis=0,
            )
            total = jnp.zeros((block, width), F32)
            for head in range(heads):
                own_query = head_lanes(query, head)
                own_grad = head_lanes(grad, head)
                scores = lax.dot_general(own_query, key, last, preferred_element_type=F32)
                probs = jnp.where(
                    allowed, jnp.exp(scores - lse_ref[pl.ds(at, block), head : head + 1]), 0.0
                )
                grad_probs = lax.dot_general(own_grad, value, last, preferred_element_type=F32)
                delta = jnp.sum(probs * grad_probs, axis=-1, keepdims=True)
                grad_scores = (probs * (grad_probs - delta)).astype(BF16)
                total = total + head_lanes(
                    jnp.dot(grad_scores, key, preferred_element_type=F32), head
                )
                grad_key[0:keys, :] += lax.dot_general(
                    grad_scores, own_query, across, preferred_element_type=F32
                )
                grad_value[0:keys, :] += lax.dot_general(
                    probs.astype(BF16), own_grad, across, preferred_element_type=F32
                )
            out_ref[pl.ds(at, block), 0:width] = (total * HD ** (-0.5)).astype(BF16)
        every = pl.ds(pl.multiple_of(base, length), length)
        out_ref[every, width : 2 * width] = grad_key[...].astype(BF16)
        out_ref[every, 2 * width : 3 * width] = grad_value[...].astype(BF16)

        def leave(b, c):
            target = seq * per_seq + b

            @pl.when(target != me)
            def _():
                b_copy(target, me).start()

            return c

        lax.fori_loop(0, per_seq, leave, 0)
        return carry

    lax.fori_loop(0, seqs, sequence, 0)

    for z in range(1, first):
        for j in range(1, second):
            k_copy(z, j).start()
    loads[8].wait()
    qkv_part = lax.dot_general(
        out_ref[...], one_ref[...], across, preferred_element_type=F32
    ).astype(BF16)
    for w in range(wid):
        qkv_out[w] = qkv_part[:, w * columns : (w + 1) * columns]
    for i in range(1, wid):
        w_copy(i).start()

    w_own = chip * 2 + core
    c_copy(chip).wait_recv()
    tail_sum[...] = product_tail(w_own) + core_in[chip, tail_rows, :].astype(F32)
    for i in range(1, outer):
        x_copy(i, 0, tail_rows).wait_recv()
        tail_sum[...] += chip_in[i - 1, tail_rows, :].astype(F32)
    for j in range(1, second):
        column = lax.rem(yb + j, second)
        for z in range(first):
            at = pl.ds(pl.multiple_of((z * second + column) * local, local), local)
            turn_out[j, z] = tail_sum[at, :].astype(BF16)
        y_copy(j).start()

    for n in range(9, 12):
        loads[n].wait()
    normed, inverse = normalise(input_ref[...].astype(F32))
    mine = out_ref[pl.ds(pl.multiple_of(me * tok, tok), tok), :]
    total = jnp.dot(mine, pq_ref[me, local:, :], preferred_element_type=F32)
    for k in range(1, nar):
        source = lax.rem(me + k, nar)
        b_copy(source, source).wait_recv()
        total = total + jnp.dot(
            got[source], pq_ref[source, local:, :], preferred_element_type=F32
        )
    grad = above_ref[...] + normalise_back(total, normed, inverse, gain_ref[0:1, :])
    own_ref[...] = grad.astype(BF16)

    for c in range(chunks):
        for z in range(first):

            @pl.when(za == z)
            def _(z=z, c=c):
                for slot, target in enumerate(reach[z]):
                    g_copy(za, target, slot, c, True).start()

        for j in range(1, second):
            h_copy(za, j, c, True).start()
    own_copy = pltpu.make_async_copy(own_ref, all_ref.at[me], own_sem.at[0])
    own_copy.start()
    own_sums[...] = sums_ref[...]
    own_sums[0:1, :] = jnp.sum(total * normed, axis=0, keepdims=True)
    for k in range(1, nar):
        s_copy(k).start()

    def gathered(begin, end):
        for c in range(chunks):
            for d in range(begin, end):
                for way in (-1, 1):
                    z = za + way * d

                    @pl.when((z >= 0) & (z < first))
                    def _(z=z, c=c):
                        g_copy(z, za, 0, c, False).wait_recv()
                        for middle, (target, sources) in relay.items():

                            @pl.when((za == middle) & ((z == sources[0]) | (z == sources[1])))
                            def _(target=target):
                                g_copy(z, target, 0, c, False).start()

                        for j in range(1, second):
                            h_copy(z, j, c, False).start()

    for o in range(outer):
        c_copy(o).wait_send()
    for j in range(1, second):
        y_copy(j).wait_recv()

    def line_parts(n):
        z = dest(n)
        at = pl.ds(pl.multiple_of((z * second + yb) * local, local), local)
        low_part = tail_sum[at, :]
        for j in range(1, second):
            low_part = low_part + turn_in[j, z].astype(F32)
        upper, lower = product_rows(w_own, z)
        start = pl.multiple_of(z * rows, rows)
        high, low = pl.ds(start, hidden), pl.ds(start + hidden, hidden)
        upper = upper + core_in[chip, high, :].astype(F32)
        lower = lower + core_in[chip, low, :].astype(F32)
        for i in range(1, outer):
            x_copy(i, n, span(z)).wait_recv()
            upper = upper + chip_in[i - 1, high, :].astype(F32)
            lower = lower + chip_in[i - 1, low, :].astype(F32)
        work[0:hidden, :] = upper
        work[hidden:rows, :] = lower
        work[rows:, :] = low_part

    def add_arrival(slot):
        z_arrival(slot).wait_recv()
        work[...] += line_in[slot].astype(F32)

    @pl.when(inner == 0)
    def _():
        for n in range(1, 4):
            line_parts(n)
            core_out[0, (n - 1) * line : n * line, :] = work[...].astype(BF16)
            z_copy(n).start()

    gathered(1, 2)
    gathered(2, first)

    @pl.when(inner == 1)
    def _():
        for n in range(1, 4):
            line_parts(n)
            add_arrival((0, 1, 3)[n - 1])
            core_out[0, (n - 1) * line : n * line, :] = work[...].astype(BF16)
            z_copy(n).start()

    line_parts(4)
    sums = own_sums[...]
    for k in range(1, nar):
        s_copy(k).wait_recv()
        sums = sums + all_sums[k]
    piece = total_ref.shape[1]
    for w in range(wid):
        pieces_out[w] = sums[:, w * piece : (w + 1) * piece]
    for w in range(1, wid):
        p_copy(w).start()
    qkv_sum = qkv_out[wide].astype(F32)
    for i in range(1, wid):
        w_copy(i).wait_recv()
        qkv_sum = qkv_sum + qkv_in[i].astype(F32)
    qkv_grad_ref[...] = qkv_sum

    @pl.when(inner == 0)
    def _():
        add_arrival(0)

    @pl.when(inner == 1)
    def _():
        add_arrival(2)
        add_arrival(4)

    in_grad_ref[...] = jnp.transpose(work[0:hidden, :])
    out_grad_ref[...] = work[hidden:rows, :]
    proj_grad_ref[...] = work[rows:, :]
    answer = pieces_out[wide]
    for w in range(1, wid):
        p_copy(w).wait_recv()
        answer = answer + pieces_in[w]
    total_ref[...] = answer

    for z in range(first):
        for j in range(1, second):
            for c in range(chunks):
                h_arrival(z, j, c).wait_recv()
    own_copy.wait()
    for z in range(first):
        for j in range(1, second):
            k_copy(z, j).wait()
    for k in range(1, nar):
        a_copy(lax.rem(me + k, nar), me).wait_send()
        b_copy(lax.rem(me + k, nar), me).wait_send()
        s_copy(k).wait_send()
    for w in range(1, wid):
        p_copy(w).wait_send()
        w_copy(w).wait_send()
    for i in range(1, outer):
        x_copy(i, 0, tail_rows).wait_send()
        for n in range(1, first + 1):
            x_copy(i, n, span(dest(n))).wait_send()
    for j in range(1, second):
        y_copy(j).wait_send()
    for n in range(1, first):
        z_copy(n).wait_send()
    for c in range(chunks):
        for z in range(first):

            @pl.when(za == z)
            def _(z=z, c=c):
                for slot, target in enumerate(reach[z]):
                    g_copy(za, target, slot, c, True).wait_send()
                if z in relay:
                    target, sources = relay[z]
                    for n in sources:
                        g_copy(n, target, 0, c, False).wait_send()

            for j in range(1, second):
                h_copy(z, j, c, False).wait_send()


def attention_grads(
    seg, gain, sums, grads, lines, sides, qkv, lse, one, inputs, above, pq, first, wid, name
):
    nar, tok, local = grads.shape
    rows, wide = qkv.shape
    width = inputs.shape[1]
    seqs, length = seg.shape
    second = nar // first
    outer = wid // 2
    hidden = sides[0].shape[0] // first
    piece = width // wid
    body = first * 2 * hidden + nar * local
    line = 2 * hidden + local
    chunks = 2
    vmem = pl.BlockSpec(memory_space=pltpu.VMEM)
    hbm = pl.BlockSpec(memory_space=pl.ANY)
    dma = pltpu.SemaphoreType.DMA
    late = (*sides, qkv, lse, one, inputs, above, pq)
    return pl.pallas_call(
        functools.partial(
            grad_kernel, nar, first, wid, seqs, local // HD, min(256, length), chunks
        ),
        out_shape=(
            jax.ShapeDtypeStruct((nar, tok, width), BF16),
            jax.ShapeDtypeStruct((nar, tok, width), BF16),
            jax.ShapeDtypeStruct((8, piece), F32),
            jax.ShapeDtypeStruct((piece, hidden), F32),
            jax.ShapeDtypeStruct((hidden, piece), F32),
            jax.ShapeDtypeStruct((local, piece), F32),
            jax.ShapeDtypeStruct((3 * local, piece), F32),
        ),
        in_specs=[vmem] * 3 + [hbm] * 14,
        out_specs=(hbm, hbm) + (vmem,) * 5,
        scratch_shapes=[
            pltpu.VMEM((tok, width) if x is inputs else x.shape, x.dtype) for x in late
        ]
        + [
            dma((12,)),
            pltpu.VMEM((rows, wide), BF16),
            pltpu.VMEM((nar, tok, local), BF16),
            pltpu.VMEM((nar, tok, wide), BF16),
            pltpu.VMEM((length, local), F32),
            pltpu.VMEM((length, local), F32),
            pltpu.VMEM((outer, body, piece), BF16),
            pltpu.VMEM((outer, body, piece), BF16),
            pltpu.VMEM((outer - 1, body, piece), BF16),
            pltpu.VMEM((outer - 1, body, piece), BF16),
            pltpu.VMEM((nar * local, piece), F32),
            pltpu.VMEM((second, first, local, piece), BF16),
            pltpu.VMEM((second, first, local, piece), BF16),
            pltpu.VMEM((5, line, piece), BF16),
            pltpu.VMEM((line, piece), F32),
            pltpu.VMEM((wid, 3 * local, piece), BF16),
            pltpu.VMEM((wid, 3 * local, piece), BF16),
            pltpu.VMEM((tok, width), BF16),
            pltpu.VMEM((8, width), F32),
            pltpu.VMEM((nar, 8, width), F32),
            pltpu.VMEM((wid, 8, piece), F32),
            pltpu.VMEM((wid, 8, piece), F32),
            dma((2,)),
            dma((first, second)),
            dma((first, second)),
            dma((nar,)),
            dma((nar,)),
            dma((nar,)),
            dma((nar,)),
            dma((outer,)),
            dma((outer,)),
            dma((outer, first + 1)),
            dma((outer, first + 1)),
            dma((second,)),
            dma((second,)),
            dma((first,)),
            dma((5,)),
            dma((wid,)),
            dma((wid,)),
            dma((first, 3, chunks)),
            dma((first, chunks)),
            dma((first, second, chunks)),
            dma((first, second, chunks)),
            dma((nar,)),
            dma((nar,)),
            dma((wid,)),
            dma((wid,)),
        ],
        compiler_params=pltpu.CompilerParams(
            collective_id=name, has_side_effects=True, vmem_limit_bytes=63 * 2**20
        ),
    )(seg, gain, sums, grads, lines, *late)


def neighbour_kernel(
    nar,
    first,
    tiles,
    tile,
    kept,
    ring,
    count_ref,
    target_ref,
    base_ref,
    weight_ref,
    temper_ref,
    mix_ref,
    query_ref,
    keys_ref,
    norms_any,
    ids_any,
    grad_ref,
    loss_ref,
    stat_ref,
    queries,
    partial,
    dist,
    grads,
    sends,
    slots,
    loss_own,
    norms_ref,
    ids_ref,
    load_sem,
    slot_sem,
    q_send,
    q_recv,
    d_send,
    d_recv,
    g_send,
    g_recv,
    l_send,
    l_recv,
    o_send,
    o_recv,
):
    second = nar // first
    me = lax.axis_index("z") * second + lax.axis_index("y")
    tok = query_ref.shape[1]
    depth = query_ref.shape[2]
    group = 16
    per_block = tok // tile
    late = tiles - kept

    def peer(k):
        return lax.rem(me + k, nar)

    def origin(k):
        return lax.rem(me + nar - k, nar)

    def load(index, slot):
        block, sub = index // per_block, lax.rem(index, per_block)
        row = origin(block) * tok + sub * tile
        return pltpu.make_async_copy(
            keys_ref.at[pl.ds(row, tile)], slots.at[slot], slot_sem.at[slot]
        )

    loads = [
        pltpu.make_async_copy(norms_any, norms_ref, load_sem.at[0]),
        pltpu.make_async_copy(query_ref.at[me], queries.at[0], load_sem.at[1]),
        pltpu.make_async_copy(ids_any.at[own_rows(tok, second)], ids_ref, load_sem.at[2]),
    ]
    for n in range(3):
        loads[n].start()
    for i in range(kept + ring):
        load(i, i).start()

    greet([place(peer(k), second) for k in range(1, nar)])

    def q_copy(k):
        return push(
            query_ref.at[peer(k)],
            queries.at[k],
            q_send.at[k],
            q_recv.at[k],
            place(peer(k), second),
        )

    def d_copy(k):
        return push(
            partial.at[k], dist.at[k], d_send.at[k], d_recv.at[k], place(origin(k), second)
        )

    def g_copy(k):
        return push(
            grads.at[0], grads.at[k], g_send.at[k], g_recv.at[k], place(peer(k), second)
        )

    def l_copy(k):
        return push(
            loss_own, loss_ref.at[me], l_send.at[k], l_recv.at[k], place(peer(k), second)
        )

    def o_copy(k):
        return push(
            sends.at[k], grad_ref.at[me], o_send.at[k], o_recv.at[k], place(origin(k), second)
        )

    for k in range(1, nar):
        q_copy(k).start()
    for n in range(3):
        loads[n].wait()

    row_of = lax.broadcasted_iota(jnp.int32, (group, J), 0)

    def slot_of(index):
        return jnp.where(index < kept, index, kept + lax.rem(index - kept, ring))

    def slot_late(n):
        return kept + lax.rem(n, ring)

    def forward_tile(k, sub, slot):
        def one(g, carry):
            at = pl.multiple_of(sub * tile + g * group, group)
            own = queries[k, pl.ds(at, group), :].astype(F32)
            keys = slots[slot, pl.ds(g * group, group), :, :].reshape(group * depth, J)
            wide = jnp.concatenate(
                [jnp.where(row_of[:, :depth] == t, own, 0.0) for t in range(group)], axis=1
            ).astype(BF16)
            out = jnp.dot(wide, keys, preferred_element_type=F32)
            row = pl.multiple_of(origin(k) * tok + at, group)
            partial[k, pl.ds(at, group), :] = 2.0 * out - norms_ref[pl.ds(row, group), :]
            return carry

        lax.fori_loop(0, tile // group, one, 0, unroll=True)

    def forward_block(k):
        def body(sub, carry):
            index = k * per_block + sub
            slot = slot_of(index)
            load(index, slot).wait()
            forward_tile(k, sub, slot)

            @pl.when(index >= kept)
            def _():
                nxt = index - kept + ring

                @pl.when(nxt < 2 * late)
                def _():
                    load(kept + lax.rem(nxt, late), slot).start()

            return carry

        lax.fori_loop(0, per_block, body, 0)

    forward_block(0)

    def forward_rest(k, carry):
        q_copy(k).wait_recv()
        forward_block(k)
        d_copy(k).start()
        return carry

    lax.fori_loop(1, nar, forward_rest, 0)

    def collect(k, total):
        d_copy(k).wait_recv()
        return total + dist[k]

    distance = lax.fori_loop(1, nar, collect, partial[0])
    temper_value = temper_ref[0]
    mix_value = mix_ref[0]
    per_seq = count_ref.shape[1] // tok

    def own_column(ref):
        row = jnp.zeros((1, tok), F32)
        for n in range(nar):
            at = (n % per_seq) * tok
            seq = n // per_seq
            row = jnp.where(me == n, ref[seq : seq + 1, at : at + tok].astype(F32), row)
        return jnp.transpose(jnp.broadcast_to(row, (8, tok)))[:, 0:1]

    count = own_column(count_ref)
    target = own_column(target_ref)
    base = own_column(base_ref)
    loss_weight = own_column(weight_ref)
    logits = distance / temper_value
    spot = lax.broadcasted_iota(jnp.int32, (tok, J), 1).astype(F32)
    masked = jnp.where(spot < count, logits, -1e30)
    peak = jnp.max(masked, axis=-1, keepdims=True)
    expo = jnp.exp(masked - peak)
    weights = expo / jnp.sum(expo, axis=-1, keepdims=True)
    matches = jnp.where(ids_ref[...].astype(F32) == target, 1.0, 0.0)
    knn_prob = jnp.sum(weights * matches, axis=-1, keepdims=True)
    mixture = mix_value * knn_prob + (1.0 - mix_value) * base
    grad_mixture = -loss_weight / mixture
    grad_logits = weights * (mix_value * grad_mixture) * (matches - knn_prob)
    grads[0] = (2.0 * grad_logits / temper_value).astype(BF16)
    for k in range(1, nar):
        g_copy(k).start()
    loss = jnp.transpose(jnp.broadcast_to(-jnp.log(mixture), (tok, J)))[0:8, :]
    loss_own[...] = loss
    for k in range(1, nar):
        l_copy(k).start()
    loss_ref[me] = loss
    term_temper = -jnp.sum(grad_logits * logits, axis=0, keepdims=True) / temper_value
    term_mix = jnp.sum((knn_prob - base) * grad_mixture, axis=0, keepdims=True)
    stat_ref[0:1, :] = term_temper
    stat_ref[1:2, :] = jnp.broadcast_to(term_mix, (1, J))

    def backward_tile(k, sub, slot):
        def one(g, carry):
            at = pl.multiple_of(sub * tile + g * group, group)
            own = grads[k, pl.ds(at, group), :]
            keys = slots[slot, pl.ds(g * group, group), :, :].reshape(group * depth, J)
            out = lax.dot_general(
                own, keys, (((1,), (1,)), ((), ())), preferred_element_type=F32
            )
            total = jnp.zeros((group, depth), F32)
            for t in range(group):
                total = jnp.where(
                    row_of[:, :depth] == t, out[:, t * depth : (t + 1) * depth], total
                )
            sends[k, pl.ds(at, group), :] = total.astype(BF16)
            return carry

        lax.fori_loop(0, tile // group, one, 0, unroll=True)

    def backward_block(k):
        def body(sub, carry):
            index = k * per_block + sub

            @pl.when(index < kept)
            def _():
                backward_tile(k, sub, index)

            @pl.when(index >= kept)
            def _():
                n = index - kept + late
                slot = slot_late(n)
                load(index, slot).wait()
                backward_tile(k, sub, slot)

                @pl.when(n + ring < 2 * late)
                def _():
                    load(kept + lax.rem(n + ring, late), slot).start()

            return carry

        lax.fori_loop(0, per_block, body, 0)

    backward_block(0)
    grad_ref[me] = sends[0]

    def backward_rest(k, carry):
        g_copy(k).wait_recv()
        backward_block(k)
        o_copy(k).start()
        return carry

    lax.fori_loop(1, nar, backward_rest, 0)

    for k in range(1, nar):
        q_copy(k).wait_send()
        d_copy(k).wait_send()
        g_copy(k).wait_send()
        l_copy(k).wait()
        o_copy(k).wait()


def neighbours(nar, first, columns, temper, mix, query, keys, norms, ids):
    tok, depth = query.shape[1:]
    rows = keys.shape[0]
    tile = 32
    tiles = rows // tile
    bytes_tile = tile * depth * J * 2
    ring = 4
    kept = min(tiles - 2 * ring, (KEPT_BYTES // bytes_tile))
    vmem = pl.BlockSpec(memory_space=pltpu.VMEM)
    dma = pltpu.SemaphoreType.DMA((nar,))
    return pl.pallas_call(
        functools.partial(neighbour_kernel, nar, first, tiles, tile, kept, ring),
        out_shape=(
            jax.ShapeDtypeStruct((nar, tok, depth), BF16),
            jax.ShapeDtypeStruct((nar, 8, tok), F32),
            jax.ShapeDtypeStruct((2, J), F32),
        ),
        in_specs=[vmem] * 4
        + [pl.BlockSpec(memory_space=pltpu.SMEM)] * 2
        + [pl.BlockSpec(memory_space=pl.ANY)] * 4,
        out_specs=(vmem, vmem, vmem),
        scratch_shapes=[
            pltpu.VMEM((nar, tok, depth), BF16),
            pltpu.VMEM((nar, tok, J), F32),
            pltpu.VMEM((nar, tok, J), F32),
            pltpu.VMEM((nar, tok, J), BF16),
            pltpu.VMEM((nar, tok, depth), BF16),
            pltpu.VMEM((kept + ring, tile, depth, J), BF16),
            pltpu.VMEM((8, tok), F32),
            pltpu.VMEM((rows, J), F32),
            pltpu.VMEM((tok, J), jnp.int32),
            pltpu.SemaphoreType.DMA((3,)),
            pltpu.SemaphoreType.DMA((kept + ring,)),
        ]
        + [dma] * 10,
        compiler_params=pltpu.CompilerParams(
            collective_id=1, has_side_effects=True, vmem_limit_bytes=62 * 2**20
        ),
    )(*columns, temper, mix, query, keys, norms, ids)


def on_device(
    block_input,
    output_cotangent,
    loss_weight,
    segments,
    nbr_keys,
    nbr_count,
    nbr_ids,
    targets,
    base_prob,
    w_query,
    w_key,
    w_value,
    w_proj,
    w_in,
    w_out,
    gain_attn,
    gain_ffn,
    gain_key,
    temper,
    mix_weight,
):
    seqs_here, length, width = block_input.shape
    rows = seqs_here * length
    wid = lax.axis_size("wide")
    first = lax.axis_size("z")
    nar = first * lax.axis_size("y")
    inputs = block_input.reshape(rows, width)
    keys = nbr_keys.reshape(rows, nbr_keys.shape[2], nbr_keys.shape[3])
    gain_one, gain_two, gain_last = (
        gain.reshape(1, width) for gain in (gain_attn, gain_ffn, gain_key)
    )
    normed_one, qkv, lse, part_norms, attended, in_all, out_all, pq_all = head(
        gain_one,
        segments,
        (w_proj, w_query, w_key, w_value),
        inputs,
        keys,
        w_in,
        w_out,
        first,
        nar,
        wid,
        2,
    )
    hidden_one, hidden_two, output_own, query_key, normed_two, pre_act = ffn(
        gain_two, gain_last, attended, inputs, pq_all, in_all, out_all, 3
    )
    grad_slices, losses, stats = neighbours(
        nar,
        first,
        (nbr_count, targets, base_prob, loss_weight),
        temper,
        mix_weight,
        query_key,
        keys,
        part_norms,
        nbr_ids.reshape(rows, -1),
    )
    sums, grad_hidden_one, grad_attended, *sides, lines = ffn_back(
        gain_two,
        gain_last,
        grad_slices,
        stats,
        hidden_two,
        output_cotangent.reshape(rows, width),
        out_all,
        pre_act,
        in_all,
        attended,
        normed_two,
        hidden_one,
        pq_all,
        output_own,
        wid,
        5,
    )
    grad_input, block_output, totals, grad_in, grad_out, grad_proj, grad_qkv = attention_grads(
        segments,
        gain_one,
        sums,
        grad_attended,
        lines,
        sides,
        qkv,
        lse,
        normed_one,
        inputs,
        grad_hidden_one,
        pq_all,
        first,
        wid,
        6,
    )
    results = finish(
        grad_input,
        block_output,
        lines,
        totals,
        losses,
        grad_qkv,
        grad_proj,
        grad_in,
        grad_out,
        seqs_here,
    )
    block_output, token_loss, grad_input, *weights, total_one, total_two, total_last = results[:12]
    piece = width // wid
    return (
        block_output.reshape(seqs_here, length, width),
        token_loss,
        grad_input.reshape(seqs_here, length, width),
        *weights,
        total_one.reshape(piece),
        total_two.reshape(piece),
        total_last.reshape(piece),
        results[12].reshape(1),
        results[13].reshape(1),
    )


def solution(mesh):
    wide, narrow = mesh.devices.shape
    first = 4
    split = jax.sharding.Mesh(
        mesh.devices.reshape(wide, first, narrow // first), ("wide", "z", "y")
    )
    narrow = ("z", "y")
    return jax.shard_map(
        on_device,
        mesh=split,
        in_specs=(
            P("wide", None, None),
            P("wide", None, None),
            P("wide", None),
            P("wide", None),
            P("wide", None, narrow, None),
            P("wide", None),
            P("wide", None, None),
            P("wide", None),
            P("wide", None),
            P(narrow, None),
            P(narrow, None),
            P(narrow, None),
            P(narrow, None),
            P(None, narrow),
            P(narrow, None),
            P(),
            P(),
            P(),
            P(),
            P(),
        ),
        out_specs=(
            P("wide", None, None),
            P("wide", None),
            P("wide", None, None),
            P(narrow, "wide"),
            P(narrow, "wide"),
            P(narrow, "wide"),
            P(narrow, "wide"),
            P("wide", narrow),
            P(narrow, "wide"),
            P("wide"),
            P("wide"),
            P("wide"),
            P(),
            P(),
        ),
        check_vma=False,
    )
```

```python
import functools

import jax
import jax.numpy as jnp
from jax import lax
from jax.experimental import pallas as pl
from jax.experimental.pallas import tpu as pltpu
from jax.sharding import PartitionSpec as P

HD = 64
EPSILON = 1e-05
F32 = jnp.float32
BF16 = jnp.bfloat16
MESH = pl.DeviceIdType.MESH
J = 128
KEPT_BYTES = 44 * 2**20


def place(index, second):
    return {"z": index // second, "y": lax.rem(index, second)}


def push(src, dst, send, recv, target):
    return pltpu.make_async_remote_copy(
        src_ref=src,
        dst_ref=dst,
        send_sem=send,
        recv_sem=recv,
        device_id=target,
        device_id_type=MESH,
    )


def greet(peers):
    barrier = pltpu.get_barrier_semaphore()
    for peer in peers:
        pl.semaphore_signal(barrier, inc=1, device_id=peer, device_id_type=MESH)
    pl.semaphore_wait(barrier, len(peers))


def normalise(values):
    centred = values - jnp.mean(values, axis=-1, keepdims=True)
    inverse = lax.rsqrt(jnp.mean(centred * centred, axis=-1, keepdims=True) + EPSILON)
    return centred * inverse, inverse


def normalise_back(grad_out, normed, inverse, gain):
    scaled = grad_out * gain
    return inverse * (
        scaled
        - jnp.mean(scaled, axis=-1, keepdims=True)
        - normed * jnp.mean(scaled * normed, axis=-1, keepdims=True)
    )


def head_lanes(values, head):
    lanes = lax.broadcasted_iota(jnp.int32, values.shape, 1)
    return jnp.where(lanes // HD == head, values, jnp.zeros_like(values))


def head_kernel(
    nar,
    first,
    wid,
    seqs,
    heads,
    block,
    tile,
    ring,
    gain_ref,
    seg_ref,
    proj_any,
    query_any,
    key_any,
    value_any,
    input_any,
    keys_ref,
    in_any,
    out_any,
    normed_out,
    qkv_out,
    lse_out,
    norms_out,
    att_ref,
    in_all,
    out_all,
    pq_all,
    pq_ref,
    in_ref,
    out_ref,
    input_ref,
    normed_ref,
    qkv_ref,
    lse_ref,
    norms_ref,
    attended,
    slots,
    load_sem,
    store_sem,
    slot_sem,
    own_sem,
    a_send,
    a_recv,
    z_send,
    z_recv,
    y_send,
    y_recv,
    x_send,
    x_recv,
    c_send,
    c_recv,
):
    second = nar // first
    outer = wid // 2
    za, yb = lax.axis_index("z"), lax.axis_index("y")
    me = za * second + yb
    wide = lax.axis_index("wide")
    chip, core = wide // 2, lax.rem(wide, 2)
    rows, width = input_ref.shape
    tok = rows // nar
    length = rows // seqs
    local = heads * HD
    tiles = rows // tile
    last = (((1,), (1,)), ((), ()))

    def fetch(index, slot):
        return pltpu.make_async_copy(
            keys_ref.at[pl.ds(index * tile, tile)], slots.at[slot], slot_sem.at[slot]
        )

    loads = [
        pltpu.make_async_copy(src, pq_ref.at[pl.ds(n * local, local)], load_sem.at[n])
        for n, src in enumerate((proj_any, query_any, key_any, value_any))
    ] + [
        pltpu.make_async_copy(src, dst, load_sem.at[4 + n])
        for n, (src, dst) in enumerate(
            ((in_any, in_ref), (out_any, out_ref), (input_any, input_ref))
        )
    ]
    for load in loads:
        load.start()
    stores = [
        pltpu.make_async_copy(src, dst, store_sem.at[n])
        for n, (src, dst) in enumerate(
            (
                (normed_ref, normed_out),
                (qkv_ref, qkv_out),
                (lse_ref, lse_out),
                (norms_ref, norms_out),
            )
        )
    ]

    greet(
        [place(lax.rem(me + k, nar), second) for k in range(1, nar)]
        + [{"wide": chip * 2 + (1 - core)}]
        + [{"wide": lax.rem(chip + o, outer) * 2 + core} for o in range(1, outer)]
    )

    stacks = ((pq_ref, pq_all), (in_ref, in_all), (out_ref, out_all))

    def shard_of(t, source):
        return source if t == 0 else source // second

    def quarter(t, source, owner):
        own, stack = stacks[t]
        count = own.shape[0] // wid
        at = pl.ds(pl.multiple_of(owner * count, count), count)
        return stack.at[shard_of(t, source), at]

    def own_quarter(t):
        own, _ = stacks[t]
        count = own.shape[0] // wid
        return own.at[pl.ds(pl.multiple_of(wide * count, count), count)]

    reach, relay = REACH, RELAY

    def line_copy(t, source, z, slot, own):
        return push(
            own_quarter(t) if own else quarter(t, source, wide),
            quarter(t, source, wide),
            z_send.at[t, source // second, slot],
            z_recv.at[t, source // second],
            {"z": z, "y": yb},
        )

    def owner_of(o):
        return lax.rem(chip + outer - o, outer) * 2 + core

    def row_copy(source, j, o, own):
        owner = owner_of(o)
        count = pq_ref.shape[0] // wid
        at = pl.ds(pl.multiple_of(owner * count, count), count)
        return push(
            pq_ref.at[at] if own else quarter(0, source, owner),
            quarter(0, source, owner),
            y_send.at[source, j, o],
            y_recv.at[source, j, o],
            {"z": za, "y": lax.rem(yb + j, second)},
        )

    def chip_copy(t, source, o):
        return push(
            quarter(t, source, wide),
            quarter(t, source, wide),
            x_send.at[t, source, o],
            x_recv.at[t, source, o],
            {"wide": lax.rem(chip + o, outer) * 2 + core},
        )

    def chip_arrival(t, source, o):
        owner = owner_of(o)
        return push(
            quarter(t, source, owner),
            quarter(t, source, owner),
            x_send.at[t, source, o],
            x_recv.at[t, source, o],
            {"wide": owner},
        )

    def core_copy(t, source, o, away):
        owner = lax.rem(chip + outer - o, outer) * 2 + jnp.where(away, 1 - core, core)
        return push(
            quarter(t, source, owner),
            quarter(t, source, owner),
            c_send.at[t, source, o],
            c_recv.at[t, source, o],
            {"wide": chip * 2 + (1 - core)},
        )

    def att_copy(target, source):
        return push(
            attended.at[target],
            att_ref.at[source],
            a_send.at[target],
            a_recv.at[source],
            place(target, second),
        )

    own_copies = [
        pltpu.make_async_copy(own, stack.at[shard_of(t, me)], own_sem.at[t])
        for t, (own, stack) in enumerate(stacks)
    ]

    def send_own(t):
        for z in range(first):

            @pl.when(za == z)
            def _(z=z):
                for slot, target in enumerate(reach[z]):
                    line_copy(t, me, target, slot, True).start()

        if t == 0:
            for j in range(1, second):
                for o in range(outer):
                    row_copy(me, j, o, True).start()
        own_copies[t].start()

    def line_arrivals(t, begin, end):
        for d in range(begin, end):
            for way in (-1, 1):
                z = za + way * d

                @pl.when((z >= 0) & (z < first))
                def _(z=z):
                    source = z * second + yb
                    line_copy(t, source, za, 0, False).wait_recv()
                    for middle, (target, sources) in relay.items():

                        @pl.when((za == middle) & ((z == sources[0]) | (z == sources[1])))
                        def _(target=target):
                            line_copy(t, source, target, 0, False).start()

                    for o in range(1, outer):
                        chip_copy(t, source, o).start()
                    core_copy(t, source, 0, False).start()

    def chip_arrivals(t, begin, end):
        for d in range(begin, end):
            for way in (-1, 1):
                z = za + way * d

                @pl.when((z >= 0) & (z < first))
                def _(z=z):
                    source = z * second + yb
                    for o in range(1, outer):
                        chip_arrival(t, source, o).wait_recv()
                        core_copy(t, source, o, False).start()
                    if t == 0:
                        for j in range(1, second):
                            for o in range(outer):
                                row_copy(source, j, o, False).start()

    def row_arrivals():
        for j in range(1, second):
            for z in range(first):
                source = z * second + lax.rem(yb + second - j, second)
                for o in range(outer):
                    row_copy(source, j, o, False).wait_recv()
                    core_copy(0, source, o, False).start()

    def each_source(t, do):
        for n in range(nar if t == 0 else first):
            source = n if t == 0 else n * second + yb

            @pl.when(source != me)
            def _(source=source):
                do(source)

    def core_arrivals(t):
        def do(source):
            for o in range(outer):
                core_copy(t, source, o, True).wait_recv()

        each_source(t, do)

    for n in range(6):
        loads[n].wait()
    for t in range(3):
        send_own(t)
    for i in range(ring):
        fetch(i, i).start()
    loads[6].wait()

    def project(r, carry):
        at = pl.ds(pl.multiple_of(r * block, block), block)
        normed, _ = normalise(input_ref[at, :].astype(F32))
        low = (normed * gain_ref[0:1, :]).astype(BF16)
        normed_ref[at, :] = low
        out = lax.dot_general(low, pq_ref[local:, :], last, preferred_element_type=F32)
        lanes = lax.broadcasted_iota(jnp.int32, out.shape, 1)
        qkv_ref[at, :] = jnp.where(lanes < local, out * HD ** (-0.5), out).astype(BF16)
        return carry

    lax.fori_loop(0, rows // block, project, 0)
    stores[0].start()
    stores[1].start()
    line_arrivals(0, 1, 2)
    middle = (za == 1) | (za == 2)
    at_end = jnp.logical_not(middle)

    @pl.when(middle)
    def _():
        line_arrivals(0, 2, first)

    def sequence(seq, carry):
        base = seq * length
        for start in range(0, length, block):
            keys = start + block
            at = pl.ds(pl.multiple_of(base + start, block), block)
            whole = pl.ds(pl.multiple_of(base, length), keys)
            query_segment = segment_column(seg_ref, seq, start, block)
            key_segment = seg_ref[pl.ds(seq, 1), 0:keys].astype(F32)
            spot = lax.broadcasted_iota(jnp.int32, (block, keys), 1)
            own = lax.broadcasted_iota(jnp.int32, (block, keys), 0) + start
            allowed = (spot <= own) & (query_segment == key_segment)
            query = qkv_ref[at, 0:local]
            key = qkv_ref[whole, local : 2 * local]
            value = qkv_ref[whole, 2 * local : 3 * local]
            total = jnp.zeros((block, local), F32)
            for head in range(heads):
                scores = lax.dot_general(
                    head_lanes(query, head), key, last, preferred_element_type=F32
                )
                scores = jnp.where(allowed, scores, -1e30)
                peak = jnp.max(scores, axis=-1, keepdims=True)
                expo = jnp.exp(scores - peak)
                sums = jnp.sum(expo, axis=-1, keepdims=True)
                out = jnp.dot(expo.astype(BF16), value, preferred_element_type=F32) / sums
                total = total + head_lanes(out, head)
                lse_ref[at, head : head + 1] = peak + jnp.log(sums)
            each = min(tok, block)
            for r in range(0, block, each):
                target = seq * (nar // seqs) + (start + r) // tok
                spot_row = (start + r) % tok
                attended[target, spot_row : spot_row + each, :] = total[r : r + each, :].astype(
                    BF16
                )

        def leave(b, c):
            target = seq * (nar // seqs) + b

            @pl.when(target != me)
            def _():
                att_copy(target, me).start()

            return c

        lax.fori_loop(0, nar // seqs, leave, 0)
        return carry

    lax.fori_loop(0, seqs, sequence, 0)
    stores[2].start()
    own_att = pltpu.make_async_copy(attended.at[me], att_ref.at[me], own_sem.at[3])
    own_att.start()

    def norms(begin, end):
        def body(index, carry):
            slot = lax.rem(index, ring)
            fetch(index, slot).wait()
            keys = slots[slot].astype(F32)
            at = pl.ds(pl.multiple_of(index * tile, tile), tile)
            norms_ref[at, :] = jnp.sum(keys * keys, axis=1)

            @pl.when(index + ring < tiles)
            def _():
                fetch(index + ring, slot).start()

            return carry

        lax.fori_loop(begin, end, body, 0)

    @pl.when(at_end)
    def _():
        line_arrivals(1, 1, 2)
        line_arrivals(2, 1, 2)
        chip_arrivals(0, 1, 2)
        line_arrivals(0, 2, first)

    @pl.when(middle)
    def _():
        line_arrivals(1, 1, first)
        chip_arrivals(0, 1, first)

    norms(0, tiles // 3)

    @pl.when(at_end)
    def _():
        chip_arrivals(0, 2, first)
        line_arrivals(1, 2, first)

    @pl.when(middle)
    def _():
        line_arrivals(2, 1, first)

    norms(tiles // 3, 2 * tiles // 3)

    @pl.when(at_end)
    def _():
        line_arrivals(2, 2, first)

    norms(2 * tiles // 3, tiles)
    stores[3].start()
    row_arrivals()
    chip_arrivals(1, 1, first)
    chip_arrivals(2, 1, first)
    for t in range(3):
        core_arrivals(t)
    for k in range(1, nar):
        source = lax.rem(me + k, nar)
        att_copy(source, source).wait_recv()
        att_copy(source, me).wait_send()
    for t in range(3):
        own_copies[t].wait()

        def sent(source, t=t):
            for o in range(outer):
                core_copy(t, source, o, False).wait_send()

        each_source(t, sent)
        for n in range(first):
            source = n * second + yb

            @pl.when(source != me)
            def _(source=source, t=t):
                for o in range(1, outer):
                    chip_copy(t, source, o).wait_send()

        for z in range(first):

            @pl.when(za == z)
            def _(z=z, t=t):
                for slot, target in enumerate(reach[z]):
                    line_copy(t, me, target, slot, True).wait_send()
                if z in relay:
                    target, sources = relay[z]
                    for n in sources:
                        line_copy(t, n * second + yb, target, 0, False).wait_send()

    for z in range(first):
        for j in range(1, second):
            for o in range(outer):
                row_copy(z * second + yb, j, o, False).wait_send()
    own_att.wait()
    for store in stores:
        store.wait()


def head(gain, seg, weights, block_input, keys, w_in, w_out, first, nar, wid, name):
    rows, width = block_input.shape
    seqs, length = seg.shape
    second = nar // first
    outer = wid // 2
    local = weights[0].shape[0]
    heads = local // HD
    hidden = w_in.shape[1]
    tok = rows // nar
    depth = keys.shape[1]
    tile, ring = 32, 4
    block = min(256, length)
    vmem = pl.BlockSpec(memory_space=pltpu.VMEM)
    hbm = pl.BlockSpec(memory_space=pl.ANY)
    dma = pltpu.SemaphoreType.DMA
    kept = (
        ((rows, width), BF16),
        ((rows, 3 * local), BF16),
        ((rows, heads), F32),
        ((rows, J), F32),
    )
    return pl.pallas_call(
        functools.partial(head_kernel, nar, first, wid, seqs, heads, block, tile, ring),
        out_shape=tuple(jax.ShapeDtypeStruct(*x) for x in kept)
        + (
            jax.ShapeDtypeStruct((nar, tok, local), BF16),
            jax.ShapeDtypeStruct((first, width, hidden), BF16),
            jax.ShapeDtypeStruct((first, hidden, width), BF16),
            jax.ShapeDtypeStruct((nar, 4 * local, width), BF16),
        ),
        in_specs=[vmem] * 2 + [hbm] * 8,
        out_specs=(hbm,) * 8,
        scratch_shapes=[
            pltpu.VMEM((4 * local, width), BF16),
            pltpu.VMEM((width, hidden), BF16),
            pltpu.VMEM((hidden, width), BF16),
            pltpu.VMEM((rows, width), BF16),
        ]
        + [pltpu.VMEM(*x) for x in kept]
        + [
            pltpu.VMEM((nar, tok, local), BF16),
            pltpu.VMEM((ring, tile, depth, J), BF16),
            dma((7,)),
            dma((4,)),
            dma((ring,)),
            dma((4,)),
            dma((nar,)),
            dma((nar,)),
            dma((3, first, 3)),
            dma((3, first)),
            dma((nar, second, outer)),
            dma((nar, second, outer)),
            dma((3, nar, outer)),
            dma((3, nar, outer)),
            dma((3, nar, outer)),
            dma((3, nar, outer)),
        ],
        compiler_params=pltpu.CompilerParams(
            collective_id=name, has_side_effects=True, vmem_limit_bytes=62 * 2**20
        ),
    )(gain, seg, *weights, block_input, keys, w_in, w_out)


INNER = 0.7978845608028654
CUBIC = 0.044715


def gelu_parts(values):
    tanh = jnp.tanh(INNER * (values + CUBIC * values * values * values))
    return 0.5 * values * (1.0 + tanh), tanh


def own_rows(tok, second):
    me = lax.axis_index("z") * second + lax.axis_index("y")
    return pl.ds(pl.multiple_of(me * tok, tok), tok)


def ffn_kernel(
    chunks,
    gain_two_ref,
    gain_key_ref,
    att_any,
    input_any,
    pq_any,
    in_any,
    mid_any,
    one_out,
    two_out,
    output_out,
    key_out,
    normed_out,
    pre_out,
    att_ref,
    input_ref,
    proj_ref,
    in_ref,
    mid_ref,
    one_ref,
    two_ref,
    output_ref,
    key_ref,
    normed_ref,
    pre_ref,
    back_out,
    back_in,
    load_sem,
    store_sem,
    n_send,
    n_recv,
    b_send,
    b_recv,
):
    nar, tok, local = att_ref.shape
    first, width, hidden = in_ref.shape
    second = nar // first
    part = tok // chunks
    za, yb = lax.axis_index("z"), lax.axis_index("y")

    pairs = (
        (att_any, att_ref),
        (pq_any.at[:, pl.ds(0, local)], proj_ref),
        (input_any.at[own_rows(tok, second)], input_ref),
        (in_any, in_ref),
        (mid_any, mid_ref),
    )
    loads = [
        pltpu.make_async_copy(src, dst, load_sem.at[n]) for n, (src, dst) in enumerate(pairs)
    ]
    for load in loads:
        load.start()
    kept = (
        (one_ref, one_out),
        (normed_ref, normed_out),
        (pre_ref, pre_out),
        (key_ref, key_out),
        (two_ref, two_out),
        (output_ref, output_out),
    )
    stores = [
        pltpu.make_async_copy(src, dst, store_sem.at[n]) for n, (src, dst) in enumerate(kept)
    ]

    greet([{"z": za, "y": lax.rem(yb + j, second)} for j in range(1, second)])

    def n_copy(j, c):
        at = pl.ds(c * part, part)
        target = {"z": za, "y": lax.rem(yb + j, second)}
        return push(
            normed_ref.at[0, at], normed_ref.at[j, at], n_send.at[j, c], n_recv.at[j, c], target
        )

    def b_copy(j, c):
        at = pl.ds(c * part, part)
        target = {"z": za, "y": lax.rem(yb + second - j, second)}
        return push(
            back_out.at[j, at], back_in.at[j, at], b_send.at[j, c], b_recv.at[j, c], target
        )

    def through(j, start, count):
        total = jnp.zeros((count, width), F32)
        for z in range(first):
            pre = jnp.dot(
                normed_ref[j, start : start + count, :], in_ref[z], preferred_element_type=F32
            )
            pre_ref[j, start : start + count, z * hidden : (z + 1) * hidden] = pre
            activated = gelu_parts(pre)[0].astype(BF16)
            total = total + jnp.dot(activated, mid_ref[z], preferred_element_type=F32)
        return total

    for n in range(3):
        loads[n].wait()
    att = jnp.concatenate([att_ref[n] for n in range(nar)], axis=1)
    one = input_ref[...].astype(F32) + jnp.dot(
        att, proj_ref[...].reshape(nar * local, width), preferred_element_type=F32
    )
    one_ref[...] = one
    normed, _ = normalise(one)
    normed_ref[0] = (normed * gain_two_ref[...]).astype(BF16)
    for c in range(chunks):
        for j in range(1, second):
            n_copy(j, c).start()
    stores[0].start()
    for n in range(3, 5):
        loads[n].wait()
    two_ref[...] = one_ref[...] + through(0, 0, tok)
    for c in range(chunks):
        for j in range(1, second):
            n_copy(j, c).wait_recv()
            back_out[j, c * part : (c + 1) * part, :] = through(j, c * part, part).astype(BF16)
            b_copy(j, c).start()
    stores[1].start()
    stores[2].start()
    for c in range(chunks):
        at = slice(c * part, (c + 1) * part)
        for j in range(1, second):
            b_copy(j, c).wait_recv()
            two_ref[at, :] += back_in[j, at, :].astype(F32)
    hidden_two = two_ref[...]
    normed, _ = normalise(hidden_two)
    query_key = (normed * gain_key_ref[...]).astype(BF16)
    for n in range(nar):
        key_ref[n] = query_key[:, n * (width // nar) : (n + 1) * (width // nar)]
    stores[3].start()
    stores[4].start()
    output_ref[...] = hidden_two.astype(BF16)
    stores[5].start()
    for c in range(chunks):
        for j in range(1, second):
            n_copy(j, c).wait_send()
            b_copy(j, c).wait_send()
    for store in stores:
        store.wait()


def ffn(gain_two, gain_key, att, inputs, pq, in_all, out_all, name):
    nar, tok, local = att.shape
    first, width, hidden = in_all.shape
    second = nar // first
    chunks = 2
    vmem = pl.BlockSpec(memory_space=pltpu.VMEM)
    hbm = pl.BlockSpec(memory_space=pl.ANY)
    dma = pltpu.SemaphoreType.DMA
    outs = (
        ((tok, width), F32),
        ((tok, width), F32),
        ((tok, width), BF16),
        ((nar, tok, width // nar), BF16),
        ((second, tok, width), BF16),
        ((second, tok, first * hidden), F32),
    )
    return pl.pallas_call(
        functools.partial(ffn_kernel, chunks),
        out_shape=tuple(jax.ShapeDtypeStruct(*x) for x in outs),
        in_specs=[vmem] * 2 + [hbm] * 5,
        out_specs=(hbm,) * 6,
        scratch_shapes=[
            pltpu.VMEM(att.shape, BF16),
            pltpu.VMEM((tok, width), BF16),
            pltpu.VMEM((nar, local, width), BF16),
            pltpu.VMEM(in_all.shape, BF16),
            pltpu.VMEM(out_all.shape, BF16),
        ]
        + [pltpu.VMEM(*x) for x in outs]
        + [pltpu.VMEM((second, tok, width), BF16)] * 2
        + [dma((5,)), dma((6,))]
        + [dma((second, chunks))] * 4,
        compiler_params=pltpu.CompilerParams(
            collective_id=name, has_side_effects=True, vmem_limit_bytes=62 * 2**20
        ),
    )(gain_two, gain_key, att, inputs, pq, in_all, out_all)


def ffn_back_kernel(
    chunks,
    gain_two_ref,
    gain_key_ref,
    slices_ref,
    stat_ref,
    two_any,
    cot_any,
    mid_any,
    pre_any,
    in_any,
    att_any,
    normed_any,
    one_any,
    pq_any,
    share_any,
    sums_ref,
    grad_one_out,
    grad_att_out,
    pre_turned_out,
    act_turned_out,
    att_turned_out,
    normed_cols_out,
    ffn_cols_out,
    branch_cols_out,
    line_ref,
    two_ref,
    cot_ref,
    mid_ref,
    pre_ref,
    in_ref,
    att_ref,
    normed_ref,
    one_ref,
    proj_ref,
    share_ref,
    grad_one_ref,
    grad_att_ref,
    pre_turned_ref,
    act_turned_ref,
    att_turned_ref,
    normed_cols_ref,
    ffn_cols_ref,
    branch_cols_ref,
    grads,
    grad_two,
    total,
    back_out,
    back_in,
    load_sem,
    store_sem,
    own_sem,
    n_send,
    n_recv,
    b_send,
    b_recv,
    g_send,
    g_recv,
):
    nar, tok, local = att_ref.shape
    first, width, hidden = in_ref.shape
    second = nar // first
    wid = branch_cols_ref.shape[0]
    columns = width // wid
    part = tok // chunks
    last = (((1,), (1,)), ((), ()))
    za, yb = lax.axis_index("z"), lax.axis_index("y")
    reach, relay = REACH, RELAY

    pairs = (
        (share_any, share_ref),
        (two_any, two_ref),
        (cot_any.at[own_rows(tok, second)], cot_ref),
        (mid_any, mid_ref),
        (pre_any, pre_ref),
        (in_any, in_ref),
        (att_any, att_ref),
        (normed_any, normed_ref),
        (one_any, one_ref),
        (pq_any.at[:, pl.ds(0, local)], proj_ref),
    )
    loads = [
        pltpu.make_async_copy(src, dst, load_sem.at[n]) for n, (src, dst) in enumerate(pairs)
    ]
    for load in loads:
        load.start()
    kept = (
        (ffn_cols_ref, ffn_cols_out),
        (pre_turned_ref, pre_turned_out),
        (act_turned_ref, act_turned_out),
        (att_turned_ref, att_turned_out),
        (normed_cols_ref, normed_cols_out),
        (grad_att_ref, grad_att_out),
        (branch_cols_ref, branch_cols_out),
        (grad_one_ref, grad_one_out),
    )
    stores = [
        pltpu.make_async_copy(src, dst, store_sem.at[n]) for n, (src, dst) in enumerate(kept)
    ]

    greet(
        [{"z": za, "y": lax.rem(yb + j, second)} for j in range(1, second)]
        + [{"z": lax.rem(za + i, first), "y": yb} for i in range(1, first)]
    )

    def n_copy(j, c):
        at = pl.ds(c * part, part)
        target = {"z": za, "y": lax.rem(yb + j, second)}
        return push(grads.at[0, at], grads.at[j, at], n_send.at[j, c], n_recv.at[j, c], target)

    def b_copy(j, c):
        at = pl.ds(c * part, part)
        target = {"z": za, "y": lax.rem(yb + second - j, second)}
        return push(
            back_out.at[j, at], back_in.at[j, at], b_send.at[j, c], b_recv.at[j, c], target
        )

    def g_copy(source, target, slot, c, own):
        at = pl.ds(c * part, part)
        return push(
            share_ref.at[at] if own else line_ref.at[source, at],
            line_ref.at[source, at],
            g_send.at[source, slot, c],
            g_recv.at[source, c],
            {"z": target, "y": yb},
        )

    def gathered(c, begin, end):
        for d in range(begin, end):
            for way in (-1, 1):
                z = za + way * d

                @pl.when((z >= 0) & (z < first))
                def _(z=z):
                    g_copy(z, za, 0, c, False).wait_recv()
                    for middle, (target, sources) in relay.items():

                        @pl.when((za == middle) & ((z == sources[0]) | (z == sources[1])))
                        def _(target=target):
                            g_copy(z, target, 0, c, False).start()

    loads[0].wait()
    for c in range(chunks):
        for z in range(first):

            @pl.when(za == z)
            def _(z=z, c=c):
                for slot, target in enumerate(reach[z]):
                    g_copy(za, target, slot, c, True).start()

    own_copy = pltpu.make_async_copy(share_ref, line_ref.at[za], own_sem)
    own_copy.start()

    def through(j, start, count):
        at = slice(start, start + count)
        sums = jnp.zeros((count, width), F32)
        for z in range(first):
            own = slice(z * hidden, (z + 1) * hidden)
            pre = pre_ref[j, at, own]
            activated, tanh = gelu_parts(pre)
            slope = 0.5 * (1.0 + tanh) + 0.5 * pre * (1.0 - tanh * tanh) * INNER * (
                1.0 + 3.0 * CUBIC * pre * pre
            )
            grad_act = lax.dot_general(
                grads[j, at, :], mid_ref[z], last, preferred_element_type=F32
            )
            grad_pre = slope * grad_act
            to = slice(j * tok + start, j * tok + start + count)
            act_turned_ref[own, to] = jnp.transpose(activated).astype(BF16)
            pre_turned_ref[own, to] = jnp.transpose(grad_pre).astype(BF16)
            sums = sums + lax.dot_general(
                grad_pre.astype(BF16), in_ref[z], last, preferred_element_type=F32
            )
        return sums

    for n in range(1, 3):
        loads[n].wait()
    grad_key = jnp.concatenate([slices_ref[n] for n in range(nar)], axis=1).astype(F32)
    normed, inverse = normalise(two_ref[...])
    sums_ref[...] = jnp.zeros_like(sums_ref)
    sums_ref[2:3, :] = jnp.sum(grad_key * normed, axis=0, keepdims=True)
    temper_sum = jnp.sum(stat_ref[0:1, :], axis=1, keepdims=True)
    sums_ref[3:4, :] = jnp.broadcast_to(temper_sum, (1, width))
    sums_ref[4:5, :] = jnp.broadcast_to(stat_ref[1:2, 0:1], (1, width))
    grad = cot_ref[...].astype(F32) + normalise_back(
        grad_key, normed, inverse, gain_key_ref[...]
    )
    grad_two[...] = grad
    grads[0] = grad.astype(BF16)
    for c in range(chunks):
        for j in range(1, second):
            n_copy(j, c).start()
    for n in range(3, 6):
        loads[n].wait()
    total[...] = through(0, 0, tok)
    gathered(0, 1, 2)
    for c in range(chunks):
        for j in range(1, second):
            n_copy(j, c).wait_recv()
            back_out[j, c * part : (c + 1) * part, :] = through(j, c * part, part).astype(BF16)
            b_copy(j, c).start()
    gathered(0, 2, first)
    gathered(1, 1, first)
    for n in range(6, 10):
        loads[n].wait()
    for j in range(second):
        for w in range(wid):
            own = slice(w * columns, (w + 1) * columns)
            normed_cols_ref[w, j * tok : (j + 1) * tok, :] = normed_ref[j, :, own]
            ffn_cols_ref[w, j * tok : (j + 1) * tok, :] = grads[j, :, own]
    att_turned_ref[...] = jnp.concatenate(
        [jnp.transpose(att_ref[n].astype(F32)).astype(BF16) for n in range(nar)], axis=0
    )
    for n in range(5):
        stores[n].start()
    for c in range(chunks):
        at = slice(c * part, (c + 1) * part)
        for j in range(1, second):
            b_copy(j, c).wait_recv()
            total[at, :] += back_in[j, at, :].astype(F32)
    normed, inverse = normalise(one_ref[...])
    sums_ref[1:2, :] = jnp.sum(total[...] * normed, axis=0, keepdims=True)
    grad = grad_two[...] + normalise_back(total[...], normed, inverse, gain_two_ref[...])
    branch = grad.astype(BF16)
    grad_att = lax.dot_general(
        branch, proj_ref[...].reshape(nar * local, width), last, preferred_element_type=F32
    ).astype(BF16)
    for n in range(nar):
        grad_att_ref[n] = grad_att[:, n * local : (n + 1) * local]
    stores[5].start()
    for w in range(wid):
        branch_cols_ref[w] = branch[:, w * columns : (w + 1) * columns]
    stores[6].start()
    grad_one_ref[...] = grad
    stores[7].start()
    own_copy.wait()
    for c in range(chunks):
        for j in range(1, second):
            n_copy(j, c).wait_send()
            b_copy(j, c).wait_send()
        for z in range(first):

            @pl.when(za == z)
            def _(z=z, c=c):
                for slot, target in enumerate(reach[z]):
                    g_copy(za, target, slot, c, True).wait_send()
                if z in relay:
                    target, sources = relay[z]
                    for n in sources:
                        g_copy(n, target, 0, c, False).wait_send()

    for store in stores:
        store.wait()


def ffn_back(
    gain_two,
    gain_key,
    slices,
    stats,
    two,
    cot,
    out_all,
    pre,
    in_all,
    att,
    normed,
    one,
    pq,
    share,
    wid,
    name,
):
    nar, tok, local = att.shape
    first, width, hidden = in_all.shape
    second = nar // first
    chunks = 2
    columns = width // wid
    vmem = pl.BlockSpec(memory_space=pltpu.VMEM)
    hbm = pl.BlockSpec(memory_space=pl.ANY)
    dma = pltpu.SemaphoreType.DMA
    outs = (
        ((tok, width), F32),
        ((nar, tok, local), BF16),
        ((first * hidden, second * tok), BF16),
        ((first * hidden, second * tok), BF16),
        ((nar * local, tok), BF16),
        ((wid, second * tok, columns), BF16),
        ((wid, second * tok, columns), BF16),
        ((wid, tok, columns), BF16),
    )
    return pl.pallas_call(
        functools.partial(ffn_back_kernel, chunks),
        out_shape=(jax.ShapeDtypeStruct((8, width), F32),)
        + tuple(jax.ShapeDtypeStruct(*x) for x in outs)
        + (jax.ShapeDtypeStruct((first, tok, width), BF16),),
        in_specs=[vmem] * 4 + [hbm] * 10,
        out_specs=(vmem,) + (hbm,) * 9,
        scratch_shapes=[
            pltpu.VMEM((tok, width), F32),
            pltpu.VMEM((tok, width), BF16),
            pltpu.VMEM(out_all.shape, BF16),
            pltpu.VMEM(pre.shape, F32),
            pltpu.VMEM(in_all.shape, BF16),
            pltpu.VMEM(att.shape, BF16),
            pltpu.VMEM(normed.shape, BF16),
            pltpu.VMEM((tok, width), F32),
            pltpu.VMEM((nar, local, width), BF16),
            pltpu.VMEM((tok, width), BF16),
        ]
        + [pltpu.VMEM(*x) for x in outs]
        + [
            pltpu.VMEM((second, tok, width), BF16),
            pltpu.VMEM((tok, width), F32),
            pltpu.VMEM((tok, width), F32),
            pltpu.VMEM((second, tok, width), BF16),
            pltpu.VMEM((second, tok, width), BF16),
            dma((10,)),
            dma((8,)),
            dma,
        ]
        + [dma((second, chunks))] * 4
        + [dma((first, 3, chunks)), dma((first, chunks))],
        compiler_params=pltpu.CompilerParams(
            collective_id=name, has_side_effects=True, vmem_limit_bytes=62 * 2**20
        ),
    )(
        gain_two,
        gain_key,
        slices,
        stats,
        two,
        cot,
        out_all,
        pre,
        in_all,
        att,
        normed,
        one,
        pq,
        share,
    )


def finish_kernel(
    second, grad_ref, block_ref, line_ref, total_ref, loss_ref, qkv_ref, proj_ref, in_ref, mid_ref, *outs
):
    (
        block_out,
        loss_out,
        grad_out,
        query_out,
        key_out,
        value_out,
        proj_out,
        in_out,
        mid_out,
        attn_out,
        ffn_out,
        last_out,
        temper_out,
        mix_out,
    ) = outs
    grad_out[...] = grad_ref[...].astype(F32)
    near = lax.rem(pl.program_id(0), second) == lax.axis_index("y")

    @pl.when(near)
    def _():
        block_out[...] = line_ref[...]

    @pl.when(jnp.logical_not(near))
    def _():
        block_out[...] = block_ref[...]

    @pl.when(pl.program_id(0) == 0)
    def _():
        local = proj_ref.shape[0]
        query_out[...] = qkv_ref[0:local, :]
        key_out[...] = qkv_ref[local : 2 * local, :]
        value_out[...] = qkv_ref[2 * local : 3 * local, :]
        proj_out[...] = proj_ref[...]
        in_out[...] = in_ref[...]
        mid_out[...] = mid_ref[...]
        attn_out[...] = total_ref[0:1, :]
        ffn_out[...] = total_ref[1:2, :]
        last_out[...] = total_ref[2:3, :]
        temper_out[...] = total_ref[3:4, 0:1]
        mix_out[...] = total_ref[4:5, 0:1]
        nar, _, tok = loss_ref.shape
        seqs = loss_out.shape[0]
        per_seq = nar // seqs
        for n in range(nar):
            at = (n % per_seq) * tok
            loss_out[n // per_seq : n // per_seq + 1, at : at + tok] = loss_ref[n, 0:1, :]


def finish(grad, block, lines, totals, losses, qkv, proj, w_in, w_out, seqs):
    nar, tok, width = grad.shape
    second = nar // lines.shape[0]
    local, piece = proj.shape

    def whole(shape):
        return pl.BlockSpec(shape, lambda i: (0,) * len(shape))

    def each():
        return pl.BlockSpec((1, tok, width), lambda i: (i, 0, 0))

    small = [
        ((local, piece), F32),
        ((local, piece), F32),
        ((local, piece), F32),
        (proj.shape, F32),
        (w_in.shape, F32),
        (w_out.shape, F32),
        ((1, piece), F32),
        ((1, piece), F32),
        ((1, piece), F32),
        ((1, 1), F32),
        ((1, 1), F32),
    ]
    loss_shape = (seqs, nar * tok // seqs)
    return pl.pallas_call(
        functools.partial(finish_kernel, second),
        grid=(nar,),
        out_shape=(
            jax.ShapeDtypeStruct((nar, tok, width), BF16),
            jax.ShapeDtypeStruct(loss_shape, F32),
            jax.ShapeDtypeStruct((nar, tok, width), F32),
        )
        + tuple(jax.ShapeDtypeStruct(*x) for x in small),
        in_specs=[each(), each(), pl.BlockSpec((1, tok, width), lambda i: (i // second, 0, 0))]
        + [whole(x.shape) for x in (totals, losses, qkv, proj, w_in, w_out)],
        out_specs=(each(), whole(loss_shape), each()) + tuple(whole(x[0]) for x in small),
        compiler_params=pltpu.CompilerParams(vmem_limit_bytes=62 * 2**20),
    )(grad, block, lines, totals, losses, qkv, proj, w_in, w_out)


REACH = ((1, 2), (0, 2), (1, 3), (2, 1))
RELAY = {1: (0, (2, 3)), 2: (3, (0, 1))}


def segment_column(seg_ref, seq, start, block):
    row = seg_ref[pl.ds(seq, 1), start : start + block].astype(F32)
    return jnp.transpose(jnp.broadcast_to(row, (8, block)))[:, 0:1]


def grad_kernel(
    nar,
    first,
    wid,
    seqs,
    heads,
    block,
    chunks,
    seg_ref,
    gain_ref,
    sums_ref,
    grad_ref,
    line_any,
    pre_any,
    act_any,
    att_any,
    normed_any,
    ffn_any,
    branch_any,
    qkv_any,
    lse_any,
    one_any,
    input_any,
    above_any,
    pq_any,
    all_ref,
    block_ref,
    total_ref,
    in_grad_ref,
    out_grad_ref,
    proj_grad_ref,
    qkv_grad_ref,
    pre_ref,
    act_ref,
    att_ref,
    normed_ref,
    ffn_ref,
    branch_ref,
    qkv_ref,
    lse_ref,
    one_ref,
    input_ref,
    above_ref,
    pq_ref,
    load_sem,
    out_ref,
    grads,
    got,
    grad_key,
    grad_value,
    core_out,
    core_in,
    chip_out,
    chip_in,
    tail_sum,
    turn_out,
    turn_in,
    line_in,
    work,
    qkv_out,
    qkv_in,
    own_ref,
    own_sums,
    all_sums,
    pieces_out,
    pieces_in,
    own_sem,
    k_send,
    k_recv,
    a_send,
    a_recv,
    b_send,
    b_recv,
    c_send,
    c_recv,
    x_send,
    x_recv,
    y_send,
    y_recv,
    z_send,
    z_recv,
    w_send,
    w_recv,
    g_send,
    g_recv,
    h_send,
    h_recv,
    s_send,
    s_recv,
    p_send,
    p_recv,
):
    second = nar // first
    outer = wid // 2
    za, yb = lax.axis_index("z"), lax.axis_index("y")
    me = za * second + yb
    wide = lax.axis_index("wide")
    chip, core = wide // 2, lax.rem(wide, 2)
    tok, local = grads.shape[1:]
    hidden = pre_ref.shape[0] // first
    columns = normed_ref.shape[2]
    rows = 2 * hidden
    body = first * rows
    line = rows + local
    length = nar * tok // seqs
    per_seq = nar // seqs
    width = heads * HD
    part = tok // chunks
    across = (((0,), (0,)), ((), ()))
    last = (((1,), (1,)), ((), ()))
    reach, relay = REACH, RELAY

    pairs = (
        (pre_any, pre_ref),
        (act_any, act_ref),
        (att_any, att_ref),
        (normed_any, normed_ref),
        (ffn_any, ffn_ref),
        (branch_any, branch_ref),
        (qkv_any, qkv_ref),
        (lse_any, lse_ref),
        (one_any, one_ref),
        (input_any.at[own_rows(tok, second)], input_ref),
        (above_any, above_ref),
        (pq_any, pq_ref),
    )
    loads = [
        pltpu.make_async_copy(src, dst, load_sem.at[n]) for n, (src, dst) in enumerate(pairs)
    ]
    for load in loads:
        load.start()

    greet(
        [place(lax.rem(me + k, nar), second) for k in range(1, nar)]
        + [{"wide": lax.rem(wide + w, wid)} for w in range(1, wid)]
    )

    def a_copy(target, source):
        return push(
            grad_ref.at[target],
            grads.at[source],
            a_send.at[target],
            a_recv.at[source],
            place(target, second),
        )

    def b_copy(target, source):
        return push(
            out_ref.at[pl.ds(pl.multiple_of(target * tok, tok), tok)],
            got.at[source],
            b_send.at[target],
            b_recv.at[source],
            place(target, second),
        )

    def k_copy(z, j):
        return push(
            line_any.at[z],
            block_ref.at[z * second + yb],
            k_send.at[z, j],
            k_recv.at[z, j],
            {"z": za, "y": lax.rem(yb + j, second)},
        )

    def c_copy(o):
        return push(
            core_out.at[o],
            core_in.at[o],
            c_send.at[o],
            c_recv.at[o],
            {"wide": chip * 2 + (1 - core)},
        )

    def span(z):
        return pl.ds(pl.multiple_of(z * rows, rows), rows)

    tail_rows = pl.ds(body, nar * local)

    def x_copy(i, q, at):
        return push(
            chip_out.at[i - 1, at],
            chip_in.at[i - 1, at],
            x_send.at[i, q],
            x_recv.at[i, q],
            {"wide": lax.rem(chip + i, outer) * 2 + core},
        )

    def y_copy(j):
        target = {"z": za, "y": lax.rem(yb + j, second)}
        return push(turn_out.at[j], turn_in.at[j], y_send.at[j], y_recv.at[j], target)

    inner = jnp.where((za == 1) | (za == 2), 1, 0)

    def mirror(z):
        return jnp.where(za < 2, z, 3 - z)

    def dest(n):
        return mirror(jnp.where(n == 1, 3, jnp.where(n == 2, 2, jnp.where(n == 3, 1 - inner, inner))))

    def z_copy(n):
        slot = jnp.where(inner == 1, (3, 4, 0)[n - 1], n - 1)
        target = mirror(jnp.where(inner == 1, (2, 2, 0)[n - 1], 1))
        return push(
            core_out.at[0, pl.ds((n - 1) * line, line)],
            line_in.at[slot],
            z_send.at[n],
            z_recv.at[slot],
            {"z": target, "y": yb},
        )

    def z_arrival(slot):
        return push(
            core_out.at[0, pl.ds(0, line)],
            line_in.at[slot],
            z_send.at[0],
            z_recv.at[slot],
            {"z": mirror(jnp.where(inner == 1, 0, 1)), "y": yb},
        )

    def w_copy(i):
        target = lax.rem(wide + i, wid)
        return push(
            qkv_out.at[target], qkv_in.at[i], w_send.at[i], w_recv.at[i], {"wide": target}
        )

    def g_copy(source_z, target_z, slot, c, own):
        at = pl.ds(c * part, part)
        source = source_z * second + yb
        return push(
            own_ref.at[at] if own else all_ref.at[source, at],
            all_ref.at[source, at],
            g_send.at[source_z, slot, c],
            g_recv.at[source_z, c],
            {"z": target_z, "y": yb},
        )

    def h_copy(source_z, j, c, own):
        at = pl.ds(c * part, part)
        source = source_z * second + yb
        return push(
            own_ref.at[at] if own else all_ref.at[source, at],
            all_ref.at[source, at],
            h_send.at[source_z, j, c],
            h_recv.at[source_z, j, c],
            {"z": za, "y": lax.rem(yb + j, second)},
        )

    def h_arrival(source_z, j, c):
        at = pl.ds(c * part, part)
        source = source_z * second + lax.rem(yb + second - j, second)
        return push(
            all_ref.at[source, at],
            all_ref.at[source, at],
            h_send.at[source_z, j, c],
            h_recv.at[source_z, j, c],
            {"z": za, "y": lax.rem(yb + j, second)},
        )

    def s_copy(k):
        target = place(lax.rem(me + k, nar), second)
        return push(own_sums, all_sums.at[k], s_send.at[k], s_recv.at[k], target)

    def p_copy(w):
        target = lax.rem(wide + w, wid)
        return push(
            pieces_out.at[target], pieces_in.at[w], p_send.at[w], p_recv.at[w], {"wide": target}
        )

    def product_rows(w, z):
        own = pl.ds(pl.multiple_of(z * hidden, hidden), hidden)
        return (
            jnp.dot(pre_ref[own, :], normed_ref[w], preferred_element_type=F32),
            jnp.dot(act_ref[own, :], ffn_ref[w], preferred_element_type=F32),
        )

    def product_tail(w):
        return jnp.dot(att_ref[...], branch_ref[w], preferred_element_type=F32)

    for k in range(1, nar):
        a_copy(lax.rem(me + k, nar), me).start()
    own_grad = pltpu.make_async_copy(grad_ref.at[me], grads.at[me], own_sem.at[1])
    own_grad.start()
    for z in range(2):
        for j in range(1, second):
            k_copy(z, j).start()
    for n in range(6):
        loads[n].wait()

    for i in range(1, outer + 1):
        o = lax.rem(chip + i, outer)
        w = o * 2 + (1 - core)

        def for_core(z, carry, o=o, w=w):
            upper, lower = product_rows(w, z)
            at = pl.multiple_of(z * rows, rows)
            core_out[o, pl.ds(at, hidden), :] = upper.astype(BF16)
            core_out[o, pl.ds(at + hidden, hidden), :] = lower.astype(BF16)
            return carry

        lax.fori_loop(0, first, for_core, 0)
        core_out[o, tail_rows, :] = product_tail(w).astype(BF16)
        c_copy(o).start()

    for i in range(1, outer):
        o = lax.rem(chip + i, outer)
        w = o * 2 + core
        c_copy(o).wait_recv()
        total = product_tail(w) + core_in[o, tail_rows, :].astype(F32)
        chip_out[i - 1, tail_rows, :] = total.astype(BF16)
        x_copy(i, 0, tail_rows).start()

        def for_chip(n, carry, o=o, w=w, i=i):
            z = dest(n)
            upper, lower = product_rows(w, z)
            at = pl.multiple_of(z * rows, rows)
            high, low = pl.ds(at, hidden), pl.ds(at + hidden, hidden)
            chip_out[i - 1, high, :] = (upper + core_in[o, high, :].astype(F32)).astype(BF16)
            chip_out[i - 1, low, :] = (lower + core_in[o, low, :].astype(F32)).astype(BF16)
            x_copy(i, n, span(z)).start()
            return carry

        lax.fori_loop(1, first + 1, for_chip, 0)

    loads[6].wait()
    loads[7].wait()
    own_grad.wait()

    def sequence(seq, carry):
        base = seq * length

        def arrive(b, c):
            source = seq * per_seq + b

            @pl.when(source != me)
            def _():
                a_copy(source, source).wait_recv()

            return c

        lax.fori_loop(0, per_seq, arrive, 0)
        grad_key[...] = jnp.zeros_like(grad_key)
        grad_value[...] = jnp.zeros_like(grad_value)
        for start in range(0, length, block):
            keys = start + block
            at = pl.multiple_of(base + start, block)
            query_segment = segment_column(seg_ref, seq, start, block)
            key_segment = seg_ref[pl.ds(seq, 1), 0:keys].astype(F32)
            spot = lax.broadcasted_iota(jnp.int32, (block, keys), 1)
            own = lax.broadcasted_iota(jnp.int32, (block, keys), 0) + start
            allowed = (spot <= own) & (query_segment == key_segment)
            whole = pl.ds(pl.multiple_of(base, length), keys)
            query = qkv_ref[pl.ds(at, block), 0:width]
            key = qkv_ref[whole, width : 2 * width]
            value = qkv_ref[whole, 2 * width : 3 * width]
            each = min(tok, block)
            grad = jnp.concatenate(
                [
                    grads[
                        seq * per_seq + (start + r) // tok,
                        (start + r) % tok : (start + r) % tok + each,
                        :,
                    ]
                    for r in range(0, block, each)
                ],
                axis=0,
            )
            total = jnp.zeros((block, width), F32)
            for head in range(heads):
                own_query = head_lanes(query, head)
                own_grad = head_lanes(grad, head)
                scores = lax.dot_general(own_query, key, last, preferred_element_type=F32)
                probs = jnp.where(
                    allowed, jnp.exp(scores - lse_ref[pl.ds(at, block), head : head + 1]), 0.0
                )
                grad_probs = lax.dot_general(own_grad, value, last, preferred_element_type=F32)
                delta = jnp.sum(probs * grad_probs, axis=-1, keepdims=True)
                grad_scores = (probs * (grad_probs - delta)).astype(BF16)
                total = total + head_lanes(
                    jnp.dot(grad_scores, key, preferred_element_type=F32), head
                )
                grad_key[0:keys, :] += lax.dot_general(
                    grad_scores, own_query, across, preferred_element_type=F32
                )
                grad_value[0:keys, :] += lax.dot_general(
                    probs.astype(BF16), own_grad, across, preferred_element_type=F32
                )
            out_ref[pl.ds(at, block), 0:width] = (total * HD ** (-0.5)).astype(BF16)
        every = pl.ds(pl.multiple_of(base, length), length)
        out_ref[every, width : 2 * width] = grad_key[...].astype(BF16)
        out_ref[every, 2 * width : 3 * width] = grad_value[...].astype(BF16)

        def leave(b, c):
            target = seq * per_seq + b

            @pl.when(target != me)
            def _():
                b_copy(target, me).start()

            return c

        lax.fori_loop(0, per_seq, leave, 0)
        return carry

    lax.fori_loop(0, seqs, sequence, 0)

    for z in range(2, first):
        for j in range(1, second):
            k_copy(z, j).start()
    loads[8].wait()
    qkv_part = lax.dot_general(
        out_ref[...], one_ref[...], across, preferred_element_type=F32
    ).astype(BF16)
    for w in range(wid):
        qkv_out[w] = qkv_part[:, w * columns : (w + 1) * columns]
    for i in range(1, wid):
        w_copy(i).start()

    w_own = chip * 2 + core
    c_copy(chip).wait_recv()
    tail_sum[...] = product_tail(w_own) + core_in[chip, tail_rows, :].astype(F32)
    for i in range(1, outer):
        x_copy(i, 0, tail_rows).wait_recv()
        tail_sum[...] += chip_in[i - 1, tail_rows, :].astype(F32)
    for j in range(1, second):
        column = lax.rem(yb + j, second)
        for z in range(first):
            at = pl.ds(pl.multiple_of((z * second + column) * local, local), local)
            turn_out[j, z] = tail_sum[at, :].astype(BF16)
        y_copy(j).start()

    for n in range(9, 12):
        loads[n].wait()
    normed, inverse = normalise(input_ref[...].astype(F32))
    mine = out_ref[pl.ds(pl.multiple_of(me * tok, tok), tok), :]
    total = jnp.dot(mine, pq_ref[me, local:, :], preferred_element_type=F32)
    for k in range(1, nar):
        source = lax.rem(me + k, nar)
        b_copy(source, source).wait_recv()
        total = total + jnp.dot(
            got[source], pq_ref[source, local:, :], preferred_element_type=F32
        )
    grad = above_ref[...] + normalise_back(total, normed, inverse, gain_ref[0:1, :])
    own_ref[...] = grad.astype(BF16)

    for c in range(chunks):
        for z in range(first):

            @pl.when(za == z)
            def _(z=z, c=c):
                for slot, target in enumerate(reach[z]):
                    g_copy(za, target, slot, c, True).start()

        for j in range(1, second):
            h_copy(za, j, c, True).start()
    own_copy = pltpu.make_async_copy(own_ref, all_ref.at[me], own_sem.at[0])
    own_copy.start()
    own_sums[...] = sums_ref[...]
    own_sums[0:1, :] = jnp.sum(total * normed, axis=0, keepdims=True)
    for k in range(1, nar):
        s_copy(k).start()

    def gathered(begin, end):
        for c in range(chunks):
            for d in range(begin, end):
                for way in (-1, 1):
                    z = za + way * d

                    @pl.when((z >= 0) & (z < first))
                    def _(z=z, c=c):
                        g_copy(z, za, 0, c, False).wait_recv()
                        for middle, (target, sources) in relay.items():

                            @pl.when((za == middle) & ((z == sources[0]) | (z == sources[1])))
                            def _(target=target):
                                g_copy(z, target, 0, c, False).start()

                        for j in range(1, second):
                            h_copy(z, j, c, False).start()

    for o in range(outer):
        c_copy(o).wait_send()
    for j in range(1, second):
        y_copy(j).wait_recv()

    def line_parts(n):
        z = dest(n)
        at = pl.ds(pl.multiple_of((z * second + yb) * local, local), local)
        low_part = tail_sum[at, :]
        for j in range(1, second):
            low_part = low_part + turn_in[j, z].astype(F32)
        upper, lower = product_rows(w_own, z)
        start = pl.multiple_of(z * rows, rows)
        high, low = pl.ds(start, hidden), pl.ds(start + hidden, hidden)
        upper = upper + core_in[chip, high, :].astype(F32)
        lower = lower + core_in[chip, low, :].astype(F32)
        for i in range(1, outer):
            x_copy(i, n, span(z)).wait_recv()
            upper = upper + chip_in[i - 1, high, :].astype(F32)
            lower = lower + chip_in[i - 1, low, :].astype(F32)
        work[0:hidden, :] = upper
        work[hidden:rows, :] = lower
        work[rows:, :] = low_part

    def add_arrival(slot):
        z_arrival(slot).wait_recv()
        work[...] += line_in[slot].astype(F32)

    @pl.when(inner == 0)
    def _():
        for n in range(1, 4):
            line_parts(n)
            core_out[0, (n - 1) * line : n * line, :] = work[...].astype(BF16)
            z_copy(n).start()

    gathered(1, 2)
    gathered(2, first)

    @pl.when(inner == 1)
    def _():
        for n in range(1, 4):
            line_parts(n)
            add_arrival((0, 1, 3)[n - 1])
            core_out[0, (n - 1) * line : n * line, :] = work[...].astype(BF16)
            z_copy(n).start()

    line_parts(4)
    sums = own_sums[...]
    for k in range(1, nar):
        s_copy(k).wait_recv()
        sums = sums + all_sums[k]
    piece = total_ref.shape[1]
    for w in range(wid):
        pieces_out[w] = sums[:, w * piece : (w + 1) * piece]
    for w in range(1, wid):
        p_copy(w).start()
    qkv_sum = qkv_out[wide].astype(F32)
    for i in range(1, wid):
        w_copy(i).wait_recv()
        qkv_sum = qkv_sum + qkv_in[i].astype(F32)
    qkv_grad_ref[...] = qkv_sum

    @pl.when(inner == 0)
    def _():
        add_arrival(0)

    @pl.when(inner == 1)
    def _():
        add_arrival(2)
        add_arrival(4)

    in_grad_ref[...] = jnp.transpose(work[0:hidden, :])
    out_grad_ref[...] = work[hidden:rows, :]
    proj_grad_ref[...] = work[rows:, :]
    answer = pieces_out[wide]
    for w in range(1, wid):
        p_copy(w).wait_recv()
        answer = answer + pieces_in[w]
    total_ref[...] = answer

    for z in range(first):
        for j in range(1, second):
            for c in range(chunks):
                h_arrival(z, j, c).wait_recv()
    own_copy.wait()
    for z in range(first):
        for j in range(1, second):
            k_copy(z, j).wait()
    for k in range(1, nar):
        a_copy(lax.rem(me + k, nar), me).wait_send()
        b_copy(lax.rem(me + k, nar), me).wait_send()
        s_copy(k).wait_send()
    for w in range(1, wid):
        p_copy(w).wait_send()
        w_copy(w).wait_send()
    for i in range(1, outer):
        x_copy(i, 0, tail_rows).wait_send()
        for n in range(1, first + 1):
            x_copy(i, n, span(dest(n))).wait_send()
    for j in range(1, second):
        y_copy(j).wait_send()
    for n in range(1, first):
        z_copy(n).wait_send()
    for c in range(chunks):
        for z in range(first):

            @pl.when(za == z)
            def _(z=z, c=c):
                for slot, target in enumerate(reach[z]):
                    g_copy(za, target, slot, c, True).wait_send()
                if z in relay:
                    target, sources = relay[z]
                    for n in sources:
                        g_copy(n, target, 0, c, False).wait_send()

            for j in range(1, second):
                h_copy(z, j, c, False).wait_send()


def attention_grads(
    seg, gain, sums, grads, lines, sides, qkv, lse, one, inputs, above, pq, first, wid, name
):
    nar, tok, local = grads.shape
    rows, wide = qkv.shape
    width = inputs.shape[1]
    seqs, length = seg.shape
    second = nar // first
    outer = wid // 2
    hidden = sides[0].shape[0] // first
    piece = width // wid
    body = first * 2 * hidden + nar * local
    line = 2 * hidden + local
    chunks = 2
    vmem = pl.BlockSpec(memory_space=pltpu.VMEM)
    hbm = pl.BlockSpec(memory_space=pl.ANY)
    dma = pltpu.SemaphoreType.DMA
    late = (*sides, qkv, lse, one, inputs, above, pq)
    return pl.pallas_call(
        functools.partial(
            grad_kernel, nar, first, wid, seqs, local // HD, min(256, length), chunks
        ),
        out_shape=(
            jax.ShapeDtypeStruct((nar, tok, width), BF16),
            jax.ShapeDtypeStruct((nar, tok, width), BF16),
            jax.ShapeDtypeStruct((8, piece), F32),
            jax.ShapeDtypeStruct((piece, hidden), F32),
            jax.ShapeDtypeStruct((hidden, piece), F32),
            jax.ShapeDtypeStruct((local, piece), F32),
            jax.ShapeDtypeStruct((3 * local, piece), F32),
        ),
        in_specs=[vmem] * 3 + [hbm] * 14,
        out_specs=(hbm, hbm) + (vmem,) * 5,
        scratch_shapes=[
            pltpu.VMEM((tok, width) if x is inputs else x.shape, x.dtype) for x in late
        ]
        + [
            dma((12,)),
            pltpu.VMEM((rows, wide), BF16),
            pltpu.VMEM((nar, tok, local), BF16),
            pltpu.VMEM((nar, tok, wide), BF16),
            pltpu.VMEM((length, local), F32),
            pltpu.VMEM((length, local), F32),
            pltpu.VMEM((outer, body, piece), BF16),
            pltpu.VMEM((outer, body, piece), BF16),
            pltpu.VMEM((outer - 1, body, piece), BF16),
            pltpu.VMEM((outer - 1, body, piece), BF16),
            pltpu.VMEM((nar * local, piece), F32),
            pltpu.VMEM((second, first, local, piece), BF16),
            pltpu.VMEM((second, first, local, piece), BF16),
            pltpu.VMEM((5, line, piece), BF16),
            pltpu.VMEM((line, piece), F32),
            pltpu.VMEM((wid, 3 * local, piece), BF16),
            pltpu.VMEM((wid, 3 * local, piece), BF16),
            pltpu.VMEM((tok, width), BF16),
            pltpu.VMEM((8, width), F32),
            pltpu.VMEM((nar, 8, width), F32),
            pltpu.VMEM((wid, 8, piece), F32),
            pltpu.VMEM((wid, 8, piece), F32),
            dma((2,)),
            dma((first, second)),
            dma((first, second)),
            dma((nar,)),
            dma((nar,)),
            dma((nar,)),
            dma((nar,)),
            dma((outer,)),
            dma((outer,)),
            dma((outer, first + 1)),
            dma((outer, first + 1)),
            dma((second,)),
            dma((second,)),
            dma((first,)),
            dma((5,)),
            dma((wid,)),
            dma((wid,)),
            dma((first, 3, chunks)),
            dma((first, chunks)),
            dma((first, second, chunks)),
            dma((first, second, chunks)),
            dma((nar,)),
            dma((nar,)),
            dma((wid,)),
            dma((wid,)),
        ],
        compiler_params=pltpu.CompilerParams(
            collective_id=name, has_side_effects=True, vmem_limit_bytes=63 * 2**20
        ),
    )(seg, gain, sums, grads, lines, *late)


def neighbour_kernel(
    nar,
    first,
    tiles,
    tile,
    kept,
    ring,
    count_ref,
    target_ref,
    base_ref,
    weight_ref,
    temper_ref,
    mix_ref,
    query_ref,
    keys_ref,
    norms_any,
    ids_any,
    grad_ref,
    loss_ref,
    stat_ref,
    queries,
    partial,
    dist,
    grads,
    sends,
    slots,
    loss_own,
    norms_ref,
    ids_ref,
    load_sem,
    slot_sem,
    q_send,
    q_recv,
    d_send,
    d_recv,
    g_send,
    g_recv,
    l_send,
    l_recv,
    o_send,
    o_recv,
):
    second = nar // first
    me = lax.axis_index("z") * second + lax.axis_index("y")
    tok = query_ref.shape[1]
    depth = query_ref.shape[2]
    group = 16
    per_block = tok // tile
    late = tiles - kept

    def peer(k):
        return lax.rem(me + k, nar)

    def origin(k):
        return lax.rem(me + nar - k, nar)

    def load(index, slot):
        block, sub = index // per_block, lax.rem(index, per_block)
        row = origin(block) * tok + sub * tile
        return pltpu.make_async_copy(
            keys_ref.at[pl.ds(row, tile)], slots.at[slot], slot_sem.at[slot]
        )

    loads = [
        pltpu.make_async_copy(norms_any, norms_ref, load_sem.at[0]),
        pltpu.make_async_copy(query_ref.at[me], queries.at[0], load_sem.at[1]),
        pltpu.make_async_copy(ids_any.at[own_rows(tok, second)], ids_ref, load_sem.at[2]),
    ]
    for n in range(3):
        loads[n].start()
    for i in range(kept + ring):
        load(i, i).start()

    greet([place(peer(k), second) for k in range(1, nar)])

    def q_copy(k):
        return push(
            query_ref.at[peer(k)],
            queries.at[k],
            q_send.at[k],
            q_recv.at[k],
            place(peer(k), second),
        )

    def d_copy(k):
        return push(
            partial.at[k], dist.at[k], d_send.at[k], d_recv.at[k], place(origin(k), second)
        )

    def g_copy(k):
        return push(
            grads.at[0], grads.at[k], g_send.at[k], g_recv.at[k], place(peer(k), second)
        )

    def l_copy(k):
        return push(
            loss_own, loss_ref.at[me], l_send.at[k], l_recv.at[k], place(peer(k), second)
        )

    def o_copy(k):
        return push(
            sends.at[k], grad_ref.at[me], o_send.at[k], o_recv.at[k], place(origin(k), second)
        )

    for k in range(1, nar):
        q_copy(k).start()
    for n in range(3):
        loads[n].wait()

    row_of = lax.broadcasted_iota(jnp.int32, (group, J), 0)

    def slot_of(index):
        return jnp.where(index < kept, index, kept + lax.rem(index - kept, ring))

    def slot_late(n):
        return kept + lax.rem(n, ring)

    def forward_tile(k, sub, slot):
        def one(g, carry):
            at = pl.multiple_of(sub * tile + g * group, group)
            own = queries[k, pl.ds(at, group), :].astype(F32)
            keys = slots[slot, pl.ds(g * group, group), :, :].reshape(group * depth, J)
            wide = jnp.concatenate(
                [jnp.where(row_of[:, :depth] == t, own, 0.0) for t in range(group)], axis=1
            ).astype(BF16)
            out = jnp.dot(wide, keys, preferred_element_type=F32)
            row = pl.multiple_of(origin(k) * tok + at, group)
            partial[k, pl.ds(at, group), :] = 2.0 * out - norms_ref[pl.ds(row, group), :]
            return carry

        lax.fori_loop(0, tile // group, one, 0, unroll=True)

    def forward_block(k):
        def body(sub, carry):
            index = k * per_block + sub
            slot = slot_of(index)
            load(index, slot).wait()
            forward_tile(k, sub, slot)

            @pl.when(index >= kept)
            def _():
                nxt = index - kept + ring

                @pl.when(nxt < 2 * late)
                def _():
                    load(kept + lax.rem(nxt, late), slot).start()

            return carry

        lax.fori_loop(0, per_block, body, 0)

    forward_block(0)

    def forward_rest(k, carry):
        q_copy(k).wait_recv()
        forward_block(k)
        d_copy(k).start()
        return carry

    lax.fori_loop(1, nar, forward_rest, 0)

    def collect(k, total):
        d_copy(k).wait_recv()
        return total + dist[k]

    distance = lax.fori_loop(1, nar, collect, partial[0])
    temper_value = temper_ref[0]
    mix_value = mix_ref[0]
    per_seq = count_ref.shape[1] // tok

    def own_column(ref):
        row = jnp.zeros((1, tok), F32)
        for n in range(nar):
            at = (n % per_seq) * tok
            seq = n // per_seq
            row = jnp.where(me == n, ref[seq : seq + 1, at : at + tok].astype(F32), row)
        return jnp.transpose(jnp.broadcast_to(row, (8, tok)))[:, 0:1]

    count = own_column(count_ref)
    target = own_column(target_ref)
    base = own_column(base_ref)
    loss_weight = own_column(weight_ref)
    logits = distance / temper_value
    spot = lax.broadcasted_iota(jnp.int32, (tok, J), 1).astype(F32)
    masked = jnp.where(spot < count, logits, -1e30)
    peak = jnp.max(masked, axis=-1, keepdims=True)
    expo = jnp.exp(masked - peak)
    weights = expo / jnp.sum(expo, axis=-1, keepdims=True)
    matches = jnp.where(ids_ref[...].astype(F32) == target, 1.0, 0.0)
    knn_prob = jnp.sum(weights * matches, axis=-1, keepdims=True)
    mixture = mix_value * knn_prob + (1.0 - mix_value) * base
    grad_mixture = -loss_weight / mixture
    grad_logits = weights * (mix_value * grad_mixture) * (matches - knn_prob)
    grads[0] = (2.0 * grad_logits / temper_value).astype(BF16)
    for k in range(1, nar):
        g_copy(k).start()
    loss = jnp.transpose(jnp.broadcast_to(-jnp.log(mixture), (tok, J)))[0:8, :]
    loss_own[...] = loss
    for k in range(1, nar):
        l_copy(k).start()
    loss_ref[me] = loss
    term_temper = -jnp.sum(grad_logits * logits, axis=0, keepdims=True) / temper_value
    term_mix = jnp.sum((knn_prob - base) * grad_mixture, axis=0, keepdims=True)
    stat_ref[0:1, :] = term_temper
    stat_ref[1:2, :] = jnp.broadcast_to(term_mix, (1, J))

    def backward_tile(k, sub, slot):
        def one(g, carry):
            at = pl.multiple_of(sub * tile + g * group, group)
            own = grads[k, pl.ds(at, group), :]
            keys = slots[slot, pl.ds(g * group, group), :, :].reshape(group * depth, J)
            out = lax.dot_general(
                own, keys, (((1,), (1,)), ((), ())), preferred_element_type=F32
            )
            total = jnp.zeros((group, depth), F32)
            for t in range(group):
                total = jnp.where(
                    row_of[:, :depth] == t, out[:, t * depth : (t + 1) * depth], total
                )
            sends[k, pl.ds(at, group), :] = total.astype(BF16)
            return carry

        lax.fori_loop(0, tile // group, one, 0, unroll=True)

    def backward_block(k):
        def body(sub, carry):
            index = k * per_block + sub

            @pl.when(index < kept)
            def _():
                backward_tile(k, sub, index)

            @pl.when(index >= kept)
            def _():
                n = index - kept + late
                slot = slot_late(n)
                load(index, slot).wait()
                backward_tile(k, sub, slot)

                @pl.when(n + ring < 2 * late)
                def _():
                    load(kept + lax.rem(n + ring, late), slot).start()

            return carry

        lax.fori_loop(0, per_block, body, 0)

    backward_block(0)
    grad_ref[me] = sends[0]

    def backward_rest(k, carry):
        g_copy(k).wait_recv()
        backward_block(k)
        o_copy(k).start()
        return carry

    lax.fori_loop(1, nar, backward_rest, 0)

    for k in range(1, nar):
        q_copy(k).wait_send()
        d_copy(k).wait_send()
        g_copy(k).wait_send()
        l_copy(k).wait()
        o_copy(k).wait()


def neighbours(nar, first, columns, temper, mix, query, keys, norms, ids):
    tok, depth = query.shape[1:]
    rows = keys.shape[0]
    tile = 32
    tiles = rows // tile
    bytes_tile = tile * depth * J * 2
    ring = 4
    kept = min(tiles - 2 * ring, (KEPT_BYTES // bytes_tile))
    vmem = pl.BlockSpec(memory_space=pltpu.VMEM)
    dma = pltpu.SemaphoreType.DMA((nar,))
    return pl.pallas_call(
        functools.partial(neighbour_kernel, nar, first, tiles, tile, kept, ring),
        out_shape=(
            jax.ShapeDtypeStruct((nar, tok, depth), BF16),
            jax.ShapeDtypeStruct((nar, 8, tok), F32),
            jax.ShapeDtypeStruct((2, J), F32),
        ),
        in_specs=[vmem] * 4
        + [pl.BlockSpec(memory_space=pltpu.SMEM)] * 2
        + [pl.BlockSpec(memory_space=pl.ANY)] * 4,
        out_specs=(vmem, vmem, vmem),
        scratch_shapes=[
            pltpu.VMEM((nar, tok, depth), BF16),
            pltpu.VMEM((nar, tok, J), F32),
            pltpu.VMEM((nar, tok, J), F32),
            pltpu.VMEM((nar, tok, J), BF16),
            pltpu.VMEM((nar, tok, depth), BF16),
            pltpu.VMEM((kept + ring, tile, depth, J), BF16),
            pltpu.VMEM((8, tok), F32),
            pltpu.VMEM((rows, J), F32),
            pltpu.VMEM((tok, J), jnp.int32),
            pltpu.SemaphoreType.DMA((3,)),
            pltpu.SemaphoreType.DMA((kept + ring,)),
        ]
        + [dma] * 10,
        compiler_params=pltpu.CompilerParams(
            collective_id=1, has_side_effects=True, vmem_limit_bytes=62 * 2**20
        ),
    )(*columns, temper, mix, query, keys, norms, ids)


def on_device(
    block_input,
    output_cotangent,
    loss_weight,
    segments,
    nbr_keys,
    nbr_count,
    nbr_ids,
    targets,
    base_prob,
    w_query,
    w_key,
    w_value,
    w_proj,
    w_in,
    w_out,
    gain_attn,
    gain_ffn,
    gain_key,
    temper,
    mix_weight,
):
    seqs_here, length, width = block_input.shape
    rows = seqs_here * length
    wid = lax.axis_size("wide")
    first = lax.axis_size("z")
    nar = first * lax.axis_size("y")
    inputs = block_input.reshape(rows, width)
    keys = nbr_keys.reshape(rows, nbr_keys.shape[2], nbr_keys.shape[3])
    gain_one, gain_two, gain_last = (
        gain.reshape(1, width) for gain in (gain_attn, gain_ffn, gain_key)
    )
    normed_one, qkv, lse, part_norms, attended, in_all, out_all, pq_all = head(
        gain_one,
        segments,
        (w_proj, w_query, w_key, w_value),
        inputs,
        keys,
        w_in,
        w_out,
        first,
        nar,
        wid,
        2,
    )
    hidden_one, hidden_two, output_own, query_key, normed_two, pre_act = ffn(
        gain_two, gain_last, attended, inputs, pq_all, in_all, out_all, 3
    )
    grad_slices, losses, stats = neighbours(
        nar,
        first,
        (nbr_count, targets, base_prob, loss_weight),
        temper,
        mix_weight,
        query_key,
        keys,
        part_norms,
        nbr_ids.reshape(rows, -1),
    )
    sums, grad_hidden_one, grad_attended, *sides, lines = ffn_back(
        gain_two,
        gain_last,
        grad_slices,
        stats,
        hidden_two,
        output_cotangent.reshape(rows, width),
        out_all,
        pre_act,
        in_all,
        attended,
        normed_two,
        hidden_one,
        pq_all,
        output_own,
        wid,
        5,
    )
    grad_input, block_output, totals, grad_in, grad_out, grad_proj, grad_qkv = attention_grads(
        segments,
        gain_one,
        sums,
        grad_attended,
        lines,
        sides,
        qkv,
        lse,
        normed_one,
        inputs,
        grad_hidden_one,
        pq_all,
        first,
        wid,
        6,
    )
    results = finish(
        grad_input,
        block_output,
        lines,
        totals,
        losses,
        grad_qkv,
        grad_proj,
        grad_in,
        grad_out,
        seqs_here,
    )
    block_output, token_loss, grad_input, *weights, total_one, total_two, total_last = results[:12]
    piece = width // wid
    return (
        block_output.reshape(seqs_here, length, width),
        token_loss,
        grad_input.reshape(seqs_here, length, width),
        *weights,
        total_one.reshape(piece),
        total_two.reshape(piece),
        total_last.reshape(piece),
        results[12].reshape(1),
        results[13].reshape(1),
    )


def solution(mesh):
    wide, narrow = mesh.devices.shape
    first = 4
    split = jax.sharding.Mesh(
        mesh.devices.reshape(wide, first, narrow // first), ("wide", "z", "y")
    )
    narrow = ("z", "y")
    return jax.shard_map(
        on_device,
        mesh=split,
        in_specs=(
            P("wide", None, None),
            P("wide", None, None),
            P("wide", None),
            P("wide", None),
            P("wide", None, narrow, None),
            P("wide", None),
            P("wide", None, None),
            P("wide", None),
            P("wide", None),
            P(narrow, None),
            P(narrow, None),
            P(narrow, None),
            P(narrow, None),
            P(None, narrow),
            P(narrow, None),
            P(),
            P(),
            P(),
            P(),
            P(),
        ),
        out_specs=(
            P("wide", None, None),
            P("wide", None),
            P("wide", None, None),
            P(narrow, "wide"),
            P(narrow, "wide"),
            P(narrow, "wide"),
            P(narrow, "wide"),
            P("wide", narrow),
            P(narrow, "wide"),
            P("wide"),
            P("wide"),
            P("wide"),
            P(),
            P(),
        ),
        check_vma=False,
    )
```

```python
import functools

import jax
import jax.numpy as jnp
from jax import lax
from jax.experimental import pallas as pl
from jax.experimental.pallas import tpu as pltpu
from jax.sharding import PartitionSpec as P

HD = 64
EPSILON = 1e-05
F32 = jnp.float32
BF16 = jnp.bfloat16
MESH = pl.DeviceIdType.MESH
J = 128
KEPT_BYTES = 24 * 2**20


def place(index, second):
    return {"z": index // second, "y": lax.rem(index, second)}


def push(src, dst, send, recv, target):
    return pltpu.make_async_remote_copy(
        src_ref=src,
        dst_ref=dst,
        send_sem=send,
        recv_sem=recv,
        device_id=target,
        device_id_type=MESH,
    )


def greet(peers):
    barrier = pltpu.get_barrier_semaphore()
    for peer in peers:
        pl.semaphore_signal(barrier, inc=1, device_id=peer, device_id_type=MESH)
    pl.semaphore_wait(barrier, len(peers))


def normalise(values):
    centred = values - jnp.mean(values, axis=-1, keepdims=True)
    inverse = lax.rsqrt(jnp.mean(centred * centred, axis=-1, keepdims=True) + EPSILON)
    return centred * inverse, inverse


def normalise_back(grad_out, normed, inverse, gain):
    scaled = grad_out * gain
    return inverse * (
        scaled
        - jnp.mean(scaled, axis=-1, keepdims=True)
        - normed * jnp.mean(scaled * normed, axis=-1, keepdims=True)
    )


def head_lanes(values, head):
    lanes = lax.broadcasted_iota(jnp.int32, values.shape, 1)
    return jnp.where(lanes // HD == head, values, jnp.zeros_like(values))


def head_kernel(
    nar,
    first,
    wid,
    seqs,
    heads,
    block,
    tile,
    ring,
    gain_ref,
    seg_ref,
    proj_any,
    query_any,
    key_any,
    value_any,
    input_any,
    keys_ref,
    in_any,
    out_any,
    normed_out,
    qkv_out,
    lse_out,
    norms_out,
    att_ref,
    in_all,
    out_all,
    pq_all,
    pq_ref,
    in_ref,
    out_ref,
    input_ref,
    normed_ref,
    qkv_ref,
    lse_ref,
    norms_ref,
    attended,
    slots,
    load_sem,
    store_sem,
    slot_sem,
    own_sem,
    a_send,
    a_recv,
    z_send,
    z_recv,
    y_send,
    y_recv,
    x_send,
    x_recv,
    c_send,
    c_recv,
):
    second = nar // first
    outer = wid // 2
    za, yb = lax.axis_index("z"), lax.axis_index("y")
    me = za * second + yb
    wide = lax.axis_index("wide")
    chip, core = wide // 2, lax.rem(wide, 2)
    rows, width = input_ref.shape
    tok = rows // nar
    length = rows // seqs
    local = heads * HD
    tiles = rows // tile
    last = (((1,), (1,)), ((), ()))

    def fetch(index, slot):
        return pltpu.make_async_copy(
            keys_ref.at[pl.ds(index * tile, tile)], slots.at[slot], slot_sem.at[slot]
        )

    loads = [
        pltpu.make_async_copy(src, pq_ref.at[pl.ds(n * local, local)], load_sem.at[n])
        for n, src in enumerate((proj_any, query_any, key_any, value_any))
    ] + [
        pltpu.make_async_copy(src, dst, load_sem.at[4 + n])
        for n, (src, dst) in enumerate(
            ((in_any, in_ref), (out_any, out_ref), (input_any, input_ref))
        )
    ]
    for load in loads:
        load.start()
    stores = [
        pltpu.make_async_copy(src, dst, store_sem.at[n])
        for n, (src, dst) in enumerate(
            (
                (normed_ref, normed_out),
                (qkv_ref, qkv_out),
                (lse_ref, lse_out),
                (norms_ref, norms_out),
            )
        )
    ]

    greet(
        [place(lax.rem(me + k, nar), second) for k in range(1, nar)]
        + [{"wide": chip * 2 + (1 - core)}]
        + [{"wide": lax.rem(chip + o, outer) * 2 + core} for o in range(1, outer)]
    )

    stacks = ((pq_ref, pq_all), (in_ref, in_all), (out_ref, out_all))

    def shard_of(t, source):
        return source if t == 0 else source // second

    def quarter(t, source, owner):
        own, stack = stacks[t]
        count = own.shape[0] // wid
        at = pl.ds(pl.multiple_of(owner * count, count), count)
        return stack.at[shard_of(t, source), at]

    def own_quarter(t):
        own, _ = stacks[t]
        count = own.shape[0] // wid
        return own.at[pl.ds(pl.multiple_of(wide * count, count), count)]

    reach, relay = REACH, RELAY

    def line_copy(t, source, z, slot, own):
        return push(
            own_quarter(t) if own else quarter(t, source, wide),
            quarter(t, source, wide),
            z_send.at[t, source // second, slot],
            z_recv.at[t, source // second],
            {"z": z, "y": yb},
        )

    def owner_of(o):
        return lax.rem(chip + outer - o, outer) * 2 + core

    def row_copy(source, j, o, own):
        owner = owner_of(o)
        count = pq_ref.shape[0] // wid
        at = pl.ds(pl.multiple_of(owner * count, count), count)
        return push(
            pq_ref.at[at] if own else quarter(0, source, owner),
            quarter(0, source, owner),
            y_send.at[source, j, o],
            y_recv.at[source, j, o],
            {"z": za, "y": lax.rem(yb + j, second)},
        )

    def chip_copy(t, source, o):
        return push(
            quarter(t, source, wide),
            quarter(t, source, wide),
            x_send.at[t, source, o],
            x_recv.at[t, source, o],
            {"wide": lax.rem(chip + o, outer) * 2 + core},
        )

    def chip_arrival(t, source, o):
        owner = owner_of(o)
        return push(
            quarter(t, source, owner),
            quarter(t, source, owner),
            x_send.at[t, source, o],
            x_recv.at[t, source, o],
            {"wide": owner},
        )

    def core_copy(t, source, o, away):
        owner = lax.rem(chip + outer - o, outer) * 2 + jnp.where(away, 1 - core, core)
        return push(
            quarter(t, source, owner),
            quarter(t, source, owner),
            c_send.at[t, source, o],
            c_recv.at[t, source, o],
            {"wide": chip * 2 + (1 - core)},
        )

    def att_copy(target, source):
        return push(
            attended.at[target],
            att_ref.at[source],
            a_send.at[target],
            a_recv.at[source],
            place(target, second),
        )

    own_copies = [
        pltpu.make_async_copy(own, stack.at[shard_of(t, me)], own_sem.at[t])
        for t, (own, stack) in enumerate(stacks)
    ]

    def send_own(t):
        for z in range(first):

            @pl.when(za == z)
            def _(z=z):
                for slot, target in enumerate(reach[z]):
                    line_copy(t, me, target, slot, True).start()

        if t == 0:
            for j in range(1, second):
                for o in range(outer):
                    row_copy(me, j, o, True).start()
        own_copies[t].start()

    def line_arrivals(t, begin, end):
        for d in range(begin, end):
            for way in (-1, 1):
                z = za + way * d

                @pl.when((z >= 0) & (z < first))
                def _(z=z):
                    source = z * second + yb
                    line_copy(t, source, za, 0, False).wait_recv()
                    for middle, (target, sources) in relay.items():

                        @pl.when((za == middle) & ((z == sources[0]) | (z == sources[1])))
                        def _(target=target):
                            line_copy(t, source, target, 0, False).start()

                    for o in range(1, outer):
                        chip_copy(t, source, o).start()
                    core_copy(t, source, 0, False).start()

    def chip_arrivals(t, begin, end):
        for d in range(begin, end):
            for way in (-1, 1):
                z = za + way * d

                @pl.when((z >= 0) & (z < first))
                def _(z=z):
                    source = z * second + yb
                    for o in range(1, outer):
                        chip_arrival(t, source, o).wait_recv()
                        core_copy(t, source, o, False).start()
                    if t == 0:
                        for j in range(1, second):
                            for o in range(outer):
                                row_copy(source, j, o, False).start()

    def row_arrivals():
        for j in range(1, second):
            for z in range(first):
                source = z * second + lax.rem(yb + second - j, second)
                for o in range(outer):
                    row_copy(source, j, o, False).wait_recv()
                    core_copy(0, source, o, False).start()

    def each_source(t, do):
        for n in range(nar if t == 0 else first):
            source = n if t == 0 else n * second + yb

            @pl.when(source != me)
            def _(source=source):
                do(source)

    def core_arrivals(t):
        def do(source):
            for o in range(outer):
                core_copy(t, source, o, True).wait_recv()

        each_source(t, do)

    for n in range(6):
        loads[n].wait()
    for t in range(3):
        send_own(t)
    for i in range(ring):
        fetch(i, i).start()
    loads[6].wait()

    def project(r, carry):
        at = pl.ds(pl.multiple_of(r * block, block), block)
        normed, _ = normalise(input_ref[at, :].astype(F32))
        low = (normed * gain_ref[0:1, :]).astype(BF16)
        normed_ref[at, :] = low
        out = lax.dot_general(low, pq_ref[local:, :], last, preferred_element_type=F32)
        lanes = lax.broadcasted_iota(jnp.int32, out.shape, 1)
        qkv_ref[at, :] = jnp.where(lanes < local, out * HD ** (-0.5), out).astype(BF16)
        return carry

    lax.fori_loop(0, rows // block, project, 0)
    stores[0].start()
    stores[1].start()
    line_arrivals(0, 1, 2)
    middle = (za == 1) | (za == 2)
    at_end = jnp.logical_not(middle)

    @pl.when(middle)
    def _():
        line_arrivals(0, 2, first)

    def sequence(seq, carry):
        base = seq * length
        for start in range(0, length, block):
            keys = start + block
            at = pl.ds(pl.multiple_of(base + start, block), block)
            whole = pl.ds(pl.multiple_of(base, length), keys)
            query_segment = segment_column(seg_ref, seq, start, block)
            key_segment = seg_ref[pl.ds(seq, 1), 0:keys].astype(F32)
            spot = lax.broadcasted_iota(jnp.int32, (block, keys), 1)
            own = lax.broadcasted_iota(jnp.int32, (block, keys), 0) + start
            allowed = (spot <= own) & (query_segment == key_segment)
            query = qkv_ref[at, 0:local]
            key = qkv_ref[whole, local : 2 * local]
            value = qkv_ref[whole, 2 * local : 3 * local]
            total = jnp.zeros((block, local), F32)
            for head in range(heads):
                scores = lax.dot_general(
                    head_lanes(query, head), key, last, preferred_element_type=F32
                )
                scores = jnp.where(allowed, scores, -1e30)
                peak = jnp.max(scores, axis=-1, keepdims=True)
                expo = jnp.exp(scores - peak)
                sums = jnp.sum(expo, axis=-1, keepdims=True)
                out = jnp.dot(expo.astype(BF16), value, preferred_element_type=F32) / sums
                total = total + head_lanes(out, head)
                lse_ref[at, head : head + 1] = peak + jnp.log(sums)
            each = min(tok, block)
            for r in range(0, block, each):
                target = seq * (nar // seqs) + (start + r) // tok
                spot_row = (start + r) % tok
                attended[target, spot_row : spot_row + each, :] = total[r : r + each, :].astype(
                    BF16
                )

        def leave(b, c):
            target = seq * (nar // seqs) + b

            @pl.when(target != me)
            def _():
                att_copy(target, me).start()

            return c

        lax.fori_loop(0, nar // seqs, leave, 0)
        return carry

    lax.fori_loop(0, seqs, sequence, 0)
    stores[2].start()
    own_att = pltpu.make_async_copy(attended.at[me], att_ref.at[me], own_sem.at[3])
    own_att.start()

    def norms(begin, end):
        def body(index, carry):
            slot = lax.rem(index, ring)
            fetch(index, slot).wait()
            keys = slots[slot].astype(F32)
            at = pl.ds(pl.multiple_of(index * tile, tile), tile)
            norms_ref[at, :] = jnp.sum(keys * keys, axis=1)

            @pl.when(index + ring < tiles)
            def _():
                fetch(index + ring, slot).start()

            return carry

        lax.fori_loop(begin, end, body, 0)

    @pl.when(at_end)
    def _():
        line_arrivals(1, 1, 2)
        line_arrivals(2, 1, 2)
        chip_arrivals(0, 1, 2)
        line_arrivals(0, 2, first)

    @pl.when(middle)
    def _():
        line_arrivals(1, 1, first)
        chip_arrivals(0, 1, first)

    norms(0, tiles // 3)

    @pl.when(at_end)
    def _():
        chip_arrivals(0, 2, first)
        line_arrivals(1, 2, first)

    @pl.when(middle)
    def _():
        line_arrivals(2, 1, first)

    norms(tiles // 3, 2 * tiles // 3)

    @pl.when(at_end)
    def _():
        line_arrivals(2, 2, first)

    norms(2 * tiles // 3, tiles)
    stores[3].start()
    row_arrivals()
    chip_arrivals(1, 1, first)
    chip_arrivals(2, 1, first)
    for t in range(3):
        core_arrivals(t)
    for k in range(1, nar):
        source = lax.rem(me + k, nar)
        att_copy(source, source).wait_recv()
        att_copy(source, me).wait_send()
    for t in range(3):
        own_copies[t].wait()

        def sent(source, t=t):
            for o in range(outer):
                core_copy(t, source, o, False).wait_send()

        each_source(t, sent)
        for n in range(first):
            source = n * second + yb

            @pl.when(source != me)
            def _(source=source, t=t):
                for o in range(1, outer):
                    chip_copy(t, source, o).wait_send()

        for z in range(first):

            @pl.when(za == z)
            def _(z=z, t=t):
                for slot, target in enumerate(reach[z]):
                    line_copy(t, me, target, slot, True).wait_send()
                if z in relay:
                    target, sources = relay[z]
                    for n in sources:
                        line_copy(t, n * second + yb, target, 0, False).wait_send()

    for z in range(first):
        for j in range(1, second):
            for o in range(outer):
                row_copy(z * second + yb, j, o, False).wait_send()
    own_att.wait()
    for store in stores:
        store.wait()


def head(gain, seg, weights, block_input, keys, w_in, w_out, first, nar, wid, name):
    rows, width = block_input.shape
    seqs, length = seg.shape
    second = nar // first
    outer = wid // 2
    local = weights[0].shape[0]
    heads = local // HD
    hidden = w_in.shape[1]
    tok = rows // nar
    depth = keys.shape[1]
    tile, ring = 32, 4
    block = min(256, length)
    vmem = pl.BlockSpec(memory_space=pltpu.VMEM)
    hbm = pl.BlockSpec(memory_space=pl.ANY)
    dma = pltpu.SemaphoreType.DMA
    kept = (
        ((rows, width), BF16),
        ((rows, 3 * local), BF16),
        ((rows, heads), F32),
        ((rows, J), F32),
    )
    return pl.pallas_call(
        functools.partial(head_kernel, nar, first, wid, seqs, heads, block, tile, ring),
        out_shape=tuple(jax.ShapeDtypeStruct(*x) for x in kept)
        + (
            jax.ShapeDtypeStruct((nar, tok, local), BF16),
            jax.ShapeDtypeStruct((first, width, hidden), BF16),
            jax.ShapeDtypeStruct((first, hidden, width), BF16),
            jax.ShapeDtypeStruct((nar, 4 * local, width), BF16),
        ),
        in_specs=[vmem] * 2 + [hbm] * 8,
        out_specs=(hbm,) * 8,
        scratch_shapes=[
            pltpu.VMEM((4 * local, width), BF16),
            pltpu.VMEM((width, hidden), BF16),
            pltpu.VMEM((hidden, width), BF16),
            pltpu.VMEM((rows, width), BF16),
        ]
        + [pltpu.VMEM(*x) for x in kept]
        + [
            pltpu.VMEM((nar, tok, local), BF16),
            pltpu.VMEM((ring, tile, depth, J), BF16),
            dma((7,)),
            dma((4,)),
            dma((ring,)),
            dma((4,)),
            dma((nar,)),
            dma((nar,)),
            dma((3, first, 3)),
            dma((3, first)),
            dma((nar, second, outer)),
            dma((nar, second, outer)),
            dma((3, nar, outer)),
            dma((3, nar, outer)),
            dma((3, nar, outer)),
            dma((3, nar, outer)),
        ],
        compiler_params=pltpu.CompilerParams(
            collective_id=name, has_side_effects=True, vmem_limit_bytes=62 * 2**20
        ),
    )(gain, seg, *weights, block_input, keys, w_in, w_out)


INNER = 0.7978845608028654
CUBIC = 0.044715


def gelu_parts(values):
    tanh = jnp.tanh(INNER * (values + CUBIC * values * values * values))
    return 0.5 * values * (1.0 + tanh), tanh


def own_rows(tok, second):
    me = lax.axis_index("z") * second + lax.axis_index("y")
    return pl.ds(pl.multiple_of(me * tok, tok), tok)


def ffn_kernel(
    chunks,
    gain_two_ref,
    gain_key_ref,
    att_any,
    input_any,
    pq_any,
    in_any,
    mid_any,
    one_out,
    two_out,
    output_out,
    key_out,
    normed_out,
    pre_out,
    att_ref,
    input_ref,
    proj_ref,
    in_ref,
    mid_ref,
    one_ref,
    two_ref,
    output_ref,
    key_ref,
    normed_ref,
    pre_ref,
    back_out,
    back_in,
    load_sem,
    store_sem,
    n_send,
    n_recv,
    b_send,
    b_recv,
):
    nar, tok, local = att_ref.shape
    first, width, hidden = in_ref.shape
    second = nar // first
    part = tok // chunks
    za, yb = lax.axis_index("z"), lax.axis_index("y")

    pairs = (
        (att_any, att_ref),
        (pq_any.at[:, pl.ds(0, local)], proj_ref),
        (input_any.at[own_rows(tok, second)], input_ref),
        (in_any, in_ref),
        (mid_any, mid_ref),
    )
    loads = [
        pltpu.make_async_copy(src, dst, load_sem.at[n]) for n, (src, dst) in enumerate(pairs)
    ]
    for load in loads:
        load.start()
    kept = (
        (one_ref, one_out),
        (normed_ref, normed_out),
        (pre_ref, pre_out),
        (key_ref, key_out),
        (two_ref, two_out),
        (output_ref, output_out),
    )
    stores = [
        pltpu.make_async_copy(src, dst, store_sem.at[n]) for n, (src, dst) in enumerate(kept)
    ]

    greet([{"z": za, "y": lax.rem(yb + j, second)} for j in range(1, second)])

    def n_copy(j, c):
        at = pl.ds(c * part, part)
        target = {"z": za, "y": lax.rem(yb + j, second)}
        return push(
            normed_ref.at[0, at], normed_ref.at[j, at], n_send.at[j, c], n_recv.at[j, c], target
        )

    def b_copy(j, c):
        at = pl.ds(c * part, part)
        target = {"z": za, "y": lax.rem(yb + second - j, second)}
        return push(
            back_out.at[j, at], back_in.at[j, at], b_send.at[j, c], b_recv.at[j, c], target
        )

    def through(j, start, count):
        total = jnp.zeros((count, width), F32)
        for z in range(first):
            pre = jnp.dot(
                normed_ref[j, start : start + count, :], in_ref[z], preferred_element_type=F32
            )
            pre_ref[j, start : start + count, z * hidden : (z + 1) * hidden] = pre
            activated = gelu_parts(pre)[0].astype(BF16)
            total = total + jnp.dot(activated, mid_ref[z], preferred_element_type=F32)
        return total

    for n in range(3):
        loads[n].wait()
    att = jnp.concatenate([att_ref[n] for n in range(nar)], axis=1)
    one = input_ref[...].astype(F32) + jnp.dot(
        att, proj_ref[...].reshape(nar * local, width), preferred_element_type=F32
    )
    one_ref[...] = one
    normed, _ = normalise(one)
    normed_ref[0] = (normed * gain_two_ref[...]).astype(BF16)
    for c in range(chunks):
        for j in range(1, second):
            n_copy(j, c).start()
    stores[0].start()
    for n in range(3, 5):
        loads[n].wait()
    two_ref[...] = one_ref[...] + through(0, 0, tok)
    for c in range(chunks):
        for j in range(1, second):
            n_copy(j, c).wait_recv()
            back_out[j, c * part : (c + 1) * part, :] = through(j, c * part, part).astype(BF16)
            b_copy(j, c).start()
    stores[1].start()
    stores[2].start()
    for c in range(chunks):
        at = slice(c * part, (c + 1) * part)
        for j in range(1, second):
            b_copy(j, c).wait_recv()
            two_ref[at, :] += back_in[j, at, :].astype(F32)
    hidden_two = two_ref[...]
    normed, _ = normalise(hidden_two)
    query_key = (normed * gain_key_ref[...]).astype(BF16)
    for n in range(nar):
        key_ref[n] = query_key[:, n * (width // nar) : (n + 1) * (width // nar)]
    stores[3].start()
    stores[4].start()
    output_ref[...] = hidden_two.astype(BF16)
    stores[5].start()
    for c in range(chunks):
        for j in range(1, second):
            n_copy(j, c).wait_send()
            b_copy(j, c).wait_send()
    for store in stores:
        store.wait()


def ffn(gain_two, gain_key, att, inputs, pq, in_all, out_all, name):
    nar, tok, local = att.shape
    first, width, hidden = in_all.shape
    second = nar // first
    chunks = 2
    vmem = pl.BlockSpec(memory_space=pltpu.VMEM)
    hbm = pl.BlockSpec(memory_space=pl.ANY)
    dma = pltpu.SemaphoreType.DMA
    outs = (
        ((tok, width), F32),
        ((tok, width), F32),
        ((tok, width), BF16),
        ((nar, tok, width // nar), BF16),
        ((second, tok, width), BF16),
        ((second, tok, first * hidden), F32),
    )
    return pl.pallas_call(
        functools.partial(ffn_kernel, chunks),
        out_shape=tuple(jax.ShapeDtypeStruct(*x) for x in outs),
        in_specs=[vmem] * 2 + [hbm] * 5,
        out_specs=(hbm,) * 6,
        scratch_shapes=[
            pltpu.VMEM(att.shape, BF16),
            pltpu.VMEM((tok, width), BF16),
            pltpu.VMEM((nar, local, width), BF16),
            pltpu.VMEM(in_all.shape, BF16),
            pltpu.VMEM(out_all.shape, BF16),
        ]
        + [pltpu.VMEM(*x) for x in outs]
        + [pltpu.VMEM((second, tok, width), BF16)] * 2
        + [dma((5,)), dma((6,))]
        + [dma((second, chunks))] * 4,
        compiler_params=pltpu.CompilerParams(
            collective_id=name, has_side_effects=True, vmem_limit_bytes=62 * 2**20
        ),
    )(gain_two, gain_key, att, inputs, pq, in_all, out_all)


def ffn_back_kernel(
    chunks,
    gain_two_ref,
    gain_key_ref,
    slices_ref,
    stat_ref,
    two_any,
    cot_any,
    mid_any,
    pre_any,
    in_any,
    att_any,
    normed_any,
    one_any,
    pq_any,
    share_any,
    sums_ref,
    grad_one_out,
    grad_att_out,
    pre_turned_out,
    act_turned_out,
    att_turned_out,
    normed_cols_out,
    ffn_cols_out,
    branch_cols_out,
    line_ref,
    two_ref,
    cot_ref,
    mid_ref,
    pre_ref,
    in_ref,
    att_ref,
    normed_ref,
    one_ref,
    proj_ref,
    share_ref,
    grad_one_ref,
    grad_att_ref,
    pre_turned_ref,
    act_turned_ref,
    att_turned_ref,
    normed_cols_ref,
    ffn_cols_ref,
    branch_cols_ref,
    grads,
    grad_two,
    total,
    back_out,
    back_in,
    load_sem,
    store_sem,
    own_sem,
    n_send,
    n_recv,
    b_send,
    b_recv,
    g_send,
    g_recv,
):
    nar, tok, local = att_ref.shape
    first, width, hidden = in_ref.shape
    second = nar // first
    wid = branch_cols_ref.shape[0]
    columns = width // wid
    part = tok // chunks
    last = (((1,), (1,)), ((), ()))
    za, yb = lax.axis_index("z"), lax.axis_index("y")
    reach, relay = REACH, RELAY

    pairs = (
        (share_any, share_ref),
        (two_any, two_ref),
        (cot_any.at[own_rows(tok, second)], cot_ref),
        (mid_any, mid_ref),
        (pre_any, pre_ref),
        (in_any, in_ref),
        (att_any, att_ref),
        (normed_any, normed_ref),
        (one_any, one_ref),
        (pq_any.at[:, pl.ds(0, local)], proj_ref),
    )
    loads = [
        pltpu.make_async_copy(src, dst, load_sem.at[n]) for n, (src, dst) in enumerate(pairs)
    ]
    for load in loads:
        load.start()
    kept = (
        (ffn_cols_ref, ffn_cols_out),
        (pre_turned_ref, pre_turned_out),
        (act_turned_ref, act_turned_out),
        (att_turned_ref, att_turned_out),
        (normed_cols_ref, normed_cols_out),
        (grad_att_ref, grad_att_out),
        (branch_cols_ref, branch_cols_out),
        (grad_one_ref, grad_one_out),
    )
    stores = [
        pltpu.make_async_copy(src, dst, store_sem.at[n]) for n, (src, dst) in enumerate(kept)
    ]

    greet(
        [{"z": za, "y": lax.rem(yb + j, second)} for j in range(1, second)]
        + [{"z": lax.rem(za + i, first), "y": yb} for i in range(1, first)]
    )

    def n_copy(j, c):
        at = pl.ds(c * part, part)
        target = {"z": za, "y": lax.rem(yb + j, second)}
        return push(grads.at[0, at], grads.at[j, at], n_send.at[j, c], n_recv.at[j, c], target)

    def b_copy(j, c):
        at = pl.ds(c * part, part)
        target = {"z": za, "y": lax.rem(yb + second - j, second)}
        return push(
            back_out.at[j, at], back_in.at[j, at], b_send.at[j, c], b_recv.at[j, c], target
        )

    def g_copy(source, target, slot, c, own):
        at = pl.ds(c * part, part)
        return push(
            share_ref.at[at] if own else line_ref.at[source, at],
            line_ref.at[source, at],
            g_send.at[source, slot, c],
            g_recv.at[source, c],
            {"z": target, "y": yb},
        )

    def gathered(c, begin, end):
        for d in range(begin, end):
            for way in (-1, 1):
                z = za + way * d

                @pl.when((z >= 0) & (z < first))
                def _(z=z):
                    g_copy(z, za, 0, c, False).wait_recv()
                    for middle, (target, sources) in relay.items():

                        @pl.when((za == middle) & ((z == sources[0]) | (z == sources[1])))
                        def _(target=target):
                            g_copy(z, target, 0, c, False).start()

    loads[0].wait()
    for c in range(chunks):
        for z in range(first):

            @pl.when(za == z)
            def _(z=z, c=c):
                for slot, target in enumerate(reach[z]):
                    g_copy(za, target, slot, c, True).start()

    own_copy = pltpu.make_async_copy(share_ref, line_ref.at[za], own_sem)
    own_copy.start()

    def through(j, start, count):
        at = slice(start, start + count)
        sums = jnp.zeros((count, width), F32)
        for z in range(first):
            own = slice(z * hidden, (z + 1) * hidden)
            pre = pre_ref[j, at, own]
            activated, tanh = gelu_parts(pre)
            slope = 0.5 * (1.0 + tanh) + 0.5 * pre * (1.0 - tanh * tanh) * INNER * (
                1.0 + 3.0 * CUBIC * pre * pre
            )
            grad_act = lax.dot_general(
                grads[j, at, :], mid_ref[z], last, preferred_element_type=F32
            )
            grad_pre = slope * grad_act
            to = slice(j * tok + start, j * tok + start + count)
            act_turned_ref[own, to] = jnp.transpose(activated).astype(BF16)
            pre_turned_ref[own, to] = jnp.transpose(grad_pre).astype(BF16)
            sums = sums + lax.dot_general(
                grad_pre.astype(BF16), in_ref[z], last, preferred_element_type=F32
            )
        return sums

    for n in range(1, 3):
        loads[n].wait()
    grad_key = jnp.concatenate([slices_ref[n] for n in range(nar)], axis=1).astype(F32)
    normed, inverse = normalise(two_ref[...])
    sums_ref[...] = jnp.zeros_like(sums_ref)
    sums_ref[2:3, :] = jnp.sum(grad_key * normed, axis=0, keepdims=True)
    temper_sum = jnp.sum(stat_ref[0:1, :], axis=1, keepdims=True)
    sums_ref[3:4, :] = jnp.broadcast_to(temper_sum, (1, width))
    sums_ref[4:5, :] = jnp.broadcast_to(stat_ref[1:2, 0:1], (1, width))
    grad = cot_ref[...].astype(F32) + normalise_back(
        grad_key, normed, inverse, gain_key_ref[...]
    )
    grad_two[...] = grad
    grads[0] = grad.astype(BF16)
    for c in range(chunks):
        for j in range(1, second):
            n_copy(j, c).start()
    for n in range(3, 6):
        loads[n].wait()
    total[...] = through(0, 0, tok)
    gathered(0, 1, 2)
    for c in range(chunks):
        for j in range(1, second):
            n_copy(j, c).wait_recv()
            back_out[j, c * part : (c + 1) * part, :] = through(j, c * part, part).astype(BF16)
            b_copy(j, c).start()
    gathered(0, 2, first)
    gathered(1, 1, first)
    for n in range(6, 10):
        loads[n].wait()
    for j in range(second):
        for w in range(wid):
            own = slice(w * columns, (w + 1) * columns)
            normed_cols_ref[w, j * tok : (j + 1) * tok, :] = normed_ref[j, :, own]
            ffn_cols_ref[w, j * tok : (j + 1) * tok, :] = grads[j, :, own]
    att_turned_ref[...] = jnp.concatenate(
        [jnp.transpose(att_ref[n].astype(F32)).astype(BF16) for n in range(nar)], axis=0
    )
    for n in range(5):
        stores[n].start()
    for c in range(chunks):
        at = slice(c * part, (c + 1) * part)
        for j in range(1, second):
            b_copy(j, c).wait_recv()
            total[at, :] += back_in[j, at, :].astype(F32)
    normed, inverse = normalise(one_ref[...])
    sums_ref[1:2, :] = jnp.sum(total[...] * normed, axis=0, keepdims=True)
    grad = grad_two[...] + normalise_back(total[...], normed, inverse, gain_two_ref[...])
    branch = grad.astype(BF16)
    grad_att = lax.dot_general(
        branch, proj_ref[...].reshape(nar * local, width), last, preferred_element_type=F32
    ).astype(BF16)
    for n in range(nar):
        grad_att_ref[n] = grad_att[:, n * local : (n + 1) * local]
    stores[5].start()
    for w in range(wid):
        branch_cols_ref[w] = branch[:, w * columns : (w + 1) * columns]
    stores[6].start()
    grad_one_ref[...] = grad
    stores[7].start()
    own_copy.wait()
    for c in range(chunks):
        for j in range(1, second):
            n_copy(j, c).wait_send()
            b_copy(j, c).wait_send()
        for z in range(first):

            @pl.when(za == z)
            def _(z=z, c=c):
                for slot, target in enumerate(reach[z]):
                    g_copy(za, target, slot, c, True).wait_send()
                if z in relay:
                    target, sources = relay[z]
                    for n in sources:
                        g_copy(n, target, 0, c, False).wait_send()

    for store in stores:
        store.wait()


def ffn_back(
    gain_two,
    gain_key,
    slices,
    stats,
    two,
    cot,
    out_all,
    pre,
    in_all,
    att,
    normed,
    one,
    pq,
    share,
    wid,
    name,
):
    nar, tok, local = att.shape
    first, width, hidden = in_all.shape
    second = nar // first
    chunks = 2
    columns = width // wid
    vmem = pl.BlockSpec(memory_space=pltpu.VMEM)
    hbm = pl.BlockSpec(memory_space=pl.ANY)
    dma = pltpu.SemaphoreType.DMA
    outs = (
        ((tok, width), F32),
        ((nar, tok, local), BF16),
        ((first * hidden, second * tok), BF16),
        ((first * hidden, second * tok), BF16),
        ((nar * local, tok), BF16),
        ((wid, second * tok, columns), BF16),
        ((wid, second * tok, columns), BF16),
        ((wid, tok, columns), BF16),
    )
    return pl.pallas_call(
        functools.partial(ffn_back_kernel, chunks),
        out_shape=(jax.ShapeDtypeStruct((8, width), F32),)
        + tuple(jax.ShapeDtypeStruct(*x) for x in outs)
        + (jax.ShapeDtypeStruct((first, tok, width), BF16),),
        in_specs=[vmem] * 4 + [hbm] * 10,
        out_specs=(vmem,) + (hbm,) * 9,
        scratch_shapes=[
            pltpu.VMEM((tok, width), F32),
            pltpu.VMEM((tok, width), BF16),
            pltpu.VMEM(out_all.shape, BF16),
            pltpu.VMEM(pre.shape, F32),
            pltpu.VMEM(in_all.shape, BF16),
            pltpu.VMEM(att.shape, BF16),
            pltpu.VMEM(normed.shape, BF16),
            pltpu.VMEM((tok, width), F32),
            pltpu.VMEM((nar, local, width), BF16),
            pltpu.VMEM((tok, width), BF16),
        ]
        + [pltpu.VMEM(*x) for x in outs]
        + [
            pltpu.VMEM((second, tok, width), BF16),
            pltpu.VMEM((tok, width), F32),
            pltpu.VMEM((tok, width), F32),
            pltpu.VMEM((second, tok, width), BF16),
            pltpu.VMEM((second, tok, width), BF16),
            dma((10,)),
            dma((8,)),
            dma,
        ]
        + [dma((second, chunks))] * 4
        + [dma((first, 3, chunks)), dma((first, chunks))],
        compiler_params=pltpu.CompilerParams(
            collective_id=name, has_side_effects=True, vmem_limit_bytes=62 * 2**20
        ),
    )(
        gain_two,
        gain_key,
        slices,
        stats,
        two,
        cot,
        out_all,
        pre,
        in_all,
        att,
        normed,
        one,
        pq,
        share,
    )


def finish_kernel(
    second, grad_ref, block_ref, line_ref, total_ref, loss_ref, qkv_ref, proj_ref, in_ref, mid_ref, *outs
):
    (
        block_out,
        loss_out,
        grad_out,
        query_out,
        key_out,
        value_out,
        proj_out,
        in_out,
        mid_out,
        attn_out,
        ffn_out,
        last_out,
        temper_out,
        mix_out,
    ) = outs
    grad_out[...] = grad_ref[...].astype(F32)
    for j in range(second):

        @pl.when(lax.axis_index("y") == j)
        def _(j=j):
            block_out[j] = line_ref[0]

        @pl.when(lax.axis_index("y") != j)
        def _(j=j):
            block_out[j] = block_ref[j]

    @pl.when(pl.program_id(0) == 0)
    def _():
        local = proj_ref.shape[0]
        query_out[...] = qkv_ref[0:local, :]
        key_out[...] = qkv_ref[local : 2 * local, :]
        value_out[...] = qkv_ref[2 * local : 3 * local, :]
        proj_out[...] = proj_ref[...]
        in_out[...] = in_ref[...]
        mid_out[...] = mid_ref[...]
        attn_out[...] = total_ref[0:1, :]
        ffn_out[...] = total_ref[1:2, :]
        last_out[...] = total_ref[2:3, :]
        temper_out[...] = total_ref[3:4, 0:1]
        mix_out[...] = total_ref[4:5, 0:1]
        nar, _, tok = loss_ref.shape
        seqs = loss_out.shape[0]
        per_seq = nar // seqs
        for n in range(nar):
            at = (n % per_seq) * tok
            loss_out[n // per_seq : n // per_seq + 1, at : at + tok] = loss_ref[n, 0:1, :]


def finish(grad, block, lines, totals, losses, qkv, proj, w_in, w_out, seqs):
    nar, tok, width = grad.shape
    second = nar // lines.shape[0]
    local, piece = proj.shape

    def whole(shape):
        return pl.BlockSpec(shape, lambda i: (0,) * len(shape))

    def each():
        return pl.BlockSpec((second, tok, width), lambda i: (i, 0, 0))

    small = [
        ((local, piece), F32),
        ((local, piece), F32),
        ((local, piece), F32),
        (proj.shape, F32),
        (w_in.shape, F32),
        (w_out.shape, F32),
        ((1, piece), F32),
        ((1, piece), F32),
        ((1, piece), F32),
        ((1, 1), F32),
        ((1, 1), F32),
    ]
    loss_shape = (seqs, nar * tok // seqs)
    return pl.pallas_call(
        functools.partial(finish_kernel, second),
        grid=(nar // second,),
        out_shape=(
            jax.ShapeDtypeStruct((nar, tok, width), BF16),
            jax.ShapeDtypeStruct(loss_shape, F32),
            jax.ShapeDtypeStruct((nar, tok, width), F32),
        )
        + tuple(jax.ShapeDtypeStruct(*x) for x in small),
        in_specs=[each(), each(), pl.BlockSpec((1, tok, width), lambda i: (i, 0, 0))]
        + [whole(x.shape) for x in (totals, losses, qkv, proj, w_in, w_out)],
        out_specs=(each(), whole(loss_shape), each()) + tuple(whole(x[0]) for x in small),
        compiler_params=pltpu.CompilerParams(vmem_limit_bytes=62 * 2**20),
    )(grad, block, lines, totals, losses, qkv, proj, w_in, w_out)


REACH = ((1, 2), (0, 2), (1, 3), (2, 1))
RELAY = {1: (0, (2, 3)), 2: (3, (0, 1))}


def segment_column(seg_ref, seq, start, block):
    row = seg_ref[pl.ds(seq, 1), start : start + block].astype(F32)
    return jnp.transpose(jnp.broadcast_to(row, (8, block)))[:, 0:1]


def grad_kernel(
    nar,
    first,
    wid,
    seqs,
    heads,
    block,
    chunks,
    seg_ref,
    gain_ref,
    sums_ref,
    grad_ref,
    line_any,
    pre_any,
    act_any,
    att_any,
    normed_any,
    ffn_any,
    branch_any,
    qkv_any,
    lse_any,
    one_any,
    input_any,
    above_any,
    pq_any,
    all_ref,
    block_ref,
    total_ref,
    in_grad_ref,
    out_grad_ref,
    proj_grad_ref,
    qkv_grad_ref,
    pre_ref,
    act_ref,
    att_ref,
    normed_ref,
    ffn_ref,
    branch_ref,
    qkv_ref,
    lse_ref,
    one_ref,
    input_ref,
    above_ref,
    pq_ref,
    load_sem,
    out_ref,
    grads,
    got,
    grad_key,
    grad_value,
    core_out,
    core_in,
    chip_out,
    chip_in,
    tail_sum,
    turn_out,
    turn_in,
    line_in,
    work,
    qkv_out,
    qkv_in,
    own_ref,
    own_sums,
    all_sums,
    pieces_out,
    pieces_in,
    own_sem,
    k_send,
    k_recv,
    a_send,
    a_recv,
    b_send,
    b_recv,
    c_send,
    c_recv,
    x_send,
    x_recv,
    y_send,
    y_recv,
    z_send,
    z_recv,
    w_send,
    w_recv,
    g_send,
    g_recv,
    h_send,
    h_recv,
    s_send,
    s_recv,
    p_send,
    p_recv,
):
    second = nar // first
    outer = wid // 2
    za, yb = lax.axis_index("z"), lax.axis_index("y")
    me = za * second + yb
    wide = lax.axis_index("wide")
    chip, core = wide // 2, lax.rem(wide, 2)
    tok, local = grads.shape[1:]
    hidden = pre_ref.shape[0] // first
    columns = normed_ref.shape[2]
    rows = 2 * hidden
    body = first * rows
    line = rows + local
    length = nar * tok // seqs
    per_seq = nar // seqs
    width = heads * HD
    part = tok // chunks
    across = (((0,), (0,)), ((), ()))
    last = (((1,), (1,)), ((), ()))
    reach, relay = REACH, RELAY

    pairs = (
        (pre_any, pre_ref),
        (act_any, act_ref),
        (att_any, att_ref),
        (normed_any, normed_ref),
        (ffn_any, ffn_ref),
        (branch_any, branch_ref),
        (qkv_any, qkv_ref),
        (lse_any, lse_ref),
        (one_any, one_ref),
        (input_any.at[own_rows(tok, second)], input_ref),
        (above_any, above_ref),
        (pq_any, pq_ref),
    )
    loads = [
        pltpu.make_async_copy(src, dst, load_sem.at[n]) for n, (src, dst) in enumerate(pairs)
    ]
    for load in loads:
        load.start()

    greet(
        [place(lax.rem(me + k, nar), second) for k in range(1, nar)]
        + [{"wide": lax.rem(wide + w, wid)} for w in range(1, wid)]
    )

    def a_copy(target, source):
        return push(
            grad_ref.at[target],
            grads.at[source],
            a_send.at[target],
            a_recv.at[source],
            place(target, second),
        )

    def b_copy(target, source):
        return push(
            out_ref.at[pl.ds(pl.multiple_of(target * tok, tok), tok)],
            got.at[source],
            b_send.at[target],
            b_recv.at[source],
            place(target, second),
        )

    def k_copy(z, j):
        return push(
            line_any.at[z],
            block_ref.at[z * second + yb],
            k_send.at[z, j],
            k_recv.at[z, j],
            {"z": za, "y": lax.rem(yb + j, second)},
        )

    def c_copy(o):
        return push(
            core_out.at[o],
            core_in.at[o],
            c_send.at[o],
            c_recv.at[o],
            {"wide": chip * 2 + (1 - core)},
        )

    def span(z):
        return pl.ds(pl.multiple_of(z * rows, rows), rows)

    tail_rows = pl.ds(body, nar * local)

    def x_copy(i, q, at):
        return push(
            chip_out.at[i - 1, at],
            chip_in.at[i - 1, at],
            x_send.at[i, q],
            x_recv.at[i, q],
            {"wide": lax.rem(chip + i, outer) * 2 + core},
        )

    def y_copy(j):
        target = {"z": za, "y": lax.rem(yb + j, second)}
        return push(turn_out.at[j], turn_in.at[j], y_send.at[j], y_recv.at[j], target)

    inner = jnp.where((za == 1) | (za == 2), 1, 0)

    def mirror(z):
        return jnp.where(za < 2, z, 3 - z)

    def dest(n):
        return mirror(jnp.where(n == 1, 3, jnp.where(n == 2, 2, jnp.where(n == 3, 1 - inner, inner))))

    def z_copy(n):
        slot = jnp.where(inner == 1, (3, 4, 0)[n - 1], n - 1)
        target = mirror(jnp.where(inner == 1, (2, 2, 0)[n - 1], 1))
        return push(
            core_out.at[0, pl.ds((n - 1) * line, line)],
            line_in.at[slot],
            z_send.at[n],
            z_recv.at[slot],
            {"z": target, "y": yb},
        )

    def z_arrival(slot):
        return push(
            core_out.at[0, pl.ds(0, line)],
            line_in.at[slot],
            z_send.at[0],
            z_recv.at[slot],
            {"z": mirror(jnp.where(inner == 1, 0, 1)), "y": yb},
        )

    def w_copy(i):
        target = lax.rem(wide + i, wid)
        return push(
            qkv_out.at[target], qkv_in.at[i], w_send.at[i], w_recv.at[i], {"wide": target}
        )

    def g_copy(source_z, target_z, slot, c, own):
        at = pl.ds(c * part, part)
        source = source_z * second + yb
        return push(
            own_ref.at[at] if own else all_ref.at[source, at],
            all_ref.at[source, at],
            g_send.at[source_z, slot, c],
            g_recv.at[source_z, c],
            {"z": target_z, "y": yb},
        )

    def h_copy(source_z, j, c, own):
        at = pl.ds(c * part, part)
        source = source_z * second + yb
        return push(
            own_ref.at[at] if own else all_ref.at[source, at],
            all_ref.at[source, at],
            h_send.at[source_z, j, c],
            h_recv.at[source_z, j, c],
            {"z": za, "y": lax.rem(yb + j, second)},
        )

    def h_arrival(source_z, j, c):
        at = pl.ds(c * part, part)
        source = source_z * second + lax.rem(yb + second - j, second)
        return push(
            all_ref.at[source, at],
            all_ref.at[source, at],
            h_send.at[source_z, j, c],
            h_recv.at[source_z, j, c],
            {"z": za, "y": lax.rem(yb + j, second)},
        )

    def s_copy(k):
        target = place(lax.rem(me + k, nar), second)
        return push(own_sums, all_sums.at[k], s_send.at[k], s_recv.at[k], target)

    def p_copy(w):
        target = lax.rem(wide + w, wid)
        return push(
            pieces_out.at[target], pieces_in.at[w], p_send.at[w], p_recv.at[w], {"wide": target}
        )

    def product_rows(w, z):
        own = pl.ds(pl.multiple_of(z * hidden, hidden), hidden)
        return (
            jnp.dot(pre_ref[own, :], normed_ref[w], preferred_element_type=F32),
            jnp.dot(act_ref[own, :], ffn_ref[w], preferred_element_type=F32),
        )

    def product_tail(w):
        return jnp.dot(att_ref[...], branch_ref[w], preferred_element_type=F32)

    for k in range(1, nar):
        a_copy(lax.rem(me + k, nar), me).start()
    own_grad = pltpu.make_async_copy(grad_ref.at[me], grads.at[me], own_sem.at[1])
    own_grad.start()
    for z in range(2):
        for j in range(1, second):
            k_copy(z, j).start()
    for n in range(6):
        loads[n].wait()

    for i in range(1, outer + 1):
        o = lax.rem(chip + i, outer)
        w = o * 2 + (1 - core)

        def for_core(z, carry, o=o, w=w):
            upper, lower = product_rows(w, z)
            at = pl.multiple_of(z * rows, rows)
            core_out[o, pl.ds(at, hidden), :] = upper.astype(BF16)
            core_out[o, pl.ds(at + hidden, hidden), :] = lower.astype(BF16)
            return carry

        lax.fori_loop(0, first, for_core, 0)
        core_out[o, tail_rows, :] = product_tail(w).astype(BF16)
        c_copy(o).start()

    loads[6].wait()
    loads[7].wait()
    own_grad.wait()

    def sequence(seq, carry):
        base = seq * length

        def arrive(b, c):
            source = seq * per_seq + b

            @pl.when(source != me)
            def _():
                a_copy(source, source).wait_recv()

            return c

        lax.fori_loop(0, per_seq, arrive, 0)
        grad_key[...] = jnp.zeros_like(grad_key)
        grad_value[...] = jnp.zeros_like(grad_value)
        for start in range(0, length, block):
            keys = start + block
            at = pl.multiple_of(base + start, block)
            query_segment = segment_column(seg_ref, seq, start, block)
            key_segment = seg_ref[pl.ds(seq, 1), 0:keys].astype(F32)
            spot = lax.broadcasted_iota(jnp.int32, (block, keys), 1)
            own = lax.broadcasted_iota(jnp.int32, (block, keys), 0) + start
            allowed = (spot <= own) & (query_segment == key_segment)
            whole = pl.ds(pl.multiple_of(base, length), keys)
            query = qkv_ref[pl.ds(at, block), 0:width]
            key = qkv_ref[whole, width : 2 * width]
            value = qkv_ref[whole, 2 * width : 3 * width]
            each = min(tok, block)
            grad = jnp.concatenate(
                [
                    grads[
                        seq * per_seq + (start + r) // tok,
                        (start + r) % tok : (start + r) % tok + each,
                        :,
                    ]
                    for r in range(0, block, each)
                ],
                axis=0,
            )
            total = jnp.zeros((block, width), F32)
            for head in range(heads):
                own_query = head_lanes(query, head)
                own_grad = head_lanes(grad, head)
                scores = lax.dot_general(own_query, key, last, preferred_element_type=F32)
                probs = jnp.where(
                    allowed, jnp.exp(scores - lse_ref[pl.ds(at, block), head : head + 1]), 0.0
                )
                grad_probs = lax.dot_general(own_grad, value, last, preferred_element_type=F32)
                delta = jnp.sum(probs * grad_probs, axis=-1, keepdims=True)
                grad_scores = (probs * (grad_probs - delta)).astype(BF16)
                total = total + head_lanes(
                    jnp.dot(grad_scores, key, preferred_element_type=F32), head
                )
                grad_key[0:keys, :] += lax.dot_general(
                    grad_scores, own_query, across, preferred_element_type=F32
                )
                grad_value[0:keys, :] += lax.dot_general(
                    probs.astype(BF16), own_grad, across, preferred_element_type=F32
                )
            out_ref[pl.ds(at, block), 0:width] = (total * HD ** (-0.5)).astype(BF16)
        every = pl.ds(pl.multiple_of(base, length), length)
        out_ref[every, width : 2 * width] = grad_key[...].astype(BF16)
        out_ref[every, 2 * width : 3 * width] = grad_value[...].astype(BF16)

        def leave(b, c):
            target = seq * per_seq + b

            @pl.when(target != me)
            def _():
                b_copy(target, me).start()

            return c

        lax.fori_loop(0, per_seq, leave, 0)
        return carry

    lax.fori_loop(0, seqs, sequence, 0)

    for i in range(1, outer):
        o = lax.rem(chip + i, outer)
        w = o * 2 + core
        c_copy(o).wait_recv()
        total = product_tail(w) + core_in[o, tail_rows, :].astype(F32)
        chip_out[i - 1, tail_rows, :] = total.astype(BF16)
        x_copy(i, 0, tail_rows).start()

        def for_chip(n, carry, o=o, w=w, i=i):
            z = dest(n)
            upper, lower = product_rows(w, z)
            at = pl.multiple_of(z * rows, rows)
            high, low = pl.ds(at, hidden), pl.ds(at + hidden, hidden)
            chip_out[i - 1, high, :] = (upper + core_in[o, high, :].astype(F32)).astype(BF16)
            chip_out[i - 1, low, :] = (lower + core_in[o, low, :].astype(F32)).astype(BF16)
            x_copy(i, n, span(z)).start()
            return carry

        lax.fori_loop(1, first + 1, for_chip, 0)

    for z in range(2, first):
        for j in range(1, second):
            k_copy(z, j).start()
    loads[8].wait()
    qkv_part = lax.dot_general(
        out_ref[...], one_ref[...], across, preferred_element_type=F32
    ).astype(BF16)
    for w in range(wid):
        qkv_out[w] = qkv_part[:, w * columns : (w + 1) * columns]
    for i in range(1, wid):
        w_copy(i).start()

    w_own = chip * 2 + core
    c_copy(chip).wait_recv()
    tail_sum[...] = product_tail(w_own) + core_in[chip, tail_rows, :].astype(F32)
    for i in range(1, outer):
        x_copy(i, 0, tail_rows).wait_recv()
        tail_sum[...] += chip_in[i - 1, tail_rows, :].astype(F32)
    for j in range(1, second):
        column = lax.rem(yb + j, second)
        for z in range(first):
            at = pl.ds(pl.multiple_of((z * second + column) * local, local), local)
            turn_out[j, z] = tail_sum[at, :].astype(BF16)
        y_copy(j).start()

    for n in range(9, 12):
        loads[n].wait()
    normed, inverse = normalise(input_ref[...].astype(F32))
    mine = out_ref[pl.ds(pl.multiple_of(me * tok, tok), tok), :]
    total = jnp.dot(mine, pq_ref[me, local:, :], preferred_element_type=F32)
    for k in range(1, nar):
        source = lax.rem(me + k, nar)
        b_copy(source, source).wait_recv()
        total = total + jnp.dot(
            got[source], pq_ref[source, local:, :], preferred_element_type=F32
        )
    grad = above_ref[...] + normalise_back(total, normed, inverse, gain_ref[0:1, :])
    own_ref[...] = grad.astype(BF16)

    for c in range(chunks):
        for z in range(first):

            @pl.when(za == z)
            def _(z=z, c=c):
                for slot, target in enumerate(reach[z]):
                    g_copy(za, target, slot, c, True).start()

        for j in range(1, second):
            h_copy(za, j, c, True).start()
    own_copy = pltpu.make_async_copy(own_ref, all_ref.at[me], own_sem.at[0])
    own_copy.start()
    own_sums[...] = sums_ref[...]
    own_sums[0:1, :] = jnp.sum(total * normed, axis=0, keepdims=True)
    for k in range(1, nar):
        s_copy(k).start()

    def gathered(begin, end):
        for c in range(chunks):
            for d in range(begin, end):
                for way in (-1, 1):
                    z = za + way * d

                    @pl.when((z >= 0) & (z < first))
                    def _(z=z, c=c):
                        g_copy(z, za, 0, c, False).wait_recv()
                        for middle, (target, sources) in relay.items():

                            @pl.when((za == middle) & ((z == sources[0]) | (z == sources[1])))
                            def _(target=target):
                                g_copy(z, target, 0, c, False).start()

                        for j in range(1, second):
                            h_copy(z, j, c, False).start()

    for o in range(outer):
        c_copy(o).wait_send()
    for j in range(1, second):
        y_copy(j).wait_recv()

    def line_parts(n):
        z = dest(n)
        at = pl.ds(pl.multiple_of((z * second + yb) * local, local), local)
        low_part = tail_sum[at, :]
        for j in range(1, second):
            low_part = low_part + turn_in[j, z].astype(F32)
        upper, lower = product_rows(w_own, z)
        start = pl.multiple_of(z * rows, rows)
        high, low = pl.ds(start, hidden), pl.ds(start + hidden, hidden)
        upper = upper + core_in[chip, high, :].astype(F32)
        lower = lower + core_in[chip, low, :].astype(F32)
        for i in range(1, outer):
            x_copy(i, n, span(z)).wait_recv()
            upper = upper + chip_in[i - 1, high, :].astype(F32)
            lower = lower + chip_in[i - 1, low, :].astype(F32)
        work[0:hidden, :] = upper
        work[hidden:rows, :] = lower
        work[rows:, :] = low_part

    def add_arrival(slot):
        z_arrival(slot).wait_recv()
        work[...] += line_in[slot].astype(F32)

    @pl.when(inner == 0)
    def _():
        for n in range(1, 4):
            line_parts(n)
            core_out[0, (n - 1) * line : n * line, :] = work[...].astype(BF16)
            z_copy(n).start()

    gathered(1, 2)
    gathered(2, first)

    @pl.when(inner == 1)
    def _():
        for n in range(1, 4):
            line_parts(n)
            add_arrival((0, 1, 3)[n - 1])
            core_out[0, (n - 1) * line : n * line, :] = work[...].astype(BF16)
            z_copy(n).start()

    line_parts(4)
    sums = own_sums[...]
    for k in range(1, nar):
        s_copy(k).wait_recv()
        sums = sums + all_sums[k]
    piece = total_ref.shape[1]
    for w in range(wid):
        pieces_out[w] = sums[:, w * piece : (w + 1) * piece]
    for w in range(1, wid):
        p_copy(w).start()
    qkv_sum = qkv_out[wide].astype(F32)
    for i in range(1, wid):
        w_copy(i).wait_recv()
        qkv_sum = qkv_sum + qkv_in[i].astype(F32)
    qkv_grad_ref[...] = qkv_sum

    @pl.when(inner == 0)
    def _():
        add_arrival(0)

    @pl.when(inner == 1)
    def _():
        add_arrival(2)
        add_arrival(4)

    in_grad_ref[...] = jnp.transpose(work[0:hidden, :])
    out_grad_ref[...] = work[hidden:rows, :]
    proj_grad_ref[...] = work[rows:, :]
    answer = pieces_out[wide]
    for w in range(1, wid):
        p_copy(w).wait_recv()
        answer = answer + pieces_in[w]
    total_ref[...] = answer

    for z in range(first):
        for j in range(1, second):
            for c in range(chunks):
                h_arrival(z, j, c).wait_recv()
    own_copy.wait()
    for z in range(first):
        for j in range(1, second):
            k_copy(z, j).wait()
    for k in range(1, nar):
        a_copy(lax.rem(me + k, nar), me).wait_send()
        b_copy(lax.rem(me + k, nar), me).wait_send()
        s_copy(k).wait_send()
    for w in range(1, wid):
        p_copy(w).wait_send()
        w_copy(w).wait_send()
    for i in range(1, outer):
        x_copy(i, 0, tail_rows).wait_send()
        for n in range(1, first + 1):
            x_copy(i, n, span(dest(n))).wait_send()
    for j in range(1, second):
        y_copy(j).wait_send()
    for n in range(1, first):
        z_copy(n).wait_send()
    for c in range(chunks):
        for z in range(first):

            @pl.when(za == z)
            def _(z=z, c=c):
                for slot, target in enumerate(reach[z]):
                    g_copy(za, target, slot, c, True).wait_send()
                if z in relay:
                    target, sources = relay[z]
                    for n in sources:
                        g_copy(n, target, 0, c, False).wait_send()

            for j in range(1, second):
                h_copy(z, j, c, False).wait_send()


def attention_grads(
    seg, gain, sums, grads, lines, sides, qkv, lse, one, inputs, above, pq, first, wid, name
):
    nar, tok, local = grads.shape
    rows, wide = qkv.shape
    width = inputs.shape[1]
    seqs, length = seg.shape
    second = nar // first
    outer = wid // 2
    hidden = sides[0].shape[0] // first
    piece = width // wid
    body = first * 2 * hidden + nar * local
    line = 2 * hidden + local
    chunks = 2
    vmem = pl.BlockSpec(memory_space=pltpu.VMEM)
    hbm = pl.BlockSpec(memory_space=pl.ANY)
    dma = pltpu.SemaphoreType.DMA
    late = (*sides, qkv, lse, one, inputs, above, pq)
    return pl.pallas_call(
        functools.partial(
            grad_kernel, nar, first, wid, seqs, local // HD, min(256, length), chunks
        ),
        out_shape=(
            jax.ShapeDtypeStruct((nar, tok, width), BF16),
            jax.ShapeDtypeStruct((nar, tok, width), BF16),
            jax.ShapeDtypeStruct((8, piece), F32),
            jax.ShapeDtypeStruct((piece, hidden), F32),
            jax.ShapeDtypeStruct((hidden, piece), F32),
            jax.ShapeDtypeStruct((local, piece), F32),
            jax.ShapeDtypeStruct((3 * local, piece), F32),
        ),
        in_specs=[vmem] * 3 + [hbm] * 14,
        out_specs=(hbm, hbm) + (vmem,) * 5,
        scratch_shapes=[
            pltpu.VMEM((tok, width) if x is inputs else x.shape, x.dtype) for x in late
        ]
        + [
            dma((12,)),
            pltpu.VMEM((rows, wide), BF16),
            pltpu.VMEM((nar, tok, local), BF16),
            pltpu.VMEM((nar, tok, wide), BF16),
            pltpu.VMEM((length, local), F32),
            pltpu.VMEM((length, local), F32),
            pltpu.VMEM((outer, body, piece), BF16),
            pltpu.VMEM((outer, body, piece), BF16),
            pltpu.VMEM((outer - 1, body, piece), BF16),
            pltpu.VMEM((outer - 1, body, piece), BF16),
            pltpu.VMEM((nar * local, piece), F32),
            pltpu.VMEM((second, first, local, piece), BF16),
            pltpu.VMEM((second, first, local, piece), BF16),
            pltpu.VMEM((5, line, piece), BF16),
            pltpu.VMEM((line, piece), F32),
            pltpu.VMEM((wid, 3 * local, piece), BF16),
            pltpu.VMEM((wid, 3 * local, piece), BF16),
            pltpu.VMEM((tok, width), BF16),
            pltpu.VMEM((8, width), F32),
            pltpu.VMEM((nar, 8, width), F32),
            pltpu.VMEM((wid, 8, piece), F32),
            pltpu.VMEM((wid, 8, piece), F32),
            dma((2,)),
            dma((first, second)),
            dma((first, second)),
            dma((nar,)),
            dma((nar,)),
            dma((nar,)),
            dma((nar,)),
            dma((outer,)),
            dma((outer,)),
            dma((outer, first + 1)),
            dma((outer, first + 1)),
            dma((second,)),
            dma((second,)),
            dma((first,)),
            dma((5,)),
            dma((wid,)),
            dma((wid,)),
            dma((first, 3, chunks)),
            dma((first, chunks)),
            dma((first, second, chunks)),
            dma((first, second, chunks)),
            dma((nar,)),
            dma((nar,)),
            dma((wid,)),
            dma((wid,)),
        ],
        compiler_params=pltpu.CompilerParams(
            collective_id=name, has_side_effects=True, vmem_limit_bytes=63 * 2**20
        ),
    )(seg, gain, sums, grads, lines, *late)


def neighbour_kernel(
    nar,
    first,
    tiles,
    tile,
    kept,
    ring,
    count_ref,
    target_ref,
    base_ref,
    weight_ref,
    temper_ref,
    mix_ref,
    query_ref,
    keys_ref,
    norms_any,
    ids_any,
    grad_ref,
    loss_ref,
    stat_ref,
    queries,
    partial,
    dist,
    grads,
    sends,
    slots,
    loss_own,
    norms_ref,
    ids_ref,
    load_sem,
    slot_sem,
    q_send,
    q_recv,
    d_send,
    d_recv,
    g_send,
    g_recv,
    l_send,
    l_recv,
    o_send,
    o_recv,
):
    second = nar // first
    me = lax.axis_index("z") * second + lax.axis_index("y")
    tok = query_ref.shape[1]
    depth = query_ref.shape[2]
    group = 16
    per_block = tok // tile
    late = tiles - kept

    def peer(k):
        return lax.rem(me + k, nar)

    def origin(k):
        return lax.rem(me + nar - k, nar)

    def load(index, slot):
        block, sub = index // per_block, lax.rem(index, per_block)
        row = origin(block) * tok + sub * tile
        return pltpu.make_async_copy(
            keys_ref.at[pl.ds(row, tile)], slots.at[slot], slot_sem.at[slot]
        )

    loads = [
        pltpu.make_async_copy(norms_any, norms_ref, load_sem.at[0]),
        pltpu.make_async_copy(query_ref.at[me], queries.at[0], load_sem.at[1]),
        pltpu.make_async_copy(ids_any.at[own_rows(tok, second)], ids_ref, load_sem.at[2]),
    ]
    for n in range(3):
        loads[n].start()
    for i in range(kept + ring):
        load(i, i).start()

    greet([place(peer(k), second) for k in range(1, nar)])

    def q_copy(k):
        return push(
            query_ref.at[peer(k)],
            queries.at[k],
            q_send.at[k],
            q_recv.at[k],
            place(peer(k), second),
        )

    def d_copy(k):
        return push(
            partial.at[k], dist.at[k], d_send.at[k], d_recv.at[k], place(origin(k), second)
        )

    def g_copy(k):
        return push(
            grads.at[0], grads.at[k], g_send.at[k], g_recv.at[k], place(peer(k), second)
        )

    def l_copy(k):
        return push(
            loss_own, loss_ref.at[me], l_send.at[k], l_recv.at[k], place(peer(k), second)
        )

    def o_copy(k):
        return push(
            sends.at[k], grad_ref.at[me], o_send.at[k], o_recv.at[k], place(origin(k), second)
        )

    for k in range(1, nar):
        q_copy(k).start()
    for n in range(3):
        loads[n].wait()

    row_of = lax.broadcasted_iota(jnp.int32, (group, J), 0)

    def slot_of(index):
        return jnp.where(index < kept, index, kept + lax.rem(index - kept, ring))

    def slot_late(n):
        return kept + lax.rem(n, ring)

    def forward_tile(k, sub, slot):
        def one(g, carry):
            at = pl.multiple_of(sub * tile + g * group, group)
            own = queries[k, pl.ds(at, group), :].astype(F32)
            keys = slots[slot, pl.ds(g * group, group), :, :].reshape(group * depth, J)
            wide = jnp.concatenate(
                [jnp.where(row_of[:, :depth] == t, own, 0.0) for t in range(group)], axis=1
            ).astype(BF16)
            out = jnp.dot(wide, keys, preferred_element_type=F32)
            row = pl.multiple_of(origin(k) * tok + at, group)
            partial[k, pl.ds(at, group), :] = 2.0 * out - norms_ref[pl.ds(row, group), :]
            return carry

        lax.fori_loop(0, tile // group, one, 0, unroll=True)

    def forward_block(k):
        def body(sub, carry):
            index = k * per_block + sub
            slot = slot_of(index)
            load(index, slot).wait()
            forward_tile(k, sub, slot)

            @pl.when(index >= kept)
            def _():
                nxt = index - kept + ring

                @pl.when(nxt < 2 * late)
                def _():
                    load(kept + lax.rem(nxt, late), slot).start()

            return carry

        lax.fori_loop(0, per_block, body, 0)

    forward_block(0)

    def forward_rest(k, carry):
        q_copy(k).wait_recv()
        forward_block(k)
        d_copy(k).start()
        return carry

    lax.fori_loop(1, nar, forward_rest, 0)

    def collect(k, total):
        d_copy(k).wait_recv()
        return total + dist[k]

    distance = lax.fori_loop(1, nar, collect, partial[0])
    temper_value = temper_ref[0]
    mix_value = mix_ref[0]
    per_seq = count_ref.shape[1] // tok

    def own_column(ref):
        row = jnp.zeros((1, tok), F32)
        for n in range(nar):
            at = (n % per_seq) * tok
            seq = n // per_seq
            row = jnp.where(me == n, ref[seq : seq + 1, at : at + tok].astype(F32), row)
        return jnp.transpose(jnp.broadcast_to(row, (8, tok)))[:, 0:1]

    count = own_column(count_ref)
    target = own_column(target_ref)
    base = own_column(base_ref)
    loss_weight = own_column(weight_ref)
    logits = distance / temper_value
    spot = lax.broadcasted_iota(jnp.int32, (tok, J), 1).astype(F32)
    masked = jnp.where(spot < count, logits, -1e30)
    peak = jnp.max(masked, axis=-1, keepdims=True)
    expo = jnp.exp(masked - peak)
    weights = expo / jnp.sum(expo, axis=-1, keepdims=True)
    matches = jnp.where(ids_ref[...].astype(F32) == target, 1.0, 0.0)
    knn_prob = jnp.sum(weights * matches, axis=-1, keepdims=True)
    mixture = mix_value * knn_prob + (1.0 - mix_value) * base
    grad_mixture = -loss_weight / mixture
    grad_logits = weights * (mix_value * grad_mixture) * (matches - knn_prob)
    grads[0] = (2.0 * grad_logits / temper_value).astype(BF16)
    for k in range(1, nar):
        g_copy(k).start()
    loss = jnp.transpose(jnp.broadcast_to(-jnp.log(mixture), (tok, J)))[0:8, :]
    loss_own[...] = loss
    for k in range(1, nar):
        l_copy(k).start()
    loss_ref[me] = loss
    term_temper = -jnp.sum(grad_logits * logits, axis=0, keepdims=True) / temper_value
    term_mix = jnp.sum((knn_prob - base) * grad_mixture, axis=0, keepdims=True)
    stat_ref[0:1, :] = term_temper
    stat_ref[1:2, :] = jnp.broadcast_to(term_mix, (1, J))

    def backward_tile(k, sub, slot):
        def one(g, carry):
            at = pl.multiple_of(sub * tile + g * group, group)
            own = grads[k, pl.ds(at, group), :]
            keys = slots[slot, pl.ds(g * group, group), :, :].reshape(group * depth, J)
            out = lax.dot_general(
                own, keys, (((1,), (1,)), ((), ())), preferred_element_type=F32
            )
            total = jnp.zeros((group, depth), F32)
            for t in range(group):
                total = jnp.where(
                    row_of[:, :depth] == t, out[:, t * depth : (t + 1) * depth], total
                )
            sends[k, pl.ds(at, group), :] = total.astype(BF16)
            return carry

        lax.fori_loop(0, tile // group, one, 0, unroll=True)

    def backward_block(k):
        def body(sub, carry):
            index = k * per_block + sub

            @pl.when(index < kept)
            def _():
                backward_tile(k, sub, index)

            @pl.when(index >= kept)
            def _():
                n = index - kept + late
                slot = slot_late(n)
                load(index, slot).wait()
                backward_tile(k, sub, slot)

                @pl.when(n + ring < 2 * late)
                def _():
                    load(kept + lax.rem(n + ring, late), slot).start()

            return carry

        lax.fori_loop(0, per_block, body, 0)

    backward_block(0)
    grad_ref[me] = sends[0]

    def backward_rest(k, carry):
        g_copy(k).wait_recv()
        backward_block(k)
        o_copy(k).start()
        return carry

    lax.fori_loop(1, nar, backward_rest, 0)

    for k in range(1, nar):
        q_copy(k).wait_send()
        d_copy(k).wait_send()
        g_copy(k).wait_send()
        l_copy(k).wait()
        o_copy(k).wait()


def neighbours(nar, first, columns, temper, mix, query, keys, norms, ids):
    tok, depth = query.shape[1:]
    rows = keys.shape[0]
    tile = 64
    tiles = rows // tile
    bytes_tile = tile * depth * J * 2
    ring = 4
    kept = min(tiles - 2 * ring, (KEPT_BYTES // bytes_tile))
    vmem = pl.BlockSpec(memory_space=pltpu.VMEM)
    dma = pltpu.SemaphoreType.DMA((nar,))
    return pl.pallas_call(
        functools.partial(neighbour_kernel, nar, first, tiles, tile, kept, ring),
        out_shape=(
            jax.ShapeDtypeStruct((nar, tok, depth), BF16),
            jax.ShapeDtypeStruct((nar, 8, tok), F32),
            jax.ShapeDtypeStruct((2, J), F32),
        ),
        in_specs=[vmem] * 4
        + [pl.BlockSpec(memory_space=pltpu.SMEM)] * 2
        + [pl.BlockSpec(memory_space=pl.ANY)] * 4,
        out_specs=(vmem, vmem, vmem),
        scratch_shapes=[
            pltpu.VMEM((nar, tok, depth), BF16),
            pltpu.VMEM((nar, tok, J), F32),
            pltpu.VMEM((nar, tok, J), F32),
            pltpu.VMEM((nar, tok, J), BF16),
            pltpu.VMEM((nar, tok, depth), BF16),
            pltpu.VMEM((kept + ring, tile, depth, J), BF16),
            pltpu.VMEM((8, tok), F32),
            pltpu.VMEM((rows, J), F32),
            pltpu.VMEM((tok, J), jnp.int32),
            pltpu.SemaphoreType.DMA((3,)),
            pltpu.SemaphoreType.DMA((kept + ring,)),
        ]
        + [dma] * 10,
        compiler_params=pltpu.CompilerParams(
            collective_id=1, has_side_effects=True, vmem_limit_bytes=62 * 2**20
        ),
    )(*columns, temper, mix, query, keys, norms, ids)


def on_device(
    block_input,
    output_cotangent,
    loss_weight,
    segments,
    nbr_keys,
    nbr_count,
    nbr_ids,
    targets,
    base_prob,
    w_query,
    w_key,
    w_value,
    w_proj,
    w_in,
    w_out,
    gain_attn,
    gain_ffn,
    gain_key,
    temper,
    mix_weight,
):
    seqs_here, length, width = block_input.shape
    rows = seqs_here * length
    wid = lax.axis_size("wide")
    first = lax.axis_size("z")
    nar = first * lax.axis_size("y")
    inputs = block_input.reshape(rows, width)
    keys = nbr_keys.reshape(rows, nbr_keys.shape[2], nbr_keys.shape[3])
    gain_one, gain_two, gain_last = (
        gain.reshape(1, width) for gain in (gain_attn, gain_ffn, gain_key)
    )
    normed_one, qkv, lse, part_norms, attended, in_all, out_all, pq_all = head(
        gain_one,
        segments,
        (w_proj, w_query, w_key, w_value),
        inputs,
        keys,
        w_in,
        w_out,
        first,
        nar,
        wid,
        2,
    )
    hidden_one, hidden_two, output_own, query_key, normed_two, pre_act = ffn(
        gain_two, gain_last, attended, inputs, pq_all, in_all, out_all, 3
    )
    grad_slices, losses, stats = neighbours(
        nar,
        first,
        (nbr_count, targets, base_prob, loss_weight),
        temper,
        mix_weight,
        query_key,
        keys,
        part_norms,
        nbr_ids.reshape(rows, -1),
    )
    sums, grad_hidden_one, grad_attended, *sides, lines = ffn_back(
        gain_two,
        gain_last,
        grad_slices,
        stats,
        hidden_two,
        output_cotangent.reshape(rows, width),
        out_all,
        pre_act,
        in_all,
        attended,
        normed_two,
        hidden_one,
        pq_all,
        output_own,
        wid,
        5,
    )
    grad_input, block_output, totals, grad_in, grad_out, grad_proj, grad_qkv = attention_grads(
        segments,
        gain_one,
        sums,
        grad_attended,
        lines,
        sides,
        qkv,
        lse,
        normed_one,
        inputs,
        grad_hidden_one,
        pq_all,
        first,
        wid,
        6,
    )
    results = finish(
        grad_input,
        block_output,
        lines,
        totals,
        losses,
        grad_qkv,
        grad_proj,
        grad_in,
        grad_out,
        seqs_here,
    )
    block_output, token_loss, grad_input, *weights, total_one, total_two, total_last = results[:12]
    piece = width // wid
    return (
        block_output.reshape(seqs_here, length, width),
        token_loss,
        grad_input.reshape(seqs_here, length, width),
        *weights,
        total_one.reshape(piece),
        total_two.reshape(piece),
        total_last.reshape(piece),
        results[12].reshape(1),
        results[13].reshape(1),
    )


def solution(mesh):
    wide, narrow = mesh.devices.shape
    first = 4
    split = jax.sharding.Mesh(
        mesh.devices.reshape(wide, first, narrow // first), ("wide", "z", "y")
    )
    narrow = ("z", "y")
    return jax.shard_map(
        on_device,
        mesh=split,
        in_specs=(
            P("wide", None, None),
            P("wide", None, None),
            P("wide", None),
            P("wide", None),
            P("wide", None, narrow, None),
            P("wide", None),
            P("wide", None, None),
            P("wide", None),
            P("wide", None),
            P(narrow, None),
            P(narrow, None),
            P(narrow, None),
            P(narrow, None),
            P(None, narrow),
            P(narrow, None),
            P(),
            P(),
            P(),
            P(),
            P(),
        ),
        out_specs=(
            P("wide", None, None),
            P("wide", None),
            P("wide", None, None),
            P(narrow, "wide"),
            P(narrow, "wide"),
            P(narrow, "wide"),
            P(narrow, "wide"),
            P("wide", narrow),
            P(narrow, "wide"),
            P("wide"),
            P("wide"),
            P("wide"),
            P(),
            P(),
        ),
        check_vma=False,
    )
```

```python
import functools

import jax
import jax.numpy as jnp
from jax import lax
from jax.experimental import pallas as pl
from jax.experimental.pallas import tpu as pltpu
from jax.sharding import PartitionSpec as P

HD = 64
EPSILON = 1e-05
F32 = jnp.float32
BF16 = jnp.bfloat16
MESH = pl.DeviceIdType.MESH
J = 128
KEPT_BYTES = 20 * 2**20


def place(index, second):
    return {"z": index // second, "y": lax.rem(index, second)}


def push(src, dst, send, recv, target):
    return pltpu.make_async_remote_copy(
        src_ref=src,
        dst_ref=dst,
        send_sem=send,
        recv_sem=recv,
        device_id=target,
        device_id_type=MESH,
    )


def greet(peers):
    barrier = pltpu.get_barrier_semaphore()
    for peer in peers:
        pl.semaphore_signal(barrier, inc=1, device_id=peer, device_id_type=MESH)
    pl.semaphore_wait(barrier, len(peers))


def normalise(values):
    centred = values - jnp.mean(values, axis=-1, keepdims=True)
    inverse = lax.rsqrt(jnp.mean(centred * centred, axis=-1, keepdims=True) + EPSILON)
    return centred * inverse, inverse


def normalise_back(grad_out, normed, inverse, gain):
    scaled = grad_out * gain
    return inverse * (
        scaled
        - jnp.mean(scaled, axis=-1, keepdims=True)
        - normed * jnp.mean(scaled * normed, axis=-1, keepdims=True)
    )


def head_lanes(values, head):
    lanes = lax.broadcasted_iota(jnp.int32, values.shape, 1)
    return jnp.where(lanes // HD == head, values, jnp.zeros_like(values))


def head_kernel(
    nar,
    first,
    wid,
    seqs,
    heads,
    block,
    tile,
    ring,
    gain_ref,
    seg_ref,
    proj_any,
    query_any,
    key_any,
    value_any,
    input_any,
    keys_ref,
    in_any,
    out_any,
    normed_out,
    qkv_out,
    lse_out,
    norms_out,
    att_ref,
    in_all,
    out_all,
    pq_all,
    pq_ref,
    in_ref,
    out_ref,
    input_ref,
    normed_ref,
    qkv_ref,
    lse_ref,
    norms_ref,
    attended,
    slots,
    load_sem,
    store_sem,
    slot_sem,
    own_sem,
    a_send,
    a_recv,
    z_send,
    z_recv,
    y_send,
    y_recv,
    x_send,
    x_recv,
    c_send,
    c_recv,
):
    second = nar // first
    outer = wid // 2
    za, yb = lax.axis_index("z"), lax.axis_index("y")
    me = za * second + yb
    wide = lax.axis_index("wide")
    chip, core = wide // 2, lax.rem(wide, 2)
    rows, width = input_ref.shape
    tok = rows // nar
    length = rows // seqs
    local = heads * HD
    tiles = rows // tile
    last = (((1,), (1,)), ((), ()))

    def fetch(index, slot):
        return pltpu.make_async_copy(
            keys_ref.at[pl.ds(index * tile, tile)], slots.at[slot], slot_sem.at[slot]
        )

    loads = [
        pltpu.make_async_copy(src, pq_ref.at[pl.ds(n * local, local)], load_sem.at[n])
        for n, src in enumerate((proj_any, query_any, key_any, value_any))
    ] + [
        pltpu.make_async_copy(src, dst, load_sem.at[4 + n])
        for n, (src, dst) in enumerate(
            ((in_any, in_ref), (out_any, out_ref), (input_any, input_ref))
        )
    ]
    for load in loads:
        load.start()
    stores = [
        pltpu.make_async_copy(src, dst, store_sem.at[n])
        for n, (src, dst) in enumerate(
            (
                (normed_ref, normed_out),
                (qkv_ref, qkv_out),
                (lse_ref, lse_out),
                (norms_ref, norms_out),
            )
        )
    ]

    greet(
        [place(lax.rem(me + k, nar), second) for k in range(1, nar)]
        + [{"wide": chip * 2 + (1 - core)}]
        + [{"wide": lax.rem(chip + o, outer) * 2 + core} for o in range(1, outer)]
    )

    stacks = ((pq_ref, pq_all), (in_ref, in_all), (out_ref, out_all))

    def shard_of(t, source):
        return source if t == 0 else source // second

    def quarter(t, source, owner):
        own, stack = stacks[t]
        count = own.shape[0] // wid
        at = pl.ds(pl.multiple_of(owner * count, count), count)
        return stack.at[shard_of(t, source), at]

    def own_quarter(t):
        own, _ = stacks[t]
        count = own.shape[0] // wid
        return own.at[pl.ds(pl.multiple_of(wide * count, count), count)]

    reach, relay = REACH, RELAY

    def line_copy(t, source, z, slot, own):
        return push(
            own_quarter(t) if own else quarter(t, source, wide),
            quarter(t, source, wide),
            z_send.at[t, source // second, slot],
            z_recv.at[t, source // second],
            {"z": z, "y": yb},
        )

    def owner_of(o):
        return lax.rem(chip + outer - o, outer) * 2 + core

    def row_copy(source, j, o, own):
        owner = owner_of(o)
        count = pq_ref.shape[0] // wid
        at = pl.ds(pl.multiple_of(owner * count, count), count)
        return push(
            pq_ref.at[at] if own else quarter(0, source, owner),
            quarter(0, source, owner),
            y_send.at[source, j, o],
            y_recv.at[source, j, o],
            {"z": za, "y": lax.rem(yb + j, second)},
        )

    def chip_copy(t, source, o):
        return push(
            quarter(t, source, wide),
            quarter(t, source, wide),
            x_send.at[t, source, o],
            x_recv.at[t, source, o],
            {"wide": lax.rem(chip + o, outer) * 2 + core},
        )

    def chip_arrival(t, source, o):
        owner = owner_of(o)
        return push(
            quarter(t, source, owner),
            quarter(t, source, owner),
            x_send.at[t, source, o],
            x_recv.at[t, source, o],
            {"wide": owner},
        )

    def core_copy(t, source, o, away):
        owner = lax.rem(chip + outer - o, outer) * 2 + jnp.where(away, 1 - core, core)
        return push(
            quarter(t, source, owner),
            quarter(t, source, owner),
            c_send.at[t, source, o],
            c_recv.at[t, source, o],
            {"wide": chip * 2 + (1 - core)},
        )

    def att_copy(target, source):
        return push(
            attended.at[target],
            att_ref.at[source],
            a_send.at[target],
            a_recv.at[source],
            place(target, second),
        )

    own_copies = [
        pltpu.make_async_copy(own, stack.at[shard_of(t, me)], own_sem.at[t])
        for t, (own, stack) in enumerate(stacks)
    ]

    def send_own(t):
        for z in range(first):

            @pl.when(za == z)
            def _(z=z):
                for slot, target in enumerate(reach[z]):
                    line_copy(t, me, target, slot, True).start()

        if t == 0:
            for j in range(1, second):
                for o in range(outer):
                    row_copy(me, j, o, True).start()
        own_copies[t].start()

    def line_arrivals(t, begin, end):
        for d in range(begin, end):
            for way in (-1, 1):
                z = za + way * d

                @pl.when((z >= 0) & (z < first))
                def _(z=z):
                    source = z * second + yb
                    line_copy(t, source, za, 0, False).wait_recv()
                    for middle, (target, sources) in relay.items():

                        @pl.when((za == middle) & ((z == sources[0]) | (z == sources[1])))
                        def _(target=target):
                            line_copy(t, source, target, 0, False).start()

                    for o in range(1, outer):
                        chip_copy(t, source, o).start()
                    core_copy(t, source, 0, False).start()

    def chip_arrivals(t, begin, end):
        for d in range(begin, end):
            for way in (-1, 1):
                z = za + way * d

                @pl.when((z >= 0) & (z < first))
                def _(z=z):
                    source = z * second + yb
                    for o in range(1, outer):
                        chip_arrival(t, source, o).wait_recv()
                        core_copy(t, source, o, False).start()
                    if t == 0:
                        for j in range(1, second):
                            for o in range(outer):
                                row_copy(source, j, o, False).start()

    def row_arrivals():
        for j in range(1, second):
            for z in range(first):
                source = z * second + lax.rem(yb + second - j, second)
                for o in range(outer):
                    row_copy(source, j, o, False).wait_recv()
                    core_copy(0, source, o, False).start()

    def each_source(t, do):
        for n in range(nar if t == 0 else first):
            source = n if t == 0 else n * second + yb

            @pl.when(source != me)
            def _(source=source):
                do(source)

    def core_arrivals(t):
        def do(source):
            for o in range(outer):
                core_copy(t, source, o, True).wait_recv()

        each_source(t, do)

    for n in range(6):
        loads[n].wait()
    for t in range(3):
        send_own(t)
    for i in range(ring):
        fetch(i, i).start()
    loads[6].wait()

    def project(r, carry):
        at = pl.ds(pl.multiple_of(r * block, block), block)
        normed, _ = normalise(input_ref[at, :].astype(F32))
        low = (normed * gain_ref[0:1, :]).astype(BF16)
        normed_ref[at, :] = low
        out = lax.dot_general(low, pq_ref[local:, :], last, preferred_element_type=F32)
        lanes = lax.broadcasted_iota(jnp.int32, out.shape, 1)
        qkv_ref[at, :] = jnp.where(lanes < local, out * HD ** (-0.5), out).astype(BF16)
        return carry

    lax.fori_loop(0, rows // block, project, 0)
    stores[0].start()
    stores[1].start()
    line_arrivals(0, 1, 2)
    middle = (za == 1) | (za == 2)
    at_end = jnp.logical_not(middle)

    @pl.when(middle)
    def _():
        line_arrivals(0, 2, first)

    def sequence(seq, carry):
        base = seq * length
        for start in range(0, length, block):
            keys = start + block
            at = pl.ds(pl.multiple_of(base + start, block), block)
            whole = pl.ds(pl.multiple_of(base, length), keys)
            query_segment = segment_column(seg_ref, seq, start, block)
            key_segment = seg_ref[pl.ds(seq, 1), 0:keys].astype(F32)
            spot = lax.broadcasted_iota(jnp.int32, (block, keys), 1)
            own = lax.broadcasted_iota(jnp.int32, (block, keys), 0) + start
            allowed = (spot <= own) & (query_segment == key_segment)
            query = qkv_ref[at, 0:local]
            key = qkv_ref[whole, local : 2 * local]
            value = qkv_ref[whole, 2 * local : 3 * local]
            total = jnp.zeros((block, local), F32)
            for head in range(heads):
                scores = lax.dot_general(
                    head_lanes(query, head), key, last, preferred_element_type=F32
                )
                scores = jnp.where(allowed, scores, -1e30)
                peak = jnp.max(scores, axis=-1, keepdims=True)
                expo = jnp.exp(scores - peak)
                sums = jnp.sum(expo, axis=-1, keepdims=True)
                out = jnp.dot(expo.astype(BF16), value, preferred_element_type=F32) / sums
                total = total + head_lanes(out, head)
                lse_ref[at, head : head + 1] = peak + jnp.log(sums)
            each = min(tok, block)
            for r in range(0, block, each):
                target = seq * (nar // seqs) + (start + r) // tok
                spot_row = (start + r) % tok
                attended[target, spot_row : spot_row + each, :] = total[r : r + each, :].astype(
                    BF16
                )

        def leave(b, c):
            target = seq * (nar // seqs) + b

            @pl.when(target != me)
            def _():
                att_copy(target, me).start()

            return c

        lax.fori_loop(0, nar // seqs, leave, 0)
        return carry

    lax.fori_loop(0, seqs, sequence, 0)
    stores[2].start()
    own_att = pltpu.make_async_copy(attended.at[me], att_ref.at[me], own_sem.at[3])
    own_att.start()

    def norms(begin, end):
        def body(index, carry):
            slot = lax.rem(index, ring)
            fetch(index, slot).wait()
            keys = slots[slot].astype(F32)
            at = pl.ds(pl.multiple_of(index * tile, tile), tile)
            norms_ref[at, :] = jnp.sum(keys * keys, axis=1)

            @pl.when(index + ring < tiles)
            def _():
                fetch(index + ring, slot).start()

            return carry

        lax.fori_loop(begin, end, body, 0)

    @pl.when(at_end)
    def _():
        line_arrivals(1, 1, 2)
        line_arrivals(2, 1, 2)
        chip_arrivals(0, 1, 2)
        line_arrivals(0, 2, first)

    @pl.when(middle)
    def _():
        line_arrivals(1, 1, first)
        chip_arrivals(0, 1, first)

    norms(0, tiles // 3)

    @pl.when(at_end)
    def _():
        chip_arrivals(0, 2, first)
        line_arrivals(1, 2, first)

    @pl.when(middle)
    def _():
        line_arrivals(2, 1, first)

    norms(tiles // 3, 2 * tiles // 3)

    @pl.when(at_end)
    def _():
        line_arrivals(2, 2, first)

    norms(2 * tiles // 3, tiles)
    stores[3].start()
    row_arrivals()
    chip_arrivals(1, 1, first)
    chip_arrivals(2, 1, first)
    for t in range(3):
        core_arrivals(t)
    for k in range(1, nar):
        source = lax.rem(me + k, nar)
        att_copy(source, source).wait_recv()
        att_copy(source, me).wait_send()
    for t in range(3):
        own_copies[t].wait()

        def sent(source, t=t):
            for o in range(outer):
                core_copy(t, source, o, False).wait_send()

        each_source(t, sent)
        for n in range(first):
            source = n * second + yb

            @pl.when(source != me)
            def _(source=source, t=t):
                for o in range(1, outer):
                    chip_copy(t, source, o).wait_send()

        for z in range(first):

            @pl.when(za == z)
            def _(z=z, t=t):
                for slot, target in enumerate(reach[z]):
                    line_copy(t, me, target, slot, True).wait_send()
                if z in relay:
                    target, sources = relay[z]
                    for n in sources:
                        line_copy(t, n * second + yb, target, 0, False).wait_send()

    for z in range(first):
        for j in range(1, second):
            for o in range(outer):
                row_copy(z * second + yb, j, o, False).wait_send()
    own_att.wait()
    for store in stores:
        store.wait()


def head(gain, seg, weights, block_input, keys, w_in, w_out, first, nar, wid, name):
    rows, width = block_input.shape
    seqs, length = seg.shape
    second = nar // first
    outer = wid // 2
    local = weights[0].shape[0]
    heads = local // HD
    hidden = w_in.shape[1]
    tok = rows // nar
    depth = keys.shape[1]
    tile, ring = 32, 4
    block = min(256, length)
    vmem = pl.BlockSpec(memory_space=pltpu.VMEM)
    hbm = pl.BlockSpec(memory_space=pl.ANY)
    dma = pltpu.SemaphoreType.DMA
    kept = (
        ((rows, width), BF16),
        ((rows, 3 * local), BF16),
        ((rows, heads), F32),
        ((rows, J), F32),
    )
    return pl.pallas_call(
        functools.partial(head_kernel, nar, first, wid, seqs, heads, block, tile, ring),
        out_shape=tuple(jax.ShapeDtypeStruct(*x) for x in kept)
        + (
            jax.ShapeDtypeStruct((nar, tok, local), BF16),
            jax.ShapeDtypeStruct((first, width, hidden), BF16),
            jax.ShapeDtypeStruct((first, hidden, width), BF16),
            jax.ShapeDtypeStruct((nar, 4 * local, width), BF16),
        ),
        in_specs=[vmem] * 2 + [hbm] * 8,
        out_specs=(hbm,) * 8,
        scratch_shapes=[
            pltpu.VMEM((4 * local, width), BF16),
            pltpu.VMEM((width, hidden), BF16),
            pltpu.VMEM((hidden, width), BF16),
            pltpu.VMEM((rows, width), BF16),
        ]
        + [pltpu.VMEM(*x) for x in kept]
        + [
            pltpu.VMEM((nar, tok, local), BF16),
            pltpu.VMEM((ring, tile, depth, J), BF16),
            dma((7,)),
            dma((4,)),
            dma((ring,)),
            dma((4,)),
            dma((nar,)),
            dma((nar,)),
            dma((3, first, 3)),
            dma((3, first)),
            dma((nar, second, outer)),
            dma((nar, second, outer)),
            dma((3, nar, outer)),
            dma((3, nar, outer)),
            dma((3, nar, outer)),
            dma((3, nar, outer)),
        ],
        compiler_params=pltpu.CompilerParams(
            collective_id=name, has_side_effects=True, vmem_limit_bytes=62 * 2**20
        ),
    )(gain, seg, *weights, block_input, keys, w_in, w_out)


INNER = 0.7978845608028654
CUBIC = 0.044715


def gelu_parts(values):
    tanh = jnp.tanh(INNER * (values + CUBIC * values * values * values))
    return 0.5 * values * (1.0 + tanh), tanh


def own_rows(tok, second):
    me = lax.axis_index("z") * second + lax.axis_index("y")
    return pl.ds(pl.multiple_of(me * tok, tok), tok)


def ffn_kernel(
    chunks,
    gain_two_ref,
    gain_key_ref,
    att_any,
    input_any,
    pq_any,
    in_any,
    mid_any,
    one_out,
    two_out,
    output_out,
    key_out,
    normed_out,
    pre_out,
    att_ref,
    input_ref,
    proj_ref,
    in_ref,
    mid_ref,
    one_ref,
    two_ref,
    output_ref,
    key_ref,
    normed_ref,
    pre_ref,
    back_out,
    back_in,
    load_sem,
    store_sem,
    n_send,
    n_recv,
    b_send,
    b_recv,
):
    nar, tok, local = att_ref.shape
    first, width, hidden = in_ref.shape
    second = nar // first
    part = tok // chunks
    za, yb = lax.axis_index("z"), lax.axis_index("y")

    pairs = (
        (att_any, att_ref),
        (pq_any.at[:, pl.ds(0, local)], proj_ref),
        (input_any.at[own_rows(tok, second)], input_ref),
        (in_any, in_ref),
        (mid_any, mid_ref),
    )
    loads = [
        pltpu.make_async_copy(src, dst, load_sem.at[n]) for n, (src, dst) in enumerate(pairs)
    ]
    for load in loads:
        load.start()
    kept = (
        (one_ref, one_out),
        (normed_ref, normed_out),
        (pre_ref, pre_out),
        (key_ref, key_out),
        (two_ref, two_out),
        (output_ref, output_out),
    )
    stores = [
        pltpu.make_async_copy(src, dst, store_sem.at[n]) for n, (src, dst) in enumerate(kept)
    ]

    greet([{"z": za, "y": lax.rem(yb + j, second)} for j in range(1, second)])

    def n_copy(j, c):
        at = pl.ds(c * part, part)
        target = {"z": za, "y": lax.rem(yb + j, second)}
        return push(
            normed_ref.at[0, at], normed_ref.at[j, at], n_send.at[j, c], n_recv.at[j, c], target
        )

    def b_copy(j, c):
        at = pl.ds(c * part, part)
        target = {"z": za, "y": lax.rem(yb + second - j, second)}
        return push(
            back_out.at[j, at], back_in.at[j, at], b_send.at[j, c], b_recv.at[j, c], target
        )

    def through(j, start, count):
        total = jnp.zeros((count, width), F32)
        for z in range(first):
            pre = jnp.dot(
                normed_ref[j, start : start + count, :], in_ref[z], preferred_element_type=F32
            )
            pre_ref[j, start : start + count, z * hidden : (z + 1) * hidden] = pre
            activated = gelu_parts(pre)[0].astype(BF16)
            total = total + jnp.dot(activated, mid_ref[z], preferred_element_type=F32)
        return total

    for n in range(3):
        loads[n].wait()
    att = jnp.concatenate([att_ref[n] for n in range(nar)], axis=1)
    one = input_ref[...].astype(F32) + jnp.dot(
        att, proj_ref[...].reshape(nar * local, width), preferred_element_type=F32
    )
    one_ref[...] = one
    normed, _ = normalise(one)
    normed_ref[0] = (normed * gain_two_ref[...]).astype(BF16)
    for c in range(chunks):
        for j in range(1, second):
            n_copy(j, c).start()
    stores[0].start()
    for n in range(3, 5):
        loads[n].wait()
    two_ref[...] = one_ref[...] + through(0, 0, tok)
    for c in range(chunks):
        for j in range(1, second):
            n_copy(j, c).wait_recv()
            back_out[j, c * part : (c + 1) * part, :] = through(j, c * part, part).astype(BF16)
            b_copy(j, c).start()
    stores[1].start()
    stores[2].start()
    for c in range(chunks):
        at = slice(c * part, (c + 1) * part)
        for j in range(1, second):
            b_copy(j, c).wait_recv()
            two_ref[at, :] += back_in[j, at, :].astype(F32)
    hidden_two = two_ref[...]
    normed, _ = normalise(hidden_two)
    query_key = (normed * gain_key_ref[...]).astype(BF16)
    for n in range(nar):
        key_ref[n] = query_key[:, n * (width // nar) : (n + 1) * (width // nar)]
    stores[3].start()
    stores[4].start()
    output_ref[...] = hidden_two.astype(BF16)
    stores[5].start()
    for c in range(chunks):
        for j in range(1, second):
            n_copy(j, c).wait_send()
            b_copy(j, c).wait_send()
    for store in stores:
        store.wait()


def ffn(gain_two, gain_key, att, inputs, pq, in_all, out_all, name):
    nar, tok, local = att.shape
    first, width, hidden = in_all.shape
    second = nar // first
    chunks = 2
    vmem = pl.BlockSpec(memory_space=pltpu.VMEM)
    hbm = pl.BlockSpec(memory_space=pl.ANY)
    dma = pltpu.SemaphoreType.DMA
    outs = (
        ((tok, width), F32),
        ((tok, width), F32),
        ((tok, width), BF16),
        ((nar, tok, width // nar), BF16),
        ((second, tok, width), BF16),
        ((second, tok, first * hidden), F32),
    )
    return pl.pallas_call(
        functools.partial(ffn_kernel, chunks),
        out_shape=tuple(jax.ShapeDtypeStruct(*x) for x in outs),
        in_specs=[vmem] * 2 + [hbm] * 5,
        out_specs=(hbm,) * 6,
        scratch_shapes=[
            pltpu.VMEM(att.shape, BF16),
            pltpu.VMEM((tok, width), BF16),
            pltpu.VMEM((nar, local, width), BF16),
            pltpu.VMEM(in_all.shape, BF16),
            pltpu.VMEM(out_all.shape, BF16),
        ]
        + [pltpu.VMEM(*x) for x in outs]
        + [pltpu.VMEM((second, tok, width), BF16)] * 2
        + [dma((5,)), dma((6,))]
        + [dma((second, chunks))] * 4,
        compiler_params=pltpu.CompilerParams(
            collective_id=name, has_side_effects=True, vmem_limit_bytes=62 * 2**20
        ),
    )(gain_two, gain_key, att, inputs, pq, in_all, out_all)


def ffn_back_kernel(
    chunks,
    gain_two_ref,
    gain_key_ref,
    slices_ref,
    stat_ref,
    two_any,
    cot_any,
    mid_any,
    pre_any,
    in_any,
    att_any,
    normed_any,
    one_any,
    pq_any,
    share_any,
    sums_ref,
    grad_one_out,
    grad_att_out,
    pre_turned_out,
    act_turned_out,
    att_turned_out,
    normed_cols_out,
    ffn_cols_out,
    branch_cols_out,
    line_ref,
    two_ref,
    cot_ref,
    mid_ref,
    pre_ref,
    in_ref,
    att_ref,
    normed_ref,
    one_ref,
    proj_ref,
    share_ref,
    grad_one_ref,
    grad_att_ref,
    pre_turned_ref,
    act_turned_ref,
    att_turned_ref,
    normed_cols_ref,
    ffn_cols_ref,
    branch_cols_ref,
    grads,
    grad_two,
    total,
    back_out,
    back_in,
    load_sem,
    store_sem,
    own_sem,
    n_send,
    n_recv,
    b_send,
    b_recv,
    g_send,
    g_recv,
):
    nar, tok, local = att_ref.shape
    first, width, hidden = in_ref.shape
    second = nar // first
    wid = branch_cols_ref.shape[0]
    columns = width // wid
    part = tok // chunks
    last = (((1,), (1,)), ((), ()))
    za, yb = lax.axis_index("z"), lax.axis_index("y")
    reach, relay = REACH, RELAY

    pairs = (
        (share_any, share_ref),
        (two_any, two_ref),
        (cot_any.at[own_rows(tok, second)], cot_ref),
        (mid_any, mid_ref),
        (pre_any, pre_ref),
        (in_any, in_ref),
        (att_any, att_ref),
        (normed_any, normed_ref),
        (one_any, one_ref),
        (pq_any.at[:, pl.ds(0, local)], proj_ref),
    )
    loads = [
        pltpu.make_async_copy(src, dst, load_sem.at[n]) for n, (src, dst) in enumerate(pairs)
    ]
    for load in loads:
        load.start()
    kept = (
        (ffn_cols_ref, ffn_cols_out),
        (pre_turned_ref, pre_turned_out),
        (act_turned_ref, act_turned_out),
        (att_turned_ref, att_turned_out),
        (normed_cols_ref, normed_cols_out),
        (grad_att_ref, grad_att_out),
        (branch_cols_ref, branch_cols_out),
        (grad_one_ref, grad_one_out),
    )
    stores = [
        pltpu.make_async_copy(src, dst, store_sem.at[n]) for n, (src, dst) in enumerate(kept)
    ]

    greet(
        [{"z": za, "y": lax.rem(yb + j, second)} for j in range(1, second)]
        + [{"z": lax.rem(za + i, first), "y": yb} for i in range(1, first)]
    )

    def n_copy(j, c):
        at = pl.ds(c * part, part)
        target = {"z": za, "y": lax.rem(yb + j, second)}
        return push(grads.at[0, at], grads.at[j, at], n_send.at[j, c], n_recv.at[j, c], target)

    def b_copy(j, c):
        at = pl.ds(c * part, part)
        target = {"z": za, "y": lax.rem(yb + second - j, second)}
        return push(
            back_out.at[j, at], back_in.at[j, at], b_send.at[j, c], b_recv.at[j, c], target
        )

    def g_copy(source, target, slot, c, own):
        at = pl.ds(c * part, part)
        return push(
            share_ref.at[at] if own else line_ref.at[source, at],
            line_ref.at[source, at],
            g_send.at[source, slot, c],
            g_recv.at[source, c],
            {"z": target, "y": yb},
        )

    def gathered(c, begin, end):
        for d in range(begin, end):
            for way in (-1, 1):
                z = za + way * d

                @pl.when((z >= 0) & (z < first))
                def _(z=z):
                    g_copy(z, za, 0, c, False).wait_recv()
                    for middle, (target, sources) in relay.items():

                        @pl.when((za == middle) & ((z == sources[0]) | (z == sources[1])))
                        def _(target=target):
                            g_copy(z, target, 0, c, False).start()

    loads[0].wait()
    for c in range(chunks):
        for z in range(first):

            @pl.when(za == z)
            def _(z=z, c=c):
                for slot, target in enumerate(reach[z]):
                    g_copy(za, target, slot, c, True).start()

    own_copy = pltpu.make_async_copy(share_ref, line_ref.at[za], own_sem)
    own_copy.start()

    def through(j, start, count):
        at = slice(start, start + count)
        sums = jnp.zeros((count, width), F32)
        for z in range(first):
            own = slice(z * hidden, (z + 1) * hidden)
            pre = pre_ref[j, at, own]
            activated, tanh = gelu_parts(pre)
            slope = 0.5 * (1.0 + tanh) + 0.5 * pre * (1.0 - tanh * tanh) * INNER * (
                1.0 + 3.0 * CUBIC * pre * pre
            )
            grad_act = lax.dot_general(
                grads[j, at, :], mid_ref[z], last, preferred_element_type=F32
            )
            grad_pre = slope * grad_act
            to = slice(j * tok + start, j * tok + start + count)
            act_turned_ref[own, to] = jnp.transpose(activated).astype(BF16)
            pre_turned_ref[own, to] = jnp.transpose(grad_pre).astype(BF16)
            sums = sums + lax.dot_general(
                grad_pre.astype(BF16), in_ref[z], last, preferred_element_type=F32
            )
        return sums

    for n in range(1, 3):
        loads[n].wait()
    grad_key = jnp.concatenate([slices_ref[n] for n in range(nar)], axis=1).astype(F32)
    normed, inverse = normalise(two_ref[...])
    sums_ref[...] = jnp.zeros_like(sums_ref)
    sums_ref[2:3, :] = jnp.sum(grad_key * normed, axis=0, keepdims=True)
    temper_sum = jnp.sum(stat_ref[0:1, :], axis=1, keepdims=True)
    sums_ref[3:4, :] = jnp.broadcast_to(temper_sum, (1, width))
    sums_ref[4:5, :] = jnp.broadcast_to(stat_ref[1:2, 0:1], (1, width))
    grad = cot_ref[...].astype(F32) + normalise_back(
        grad_key, normed, inverse, gain_key_ref[...]
    )
    grad_two[...] = grad
    grads[0] = grad.astype(BF16)
    for c in range(chunks):
        for j in range(1, second):
            n_copy(j, c).start()
    for n in range(3, 6):
        loads[n].wait()
    total[...] = through(0, 0, tok)
    gathered(0, 1, 2)
    for c in range(chunks):
        for j in range(1, second):
            n_copy(j, c).wait_recv()
            back_out[j, c * part : (c + 1) * part, :] = through(j, c * part, part).astype(BF16)
            b_copy(j, c).start()
    gathered(0, 2, first)
    gathered(1, 1, first)
    for n in range(6, 10):
        loads[n].wait()
    for j in range(second):
        for w in range(wid):
            own = slice(w * columns, (w + 1) * columns)
            normed_cols_ref[w, j * tok : (j + 1) * tok, :] = normed_ref[j, :, own]
            ffn_cols_ref[w, j * tok : (j + 1) * tok, :] = grads[j, :, own]
    att_turned_ref[...] = jnp.concatenate(
        [jnp.transpose(att_ref[n].astype(F32)).astype(BF16) for n in range(nar)], axis=0
    )
    for n in range(5):
        stores[n].start()
    for c in range(chunks):
        at = slice(c * part, (c + 1) * part)
        for j in range(1, second):
            b_copy(j, c).wait_recv()
            total[at, :] += back_in[j, at, :].astype(F32)
    normed, inverse = normalise(one_ref[...])
    sums_ref[1:2, :] = jnp.sum(total[...] * normed, axis=0, keepdims=True)
    grad = grad_two[...] + normalise_back(total[...], normed, inverse, gain_two_ref[...])
    branch = grad.astype(BF16)
    grad_att = lax.dot_general(
        branch, proj_ref[...].reshape(nar * local, width), last, preferred_element_type=F32
    ).astype(BF16)
    for n in range(nar):
        grad_att_ref[n] = grad_att[:, n * local : (n + 1) * local]
    stores[5].start()
    for w in range(wid):
        branch_cols_ref[w] = branch[:, w * columns : (w + 1) * columns]
    stores[6].start()
    grad_one_ref[...] = grad
    stores[7].start()
    own_copy.wait()
    for c in range(chunks):
        for j in range(1, second):
            n_copy(j, c).wait_send()
            b_copy(j, c).wait_send()
        for z in range(first):

            @pl.when(za == z)
            def _(z=z, c=c):
                for slot, target in enumerate(reach[z]):
                    g_copy(za, target, slot, c, True).wait_send()
                if z in relay:
                    target, sources = relay[z]
                    for n in sources:
                        g_copy(n, target, 0, c, False).wait_send()

    for store in stores:
        store.wait()


def ffn_back(
    gain_two,
    gain_key,
    slices,
    stats,
    two,
    cot,
    out_all,
    pre,
    in_all,
    att,
    normed,
    one,
    pq,
    share,
    wid,
    name,
):
    nar, tok, local = att.shape
    first, width, hidden = in_all.shape
    second = nar // first
    chunks = 2
    columns = width // wid
    vmem = pl.BlockSpec(memory_space=pltpu.VMEM)
    hbm = pl.BlockSpec(memory_space=pl.ANY)
    dma = pltpu.SemaphoreType.DMA
    outs = (
        ((tok, width), F32),
        ((nar, tok, local), BF16),
        ((first * hidden, second * tok), BF16),
        ((first * hidden, second * tok), BF16),
        ((nar * local, tok), BF16),
        ((wid, second * tok, columns), BF16),
        ((wid, second * tok, columns), BF16),
        ((wid, tok, columns), BF16),
    )
    return pl.pallas_call(
        functools.partial(ffn_back_kernel, chunks),
        out_shape=(jax.ShapeDtypeStruct((8, width), F32),)
        + tuple(jax.ShapeDtypeStruct(*x) for x in outs)
        + (jax.ShapeDtypeStruct((first, tok, width), BF16),),
        in_specs=[vmem] * 4 + [hbm] * 10,
        out_specs=(vmem,) + (hbm,) * 9,
        scratch_shapes=[
            pltpu.VMEM((tok, width), F32),
            pltpu.VMEM((tok, width), BF16),
            pltpu.VMEM(out_all.shape, BF16),
            pltpu.VMEM(pre.shape, F32),
            pltpu.VMEM(in_all.shape, BF16),
            pltpu.VMEM(att.shape, BF16),
            pltpu.VMEM(normed.shape, BF16),
            pltpu.VMEM((tok, width), F32),
            pltpu.VMEM((nar, local, width), BF16),
            pltpu.VMEM((tok, width), BF16),
        ]
        + [pltpu.VMEM(*x) for x in outs]
        + [
            pltpu.VMEM((second, tok, width), BF16),
            pltpu.VMEM((tok, width), F32),
            pltpu.VMEM((tok, width), F32),
            pltpu.VMEM((second, tok, width), BF16),
            pltpu.VMEM((second, tok, width), BF16),
            dma((10,)),
            dma((8,)),
            dma,
        ]
        + [dma((second, chunks))] * 4
        + [dma((first, 3, chunks)), dma((first, chunks))],
        compiler_params=pltpu.CompilerParams(
            collective_id=name, has_side_effects=True, vmem_limit_bytes=62 * 2**20
        ),
    )(
        gain_two,
        gain_key,
        slices,
        stats,
        two,
        cot,
        out_all,
        pre,
        in_all,
        att,
        normed,
        one,
        pq,
        share,
    )


def finish_kernel(
    second, grad_ref, block_ref, line_ref, total_ref, loss_ref, qkv_ref, proj_ref, in_ref, mid_ref, *outs
):
    (
        block_out,
        loss_out,
        grad_out,
        query_out,
        key_out,
        value_out,
        proj_out,
        in_out,
        mid_out,
        attn_out,
        ffn_out,
        last_out,
        temper_out,
        mix_out,
    ) = outs
    grad_out[...] = grad_ref[...].astype(F32)
    for j in range(second):

        @pl.when(lax.axis_index("y") == j)
        def _(j=j):
            block_out[j] = line_ref[0]

        @pl.when(lax.axis_index("y") != j)
        def _(j=j):
            block_out[j] = block_ref[j]

    @pl.when(pl.program_id(0) == 0)
    def _():
        local = proj_ref.shape[0]
        query_out[...] = qkv_ref[0:local, :]
        key_out[...] = qkv_ref[local : 2 * local, :]
        value_out[...] = qkv_ref[2 * local : 3 * local, :]
        proj_out[...] = proj_ref[...]
        in_out[...] = in_ref[...]
        mid_out[...] = mid_ref[...]
        attn_out[...] = total_ref[0:1, :]
        ffn_out[...] = total_ref[1:2, :]
        last_out[...] = total_ref[2:3, :]
        temper_out[...] = total_ref[3:4, 0:1]
        mix_out[...] = total_ref[4:5, 0:1]
        nar, _, tok = loss_ref.shape
        seqs = loss_out.shape[0]
        per_seq = nar // seqs
        for n in range(nar):
            at = (n % per_seq) * tok
            loss_out[n // per_seq : n // per_seq + 1, at : at + tok] = loss_ref[n, 0:1, :]


def finish(grad, block, lines, totals, losses, qkv, proj, w_in, w_out, seqs):
    nar, tok, width = grad.shape
    second = nar // lines.shape[0]
    local, piece = proj.shape

    def whole(shape):
        return pl.BlockSpec(shape, lambda i: (0,) * len(shape))

    def each():
        return pl.BlockSpec((second, tok, width), lambda i: (i, 0, 0))

    small = [
        ((local, piece), F32),
        ((local, piece), F32),
        ((local, piece), F32),
        (proj.shape, F32),
        (w_in.shape, F32),
        (w_out.shape, F32),
        ((1, piece), F32),
        ((1, piece), F32),
        ((1, piece), F32),
        ((1, 1), F32),
        ((1, 1), F32),
    ]
    loss_shape = (seqs, nar * tok // seqs)
    return pl.pallas_call(
        functools.partial(finish_kernel, second),
        grid=(nar // second,),
        out_shape=(
            jax.ShapeDtypeStruct((nar, tok, width), BF16),
            jax.ShapeDtypeStruct(loss_shape, F32),
            jax.ShapeDtypeStruct((nar, tok, width), F32),
        )
        + tuple(jax.ShapeDtypeStruct(*x) for x in small),
        in_specs=[each(), each(), pl.BlockSpec((1, tok, width), lambda i: (i, 0, 0))]
        + [whole(x.shape) for x in (totals, losses, qkv, proj, w_in, w_out)],
        out_specs=(each(), whole(loss_shape), each()) + tuple(whole(x[0]) for x in small),
        compiler_params=pltpu.CompilerParams(vmem_limit_bytes=62 * 2**20),
    )(grad, block, lines, totals, losses, qkv, proj, w_in, w_out)


REACH = ((1, 2), (0, 2), (1, 3), (2, 1))
RELAY = {1: (0, (2, 3)), 2: (3, (0, 1))}


def segment_column(seg_ref, seq, start, block):
    row = seg_ref[pl.ds(seq, 1), start : start + block].astype(F32)
    return jnp.transpose(jnp.broadcast_to(row, (8, block)))[:, 0:1]


def grad_kernel(
    nar,
    first,
    wid,
    seqs,
    heads,
    block,
    chunks,
    seg_ref,
    gain_ref,
    sums_ref,
    grad_ref,
    line_any,
    pre_any,
    act_any,
    att_any,
    normed_any,
    ffn_any,
    branch_any,
    qkv_any,
    lse_any,
    one_any,
    input_any,
    above_any,
    pq_any,
    all_ref,
    block_ref,
    total_ref,
    in_grad_ref,
    out_grad_ref,
    proj_grad_ref,
    qkv_grad_ref,
    pre_ref,
    act_ref,
    att_ref,
    normed_ref,
    ffn_ref,
    branch_ref,
    qkv_ref,
    lse_ref,
    one_ref,
    input_ref,
    above_ref,
    pq_ref,
    load_sem,
    out_ref,
    grads,
    got,
    grad_key,
    grad_value,
    core_out,
    core_in,
    chip_out,
    chip_in,
    tail_sum,
    turn_out,
    turn_in,
    line_in,
    work,
    qkv_out,
    qkv_in,
    own_ref,
    own_sums,
    all_sums,
    pieces_out,
    pieces_in,
    own_sem,
    k_send,
    k_recv,
    a_send,
    a_recv,
    b_send,
    b_recv,
    c_send,
    c_recv,
    x_send,
    x_recv,
    y_send,
    y_recv,
    z_send,
    z_recv,
    w_send,
    w_recv,
    g_send,
    g_recv,
    h_send,
    h_recv,
    s_send,
    s_recv,
    p_send,
    p_recv,
):
    second = nar // first
    outer = wid // 2
    za, yb = lax.axis_index("z"), lax.axis_index("y")
    me = za * second + yb
    wide = lax.axis_index("wide")
    chip, core = wide // 2, lax.rem(wide, 2)
    tok, local = grads.shape[1:]
    hidden = pre_ref.shape[0] // first
    columns = normed_ref.shape[2]
    rows = 2 * hidden
    body = first * rows
    line = rows + local
    length = nar * tok // seqs
    per_seq = nar // seqs
    width = heads * HD
    part = tok // chunks
    across = (((0,), (0,)), ((), ()))
    last = (((1,), (1,)), ((), ()))
    reach, relay = REACH, RELAY

    pairs = (
        (pre_any, pre_ref),
        (act_any, act_ref),
        (att_any, att_ref),
        (normed_any, normed_ref),
        (ffn_any, ffn_ref),
        (branch_any, branch_ref),
        (qkv_any, qkv_ref),
        (lse_any, lse_ref),
        (one_any, one_ref),
        (input_any.at[own_rows(tok, second)], input_ref),
        (above_any, above_ref),
        (pq_any, pq_ref),
    )
    loads = [
        pltpu.make_async_copy(src, dst, load_sem.at[n]) for n, (src, dst) in enumerate(pairs)
    ]
    for load in loads:
        load.start()

    greet(
        [place(lax.rem(me + k, nar), second) for k in range(1, nar)]
        + [{"wide": lax.rem(wide + w, wid)} for w in range(1, wid)]
    )

    def a_copy(target, source):
        return push(
            grad_ref.at[target],
            grads.at[source],
            a_send.at[target],
            a_recv.at[source],
            place(target, second),
        )

    def b_copy(target, source):
        return push(
            out_ref.at[pl.ds(pl.multiple_of(target * tok, tok), tok)],
            got.at[source],
            b_send.at[target],
            b_recv.at[source],
            place(target, second),
        )

    def k_copy(z, j):
        return push(
            line_any.at[z],
            block_ref.at[z * second + yb],
            k_send.at[z, j],
            k_recv.at[z, j],
            {"z": za, "y": lax.rem(yb + j, second)},
        )

    def c_copy(o):
        return push(
            core_out.at[o],
            core_in.at[o],
            c_send.at[o],
            c_recv.at[o],
            {"wide": chip * 2 + (1 - core)},
        )

    def span(z):
        return pl.ds(pl.multiple_of(z * rows, rows), rows)

    tail_rows = pl.ds(body, nar * local)

    def x_copy(i, q, at):
        return push(
            chip_out.at[i - 1, at],
            chip_in.at[i - 1, at],
            x_send.at[i, q],
            x_recv.at[i, q],
            {"wide": lax.rem(chip + i, outer) * 2 + core},
        )

    def y_copy(j):
        target = {"z": za, "y": lax.rem(yb + j, second)}
        return push(turn_out.at[j], turn_in.at[j], y_send.at[j], y_recv.at[j], target)

    inner = jnp.where((za == 1) | (za == 2), 1, 0)

    def mirror(z):
        return jnp.where(za < 2, z, 3 - z)

    def dest(n):
        return mirror(jnp.where(n == 1, 3, jnp.where(n == 2, 2, jnp.where(n == 3, 1 - inner, inner))))

    def z_copy(n):
        slot = jnp.where(inner == 1, (3, 4, 0)[n - 1], n - 1)
        target = mirror(jnp.where(inner == 1, (2, 2, 0)[n - 1], 1))
        return push(
            core_out.at[0, pl.ds((n - 1) * line, line)],
            line_in.at[slot],
            z_send.at[n],
            z_recv.at[slot],
            {"z": target, "y": yb},
        )

    def z_arrival(slot):
        return push(
            core_out.at[0, pl.ds(0, line)],
            line_in.at[slot],
            z_send.at[0],
            z_recv.at[slot],
            {"z": mirror(jnp.where(inner == 1, 0, 1)), "y": yb},
        )

    def w_copy(i):
        target = lax.rem(wide + i, wid)
        return push(
            qkv_out.at[target], qkv_in.at[i], w_send.at[i], w_recv.at[i], {"wide": target}
        )

    def g_copy(source_z, target_z, slot, c, own):
        at = pl.ds(c * part, part)
        source = source_z * second + yb
        return push(
            own_ref.at[at] if own else all_ref.at[source, at],
            all_ref.at[source, at],
            g_send.at[source_z, slot, c],
            g_recv.at[source_z, c],
            {"z": target_z, "y": yb},
        )

    def h_copy(source_z, j, c, own):
        at = pl.ds(c * part, part)
        source = source_z * second + yb
        return push(
            own_ref.at[at] if own else all_ref.at[source, at],
            all_ref.at[source, at],
            h_send.at[source_z, j, c],
            h_recv.at[source_z, j, c],
            {"z": za, "y": lax.rem(yb + j, second)},
        )

    def h_arrival(source_z, j, c):
        at = pl.ds(c * part, part)
        source = source_z * second + lax.rem(yb + second - j, second)
        return push(
            all_ref.at[source, at],
            all_ref.at[source, at],
            h_send.at[source_z, j, c],
            h_recv.at[source_z, j, c],
            {"z": za, "y": lax.rem(yb + j, second)},
        )

    def s_copy(k):
        target = place(lax.rem(me + k, nar), second)
        return push(own_sums, all_sums.at[k], s_send.at[k], s_recv.at[k], target)

    def p_copy(w):
        target = lax.rem(wide + w, wid)
        return push(
            pieces_out.at[target], pieces_in.at[w], p_send.at[w], p_recv.at[w], {"wide": target}
        )

    def product_rows(w, z):
        own = pl.ds(pl.multiple_of(z * hidden, hidden), hidden)
        return (
            jnp.dot(pre_ref[own, :], normed_ref[w], preferred_element_type=F32),
            jnp.dot(act_ref[own, :], ffn_ref[w], preferred_element_type=F32),
        )

    def product_tail(w):
        return jnp.dot(att_ref[...], branch_ref[w], preferred_element_type=F32)

    for k in range(1, nar):
        a_copy(lax.rem(me + k, nar), me).start()
    own_grad = pltpu.make_async_copy(grad_ref.at[me], grads.at[me], own_sem.at[1])
    own_grad.start()
    for z in range(2):
        for j in range(1, second):
            k_copy(z, j).start()
    for n in range(6):
        loads[n].wait()

    for i in range(1, outer + 1):
        o = lax.rem(chip + i, outer)
        w = o * 2 + (1 - core)

        def for_core(z, carry, o=o, w=w):
            upper, lower = product_rows(w, z)
            at = pl.multiple_of(z * rows, rows)
            core_out[o, pl.ds(at, hidden), :] = upper.astype(BF16)
            core_out[o, pl.ds(at + hidden, hidden), :] = lower.astype(BF16)
            return carry

        lax.fori_loop(0, first, for_core, 0)
        core_out[o, tail_rows, :] = product_tail(w).astype(BF16)
        c_copy(o).start()

    loads[6].wait()
    loads[7].wait()
    own_grad.wait()

    def sequence(seq, carry):
        base = seq * length

        def arrive(b, c):
            source = seq * per_seq + b

            @pl.when(source != me)
            def _():
                a_copy(source, source).wait_recv()

            return c

        lax.fori_loop(0, per_seq, arrive, 0)
        grad_key[...] = jnp.zeros_like(grad_key)
        grad_value[...] = jnp.zeros_like(grad_value)
        for start in range(0, length, block):
            keys = start + block
            at = pl.multiple_of(base + start, block)
            query_segment = segment_column(seg_ref, seq, start, block)
            key_segment = seg_ref[pl.ds(seq, 1), 0:keys].astype(F32)
            spot = lax.broadcasted_iota(jnp.int32, (block, keys), 1)
            own = lax.broadcasted_iota(jnp.int32, (block, keys), 0) + start
            allowed = (spot <= own) & (query_segment == key_segment)
            whole = pl.ds(pl.multiple_of(base, length), keys)
            query = qkv_ref[pl.ds(at, block), 0:width]
            key = qkv_ref[whole, width : 2 * width]
            value = qkv_ref[whole, 2 * width : 3 * width]
            each = min(tok, block)
            grad = jnp.concatenate(
                [
                    grads[
                        seq * per_seq + (start + r) // tok,
                        (start + r) % tok : (start + r) % tok + each,
                        :,
                    ]
                    for r in range(0, block, each)
                ],
                axis=0,
            )
            total = jnp.zeros((block, width), F32)
            for head in range(heads):
                own_query = head_lanes(query, head)
                own_grad = head_lanes(grad, head)
                scores = lax.dot_general(own_query, key, last, preferred_element_type=F32)
                probs = jnp.where(
                    allowed, jnp.exp(scores - lse_ref[pl.ds(at, block), head : head + 1]), 0.0
                )
                grad_probs = lax.dot_general(own_grad, value, last, preferred_element_type=F32)
                delta = jnp.sum(probs * grad_probs, axis=-1, keepdims=True)
                grad_scores = (probs * (grad_probs - delta)).astype(BF16)
                total = total + head_lanes(
                    jnp.dot(grad_scores, key, preferred_element_type=F32), head
                )
                grad_key[0:keys, :] += lax.dot_general(
                    grad_scores, own_query, across, preferred_element_type=F32
                )
                grad_value[0:keys, :] += lax.dot_general(
                    probs.astype(BF16), own_grad, across, preferred_element_type=F32
                )
            out_ref[pl.ds(at, block), 0:width] = (total * HD ** (-0.5)).astype(BF16)
        every = pl.ds(pl.multiple_of(base, length), length)
        out_ref[every, width : 2 * width] = grad_key[...].astype(BF16)
        out_ref[every, 2 * width : 3 * width] = grad_value[...].astype(BF16)

        def leave(b, c):
            target = seq * per_seq + b

            @pl.when(target != me)
            def _():
                b_copy(target, me).start()

            return c

        lax.fori_loop(0, per_seq, leave, 0)
        return carry

    lax.fori_loop(0, seqs, sequence, 0)

    for i in range(1, outer):
        o = lax.rem(chip + i, outer)
        w = o * 2 + core
        c_copy(o).wait_recv()
        total = product_tail(w) + core_in[o, tail_rows, :].astype(F32)
        chip_out[i - 1, tail_rows, :] = total.astype(BF16)
        x_copy(i, 0, tail_rows).start()

        def for_chip(n, carry, o=o, w=w, i=i):
            z = dest(n)
            upper, lower = product_rows(w, z)
            at = pl.multiple_of(z * rows, rows)
            high, low = pl.ds(at, hidden), pl.ds(at + hidden, hidden)
            chip_out[i - 1, high, :] = (upper + core_in[o, high, :].astype(F32)).astype(BF16)
            chip_out[i - 1, low, :] = (lower + core_in[o, low, :].astype(F32)).astype(BF16)
            x_copy(i, n, span(z)).start()
            return carry

        lax.fori_loop(1, first + 1, for_chip, 0)

    for z in range(2, first):
        for j in range(1, second):
            k_copy(z, j).start()
    loads[8].wait()
    qkv_part = lax.dot_general(
        out_ref[...], one_ref[...], across, preferred_element_type=F32
    ).astype(BF16)
    for w in range(wid):
        qkv_out[w] = qkv_part[:, w * columns : (w + 1) * columns]
    for i in range(1, wid):
        w_copy(i).start()

    w_own = chip * 2 + core
    c_copy(chip).wait_recv()
    tail_sum[...] = product_tail(w_own) + core_in[chip, tail_rows, :].astype(F32)
    for i in range(1, outer):
        x_copy(i, 0, tail_rows).wait_recv()
        tail_sum[...] += chip_in[i - 1, tail_rows, :].astype(F32)
    for j in range(1, second):
        column = lax.rem(yb + j, second)
        for z in range(first):
            at = pl.ds(pl.multiple_of((z * second + column) * local, local), local)
            turn_out[j, z] = tail_sum[at, :].astype(BF16)
        y_copy(j).start()

    for n in range(9, 12):
        loads[n].wait()
    normed, inverse = normalise(input_ref[...].astype(F32))
    mine = out_ref[pl.ds(pl.multiple_of(me * tok, tok), tok), :]
    total = jnp.dot(mine, pq_ref[me, local:, :], preferred_element_type=F32)
    for k in range(1, nar):
        source = lax.rem(me + k, nar)
        b_copy(source, source).wait_recv()
        total = total + jnp.dot(
            got[source], pq_ref[source, local:, :], preferred_element_type=F32
        )
    grad = above_ref[...] + normalise_back(total, normed, inverse, gain_ref[0:1, :])
    own_ref[...] = grad.astype(BF16)

    for c in range(chunks):
        for z in range(first):

            @pl.when(za == z)
            def _(z=z, c=c):
                for slot, target in enumerate(reach[z]):
                    g_copy(za, target, slot, c, True).start()

        for j in range(1, second):
            h_copy(za, j, c, True).start()
    own_copy = pltpu.make_async_copy(own_ref, all_ref.at[me], own_sem.at[0])
    own_copy.start()
    own_sums[...] = sums_ref[...]
    own_sums[0:1, :] = jnp.sum(total * normed, axis=0, keepdims=True)
    for k in range(1, nar):
        s_copy(k).start()

    def gathered(begin, end):
        for c in range(chunks):
            for d in range(begin, end):
                for way in (-1, 1):
                    z = za + way * d

                    @pl.when((z >= 0) & (z < first))
                    def _(z=z, c=c):
                        g_copy(z, za, 0, c, False).wait_recv()
                        for middle, (target, sources) in relay.items():

                            @pl.when((za == middle) & ((z == sources[0]) | (z == sources[1])))
                            def _(target=target):
                                g_copy(z, target, 0, c, False).start()

                        for j in range(1, second):
                            h_copy(z, j, c, False).start()

    for o in range(outer):
        c_copy(o).wait_send()
    for j in range(1, second):
        y_copy(j).wait_recv()

    def line_parts(n):
        z = dest(n)
        at = pl.ds(pl.multiple_of((z * second + yb) * local, local), local)
        low_part = tail_sum[at, :]
        for j in range(1, second):
            low_part = low_part + turn_in[j, z].astype(F32)
        upper, lower = product_rows(w_own, z)
        start = pl.multiple_of(z * rows, rows)
        high, low = pl.ds(start, hidden), pl.ds(start + hidden, hidden)
        upper = upper + core_in[chip, high, :].astype(F32)
        lower = lower + core_in[chip, low, :].astype(F32)
        for i in range(1, outer):
            x_copy(i, n, span(z)).wait_recv()
            upper = upper + chip_in[i - 1, high, :].astype(F32)
            lower = lower + chip_in[i - 1, low, :].astype(F32)
        work[0:hidden, :] = upper
        work[hidden:rows, :] = lower
        work[rows:, :] = low_part

    def add_arrival(slot):
        z_arrival(slot).wait_recv()
        work[...] += line_in[slot].astype(F32)

    @pl.when(inner == 0)
    def _():
        for n in range(1, 4):
            line_parts(n)
            core_out[0, (n - 1) * line : n * line, :] = work[...].astype(BF16)
            z_copy(n).start()

    gathered(1, 2)
    gathered(2, first)

    @pl.when(inner == 1)
    def _():
        for n in range(1, 4):
            line_parts(n)
            add_arrival((0, 1, 3)[n - 1])
            core_out[0, (n - 1) * line : n * line, :] = work[...].astype(BF16)
            z_copy(n).start()

    line_parts(4)
    sums = own_sums[...]
    for k in range(1, nar):
        s_copy(k).wait_recv()
        sums = sums + all_sums[k]
    piece = total_ref.shape[1]
    for w in range(wid):
        pieces_out[w] = sums[:, w * piece : (w + 1) * piece]
    for w in range(1, wid):
        p_copy(w).start()
    qkv_sum = qkv_out[wide].astype(F32)
    for i in range(1, wid):
        w_copy(i).wait_recv()
        qkv_sum = qkv_sum + qkv_in[i].astype(F32)
    qkv_grad_ref[...] = qkv_sum

    @pl.when(inner == 0)
    def _():
        add_arrival(0)

    @pl.when(inner == 1)
    def _():
        add_arrival(2)
        add_arrival(4)

    in_grad_ref[...] = jnp.transpose(work[0:hidden, :])
    out_grad_ref[...] = work[hidden:rows, :]
    proj_grad_ref[...] = work[rows:, :]
    answer = pieces_out[wide]
    for w in range(1, wid):
        p_copy(w).wait_recv()
        answer = answer + pieces_in[w]
    total_ref[...] = answer

    for z in range(first):
        for j in range(1, second):
            for c in range(chunks):
                h_arrival(z, j, c).wait_recv()
    own_copy.wait()
    for z in range(first):
        for j in range(1, second):
            k_copy(z, j).wait()
    for k in range(1, nar):
        a_copy(lax.rem(me + k, nar), me).wait_send()
        b_copy(lax.rem(me + k, nar), me).wait_send()
        s_copy(k).wait_send()
    for w in range(1, wid):
        p_copy(w).wait_send()
        w_copy(w).wait_send()
    for i in range(1, outer):
        x_copy(i, 0, tail_rows).wait_send()
        for n in range(1, first + 1):
            x_copy(i, n, span(dest(n))).wait_send()
    for j in range(1, second):
        y_copy(j).wait_send()
    for n in range(1, first):
        z_copy(n).wait_send()
    for c in range(chunks):
        for z in range(first):

            @pl.when(za == z)
            def _(z=z, c=c):
                for slot, target in enumerate(reach[z]):
                    g_copy(za, target, slot, c, True).wait_send()
                if z in relay:
                    target, sources = relay[z]
                    for n in sources:
                        g_copy(n, target, 0, c, False).wait_send()

            for j in range(1, second):
                h_copy(z, j, c, False).wait_send()


def attention_grads(
    seg, gain, sums, grads, lines, sides, qkv, lse, one, inputs, above, pq, first, wid, name
):
    nar, tok, local = grads.shape
    rows, wide = qkv.shape
    width = inputs.shape[1]
    seqs, length = seg.shape
    second = nar // first
    outer = wid // 2
    hidden = sides[0].shape[0] // first
    piece = width // wid
    body = first * 2 * hidden + nar * local
    line = 2 * hidden + local
    chunks = 2
    vmem = pl.BlockSpec(memory_space=pltpu.VMEM)
    hbm = pl.BlockSpec(memory_space=pl.ANY)
    dma = pltpu.SemaphoreType.DMA
    late = (*sides, qkv, lse, one, inputs, above, pq)
    return pl.pallas_call(
        functools.partial(
            grad_kernel, nar, first, wid, seqs, local // HD, min(256, length), chunks
        ),
        out_shape=(
            jax.ShapeDtypeStruct((nar, tok, width), BF16),
            jax.ShapeDtypeStruct((nar, tok, width), BF16),
            jax.ShapeDtypeStruct((8, piece), F32),
            jax.ShapeDtypeStruct((piece, hidden), F32),
            jax.ShapeDtypeStruct((hidden, piece), F32),
            jax.ShapeDtypeStruct((local, piece), F32),
            jax.ShapeDtypeStruct((3 * local, piece), F32),
        ),
        in_specs=[vmem] * 3 + [hbm] * 14,
        out_specs=(hbm, hbm) + (vmem,) * 5,
        scratch_shapes=[
            pltpu.VMEM((tok, width) if x is inputs else x.shape, x.dtype) for x in late
        ]
        + [
            dma((12,)),
            pltpu.VMEM((rows, wide), BF16),
            pltpu.VMEM((nar, tok, local), BF16),
            pltpu.VMEM((nar, tok, wide), BF16),
            pltpu.VMEM((length, local), F32),
            pltpu.VMEM((length, local), F32),
            pltpu.VMEM((outer, body, piece), BF16),
            pltpu.VMEM((outer, body, piece), BF16),
            pltpu.VMEM((outer - 1, body, piece), BF16),
            pltpu.VMEM((outer - 1, body, piece), BF16),
            pltpu.VMEM((nar * local, piece), F32),
            pltpu.VMEM((second, first, local, piece), BF16),
            pltpu.VMEM((second, first, local, piece), BF16),
            pltpu.VMEM((5, line, piece), BF16),
            pltpu.VMEM((line, piece), F32),
            pltpu.VMEM((wid, 3 * local, piece), BF16),
            pltpu.VMEM((wid, 3 * local, piece), BF16),
            pltpu.VMEM((tok, width), BF16),
            pltpu.VMEM((8, width), F32),
            pltpu.VMEM((nar, 8, width), F32),
            pltpu.VMEM((wid, 8, piece), F32),
            pltpu.VMEM((wid, 8, piece), F32),
            dma((2,)),
            dma((first, second)),
            dma((first, second)),
            dma((nar,)),
            dma((nar,)),
            dma((nar,)),
            dma((nar,)),
            dma((outer,)),
            dma((outer,)),
            dma((outer, first + 1)),
            dma((outer, first + 1)),
            dma((second,)),
            dma((second,)),
            dma((first,)),
            dma((5,)),
            dma((wid,)),
            dma((wid,)),
            dma((first, 3, chunks)),
            dma((first, chunks)),
            dma((first, second, chunks)),
            dma((first, second, chunks)),
            dma((nar,)),
            dma((nar,)),
            dma((wid,)),
            dma((wid,)),
        ],
        compiler_params=pltpu.CompilerParams(
            collective_id=name, has_side_effects=True, vmem_limit_bytes=63 * 2**20
        ),
    )(seg, gain, sums, grads, lines, *late)


def neighbour_kernel(
    nar,
    first,
    tiles,
    tile,
    kept,
    ring,
    count_ref,
    target_ref,
    base_ref,
    weight_ref,
    temper_ref,
    mix_ref,
    query_ref,
    keys_ref,
    norms_any,
    ids_any,
    grad_ref,
    loss_ref,
    stat_ref,
    queries,
    partial,
    dist,
    grads,
    sends,
    slots,
    loss_own,
    norms_ref,
    ids_ref,
    load_sem,
    slot_sem,
    q_send,
    q_recv,
    d_send,
    d_recv,
    g_send,
    g_recv,
    l_send,
    l_recv,
    o_send,
    o_recv,
):
    second = nar // first
    me = lax.axis_index("z") * second + lax.axis_index("y")
    tok = query_ref.shape[1]
    depth = query_ref.shape[2]
    group = 16
    per_block = tok // tile
    late = tiles - kept

    def peer(k):
        return lax.rem(me + k, nar)

    def origin(k):
        return lax.rem(me + nar - k, nar)

    def load(index, slot):
        block, sub = index // per_block, lax.rem(index, per_block)
        row = origin(block) * tok + sub * tile
        return pltpu.make_async_copy(
            keys_ref.at[pl.ds(row, tile)], slots.at[slot], slot_sem.at[slot]
        )

    loads = [
        pltpu.make_async_copy(norms_any, norms_ref, load_sem.at[0]),
        pltpu.make_async_copy(query_ref.at[me], queries.at[0], load_sem.at[1]),
        pltpu.make_async_copy(ids_any.at[own_rows(tok, second)], ids_ref, load_sem.at[2]),
    ]
    for n in range(3):
        loads[n].start()
    for i in range(kept + ring):
        load(i, i).start()

    greet([place(peer(k), second) for k in range(1, nar)])

    def q_copy(k):
        return push(
            query_ref.at[peer(k)],
            queries.at[k],
            q_send.at[k],
            q_recv.at[k],
            place(peer(k), second),
        )

    def d_copy(k):
        return push(
            partial.at[k], dist.at[k], d_send.at[k], d_recv.at[k], place(origin(k), second)
        )

    def g_copy(k):
        return push(
            grads.at[0], grads.at[k], g_send.at[k], g_recv.at[k], place(peer(k), second)
        )

    def l_copy(k):
        return push(
            loss_own, loss_ref.at[me], l_send.at[k], l_recv.at[k], place(peer(k), second)
        )

    def o_copy(k):
        return push(
            sends.at[k], grad_ref.at[me], o_send.at[k], o_recv.at[k], place(origin(k), second)
        )

    for k in range(1, nar):
        q_copy(k).start()
    for n in range(3):
        loads[n].wait()

    row_of = lax.broadcasted_iota(jnp.int32, (group, J), 0)

    def slot_of(index):
        return jnp.where(index < kept, index, kept + lax.rem(index - kept, ring))

    def slot_late(n):
        return kept + lax.rem(n, ring)

    def forward_tile(k, sub, slot):
        def one(g, carry):
            at = pl.multiple_of(sub * tile + g * group, group)
            own = queries[k, pl.ds(at, group), :].astype(F32)
            keys = slots[slot, pl.ds(g * group, group), :, :].reshape(group * depth, J)
            wide = jnp.concatenate(
                [jnp.where(row_of[:, :depth] == t, own, 0.0) for t in range(group)], axis=1
            ).astype(BF16)
            out = jnp.dot(wide, keys, preferred_element_type=F32)
            row = pl.multiple_of(origin(k) * tok + at, group)
            partial[k, pl.ds(at, group), :] = 2.0 * out - norms_ref[pl.ds(row, group), :]
            return carry

        lax.fori_loop(0, tile // group, one, 0, unroll=True)

    def forward_block(k):
        def body(sub, carry):
            index = k * per_block + sub
            slot = slot_of(index)
            load(index, slot).wait()
            forward_tile(k, sub, slot)

            @pl.when(index >= kept)
            def _():
                nxt = index - kept + ring

                @pl.when(nxt < 2 * late)
                def _():
                    load(kept + lax.rem(nxt, late), slot).start()

            return carry

        lax.fori_loop(0, per_block, body, 0)

    forward_block(0)

    def forward_rest(k, carry):
        q_copy(k).wait_recv()
        forward_block(k)
        d_copy(k).start()
        return carry

    lax.fori_loop(1, nar, forward_rest, 0)

    def collect(k, total):
        d_copy(k).wait_recv()
        return total + dist[k]

    distance = lax.fori_loop(1, nar, collect, partial[0])
    temper_value = temper_ref[0]
    mix_value = mix_ref[0]
    per_seq = count_ref.shape[1] // tok

    def own_column(ref):
        row = jnp.zeros((1, tok), F32)
        for n in range(nar):
            at = (n % per_seq) * tok
            seq = n // per_seq
            row = jnp.where(me == n, ref[seq : seq + 1, at : at + tok].astype(F32), row)
        return jnp.transpose(jnp.broadcast_to(row, (8, tok)))[:, 0:1]

    count = own_column(count_ref)
    target = own_column(target_ref)
    base = own_column(base_ref)
    loss_weight = own_column(weight_ref)
    logits = distance / temper_value
    spot = lax.broadcasted_iota(jnp.int32, (tok, J), 1).astype(F32)
    masked = jnp.where(spot < count, logits, -1e30)
    peak = jnp.max(masked, axis=-1, keepdims=True)
    expo = jnp.exp(masked - peak)
    weights = expo / jnp.sum(expo, axis=-1, keepdims=True)
    matches = jnp.where(ids_ref[...].astype(F32) == target, 1.0, 0.0)
    knn_prob = jnp.sum(weights * matches, axis=-1, keepdims=True)
    mixture = mix_value * knn_prob + (1.0 - mix_value) * base
    grad_mixture = -loss_weight / mixture
    grad_logits = weights * (mix_value * grad_mixture) * (matches - knn_prob)
    grads[0] = (2.0 * grad_logits / temper_value).astype(BF16)
    for k in range(1, nar):
        g_copy(k).start()
    loss = jnp.transpose(jnp.broadcast_to(-jnp.log(mixture), (tok, J)))[0:8, :]
    loss_own[...] = loss
    for k in range(1, nar):
        l_copy(k).start()
    loss_ref[me] = loss
    term_temper = -jnp.sum(grad_logits * logits, axis=0, keepdims=True) / temper_value
    term_mix = jnp.sum((knn_prob - base) * grad_mixture, axis=0, keepdims=True)
    stat_ref[0:1, :] = term_temper
    stat_ref[1:2, :] = jnp.broadcast_to(term_mix, (1, J))

    def backward_tile(k, sub, slot):
        def one(g, carry):
            at = pl.multiple_of(sub * tile + g * group, group)
            own = grads[k, pl.ds(at, group), :]
            keys = slots[slot, pl.ds(g * group, group), :, :].reshape(group * depth, J)
            out = lax.dot_general(
                own, keys, (((1,), (1,)), ((), ())), preferred_element_type=F32
            )
            total = jnp.zeros((group, depth), F32)
            for t in range(group):
                total = jnp.where(
                    row_of[:, :depth] == t, out[:, t * depth : (t + 1) * depth], total
                )
            sends[k, pl.ds(at, group), :] = total.astype(BF16)
            return carry

        lax.fori_loop(0, tile // group, one, 0, unroll=True)

    def backward_block(k):
        def body(sub, carry):
            index = k * per_block + sub

            @pl.when(index < kept)
            def _():
                backward_tile(k, sub, index)

            @pl.when(index >= kept)
            def _():
                n = index - kept + late
                slot = slot_late(n)
                load(index, slot).wait()
                backward_tile(k, sub, slot)

                @pl.when(n + ring < 2 * late)
                def _():
                    load(kept + lax.rem(n + ring, late), slot).start()

            return carry

        lax.fori_loop(0, per_block, body, 0)

    backward_block(0)
    grad_ref[me] = sends[0]

    def backward_rest(k, carry):
        g_copy(k).wait_recv()
        backward_block(k)
        o_copy(k).start()
        return carry

    lax.fori_loop(1, nar, backward_rest, 0)

    for k in range(1, nar):
        q_copy(k).wait_send()
        d_copy(k).wait_send()
        g_copy(k).wait_send()
        l_copy(k).wait()
        o_copy(k).wait()


def neighbours(nar, first, columns, temper, mix, query, keys, norms, ids):
    tok, depth = query.shape[1:]
    rows = keys.shape[0]
    tile = 64
    tiles = rows // tile
    bytes_tile = tile * depth * J * 2
    ring = 6
    kept = min(tiles - 2 * ring, (KEPT_BYTES // bytes_tile))
    vmem = pl.BlockSpec(memory_space=pltpu.VMEM)
    dma = pltpu.SemaphoreType.DMA((nar,))
    return pl.pallas_call(
        functools.partial(neighbour_kernel, nar, first, tiles, tile, kept, ring),
        out_shape=(
            jax.ShapeDtypeStruct((nar, tok, depth), BF16),
            jax.ShapeDtypeStruct((nar, 8, tok), F32),
            jax.ShapeDtypeStruct((2, J), F32),
        ),
        in_specs=[vmem] * 4
        + [pl.BlockSpec(memory_space=pltpu.SMEM)] * 2
        + [pl.BlockSpec(memory_space=pl.ANY)] * 4,
        out_specs=(vmem, vmem, vmem),
        scratch_shapes=[
            pltpu.VMEM((nar, tok, depth), BF16),
            pltpu.VMEM((nar, tok, J), F32),
            pltpu.VMEM((nar, tok, J), F32),
            pltpu.VMEM((nar, tok, J), BF16),
            pltpu.VMEM((nar, tok, depth), BF16),
            pltpu.VMEM((kept + ring, tile, depth, J), BF16),
            pltpu.VMEM((8, tok), F32),
            pltpu.VMEM((rows, J), F32),
            pltpu.VMEM((tok, J), jnp.int32),
            pltpu.SemaphoreType.DMA((3,)),
            pltpu.SemaphoreType.DMA((kept + ring,)),
        ]
        + [dma] * 10,
        compiler_params=pltpu.CompilerParams(
            collective_id=1, has_side_effects=True, vmem_limit_bytes=62 * 2**20
        ),
    )(*columns, temper, mix, query, keys, norms, ids)


def on_device(
    block_input,
    output_cotangent,
    loss_weight,
    segments,
    nbr_keys,
    nbr_count,
    nbr_ids,
    targets,
    base_prob,
    w_query,
    w_key,
    w_value,
    w_proj,
    w_in,
    w_out,
    gain_attn,
    gain_ffn,
    gain_key,
    temper,
    mix_weight,
):
    seqs_here, length, width = block_input.shape
    rows = seqs_here * length
    wid = lax.axis_size("wide")
    first = lax.axis_size("z")
    nar = first * lax.axis_size("y")
    inputs = block_input.reshape(rows, width)
    keys = nbr_keys.reshape(rows, nbr_keys.shape[2], nbr_keys.shape[3])
    gain_one, gain_two, gain_last = (
        gain.reshape(1, width) for gain in (gain_attn, gain_ffn, gain_key)
    )
    normed_one, qkv, lse, part_norms, attended, in_all, out_all, pq_all = head(
        gain_one,
        segments,
        (w_proj, w_query, w_key, w_value),
        inputs,
        keys,
        w_in,
        w_out,
        first,
        nar,
        wid,
        2,
    )
    hidden_one, hidden_two, output_own, query_key, normed_two, pre_act = ffn(
        gain_two, gain_last, attended, inputs, pq_all, in_all, out_all, 3
    )
    grad_slices, losses, stats = neighbours(
        nar,
        first,
        (nbr_count, targets, base_prob, loss_weight),
        temper,
        mix_weight,
        query_key,
        keys,
        part_norms,
        nbr_ids.reshape(rows, -1),
    )
    sums, grad_hidden_one, grad_attended, *sides, lines = ffn_back(
        gain_two,
        gain_last,
        grad_slices,
        stats,
        hidden_two,
        output_cotangent.reshape(rows, width),
        out_all,
        pre_act,
        in_all,
        attended,
        normed_two,
        hidden_one,
        pq_all,
        output_own,
        wid,
        5,
    )
    grad_input, block_output, totals, grad_in, grad_out, grad_proj, grad_qkv = attention_grads(
        segments,
        gain_one,
        sums,
        grad_attended,
        lines,
        sides,
        qkv,
        lse,
        normed_one,
        inputs,
        grad_hidden_one,
        pq_all,
        first,
        wid,
        6,
    )
    results = finish(
        grad_input,
        block_output,
        lines,
        totals,
        losses,
        grad_qkv,
        grad_proj,
        grad_in,
        grad_out,
        seqs_here,
    )
    block_output, token_loss, grad_input, *weights, total_one, total_two, total_last = results[:12]
    piece = width // wid
    return (
        block_output.reshape(seqs_here, length, width),
        token_loss,
        grad_input.reshape(seqs_here, length, width),
        *weights,
        total_one.reshape(piece),
        total_two.reshape(piece),
        total_last.reshape(piece),
        results[12].reshape(1),
        results[13].reshape(1),
    )


def solution(mesh):
    wide, narrow = mesh.devices.shape
    first = 4
    split = jax.sharding.Mesh(
        mesh.devices.reshape(wide, first, narrow // first), ("wide", "z", "y")
    )
    narrow = ("z", "y")
    return jax.shard_map(
        on_device,
        mesh=split,
        in_specs=(
            P("wide", None, None),
            P("wide", None, None),
            P("wide", None),
            P("wide", None),
            P("wide", None, narrow, None),
            P("wide", None),
            P("wide", None, None),
            P("wide", None),
            P("wide", None),
            P(narrow, None),
            P(narrow, None),
            P(narrow, None),
            P(narrow, None),
            P(None, narrow),
            P(narrow, None),
            P(),
            P(),
            P(),
            P(),
            P(),
        ),
        out_specs=(
            P("wide", None, None),
            P("wide", None),
            P("wide", None, None),
            P(narrow, "wide"),
            P(narrow, "wide"),
            P(narrow, "wide"),
            P(narrow, "wide"),
            P("wide", narrow),
            P(narrow, "wide"),
            P("wide"),
            P("wide"),
            P("wide"),
            P(),
            P(),
        ),
        check_vma=False,
    )
```
